32 devices in a mesh: groups: 2 (over y), head: 4 (over z), req: 2 (over x), seq: 2 (over core).
Axes of the slice: x: 2, y: 2, z: 4, core: 2. Of those that a mesh axis runs over, the one named last changes fastest.
Arguments:
- queries: bfloat16 [4, 256, 6144], P(('groups', 'req'), 'seq', 'head'), parts along dimension 0, may hold values from -400 to 400
- hidden: bfloat16 [4, 256, 7168], P(('groups', 'req'), 'seq', 'head'), parts along dimension 0, may hold values from -6 to 6
- w_dkv: bfloat16 [7168, 576], P('head'), may hold values from -0.0625 to 0.0625
- kv_gain: float32 [512], replicated, may hold values from 0.1 to 1.9
- w_uk: bfloat16 [32, 128, 512], P('head'), may hold values from -0.5 to 0.5
- value_up_weight: bfloat16 [32, 512, 128], P('head'), may hold values from -0.25 to 0.25
- page_pool: bfloat16 [512, 36864], P(('groups', 'head', 'req')), parts along dimension 0, may hold values from -6 to 6
- page_owner: int32 [4, 64, 1], P('groups'), parts along dimension 0, may hold values from 0 to 7; in each aligned block of 64 rows (0 to 63, 64 to 127, ..., all dimensions but the last counted through in order) at most 16 rows name the same one
- page_slot: int32 [4, 64], P('groups'), parts along dimension 0, may hold values from 0 to 31
- prefix_len: int32 [4], P('groups'), parts along dimension 0, may hold values from 64 to 4096, as said below
- suffix_len: int32 [4], P('groups'), parts along dimension 0, may hold values from 128 to 256, as said below
Outputs:
- attn_out: bfloat16 [4, 256, 4096], P(('groups', 'req'), 'seq', 'head'), parts along dimension 0
- new_pages: bfloat16 [4, 4, 36864], P(('groups', 'req'), 'seq'), parts along dimension 0
The draws below stay inside these ranges and needn't reach their ends.
There are 2 independent parts, one for each index of `groups`. The reference program is written for one: setup_inputs(seed, part) draws one part's arguments, and reference() takes and returns one part's arrays. A program takes and returns all parts, laid end to end along the dimension named above; an argument that names none is the same for every part. Nothing has to cross between parts.
Inputs may be any that keep to these rules, and one draw needn't show every extreme that they name: `page_owner`: in the rows of one request batch (1 request) no owner holds more than 16 pages, and some owner holds exactly 16. `prefix_len`: some request has the longest prefix. `suffix_len`: some request fills all suffix slots.
All inputs are finite; a program needn't handle non-finite values.
Results may differ from the reference program's by a relative error of at most 0.0055.
The reference program's roundings to bfloat16 on the way count: a program that leaves them out, or rounds other values in their place, can miss the bound.
Values may be sent and summed in bfloat16 or wider, within the bound.
No kernel may reach another device: no remote copies, remote signals or barrier semaphores. Data moves between devices by JAX's collectives and lax.ppermute only.
A program may use at most 128 MiB of HBM per device.

```python
import math
import jax
import jax.numpy as jnp
import numpy as np
from jax import lax

D = 7168
KVL = 512
ROPE = 64
NOPE = 128
VALUE_EXTENT = 128
PAGE = 64
REQ_DEV = 1
SUFFIX_SLOTS = 256
PAGES_REQ = 64
POOL_DEV = 32
HEAD_TOTAL = 32
LAT = 576
REQ = 2
CAP = 16
N_HEAD = 4
N_REQ = 2


def draw_queries(key, part):
    key = jax.random.fold_in(key, 11)
    starting_sample = jax.random.truncated_normal(key, -6.0, 6.0, (REQ, SUFFIX_SLOTS, HEAD_TOTAL * (NOPE + ROPE)), jnp.float32)
    return starting_sample.astype(jnp.bfloat16)


def draw_prefix_len(key, part):
    key = jax.random.fold_in(key, 21)
    lengths = jax.random.randint(key, (REQ,), PAGE, PAGES_REQ * PAGE + 1)
    longest = jax.random.randint(jax.random.fold_in(key, 2), (), 0, REQ)
    places = jnp.arange(REQ)
    lengths = jnp.where(places == longest, PAGES_REQ * PAGE, lengths)
    return lengths.astype(jnp.int32)


def draw_suffix_len(key, part):
    key = jax.random.fold_in(key, 31)
    lengths = jax.random.randint(key, (REQ,), SUFFIX_SLOTS // 2, SUFFIX_SLOTS + 1)
    longest = jax.random.randint(jax.random.fold_in(key, 2), (), 0, REQ)
    places = jnp.arange(REQ)
    lengths = jnp.where(places == longest, SUFFIX_SLOTS, lengths)
    return lengths.astype(jnp.int32)


def place_ends(drawn, rng, smallest, top_value):
    shape = drawn.shape
    place = [jax.random.randint(jax.random.fold_in(rng, axis), (), 0, shape[axis]) for axis in range(len(shape))]
    drawn = drawn.at[tuple(place)].set(smallest)
    longest = shape.index(max(shape))
    place[longest] = (place[longest] + 1) % shape[longest]
    return drawn.at[tuple(place)].set(top_value)


def steps_of(own_key, shape, pieces, smallest, largest):
    gain = 1.0
    for dim, parts in pieces:
        heights = jax.random.uniform(jax.random.fold_in(jax.random.fold_in(own_key, 6), dim), (parts,), jnp.float32, smallest / len(pieces), largest / len(pieces))
        gain = gain * jnp.repeat(jnp.exp(heights), shape[dim] // parts).reshape((-1,) + (1,) * (len(shape) - 1 - dim))
    return gain


def assign_block(key, own, number, rows, number_of, top, most, slope):
    order = jax.random.permutation(key, number_of)
    crowded, common = shares(number_of, rows * top, most, slope, True), shares(number_of, rows * top, most, slope, False)
    places = jnp.arange(number_of)

    def named(sizes, turn):
        used = int((sizes > 0).sum())
        fixed = max(1, used // 4)
        shifted = fixed + (places - fixed + turn * (used - fixed)) % max(1, number_of - fixed)
        return jnp.zeros((number_of,), jnp.int32).at[order[jnp.where(places < fixed, places, shifted)]].set(jnp.asarray(sizes, jnp.int32))

    sizes = jnp.where(number % 4 == 0, named(crowded, number // 4), named(common, number - number // 4 - 1))
    mixed = jax.random.permutation(jax.random.fold_in(own, 3), number_of)
    donor, taker = mixed[0:number_of // 2 * 2:2], mixed[1:number_of // 2 * 2:2]
    slack = jnp.minimum(sizes[donor] - 1, most - sizes[taker]) // 2
    slack = jnp.where((donor == order[0]) | (taker == order[0]) | (sizes[taker] == 0), 0, jnp.maximum(slack, 0))
    shifted = jax.random.randint(jax.random.fold_in(own, 4), (number_of // 2,), 0, 1 << 20) % (slack + 1)
    sizes = sizes.at[donor].add(-shifted).at[taker].add(shifted)
    members = jnp.searchsorted(jnp.cumsum(sizes), jnp.arange(rows * top), side="right").astype(jnp.int32)
    table = members.reshape(top, rows).T
    table = table[jax.random.permutation(jax.random.fold_in(own, 1), rows)]
    turn = jax.random.randint(jax.random.fold_in(own, 2), (rows, 1), 0, top)
    return jnp.take_along_axis(table, (jnp.arange(top)[None, :] + turn) % top, axis=1)


def shares(count, total, limit, skew, full):
    loads = [(1 << 20) // math.isqrt(rank ** skew) + 1 for rank in range(1, count + 1)]
    largest = limit if full else min(limit, max(-(-total // count), total * loads[0] // sum(loads)))
    least = 1 if total - largest >= count - 1 else 0
    given, rest = [largest] + [least] * (count - 1), total - largest - least * (count - 1)
    while rest > 0:
        candidates = [i for i in range(1, count) if given[i] < largest] or [i for i in range(1, count) if given[i] < limit]
        pool, left = sum([loads[i] for i in candidates]), rest
        for i in candidates:
            extra = min(limit - given[i], max(1, left * loads[i] // pool), rest)
            given[i] = given[i] + extra
            rest = rest - extra
    return np.array(given)


def normal_values(rng, dims, deviation, reach, cuts=(), kind=jnp.bfloat16):
    level = steps_of(rng, dims, cuts, -0.22, 0.18) if cuts else 1.0
    drawn = jax.random.normal(rng, dims, jnp.float32) * deviation * level
    return jnp.minimum(jnp.maximum(drawn, -reach), reach).astype(kind)


def setup_inputs(seed: int = 0, part: int = 0) -> dict:
    splits = jax.random.split(jax.random.key(seed), 12)
    part_splits = jax.random.split(jax.random.fold_in(splits[11], part), 12)
    queries = draw_queries(jax.random.fold_in(jax.random.fold_in(splits[11], part), 71), part)
    hidden = normal_values(part_splits[1], (REQ, SUFFIX_SLOTS, D), 1.0, 6.0, ((0, 2), (1, 2), (2, 4)))
    w_dkv = normal_values(splits[2], (D, LAT), D ** -0.5, 0.0625, ((0, 4),))
    kv_gain = jnp.clip(1.0 + 0.18 * jax.random.normal(splits[3], (KVL,), jnp.float32), 0.1, 1.9)
    w_uk = normal_values(splits[4], (HEAD_TOTAL, NOPE, KVL), NOPE ** -0.5, 0.5, ((0, 4),))
    value_up_weight = normal_values(splits[5], (HEAD_TOTAL, KVL, VALUE_EXTENT), KVL ** -0.5, 0.25, ((0, 4),))
    page_pool = normal_values(part_splits[6], (N_HEAD * N_REQ * POOL_DEV, PAGE * LAT), 1.0, 6.0, ((0, 8),))
    page_owner_keys = jax.random.split(jax.random.fold_in(part_splits[7], 1), REQ * PAGES_REQ // (REQ_DEV * PAGES_REQ))
    page_owner_turns = jax.random.permutation(jax.random.fold_in(part_splits[7], 3), REQ * PAGES_REQ // (REQ_DEV * PAGES_REQ))
    page_owner = jax.vmap(lambda own, number: assign_block(jax.random.fold_in(part_splits[7], 2), own, number, REQ_DEV * PAGES_REQ, N_HEAD * N_REQ, 1, CAP, 1))(page_owner_keys, page_owner_turns).reshape((REQ, PAGES_REQ, 1))
    page_slot = place_ends(jax.random.randint(part_splits[8], (REQ, PAGES_REQ), 0, POOL_DEV), jax.random.fold_in(part_splits[8], 1), 0, POOL_DEV - 1).astype(jnp.int32)
    prefix_len = draw_prefix_len(jax.random.fold_in(jax.random.fold_in(splits[11], part), 71), part)
    suffix_len = draw_suffix_len(jax.random.fold_in(jax.random.fold_in(splits[11], part), 71), part)
    return dict(queries=queries, hidden=hidden, w_dkv=w_dkv, kv_gain=kv_gain, w_uk=w_uk, value_up_weight=value_up_weight, page_pool=page_pool, page_owner=page_owner, page_slot=page_slot, prefix_len=prefix_len, suffix_len=suffix_len)


def rotate(vector, cosine_table, sine_table):
    half_width = vector.shape[-1] // 2
    first_half = vector[..., :half_width]
    second_half = vector[..., half_width:]
    return jnp.concatenate([first_half * cosine_table - second_half * sine_table, first_half * sine_table + second_half * cosine_table], axis=-1)

def angles(positions, rope_width):
    half_width = rope_width // 2
    frequency = 10000.0 ** (-2.0 * jnp.arange(half_width, dtype=jnp.float32) / rope_width)
    phases = positions.astype(jnp.float32)[:, None] * frequency[None, :]
    return (jnp.cos(phases), jnp.sin(phases))

def finish_latent(summed, positions, live_rows, kv_gain, latent_width):
    latent_part = summed[:, :latent_width]
    mean_square = lax.optimization_barrier(jnp.mean(latent_part * latent_part, axis=-1, keepdims=True))
    normed = latent_part * lax.rsqrt(mean_square + 1e-06) * kv_gain
    cosine_table, sine_table = angles(positions, summed.shape[1] - latent_width)
    rotated = rotate(summed[:, latent_width:], cosine_table, sine_table)
    joined = jnp.concatenate([normed, rotated], axis=-1).astype(jnp.bfloat16)
    return jnp.where(live_rows[:, None], joined, jnp.zeros_like(joined))

def reference(queries, hidden, w_dkv, kv_gain, w_uk, value_up_weight, page_pool, page_owner, page_slot, prefix_len, suffix_len):
    lat_width = KVL + ROPE
    score_scale = float(NOPE + ROPE) ** (-0.5)
    suffix_steps = jnp.arange(SUFFIX_SLOTS, dtype=jnp.int32)
    positions = prefix_len[:, None] + suffix_steps[None, :]
    live_rows = suffix_steps[None, :] < suffix_len[:, None]
    summed = jnp.dot(hidden.reshape(REQ * SUFFIX_SLOTS, D), w_dkv, preferred_element_type=jnp.float32)
    fresh_latent = finish_latent(summed, positions.reshape(-1), live_rows.reshape(-1), kv_gain, KVL).reshape(REQ, SUFFIX_SLOTS, lat_width)
    new_pages = fresh_latent.reshape(REQ, SUFFIX_SLOTS // PAGE, PAGE * lat_width)
    prefix_width = PAGES_REQ * PAGE
    key_places = jnp.arange(prefix_width + SUFFIX_SLOTS, dtype=jnp.int32)
    suffix_places = key_places - prefix_width

    def one_request(number):
        pool_rows = page_owner[number, :, 0] * POOL_DEV + page_slot[number]
        cached = page_pool[pool_rows].reshape(prefix_width, lat_width)
        key_latent = jnp.concatenate([cached, fresh_latent[number]], axis=0)
        query_rows = queries[number].reshape(SUFFIX_SLOTS, HEAD_TOTAL, NOPE + ROPE)
        q_latent = jnp.einsum('thn,hnk->thk', query_rows[..., :NOPE].astype(jnp.float32), w_uk.astype(jnp.float32)).astype(jnp.bfloat16)
        cosine_table, sine_table = angles(positions[number], ROPE)
        q_rotated = rotate(query_rows[..., NOPE:].astype(jnp.float32), cosine_table[:, None, :], sine_table[:, None, :]).astype(jnp.bfloat16)
        q_full = jnp.concatenate([q_latent, q_rotated], axis=-1)
        scores = jnp.einsum('thk,jk->htj', q_full.astype(jnp.float32), key_latent.astype(jnp.float32)) * score_scale
        allowed = jnp.where(key_places[None, :] < prefix_width, key_places[None, :] < prefix_len[number], (suffix_places[None, :] <= suffix_steps[:, None]) & (suffix_places[None, :] < suffix_len[number]))
        scores = jnp.where(allowed[None], scores, -jnp.inf)
        row_max = lax.optimization_barrier(jnp.max(scores, axis=-1, keepdims=True))
        exponent = jnp.exp(scores - row_max)
        weights = (exponent / lax.optimization_barrier(jnp.sum(exponent, axis=-1, keepdims=True))).astype(jnp.bfloat16)
        output_latent = jnp.einsum('htj,jk->thk', weights.astype(jnp.float32), key_latent[:, :KVL].astype(jnp.float32)).astype(jnp.bfloat16)
        per_head_output = jnp.einsum('wsd,sdp->wsp', output_latent.astype(jnp.float32), value_up_weight.astype(jnp.float32)).reshape(SUFFIX_SLOTS, HEAD_TOTAL * VALUE_EXTENT)
        return jnp.where(live_rows[number][:, None], per_head_output, jnp.zeros_like(per_head_output)).astype(jnp.bfloat16)
    attn_out = lax.map(one_request, jnp.arange(REQ, dtype=jnp.int32))
    return (attn_out, new_pages)
```

```python
import jax
import jax.numpy as jnp
from jax import lax
from jax.sharding import PartitionSpec as P


def from_behind(block, axis, distance):
    devices = range(lax.axis_size(axis))
    route = [(i - distance, i) for i in devices if i - distance in devices]
    return lax.ppermute(block, axis, route)


def rotate(vector, cosine_table, sine_table):
    half_width = vector.shape[-1] // 2
    first_half = vector[..., :half_width]
    second_half = vector[..., half_width:]
    return jnp.concatenate(
        [
            first_half * cosine_table - second_half * sine_table,
            first_half * sine_table + second_half * cosine_table,
        ],
        axis=-1,
    )


def angles(positions, rope_width):
    half_width = rope_width // 2
    frequency = 10000.0 ** (-2.0 * jnp.arange(half_width, dtype=jnp.float32) / rope_width)
    phases = positions.astype(jnp.float32)[:, None] * frequency[None, :]
    return (jnp.cos(phases), jnp.sin(phases))


def finish_latent(summed, positions, live_rows, kv_gain, latent_width):
    latent_part = summed[:, :latent_width]
    mean_square = jnp.mean(latent_part * latent_part, axis=-1, keepdims=True)
    normed = latent_part * lax.rsqrt(mean_square + 1e-06) * kv_gain
    cosine_table, sine_table = angles(positions, summed.shape[1] - latent_width)
    rotated = rotate(summed[:, latent_width:], cosine_table, sine_table)
    joined = jnp.concatenate([normed, rotated], axis=-1).astype(jnp.bfloat16)
    return jnp.where(live_rows[:, None], joined, jnp.zeros_like(joined))


def local(
    queries,
    hidden,
    w_dkv,
    kv_gain,
    w_uk,
    value_up_weight,
    page_pool,
    page_owner,
    page_slot,
    prefix_len,
    suffix_len,
):
    n_head = lax.axis_size("head")
    n_req = lax.axis_size("req")
    head_idx = lax.axis_index("head")
    req_idx = lax.axis_index("req")
    seq_idx = lax.axis_index("seq")
    req_dev, half_len, d_local = hidden.shape
    heads_dev, nope_width, latent_width = w_uk.shape
    value_width = value_up_weight.shape[2]
    lat_width = w_dkv.shape[1]
    rope_width = lat_width - latent_width
    query_width = queries.shape[2] // heads_dev
    page_width = page_pool.shape[1]
    page_len = page_width // lat_width
    pages_req = page_slot.shape[1]
    batch_rows = req_dev * pages_req
    owners = n_head * n_req
    slot_cap = max(2, 2 * batch_rows // owners)
    score_scale = float(query_width) ** (-0.5)
    my_prefix = lax.dynamic_slice_in_dim(prefix_len, req_idx * req_dev, req_dev)
    my_suffix = lax.dynamic_slice_in_dim(suffix_len, req_idx * req_dev, req_dev)
    local_t = jnp.arange(half_len, dtype=jnp.int32)
    glob_t = seq_idx * half_len + local_t
    positions = my_prefix[:, None] + glob_t[None, :]
    live_rows = glob_t[None, :] < my_suffix[:, None]
    partial_value = jnp.dot(
        hidden.reshape(req_dev * half_len, d_local), w_dkv, preferred_element_type=jnp.float32
    )
    summed = lax.psum(partial_value, "head")
    new_flat = finish_latent(
        summed, positions.reshape(-1), live_rows.reshape(-1), kv_gain, latent_width
    )
    fresh_latent = new_flat.reshape(req_dev, half_len, lat_width)
    new_pages = fresh_latent.reshape(req_dev, half_len // page_len, page_len * lat_width)
    earlier = from_behind(fresh_latent, "seq", 1)
    owner_rows = page_owner[:, :, 0]
    row_order = jnp.arange(batch_rows, dtype=jnp.int32)
    before = row_order[None, :] < row_order[:, None]
    same_owner = owner_rows[:, :, None] == owner_rows[:, None, :]
    owner_rank = jnp.sum((same_owner & before[None]).astype(jnp.int32), axis=2)
    self_owner = head_idx * n_req + req_idx
    slot_ids = jnp.arange(slot_cap, dtype=jnp.int32)
    picked = (owner_rows == self_owner)[:, None, :] & (
        owner_rank[:, None, :] == slot_ids[None, :, None]
    )
    chosen = jnp.sum(jnp.where(picked, page_slot[:, None, :], 0), axis=2)
    present = jnp.any(picked, axis=2)
    n_seq = lax.axis_size("seq")
    part_width = page_width // n_seq
    part_pool = lax.dynamic_slice_in_dim(page_pool, seq_idx * part_width, part_width, axis=1)
    outgoing = jnp.where(present[:, :, None], part_pool[chosen], jnp.zeros((), page_pool.dtype))
    arrived = lax.all_to_all(outgoing, "req", split_axis=0, concat_axis=0, tiled=True)
    received = lax.all_gather(arrived, ("head", "seq"), axis=0, tiled=False)
    received = received.reshape(n_head, n_seq, n_req * slot_cap, part_width)
    received = jnp.swapaxes(received, 1, 2).reshape(owners * slot_cap, n_seq, part_width)
    own_owner = lax.dynamic_index_in_dim(owner_rows, req_idx, 0, keepdims=False)
    own_rank = lax.dynamic_index_in_dim(owner_rank, req_idx, 0, keepdims=False)
    cached = received[own_owner * slot_cap + own_rank]
    prefix_width = pages_req * page_len
    cached = cached.reshape(req_dev, prefix_width, lat_width)
    key_places = jnp.arange(prefix_width, dtype=jnp.int32)
    suffix_places = jnp.concatenate([(seq_idx - 1) * half_len + local_t, glob_t], axis=0)
    key_latent = jnp.concatenate([cached[0], earlier[0], fresh_latent[0]], axis=0)
    query_rows = queries[0].reshape(half_len, heads_dev, query_width)
    q_latent = jnp.einsum(
        "thn,hnk->thk", query_rows[..., :nope_width], w_uk, preferred_element_type=jnp.float32
    ).astype(jnp.bfloat16)
    cosine_table, sine_table = angles(positions[0], rope_width)
    q_rotated = rotate(
        query_rows[..., nope_width:].astype(jnp.float32),
        cosine_table[:, None, :],
        sine_table[:, None, :],
    ).astype(jnp.bfloat16)
    q_full = jnp.concatenate([q_latent, q_rotated], axis=-1)
    scores = (
        jnp.einsum("thk,jk->htj", q_full, key_latent, preferred_element_type=jnp.float32)
        * score_scale
    )
    far_allowed = jnp.broadcast_to(key_places[None, :] < my_prefix[0], (half_len, prefix_width))
    near_allowed = (
        (suffix_places[None, :] >= 0)
        & (suffix_places[None, :] <= glob_t[:, None])
        & (suffix_places[None, :] < my_suffix[0])
    )
    allowed = jnp.concatenate([far_allowed, near_allowed], axis=1)
    scores = jnp.where(allowed[None], scores, -jnp.inf)
    row_max = jnp.max(scores, axis=-1, keepdims=True)
    exponent = jnp.exp(scores - row_max)
    weights = (exponent / jnp.sum(exponent, axis=-1, keepdims=True)).astype(jnp.bfloat16)
    output_latent = jnp.einsum(
        "htj,jk->thk", weights, key_latent[:, :latent_width], preferred_element_type=jnp.float32
    ).astype(jnp.bfloat16)
    per_head_output = jnp.einsum(
        "wsd,sdp->wsp", output_latent, value_up_weight, preferred_element_type=jnp.float32
    ).reshape(half_len, heads_dev * value_width)
    outputs = [
        jnp.where(live_rows[0][:, None], per_head_output, jnp.zeros_like(per_head_output)).astype(
            jnp.bfloat16
        )
    ]
    attn_out = jnp.stack(outputs, axis=0)
    return (attn_out, new_pages)


def solution(mesh):
    placed = (
        P(("groups", "req"), "seq", "head"),
        P(("groups", "req"), "seq", "head"),
        P("head", None),
        P(),
        P("head", None, None),
        P("head", None, None),
        P(("groups", "head", "req"), None),
        P("groups", None, None),
        P("groups", None),
        P("groups"),
        P("groups"),
    )
    return jax.shard_map(
        local,
        mesh=mesh,
        in_specs=placed,
        out_specs=(P(("groups", "req"), "seq", "head"), P(("groups", "req"), "seq", None)),
        check_vma=False,
    )
```

```python
import functools
import math

import jax
import jax.numpy as jnp
from jax import lax
from jax.experimental import pallas as pl
from jax.experimental.pallas import tpu as pltpu
from jax.sharding import PartitionSpec as P

LOWEST = -1e30
VMEM_LIMIT = 48 * 1024 * 1024


def from_behind(block, axis, distance):
    devices = range(lax.axis_size(axis))
    route = [(i - distance, i) for i in devices if i - distance in devices]
    return lax.ppermute(block, axis, route)


def rotate(vector, cosine_table, sine_table):
    half_width = vector.shape[-1] // 2
    first_half = vector[..., :half_width]
    second_half = vector[..., half_width:]
    return jnp.concatenate(
        [
            first_half * cosine_table - second_half * sine_table,
            first_half * sine_table + second_half * cosine_table,
        ],
        axis=-1,
    )


def angles(positions, rope_width):
    half_width = rope_width // 2
    frequency = 10000.0 ** (-2.0 * jnp.arange(half_width, dtype=jnp.float32) / rope_width)
    phases = positions.astype(jnp.float32)[:, None] * frequency[None, :]
    return (jnp.cos(phases), jnp.sin(phases))


def finish_latent(summed, positions, live_rows, kv_gain, latent_width):
    latent_part = summed[:, :latent_width]
    mean_square = jnp.mean(latent_part * latent_part, axis=-1, keepdims=True)
    normed = latent_part * lax.rsqrt(mean_square + 1e-06) * kv_gain
    cosine_table, sine_table = angles(positions, summed.shape[1] - latent_width)
    rotated = rotate(summed[:, latent_width:], cosine_table, sine_table)
    joined = jnp.concatenate([normed, rotated], axis=-1).astype(jnp.bfloat16)
    return jnp.where(live_rows[:, None], joined, jnp.zeros_like(joined))


def any_spec():
    return pl.BlockSpec(memory_space=pl.ANY)


def smem_spec():
    return pl.BlockSpec(memory_space=pltpu.SMEM)


def vmem_spec():
    return pl.BlockSpec(memory_space=pltpu.VMEM)


def pick_kernel(cap, owner_ref, slot_ref, pool_ref, count_ref, own_ref, foreign_ref, pages, lists, sems):
    n_req = lax.axis_size("req")
    head_idx = lax.axis_index("head")
    req_idx = lax.axis_index("req")
    seq_idx = lax.axis_index("seq")
    n_pages = owner_ref.shape[1]
    pool_pages, pairs, pair_width = pages.shape
    step = 16
    row = lax.broadcasted_iota(jnp.int32, (step * step, step * step), 0)
    column = lax.broadcasted_iota(jnp.int32, (step * step, step * step), 1)
    swap = ((row // step == column % step) & (row % step == column // step)).astype(jnp.bfloat16)
    for page in range(0, pool_pages, step):
        for pair in range(0, pairs, step):
            rows = jnp.concatenate(
                [
                    pool_ref[page : page + step, (pair + i) * pair_width : (pair + i + 1) * pair_width]
                    for i in range(step)
                ],
                axis=0,
            )
            turned = jnp.dot(swap, rows, preferred_element_type=jnp.float32).astype(jnp.bfloat16)
            pages[page : page + step, pair : pair + step, :] = turned.reshape(step, step, pair_width)
    self_owner = head_idx * n_req + req_idx
    for shift in range(n_req):
        request = lax.rem(req_idx + shift, n_req)

        def note(page, found, shift=shift, request=request):
            lists[shift, found] = slot_ref[request, page]
            return found + (owner_ref[request, page] == self_owner).astype(jnp.int32)

        found = lax.fori_loop(0, n_pages, note, jnp.int32(0), unroll=8)
        ranks = cap if shift == 0 else foreign_ref.shape[1]
        first = 0 if shift == 0 else seq_idx * ranks
        for j in range(ranks):
            rank = first + j
            slot = jnp.where(rank < found, lists[shift, rank], 0)
            target = own_ref.at[j] if shift == 0 else foreign_ref.at[shift - 1, j]
            pltpu.make_async_copy(pages.at[slot], target, sems.at[min(shift, 1)]).start()

    def tally(page, counts):
        owner = owner_ref[req_idx, page]
        return tuple(
            counts[shift]
            + (owner == head_idx * n_req + lax.rem(req_idx + n_req - shift, n_req)).astype(jnp.int32)
            for shift in range(n_req)
        )

    counts = lax.fori_loop(0, n_pages, tally, (jnp.int32(0),) * n_req, unroll=8)
    for shift in range(n_req):
        count_ref[shift] = counts[shift]
    pltpu.make_async_copy(own_ref, own_ref, sems.at[0]).wait()
    pltpu.make_async_copy(foreign_ref, foreign_ref, sems.at[1]).wait()


def pick_pages(page_owner, page_slot, page_pool, cap, n_req, n_seq, pairs):
    pool_pages, page_width = page_pool.shape
    pair_width = page_width // pairs
    page = (pairs, pair_width)
    return pl.pallas_call(
        functools.partial(pick_kernel, cap),
        out_shape=(
            jax.ShapeDtypeStruct((n_req,), jnp.int32),
            jax.ShapeDtypeStruct((cap, *page), jnp.bfloat16),
            jax.ShapeDtypeStruct((n_req - 1, cap // n_seq, *page), jnp.bfloat16),
        ),
        in_specs=[smem_spec(), smem_spec(), vmem_spec()],
        out_specs=(smem_spec(), any_spec(), any_spec()),
        scratch_shapes=[
            pltpu.VMEM((pool_pages, *page), jnp.bfloat16),
            pltpu.SMEM((n_req, cap + 1), jnp.int32),
            pltpu.SemaphoreType.DMA((2,)),
        ],
        compiler_params=pltpu.CompilerParams(vmem_limit_bytes=VMEM_LIMIT),
        cost_estimate=pl.CostEstimate(flops=10**9, bytes_accessed=6 * 10**6, transcendentals=0),
        name="pick_pages",
    )(page_owner, page_slot, page_pool)


def join_kernel(chunk, count_ref, own_ref, mine_ref, other_ref, joined_ref, first_ref, second_ref, sems):
    seq_idx = lax.axis_index("seq")
    n_req = count_ref.shape[0]
    half_cap = mine_ref.shape[1]
    for j in range(joined_ref.shape[0]):
        targets = [(joined_ref.at[j], sems.at[0])]
        if j < chunk:
            targets.append((first_ref.at[j], sems.at[1]))
        elif j < 2 * chunk:
            targets.append((second_ref.at[j - chunk], sems.at[2]))

        def fetch(condition, source):
            @pl.when(condition)
            def _():
                for target, sem in targets:
                    pltpu.make_async_copy(source, target, sem).start()

        rank = jnp.int32(j)
        taken = rank < count_ref[0]
        fetch(taken, own_ref.at[jnp.minimum(rank, own_ref.shape[0] - 1)])
        rank = rank - count_ref[0]
        for shift in range(1, n_req):
            here = jnp.logical_not(taken) & (rank < count_ref[shift])
            place = jnp.clip(lax.rem(rank, half_cap), 0, half_cap - 1)
            local = rank // half_cap == seq_idx
            fetch(here & local, mine_ref.at[shift - 1, place])
            fetch(here & jnp.logical_not(local), other_ref.at[shift - 1, place])
            taken = taken | here
            rank = rank - count_ref[shift]
        fetch(jnp.logical_not(taken), own_ref.at[0])
    for i, ref in enumerate((joined_ref, first_ref, second_ref)):
        pltpu.make_async_copy(ref, ref, sems.at[i]).wait()


def join_pages(counts, own, mine, other, chunk):
    page = own.shape[1:]
    return pl.pallas_call(
        functools.partial(join_kernel, chunk),
        out_shape=(
            jax.ShapeDtypeStruct((4 * chunk, *page), jnp.bfloat16),
            jax.ShapeDtypeStruct((chunk, *page), jnp.bfloat16),
            jax.ShapeDtypeStruct((chunk, *page), jnp.bfloat16),
        ),
        in_specs=[smem_spec(), any_spec(), any_spec(), any_spec()],
        out_specs=(any_spec(), any_spec(), any_spec()),
        scratch_shapes=[pltpu.SemaphoreType.DMA((3,))],
        cost_estimate=pl.CostEstimate(flops=0, bytes_accessed=6 * 10**6, transcendentals=0),
        name="join_pages",
    )(counts, own, mine, other)


def queue_kernel(step, chunk, earliest, held_ref, joined_ref, *refs):
    arrived, target_ref, sem = refs[:-2], refs[-2], refs[-1]
    held = held_ref[0]
    offset = jnp.maximum(held, 2 * chunk)
    for j in range(chunk):
        entry = step * chunk + j

        def fetch(condition, source, j=j):
            @pl.when(condition)
            def _():
                pltpu.make_async_copy(source, target_ref.at[j], sem).start()

        taken = entry < held
        if entry < joined_ref.shape[0]:
            fetch(taken, joined_ref.at[entry])
        place = entry - offset - earliest * chunk
        for i, source in enumerate(arrived):
            here = (place >= i * chunk) & (place < (i + 1) * chunk)
            fetch(here, source.at[jnp.clip(place - i * chunk, 0, chunk - 1)])
            taken = taken | here
        fetch(jnp.logical_not(taken), joined_ref.at[0])
    pltpu.make_async_copy(target_ref, target_ref, sem).wait()


def queue_chunk(step, held, joined, arrived):
    chunk = joined.shape[0] // 4
    earliest = max(0, step - 4)
    sources = arrived[earliest : step - 1]
    return pl.pallas_call(
        functools.partial(queue_kernel, step, chunk, earliest),
        out_shape=jax.ShapeDtypeStruct((chunk, *joined.shape[1:]), jnp.bfloat16),
        in_specs=[smem_spec()] + [any_spec()] * (1 + len(sources)),
        out_specs=any_spec(),
        scratch_shapes=[pltpu.SemaphoreType.DMA],
        cost_estimate=pl.CostEstimate(flops=0, bytes_accessed=10**6, transcendentals=0),
        name="queue_chunk",
    )(held, joined, *sources)


def token_limits(owners, prefix, head_idx, req_idx, seq_idx, n_head, n_req, chunk, steps, page_len):
    pages = owners.shape[0]
    order = jnp.arange(pages, dtype=jnp.int32)
    place = owners // n_req
    key = lax.rem(req_idx + n_req - lax.rem(owners, n_req), n_req) * pages + order
    ahead = (place[None, :] == place[:, None]) & (key[None, :] < key[:, None])
    rank = jnp.sum(ahead.astype(jnp.int32), axis=1)
    heads = jnp.arange(n_head, dtype=jnp.int32)
    held = jnp.sum((place[None, :] == heads[:, None]).astype(jnp.int32), axis=1)
    widths = jnp.maximum(held, 2 * chunk)

    def before(position):
        return jnp.sum(jnp.where(heads[None, :] < position[:, None], widths[None, :], 0), axis=1)

    here = jnp.full((pages,), head_idx, jnp.int32)
    upward = rank + before(here) - before(place + 1)
    downward = rank + before(place) - before(here + 1)
    up_base = 4 * chunk + seq_idx * steps * chunk
    down_base = 4 * chunk + (1 - seq_idx) * steps * chunk
    slot = jnp.where(
        place == here, rank, jnp.where(place < here, up_base + upward, down_base + downward)
    )
    tokens = jnp.clip(prefix - order * page_len, 0, page_len)
    slots = jnp.arange(4 * chunk + 2 * steps * chunk, dtype=jnp.int32)
    limits = jnp.sum(jnp.where(slot[None, :] == slots[:, None], tokens[None, :], 0), axis=1)
    held_here = jnp.sum((place == here).astype(jnp.int32))
    return limits, held_here.reshape(1)


def attend_kernel(shape, first, last, *refs):
    rows, tile, scale, n_blocks, chunk, half_len = shape
    refs = list(refs)
    limit_ref, q_ref = refs.pop(0), refs.pop(0)
    state = [] if first else [refs.pop(0) for _ in range(3)]
    if last:
        suffix_ref, earlier_ref, fresh_ref, up_ref = [refs.pop(0) for _ in range(4)]
    sources = []
    total = 0
    while total < n_blocks:
        source = refs.pop(0)
        sources.append((source, source.shape[0] // chunk))
        total += sources[-1][1]
    if last:
        out_ref = refs.pop(0)
    values, highest, weight_sum, blocks, keys, sems = refs
    latent_width = values.shape[1]
    key_width = keys.shape[1]
    index = 0
    for source, count in sources:
        for i in range(count):
            pltpu.make_async_copy(
                source.at[i * chunk : (i + 1) * chunk], blocks.at[index], sems.at[index]
            ).start()
            index += 1
    if first:
        values[...] = jnp.zeros_like(values)
        highest[...] = jnp.full_like(highest, LOWEST)
        weight_sum[...] = jnp.zeros_like(weight_sum)
    else:
        values[...] = state[0][...]
        highest[...] = state[1][...]
        weight_sum[...] = state[2][...]

    def visit(key_block, mask_of):
        for start in range(0, rows, tile):
            part = slice(start, start + tile)
            scores = lax.dot_general(
                q_ref[part, :], key_block[...], (((1,), (1,)), ((), ())), preferred_element_type=jnp.float32
            )
            scores = mask_of(scores * scale, start)
            old = highest[part, :]
            new = jnp.maximum(old, jnp.max(scores, axis=1, keepdims=True))
            weights = jnp.exp2(scores - new)
            shrink = jnp.exp2(old - new)
            highest[part, :] = new
            weight_sum[part, :] = weight_sum[part, :] * shrink + jnp.sum(weights, axis=1, keepdims=True)
            values[part, :] = values[part, :] * shrink + jnp.dot(
                weights.astype(jnp.bfloat16),
                key_block[:, :latent_width],
                preferred_element_type=jnp.float32,
            )

    pairs = blocks.shape[2]
    pair_rows = chunk * pairs

    def one_block(block, carry):
        pltpu.make_async_copy(blocks.at[block], blocks.at[block], sems.at[block]).wait()
        limits = [limit_ref[block * chunk + j] for j in range(chunk)]
        some = functools.reduce(jnp.maximum, limits)

        @pl.when(some > 0)
        def _():
            page_rows = blocks[block].reshape(pair_rows, blocks.shape[3])
            keys[:pair_rows, :] = page_rows[:, :key_width]
            keys[pair_rows : 2 * pair_rows, :] = page_rows[:, key_width:]
            lane = lax.broadcasted_iota(jnp.int32, (1, 2 * pair_rows), 1)
            within = lax.rem(lane, pair_rows)
            token = 2 * lax.rem(within, pairs) + lane // pair_rows
            limit = jnp.zeros_like(lane)
            for j in range(chunk):
                limit = jnp.where(within // pairs == j, limits[j], limit)
            bias = jnp.where(token < limit, 0.0, -jnp.inf)
            visit(keys.at[: 2 * pair_rows], lambda scores, start: scores + bias)

        return carry

    lax.fori_loop(0, n_blocks, one_block, 0)
    if not last:
        return
    live = suffix_ref[0]
    seq_idx = lax.axis_index("seq")
    keys[:half_len, :] = earlier_ref[...]
    keys[half_len : 2 * half_len, :] = fresh_ref[...]

    def near(scores, start):
        row = lax.broadcasted_iota(jnp.int32, scores.shape, 0) + start
        place = lax.broadcasted_iota(jnp.int32, scores.shape, 1) + (seq_idx - 1) * half_len
        query = lax.rem(row, half_len) + seq_idx * half_len
        allowed = (place >= 0) & (place <= query) & (place < live)
        return jnp.where(allowed, scores, -jnp.inf)

    visit(keys.at[: 2 * half_len], near)
    heads, _, value_width = up_ref.shape
    steps = lax.broadcasted_iota(jnp.int32, (half_len, value_width), 0) + seq_idx * half_len
    for head in range(heads):
        part = slice(head * half_len, (head + 1) * half_len)
        latent = (values[part, :] / weight_sum[part, :]).astype(jnp.bfloat16)
        raised = jnp.dot(latent, up_ref[head], preferred_element_type=jnp.float32)
        out_ref[:, head * value_width : (head + 1) * value_width] = jnp.where(
            steps < live, raised, 0.0
        ).astype(jnp.bfloat16)


def attend(limits, q_rows, blocks, chunk, latent_width, half_len, scale, state=None, tail=None):
    rows, key_width = q_rows.shape
    pairs, pair_width = blocks[0].shape[1:]
    n_blocks = sum(b.shape[0] for b in blocks) // chunk
    block_keys = max(2 * pairs * chunk, 2 * half_len)
    state_shapes = [
        jax.ShapeDtypeStruct((rows, latent_width), jnp.float32),
        jax.ShapeDtypeStruct((rows, 1), jnp.float32),
        jax.ShapeDtypeStruct((rows, 1), jnp.float32),
    ]
    state_scratch = [pltpu.VMEM(s.shape, s.dtype) for s in state_shapes]
    scratch = [
        pltpu.VMEM((n_blocks, chunk, pairs, pair_width), jnp.bfloat16),
        pltpu.VMEM((block_keys, key_width), jnp.bfloat16),
        pltpu.SemaphoreType.DMA((n_blocks,)),
    ]
    operands = [limits, q_rows]
    specs = [smem_spec(), vmem_spec()]
    if state is not None:
        operands += list(state)
        specs += [vmem_spec()] * 3
    if tail is not None:
        operands += list(tail)
        specs += [smem_spec()] + [vmem_spec()] * 3
        heads, _, value_width = tail[-1].shape
        out_shape = jax.ShapeDtypeStruct((half_len, heads * value_width), jnp.bfloat16)
        out_specs = vmem_spec()
        scratch = state_scratch + scratch
    else:
        out_shape = tuple(state_shapes)
        out_specs = (vmem_spec(),) * 3
    operands += list(blocks)
    specs += [any_spec()] * len(blocks)
    shape = (rows, 256 if rows % 256 == 0 else rows, scale * math.log2(math.e), n_blocks, chunk, half_len)
    work = n_blocks * 2 * pairs * chunk * rows
    return pl.pallas_call(
        functools.partial(attend_kernel, shape, state is None, tail is not None),
        out_shape=out_shape,
        in_specs=specs,
        out_specs=out_specs,
        scratch_shapes=scratch,
        compiler_params=pltpu.CompilerParams(vmem_limit_bytes=VMEM_LIMIT),
        cost_estimate=pl.CostEstimate(
            flops=2 * work * (key_width + latent_width) // 2, bytes_accessed=10**7, transcendentals=work // 2
        ),
        name="attend",
    )(*operands)


def local(
    queries,
    hidden,
    w_dkv,
    kv_gain,
    w_uk,
    value_up_weight,
    page_pool,
    page_owner,
    page_slot,
    prefix_len,
    suffix_len,
):
    n_head = lax.axis_size("head")
    n_req = lax.axis_size("req")
    n_seq = lax.axis_size("seq")
    head_idx = lax.axis_index("head")
    req_idx = lax.axis_index("req")
    seq_idx = lax.axis_index("seq")
    _, half_len, d_local = hidden.shape
    heads_dev, nope_width, latent_width = w_uk.shape
    lat_width = w_dkv.shape[1]
    rope_width = lat_width - latent_width
    query_width = queries.shape[2] // heads_dev
    page_width = page_pool.shape[1]
    page_len = page_width // lat_width
    pairs = page_len // 2
    pages_req = page_slot.shape[1]
    cap = max(2, 2 * pages_req // (n_head * n_req))
    chunk = n_req * cap // 4
    steps = 3 * n_head - 2
    score_scale = float(query_width) ** (-0.5)

    owner_rows = page_owner[:, :, 0]
    counts, own, foreign = pick_pages(owner_rows, page_slot, page_pool, cap, n_req, n_seq, pairs)
    swap_route = [(i, n_seq - 1 - i) for i in range(n_seq)]
    mine = jnp.stack(
        [
            lax.ppermute(foreign[s - 1], "req", [(i, (i + s) % n_req) for i in range(n_req)])
            for s in range(1, n_req)
        ]
    )
    other = lax.ppermute(mine, "seq", swap_route)
    joined, first_chunk, second_chunk = join_pages(counts, own, mine, other, chunk)

    my_prefix = lax.dynamic_index_in_dim(prefix_len, req_idx, 0, keepdims=False)
    my_suffix = lax.dynamic_index_in_dim(suffix_len, req_idx, 0, keepdims=False)
    own_owners = lax.dynamic_index_in_dim(owner_rows, req_idx, 0, keepdims=False)
    limits, held = token_limits(
        own_owners, my_prefix, head_idx, req_idx, seq_idx, n_head, n_req, chunk, steps, page_len
    )
    local_t = jnp.arange(half_len, dtype=jnp.int32)
    glob_t = seq_idx * half_len + local_t
    positions = my_prefix + glob_t
    live_rows = glob_t < my_suffix

    partial_value = jnp.dot(hidden[0], w_dkv, preferred_element_type=jnp.float32)
    summed = lax.psum(partial_value, "head")
    fresh = finish_latent(summed, positions, live_rows, kv_gain, latent_width)
    new_pages = fresh.reshape(1, half_len // page_len, page_len * lat_width)
    earlier = from_behind(fresh, "seq", 1)

    query_rows = queries[0].reshape(half_len, heads_dev, query_width)
    q_latent = jnp.einsum(
        "thn,hnk->htk", query_rows[..., :nope_width], w_uk, preferred_element_type=jnp.float32
    ).astype(jnp.bfloat16)
    cosine_table, sine_table = angles(positions, rope_width)
    q_rotated = rotate(
        jnp.swapaxes(query_rows[..., nope_width:], 0, 1).astype(jnp.float32), cosine_table, sine_table
    ).astype(jnp.bfloat16)
    q_rows = jnp.concatenate([q_latent, q_rotated], axis=-1).reshape(heads_dev * half_len, lat_width)

    stream_route = []
    for i in range(n_head - 1):
        stream_route.append((i * n_seq, (i + 1) * n_seq))
        stream_route.append(((i + 1) * n_seq + 1, i * n_seq + 1))
    arrived, swapped = [], []
    for step in range(steps):
        if step == 0:
            outgoing = first_chunk
        elif step == 1:
            outgoing = second_chunk
        else:
            outgoing = queue_chunk(step, held, joined, arrived)
        arrived.append(lax.ppermute(outgoing, ("head", "seq"), stream_route))
        swapped.append(lax.ppermute(arrived[-1], "seq", swap_route))

    def limit_part(first, last):
        mine_base = 4 * chunk
        other_base = mine_base + steps * chunk
        return [
            limits[mine_base + first * chunk : mine_base + last * chunk],
            limits[other_base + first * chunk : other_base + last * chunk],
        ]

    run = functools.partial(
        attend, chunk=chunk, latent_width=latent_width, half_len=half_len, scale=score_scale
    )
    cuts = [0, 3 * steps // 10, 7 * steps // 10, steps]
    state = None
    for i in range(3):
        low, high = cuts[i], cuts[i + 1]
        blocks = ([joined] if i == 0 else []) + arrived[low:high] + swapped[low:high]
        part = jnp.concatenate(([limits[: 4 * chunk]] if i == 0 else []) + limit_part(low, high))
        tail = None
        if i == 2:
            tail = (my_suffix.reshape(1), earlier, fresh, value_up_weight)
        state = run(part, q_rows, blocks, state=state, tail=tail)
    return (state[None], new_pages)


def solution(mesh):
    placed = (
        P(("groups", "req"), "seq", "head"),
        P(("groups", "req"), "seq", "head"),
        P("head", None),
        P(),
        P("head", None, None),
        P("head", None, None),
        P(("groups", "head", "req"), None),
        P("groups", None, None),
        P("groups", None),
        P("groups"),
        P("groups"),
    )
    return jax.shard_map(
        local,
        mesh=mesh,
        in_specs=placed,
        out_specs=(P(("groups", "req"), "seq", "head"), P(("groups", "req"), "seq", None)),
        check_vma=False,
    )
```

```python
import functools
import math

import jax
import jax.numpy as jnp
from jax import lax
from jax.experimental import pallas as pl
from jax.experimental.pallas import tpu as pltpu
from jax.sharding import PartitionSpec as P

LOWEST = -1e30
VMEM_LIMIT = 48 * 1024 * 1024


def from_behind(block, axis, distance):
    devices = range(lax.axis_size(axis))
    route = [(i - distance, i) for i in devices if i - distance in devices]
    return lax.ppermute(block, axis, route)


def rotate(vector, cosine_table, sine_table):
    half_width = vector.shape[-1] // 2
    first_half = vector[..., :half_width]
    second_half = vector[..., half_width:]
    return jnp.concatenate(
        [
            first_half * cosine_table - second_half * sine_table,
            first_half * sine_table + second_half * cosine_table,
        ],
        axis=-1,
    )


def angles(positions, rope_width):
    half_width = rope_width // 2
    frequency = 10000.0 ** (-2.0 * jnp.arange(half_width, dtype=jnp.float32) / rope_width)
    phases = positions.astype(jnp.float32)[:, None] * frequency[None, :]
    return (jnp.cos(phases), jnp.sin(phases))


def finish_latent(summed, positions, live_rows, kv_gain, latent_width):
    latent_part = summed[:, :latent_width]
    mean_square = jnp.mean(latent_part * latent_part, axis=-1, keepdims=True)
    normed = latent_part * lax.rsqrt(mean_square + 1e-06) * kv_gain
    cosine_table, sine_table = angles(positions, summed.shape[1] - latent_width)
    rotated = rotate(summed[:, latent_width:], cosine_table, sine_table)
    joined = jnp.concatenate([normed, rotated], axis=-1).astype(jnp.bfloat16)
    return jnp.where(live_rows[:, None], joined, jnp.zeros_like(joined))


def any_spec():
    return pl.BlockSpec(memory_space=pl.ANY)


def smem_spec():
    return pl.BlockSpec(memory_space=pltpu.SMEM)


def vmem_spec():
    return pl.BlockSpec(memory_space=pltpu.VMEM)


def pick_kernel(cap, owner_ref, slot_ref, pool_ref, count_ref, own_ref, foreign_ref, pages, lists, sems):
    n_req = lax.axis_size("req")
    head_idx = lax.axis_index("head")
    req_idx = lax.axis_index("req")
    seq_idx = lax.axis_index("seq")
    n_pages = owner_ref.shape[1]
    pool_pages, pairs, pair_width = pages.shape
    step = 16
    row = lax.broadcasted_iota(jnp.int32, (step * step, step * step), 0)
    column = lax.broadcasted_iota(jnp.int32, (step * step, step * step), 1)
    swap = ((row // step == column % step) & (row % step == column // step)).astype(jnp.bfloat16)
    for page in range(0, pool_pages, step):
        for pair in range(0, pairs, step):
            rows = jnp.concatenate(
                [
                    pool_ref[page : page + step, (pair + i) * pair_width : (pair + i + 1) * pair_width]
                    for i in range(step)
                ],
                axis=0,
            )
            turned = jnp.dot(swap, rows, preferred_element_type=jnp.float32).astype(jnp.bfloat16)
            pages[page : page + step, pair : pair + step, :] = turned.reshape(step, step, pair_width)
    self_owner = head_idx * n_req + req_idx
    for shift in range(n_req):
        request = lax.rem(req_idx + shift, n_req)

        def note(page, found, shift=shift, request=request):
            lists[shift, found] = slot_ref[request, page]
            return found + (owner_ref[request, page] == self_owner).astype(jnp.int32)

        found = lax.fori_loop(0, n_pages, note, jnp.int32(0), unroll=8)
        ranks = cap if shift == 0 else foreign_ref.shape[1]
        first = 0 if shift == 0 else seq_idx * ranks
        for j in range(ranks):
            rank = first + j
            slot = jnp.where(rank < found, lists[shift, rank], 0)
            target = own_ref.at[j] if shift == 0 else foreign_ref.at[shift - 1, j]
            pltpu.make_async_copy(pages.at[slot], target, sems.at[min(shift, 1)]).start()

    def tally(page, counts):
        owner = owner_ref[req_idx, page]
        return tuple(
            counts[shift]
            + (owner == head_idx * n_req + lax.rem(req_idx + n_req - shift, n_req)).astype(jnp.int32)
            for shift in range(n_req)
        )

    counts = lax.fori_loop(0, n_pages, tally, (jnp.int32(0),) * n_req, unroll=8)
    for shift in range(n_req):
        count_ref[shift] = counts[shift]
    pltpu.make_async_copy(own_ref, own_ref, sems.at[0]).wait()
    pltpu.make_async_copy(foreign_ref, foreign_ref, sems.at[1]).wait()


def pick_pages(page_owner, page_slot, page_pool, cap, n_req, n_seq, pairs):
    pool_pages, page_width = page_pool.shape
    pair_width = page_width // pairs
    page = (pairs, pair_width)
    return pl.pallas_call(
        functools.partial(pick_kernel, cap),
        out_shape=(
            jax.ShapeDtypeStruct((n_req,), jnp.int32),
            jax.ShapeDtypeStruct((cap, *page), jnp.bfloat16),
            jax.ShapeDtypeStruct((n_req - 1, cap // n_seq, *page), jnp.bfloat16),
        ),
        in_specs=[smem_spec(), smem_spec(), vmem_spec()],
        out_specs=(smem_spec(), any_spec(), any_spec()),
        scratch_shapes=[
            pltpu.VMEM((pool_pages, *page), jnp.bfloat16),
            pltpu.SMEM((n_req, cap + 1), jnp.int32),
            pltpu.SemaphoreType.DMA((2,)),
        ],
        compiler_params=pltpu.CompilerParams(vmem_limit_bytes=VMEM_LIMIT),
        cost_estimate=pl.CostEstimate(flops=10**9, bytes_accessed=6 * 10**6, transcendentals=0),
        name="pick_pages",
    )(page_owner, page_slot, page_pool)


def join_kernel(chunk, count_ref, own_ref, mine_ref, other_ref, joined_ref, first_ref, second_ref, sems):
    seq_idx = lax.axis_index("seq")
    n_req = count_ref.shape[0]
    half_cap = mine_ref.shape[1]
    for j in range(joined_ref.shape[0]):
        targets = [(joined_ref.at[j], sems.at[0])]
        if j < chunk:
            targets.append((first_ref.at[j], sems.at[1]))
        elif j < 2 * chunk:
            targets.append((second_ref.at[j - chunk], sems.at[2]))

        def fetch(condition, source):
            @pl.when(condition)
            def _():
                for target, sem in targets:
                    pltpu.make_async_copy(source, target, sem).start()

        rank = jnp.int32(j)
        taken = rank < count_ref[0]
        fetch(taken, own_ref.at[jnp.minimum(rank, own_ref.shape[0] - 1)])
        rank = rank - count_ref[0]
        for shift in range(1, n_req):
            here = jnp.logical_not(taken) & (rank < count_ref[shift])
            place = jnp.clip(lax.rem(rank, half_cap), 0, half_cap - 1)
            local = rank // half_cap == seq_idx
            fetch(here & local, mine_ref.at[shift - 1, place])
            fetch(here & jnp.logical_not(local), other_ref.at[shift - 1, place])
            taken = taken | here
            rank = rank - count_ref[shift]
        fetch(jnp.logical_not(taken), own_ref.at[0])
    for i, ref in enumerate((joined_ref, first_ref, second_ref)):
        pltpu.make_async_copy(ref, ref, sems.at[i]).wait()


def join_pages(counts, own, mine, other, chunk):
    page = own.shape[1:]
    return pl.pallas_call(
        functools.partial(join_kernel, chunk),
        out_shape=(
            jax.ShapeDtypeStruct((4 * chunk, *page), jnp.bfloat16),
            jax.ShapeDtypeStruct((chunk, *page), jnp.bfloat16),
            jax.ShapeDtypeStruct((chunk, *page), jnp.bfloat16),
        ),
        in_specs=[smem_spec(), any_spec(), any_spec(), any_spec()],
        out_specs=(vmem_spec(), vmem_spec(), vmem_spec()),
        scratch_shapes=[pltpu.SemaphoreType.DMA((3,))],
        compiler_params=pltpu.CompilerParams(vmem_limit_bytes=VMEM_LIMIT),
        cost_estimate=pl.CostEstimate(flops=0, bytes_accessed=6 * 10**6, transcendentals=0),
        name="join_pages",
    )(counts, own, mine, other)


def queue_kernel(step, chunk, earliest, held_ref, joined_ref, *refs):
    arrived, target_ref, sem = refs[:-2], refs[-2], refs[-1]
    held = held_ref[0]
    offset = jnp.maximum(held, 2 * chunk)
    for j in range(chunk):
        entry = step * chunk + j

        def fetch(condition, source, j=j):
            @pl.when(condition)
            def _():
                pltpu.make_async_copy(source, target_ref.at[j], sem).start()

        taken = entry < held
        if entry < joined_ref.shape[0]:
            fetch(taken, joined_ref.at[entry])
        place = entry - offset - earliest * chunk
        for i, source in enumerate(arrived):
            here = (place >= i * chunk) & (place < (i + 1) * chunk)
            fetch(here, source.at[jnp.clip(place - i * chunk, 0, chunk - 1)])
            taken = taken | here
        fetch(jnp.logical_not(taken), joined_ref.at[0])
    pltpu.make_async_copy(target_ref, target_ref, sem).wait()


def queue_chunk(step, held, joined, arrived):
    chunk = joined.shape[0] // 4
    earliest = max(0, step - 4)
    sources = arrived[earliest : step - 1]
    return pl.pallas_call(
        functools.partial(queue_kernel, step, chunk, earliest),
        out_shape=jax.ShapeDtypeStruct((chunk, *joined.shape[1:]), jnp.bfloat16),
        in_specs=[smem_spec()] + [any_spec()] * (1 + len(sources)),
        out_specs=vmem_spec(),
        scratch_shapes=[pltpu.SemaphoreType.DMA],
        compiler_params=pltpu.CompilerParams(vmem_limit_bytes=VMEM_LIMIT),
        cost_estimate=pl.CostEstimate(flops=0, bytes_accessed=10**6, transcendentals=0),
        name="queue_chunk",
    )(held, joined, *sources)


def token_limits(owners, prefix, head_idx, req_idx, seq_idx, n_head, n_req, chunk, steps, page_len):
    pages = owners.shape[0]
    order = jnp.arange(pages, dtype=jnp.int32)
    place = owners // n_req
    key = lax.rem(req_idx + n_req - lax.rem(owners, n_req), n_req) * pages + order
    ahead = (place[None, :] == place[:, None]) & (key[None, :] < key[:, None])
    rank = jnp.sum(ahead.astype(jnp.int32), axis=1)
    heads = jnp.arange(n_head, dtype=jnp.int32)
    held = jnp.sum((place[None, :] == heads[:, None]).astype(jnp.int32), axis=1)
    widths = jnp.maximum(held, 2 * chunk)

    def before(position):
        return jnp.sum(jnp.where(heads[None, :] < position[:, None], widths[None, :], 0), axis=1)

    here = jnp.full((pages,), head_idx, jnp.int32)
    upward = rank + before(here) - before(place + 1)
    downward = rank + before(place) - before(here + 1)
    up_base = 4 * chunk + seq_idx * steps * chunk
    down_base = 4 * chunk + (1 - seq_idx) * steps * chunk
    slot = jnp.where(
        place == here, rank, jnp.where(place < here, up_base + upward, down_base + downward)
    )
    tokens = jnp.clip(prefix - order * page_len, 0, page_len)
    slots = jnp.arange(4 * chunk + 2 * steps * chunk, dtype=jnp.int32)
    limits = jnp.sum(jnp.where(slot[None, :] == slots[:, None], tokens[None, :], 0), axis=1)
    held_here = jnp.sum((place == here).astype(jnp.int32))
    return limits, held_here.reshape(1)


def attend_kernel(shape, first, last, *refs):
    rows, tile, scale, n_blocks, chunk, half_len = shape
    refs = list(refs)
    limit_ref, q_ref = refs.pop(0), refs.pop(0)
    state = [] if first else [refs.pop(0) for _ in range(3)]
    if last:
        suffix_ref, earlier_ref, fresh_ref, up_ref = [refs.pop(0) for _ in range(4)]
    sources = []
    total = 0
    while total < n_blocks:
        source = refs.pop(0)
        sources.append((source, source.shape[0] // chunk))
        total += sources[-1][1]
    if last:
        out_ref = refs.pop(0)
    values, highest, weight_sum, blocks, keys, sems = refs
    latent_width = values.shape[1]
    key_width = keys.shape[1]
    index = 0
    for source, count in sources:
        for i in range(count):
            pltpu.make_async_copy(
                source.at[i * chunk : (i + 1) * chunk], blocks.at[index], sems.at[index]
            ).start()
            index += 1
    if first:
        values[...] = jnp.zeros_like(values)
        highest[...] = jnp.full_like(highest, LOWEST)
        weight_sum[...] = jnp.zeros_like(weight_sum)
    else:
        values[...] = state[0][...]
        highest[...] = state[1][...]
        weight_sum[...] = state[2][...]

    def visit(key_block, mask_of):
        for start in range(0, rows, tile):
            part = slice(start, start + tile)
            scores = lax.dot_general(
                q_ref[part, :], key_block[...], (((1,), (1,)), ((), ())), preferred_element_type=jnp.float32
            )
            scores = mask_of(scores * scale, start)
            old = highest[part, :]
            new = jnp.maximum(old, jnp.max(scores, axis=1, keepdims=True))
            weights = jnp.exp2(scores - new)
            shrink = jnp.exp2(old - new)
            highest[part, :] = new
            weight_sum[part, :] = weight_sum[part, :] * shrink + jnp.sum(weights, axis=1, keepdims=True)
            values[part, :] = values[part, :] * shrink + jnp.dot(
                weights.astype(jnp.bfloat16),
                key_block[:, :latent_width],
                preferred_element_type=jnp.float32,
            )

    pairs = blocks.shape[2]
    pair_rows = chunk * pairs

    def one_block(block, carry):
        pltpu.make_async_copy(blocks.at[block], blocks.at[block], sems.at[block]).wait()
        limits = [limit_ref[block * chunk + j] for j in range(chunk)]
        some = functools.reduce(jnp.maximum, limits)

        @pl.when(some > 0)
        def _():
            page_rows = blocks[block].reshape(pair_rows, blocks.shape[3])
            keys[:pair_rows, :] = page_rows[:, :key_width]
            keys[pair_rows : 2 * pair_rows, :] = page_rows[:, key_width:]
            lane = lax.broadcasted_iota(jnp.int32, (1, 2 * pair_rows), 1)
            within = lax.rem(lane, pair_rows)
            token = 2 * lax.rem(within, pairs) + lane // pair_rows
            limit = jnp.zeros_like(lane)
            for j in range(chunk):
                limit = jnp.where(within // pairs == j, limits[j], limit)
            bias = jnp.where(token < limit, 0.0, -jnp.inf)
            visit(keys.at[: 2 * pair_rows], lambda scores, start: scores + bias)

        return carry

    lax.fori_loop(0, n_blocks, one_block, 0)
    if not last:
        return
    live = suffix_ref[0]
    seq_idx = lax.axis_index("seq")
    keys[:half_len, :] = earlier_ref[...]
    keys[half_len : 2 * half_len, :] = fresh_ref[...]

    def near(scores, start):
        row = lax.broadcasted_iota(jnp.int32, scores.shape, 0) + start
        place = lax.broadcasted_iota(jnp.int32, scores.shape, 1) + (seq_idx - 1) * half_len
        query = lax.rem(row, half_len) + seq_idx * half_len
        allowed = (place >= 0) & (place <= query) & (place < live)
        return jnp.where(allowed, scores, -jnp.inf)

    visit(keys.at[: 2 * half_len], near)
    heads, _, value_width = up_ref.shape
    steps = lax.broadcasted_iota(jnp.int32, (half_len, value_width), 0) + seq_idx * half_len
    for head in range(heads):
        part = slice(head * half_len, (head + 1) * half_len)
        latent = (values[part, :] / weight_sum[part, :]).astype(jnp.bfloat16)
        raised = jnp.dot(latent, up_ref[head], preferred_element_type=jnp.float32)
        out_ref[:, head * value_width : (head + 1) * value_width] = jnp.where(
            steps < live, raised, 0.0
        ).astype(jnp.bfloat16)


def attend(limits, q_rows, blocks, chunk, latent_width, half_len, scale, state=None, tail=None):
    rows, key_width = q_rows.shape
    pairs, pair_width = blocks[0].shape[1:]
    n_blocks = sum(b.shape[0] for b in blocks) // chunk
    block_keys = max(2 * pairs * chunk, 2 * half_len)
    state_shapes = [
        jax.ShapeDtypeStruct((rows, latent_width), jnp.float32),
        jax.ShapeDtypeStruct((rows, 1), jnp.float32),
        jax.ShapeDtypeStruct((rows, 1), jnp.float32),
    ]
    state_scratch = [pltpu.VMEM(s.shape, s.dtype) for s in state_shapes]
    scratch = [
        pltpu.VMEM((n_blocks, chunk, pairs, pair_width), jnp.bfloat16),
        pltpu.VMEM((block_keys, key_width), jnp.bfloat16),
        pltpu.SemaphoreType.DMA((n_blocks,)),
    ]
    operands = [limits, q_rows]
    specs = [smem_spec(), vmem_spec()]
    if state is not None:
        operands += list(state)
        specs += [vmem_spec()] * 3
    if tail is not None:
        operands += list(tail)
        specs += [smem_spec()] + [vmem_spec()] * 3
        heads, _, value_width = tail[-1].shape
        out_shape = jax.ShapeDtypeStruct((half_len, heads * value_width), jnp.bfloat16)
        out_specs = vmem_spec()
        scratch = state_scratch + scratch
    else:
        out_shape = tuple(state_shapes)
        out_specs = (vmem_spec(),) * 3
    operands += list(blocks)
    specs += [any_spec()] * len(blocks)
    shape = (rows, 256 if rows % 256 == 0 else rows, scale * math.log2(math.e), n_blocks, chunk, half_len)
    work = n_blocks * 2 * pairs * chunk * rows
    return pl.pallas_call(
        functools.partial(attend_kernel, shape, state is None, tail is not None),
        out_shape=out_shape,
        in_specs=specs,
        out_specs=out_specs,
        scratch_shapes=scratch,
        compiler_params=pltpu.CompilerParams(vmem_limit_bytes=VMEM_LIMIT),
        cost_estimate=pl.CostEstimate(
            flops=2 * work * (key_width + latent_width) // 2, bytes_accessed=10**7, transcendentals=work // 2
        ),
        name="attend",
    )(*operands)


def local(
    queries,
    hidden,
    w_dkv,
    kv_gain,
    w_uk,
    value_up_weight,
    page_pool,
    page_owner,
    page_slot,
    prefix_len,
    suffix_len,
):
    n_head = lax.axis_size("head")
    n_req = lax.axis_size("req")
    n_seq = lax.axis_size("seq")
    head_idx = lax.axis_index("head")
    req_idx = lax.axis_index("req")
    seq_idx = lax.axis_index("seq")
    _, half_len, d_local = hidden.shape
    heads_dev, nope_width, latent_width = w_uk.shape
    lat_width = w_dkv.shape[1]
    rope_width = lat_width - latent_width
    query_width = queries.shape[2] // heads_dev
    page_width = page_pool.shape[1]
    page_len = page_width // lat_width
    pairs = page_len // 2
    pages_req = page_slot.shape[1]
    cap = max(2, 2 * pages_req // (n_head * n_req))
    chunk = n_req * cap // 4
    steps = 3 * n_head - 2
    score_scale = float(query_width) ** (-0.5)

    owner_rows = page_owner[:, :, 0]
    counts, own, foreign = pick_pages(owner_rows, page_slot, page_pool, cap, n_req, n_seq, pairs)
    swap_route = [(i, n_seq - 1 - i) for i in range(n_seq)]
    mine = jnp.stack(
        [
            lax.ppermute(foreign[s - 1], "req", [(i, (i + s) % n_req) for i in range(n_req)])
            for s in range(1, n_req)
        ]
    )
    other = lax.ppermute(mine, "seq", swap_route)
    joined, first_chunk, second_chunk = join_pages(counts, own, mine, other, chunk)

    my_prefix = lax.dynamic_index_in_dim(prefix_len, req_idx, 0, keepdims=False)
    my_suffix = lax.dynamic_index_in_dim(suffix_len, req_idx, 0, keepdims=False)
    own_owners = lax.dynamic_index_in_dim(owner_rows, req_idx, 0, keepdims=False)
    limits, held = token_limits(
        own_owners, my_prefix, head_idx, req_idx, seq_idx, n_head, n_req, chunk, steps, page_len
    )
    local_t = jnp.arange(half_len, dtype=jnp.int32)
    glob_t = seq_idx * half_len + local_t
    positions = my_prefix + glob_t
    live_rows = glob_t < my_suffix

    partial_value = jnp.dot(hidden[0], w_dkv, preferred_element_type=jnp.float32)
    summed = lax.psum(partial_value, "head")
    fresh = finish_latent(summed, positions, live_rows, kv_gain, latent_width)
    new_pages = fresh.reshape(1, half_len // page_len, page_len * lat_width)
    earlier = from_behind(fresh, "seq", 1)

    query_rows = queries[0].reshape(half_len, heads_dev, query_width)
    q_latent = jnp.einsum(
        "thn,hnk->htk", query_rows[..., :nope_width], w_uk, preferred_element_type=jnp.float32
    ).astype(jnp.bfloat16)
    cosine_table, sine_table = angles(positions, rope_width)
    q_rotated = rotate(
        jnp.swapaxes(query_rows[..., nope_width:], 0, 1).astype(jnp.float32), cosine_table, sine_table
    ).astype(jnp.bfloat16)
    q_rows = jnp.concatenate([q_latent, q_rotated], axis=-1).reshape(heads_dev * half_len, lat_width)

    stream_route = []
    for i in range(n_head - 1):
        stream_route.append((i * n_seq, (i + 1) * n_seq))
        stream_route.append(((i + 1) * n_seq + 1, i * n_seq + 1))
    arrived, swapped = [], []
    for step in range(steps):
        if step == 0:
            outgoing = first_chunk
        elif step == 1:
            outgoing = second_chunk
        else:
            outgoing = queue_chunk(step, held, joined, arrived)
        arrived.append(lax.ppermute(outgoing, ("head", "seq"), stream_route))
        swapped.append(lax.ppermute(arrived[-1], "seq", swap_route))

    def limit_part(first, last):
        mine_base = 4 * chunk
        other_base = mine_base + steps * chunk
        return [
            limits[mine_base + first * chunk : mine_base + last * chunk],
            limits[other_base + first * chunk : other_base + last * chunk],
        ]

    run = functools.partial(
        attend, chunk=chunk, latent_width=latent_width, half_len=half_len, scale=score_scale
    )
    cuts = [0, 3 * steps // 10, 7 * steps // 10, steps]
    state = None
    for i in range(3):
        low, high = cuts[i], cuts[i + 1]
        blocks = ([joined] if i == 0 else []) + arrived[low:high] + swapped[low:high]
        part = jnp.concatenate(([limits[: 4 * chunk]] if i == 0 else []) + limit_part(low, high))
        tail = None
        if i == 2:
            tail = (my_suffix.reshape(1), earlier, fresh, value_up_weight)
        state = run(part, q_rows, blocks, state=state, tail=tail)
    return (state[None], new_pages)


def solution(mesh):
    placed = (
        P(("groups", "req"), "seq", "head"),
        P(("groups", "req"), "seq", "head"),
        P("head", None),
        P(),
        P("head", None, None),
        P("head", None, None),
        P(("groups", "head", "req"), None),
        P("groups", None, None),
        P("groups", None),
        P("groups"),
        P("groups"),
    )
    return jax.shard_map(
        local,
        mesh=mesh,
        in_specs=placed,
        out_specs=(P(("groups", "req"), "seq", "head"), P(("groups", "req"), "seq", None)),
        check_vma=False,
    )
```

```python
import functools
import math

import jax
import jax.numpy as jnp
from jax import lax
from jax.experimental import pallas as pl
from jax.experimental.pallas import tpu as pltpu
from jax.sharding import PartitionSpec as P

LOWEST = -1e30
VMEM_LIMIT = 48 * 1024 * 1024


def from_behind(block, axis, distance):
    devices = range(lax.axis_size(axis))
    route = [(i - distance, i) for i in devices if i - distance in devices]
    return lax.ppermute(block, axis, route)


def rotate(vector, cosine_table, sine_table):
    half_width = vector.shape[-1] // 2
    first_half = vector[..., :half_width]
    second_half = vector[..., half_width:]
    return jnp.concatenate(
        [
            first_half * cosine_table - second_half * sine_table,
            first_half * sine_table + second_half * cosine_table,
        ],
        axis=-1,
    )


def angles(positions, rope_width):
    half_width = rope_width // 2
    frequency = 10000.0 ** (-2.0 * jnp.arange(half_width, dtype=jnp.float32) / rope_width)
    phases = positions.astype(jnp.float32)[:, None] * frequency[None, :]
    return (jnp.cos(phases), jnp.sin(phases))


def finish_latent(summed, positions, live_rows, kv_gain, latent_width):
    latent_part = summed[:, :latent_width]
    mean_square = jnp.mean(latent_part * latent_part, axis=-1, keepdims=True)
    normed = latent_part * lax.rsqrt(mean_square + 1e-06) * kv_gain
    cosine_table, sine_table = angles(positions, summed.shape[1] - latent_width)
    rotated = rotate(summed[:, latent_width:], cosine_table, sine_table)
    joined = jnp.concatenate([normed, rotated], axis=-1).astype(jnp.bfloat16)
    return jnp.where(live_rows[:, None], joined, jnp.zeros_like(joined))


def any_spec():
    return pl.BlockSpec(memory_space=pl.ANY)


def smem_spec():
    return pl.BlockSpec(memory_space=pltpu.SMEM)


def vmem_spec():
    return pl.BlockSpec(memory_space=pltpu.VMEM)


def pick_kernel(
    cap, owner_hbm, slot_hbm, pool_hbm, count_ref, first_ref, rest_ref, foreign_ref,
    owner_ref, slot_ref, pool_ref, pages, lists, sems,
):
    n_req = lax.axis_size("req")
    head_idx = lax.axis_index("head")
    req_idx = lax.axis_index("req")
    seq_idx = lax.axis_index("seq")
    n_pages = owner_ref.shape[1]
    pool_pages, pairs, pair_width = pages.shape
    chunk = first_ref.shape[0]
    width = pool_ref.shape[1]
    loads = [
        pltpu.make_async_copy(owner_hbm, owner_ref, sems.at[0]),
        pltpu.make_async_copy(slot_hbm, slot_ref, sems.at[1]),
        pltpu.make_async_copy(
            pool_hbm.at[:, pl.ds(pl.multiple_of(seq_idx * width, 128), width)], pool_ref, sems.at[2]
        ),
    ]
    for load in loads:
        load.start()
    loads[0].wait()
    loads[1].wait()
    self_owner = head_idx * n_req + req_idx
    founds = []
    for shift in range(n_req):
        request = lax.rem(req_idx + shift, n_req)

        def note(page, found, shift=shift, request=request):
            lists[shift, found] = slot_ref[request, page]
            return found + (owner_ref[request, page] == self_owner).astype(jnp.int32)

        founds.append(lax.fori_loop(0, n_pages, note, jnp.int32(0), unroll=8))

    def tally(page, counts):
        owner = owner_ref[req_idx, page]
        return tuple(
            counts[shift]
            + (owner == head_idx * n_req + lax.rem(req_idx + n_req - shift, n_req)).astype(jnp.int32)
            for shift in range(n_req)
        )

    counts = lax.fori_loop(0, n_pages, tally, (jnp.int32(0),) * n_req, unroll=8)
    for shift in range(n_req):
        count_ref[shift] = counts[shift]
    loads[2].wait()
    step = 16
    row = lax.broadcasted_iota(jnp.int32, (step * step, step * step), 0)
    column = lax.broadcasted_iota(jnp.int32, (step * step, step * step), 1)
    swap = ((row // step == column % step) & (row % step == column // step)).astype(jnp.bfloat16)
    for page in range(0, pool_pages, step):
        for pair in range(0, pairs, step):
            rows = jnp.concatenate(
                [
                    pool_ref[page : page + step, (pair + i) * pair_width : (pair + i + 1) * pair_width]
                    for i in range(step)
                ],
                axis=0,
            )
            turned = jnp.dot(swap, rows, preferred_element_type=jnp.float32).astype(jnp.bfloat16)
            pages[page : page + step, pair : pair + step, :] = turned.reshape(step, step, pair_width)
    for shift in range(n_req):
        for rank in range(cap):
            slot = jnp.where(rank < founds[shift], lists[shift, rank], 0)
            if shift > 0:
                target, sem = foreign_ref.at[shift - 1, rank], sems.at[3]
            elif rank < chunk:
                target, sem = first_ref.at[rank], sems.at[4]
            else:
                target, sem = rest_ref.at[rank - chunk], sems.at[5]
            pltpu.make_async_copy(pages.at[slot], target, sem).start()
    pltpu.make_async_copy(foreign_ref, foreign_ref, sems.at[3]).wait()
    pltpu.make_async_copy(first_ref, first_ref, sems.at[4]).wait()
    if cap > chunk:
        pltpu.make_async_copy(rest_ref, rest_ref, sems.at[5]).wait()


def pick_pages(page_owner, page_slot, page_pool, cap, chunk, n_req, n_seq, pairs):
    pool_pages, page_width = page_pool.shape
    page = (pairs // n_seq, page_width // pairs)
    return pl.pallas_call(
        functools.partial(pick_kernel, cap),
        out_shape=(
            jax.ShapeDtypeStruct((n_req,), jnp.int32),
            jax.ShapeDtypeStruct((chunk, *page), jnp.bfloat16),
            jax.ShapeDtypeStruct((max(1, cap - chunk), *page), jnp.bfloat16),
            jax.ShapeDtypeStruct((n_req - 1, cap, *page), jnp.bfloat16),
        ),
        in_specs=[any_spec(), any_spec(), any_spec()],
        out_specs=(smem_spec(), any_spec(), any_spec(), any_spec()),
        scratch_shapes=[
            pltpu.SMEM(page_owner.shape, jnp.int32),
            pltpu.SMEM(page_slot.shape, jnp.int32),
            pltpu.VMEM((pool_pages, page_width // n_seq), jnp.bfloat16),
            pltpu.VMEM((pool_pages, *page), jnp.bfloat16),
            pltpu.SMEM((n_req, cap + 1), jnp.int32),
            pltpu.SemaphoreType.DMA((6,)),
        ],
        compiler_params=pltpu.CompilerParams(vmem_limit_bytes=VMEM_LIMIT),
        cost_estimate=pl.CostEstimate(flops=10**9, bytes_accessed=6 * 10**6, transcendentals=0),
        name="pick_pages",
    )(page_owner, page_slot, page_pool)


def join_kernel(chunk, cap, count_ref, rest_ref, *refs):
    n_req = count_ref.shape[0]
    foreign, targets, sems = refs[: n_req - 1], refs[n_req - 1 : -1], refs[-1]
    excess = jnp.maximum(count_ref[0] - chunk, 0)
    for j in range(chunk * len(targets)):
        part, place = divmod(j, chunk)

        def fetch(condition, source):
            @pl.when(condition)
            def _():
                pltpu.make_async_copy(source, targets[part].at[place], sems.at[part]).start()

        rank = jnp.int32(j)
        taken = rank < excess
        if cap > chunk:
            fetch(taken, rest_ref.at[jnp.minimum(rank, cap - chunk - 1)])
        rank = rank - excess
        for shift in range(1, n_req):
            here = jnp.logical_not(taken) & (rank < count_ref[shift])
            fetch(here, foreign[shift - 1].at[jnp.clip(rank, 0, cap - 1)])
            taken = taken | here
            rank = rank - count_ref[shift]
        fetch(jnp.logical_not(taken), foreign[0].at[0])
    for part, target in enumerate(targets):
        pltpu.make_async_copy(target, target, sems.at[part]).wait()


def join_pages(counts, rest, foreign, chunk, cap, parts):
    shape = jax.ShapeDtypeStruct((chunk, *rest.shape[1:]), jnp.bfloat16)
    return pl.pallas_call(
        functools.partial(join_kernel, chunk, cap),
        out_shape=(shape,) * parts,
        in_specs=[smem_spec()] + [any_spec()] * (1 + len(foreign)),
        out_specs=(vmem_spec(),) * parts,
        scratch_shapes=[pltpu.SemaphoreType.DMA((parts,))],
        compiler_params=pltpu.CompilerParams(vmem_limit_bytes=VMEM_LIMIT),
        cost_estimate=pl.CostEstimate(flops=0, bytes_accessed=3 * 10**6, transcendentals=0),
        name="join_pages",
    )(counts, rest, *foreign)


def token_limits(owners, prefix, req_idx, n_head, n_req, chunk, parts, page_len):
    pages = owners.shape[0]
    order = jnp.arange(pages, dtype=jnp.int32)
    place = owners // n_req
    shift = lax.rem(req_idx + n_req - lax.rem(owners, n_req), n_req)
    key = shift * pages + order
    together = place[None, :] == place[:, None]
    rank = jnp.sum((together & (key[None, :] < key[:, None])).astype(jnp.int32), axis=1)
    held = jnp.sum((together & (shift[None, :] == 0)).astype(jnp.int32), axis=1)
    later = rank - jnp.minimum(held, chunk)
    early = (shift == 0) & (rank < chunk)
    part = jnp.where(early, 0, 1 + later // chunk)
    within = jnp.where(early, rank, lax.rem(later, chunk))
    slot = (part * n_head + place) * chunk + within
    tokens = jnp.clip(prefix - order * page_len, 0, page_len)
    slots = jnp.arange(parts * n_head * chunk, dtype=jnp.int32)
    limits = jnp.sum(jnp.where(slot[None, :] == slots[:, None], tokens[None, :], 0), axis=1)
    return limits


def score_rows(q_ref, key_block, target, mark_of, highest, weight_sum, rows, tile, scale, mask_of):
    for start in range(0, rows, tile):
        part = slice(start, start + tile)
        scores = lax.dot_general(
            q_ref[part, :], key_block[...], (((1,), (1,)), ((), ())), preferred_element_type=jnp.float32
        )
        scores = mask_of(scores * scale, start)
        old = highest[part, :]
        new = jnp.maximum(old, jnp.max(scores, axis=1, keepdims=True))
        weights = jnp.exp2(scores - new)
        highest[part, :] = new
        weight_sum[part, :] = weight_sum[part, :] * jnp.exp2(old - new) + jnp.sum(
            weights, axis=1, keepdims=True
        )
        target[part, :] = weights
        mark_of(part, new)


def block_bias(limit_ref, block, chunk, n_seq, half_pairs, block_keys):
    pair_rows = block_keys // 2
    lane = lax.broadcasted_iota(jnp.int32, (1, block_keys), 1)
    row = lax.rem(lane, pair_rows)
    slot = lax.rem(row // half_pairs, chunk)
    token = 2 * (lax.rem(row, half_pairs) + (row // (chunk * half_pairs)) * half_pairs) + lane // pair_rows
    limit = jnp.zeros_like(lane)
    for j in range(chunk):
        limit = jnp.where(slot == j, limit_ref[block * chunk + j], limit)
    return jnp.where(token < limit, 0.0, -jnp.inf)


def any_token(limit_ref, block, chunk):
    return functools.reduce(jnp.maximum, [limit_ref[block * chunk + j] for j in range(chunk)]) > 0


def load_block(block_ref, keys, key_width):
    pair_rows = keys.shape[0] // 2
    page_rows = block_ref[...].reshape(pair_rows, block_ref.shape[-1])
    keys[:pair_rows, :] = page_rows[:, :key_width]
    keys[pair_rows:, :] = page_rows[:, key_width:]


def set_mark(marks, part, block, value):
    column = lax.broadcasted_iota(jnp.int32, (value.shape[0], marks.shape[1]), 1)
    marks[part, :] = jnp.where(column == block, value, marks[part, :])


def score_kernel(shape, number, limit_ref, q_ref, *refs):
    rows, tile, scale, chunk, n_seq, n_head = shape
    refs = list(refs)
    if number > 0:
        marks_in, sum_in, high_in = [refs.pop(0) for _ in range(3)]
        refs.pop(0), refs.pop(0)
    gathered = refs.pop(0)
    weights_ref, values_ref, marks, weight_sum, highest = [refs.pop(0) for _ in range(5)]
    blocks, keys, weights, load_sems, value_sems, weight_sems = refs
    block_keys, key_width = keys.shape[1:]
    latent_width = values_ref.shape[2]
    half_pairs = blocks.shape[3]

    def load(head):
        return pltpu.make_async_copy(gathered.at[head], blocks.at[head], load_sems.at[head])

    def value_store(head):
        return pltpu.make_async_copy(
            keys.at[head, :, pl.ds(0, latent_width)], values_ref.at[number * n_head + head], value_sems.at[head]
        )

    def weight_store(head):
        return pltpu.make_async_copy(
            weights.at[head], weights_ref.at[number * n_head + head], weight_sems.at[head]
        )

    for head in range(n_head):
        load(head).start()
    if number > 0:
        marks[...] = marks_in[...]
        weight_sum[...] = sum_in[...]
        highest[...] = high_in[...]
    else:
        marks[...] = jnp.zeros_like(marks)
        weight_sum[...] = jnp.zeros_like(weight_sum)
        highest[...] = jnp.full_like(highest, LOWEST)

    def one_block(head, carry):
        load(head).wait()
        load_block(blocks.at[head], keys.at[head], key_width)
        value_store(head).start()

        @pl.when(any_token(limit_ref, head, chunk))
        def _():
            bias = block_bias(limit_ref, head, chunk, n_seq, half_pairs, block_keys)
            score_rows(
                q_ref, keys.at[head], weights.at[head],
                lambda part, new: set_mark(marks, part, number * n_head + head, new),
                highest, weight_sum, rows, tile, scale, lambda scores, start: scores + bias,
            )

        weight_store(head).start()
        return carry

    lax.fori_loop(0, n_head, one_block, 0)
    for head in range(n_head):
        value_store(head).wait()
        weight_store(head).wait()


def score_part(number, parts, limits, q_rows, gathered, state, shape, latent_width):
    rows, tile, scale, chunk, n_seq, n_head = shape
    key_width = q_rows.shape[1]
    _, _, half_pairs, pair_width = gathered.shape[1:]
    block_keys = 2 * n_seq * chunk * half_pairs
    total = (parts - 1) * n_head
    out_shape = (
        jax.ShapeDtypeStruct((total, rows, block_keys), jnp.float32),
        jax.ShapeDtypeStruct((total, block_keys, latent_width), jnp.bfloat16),
        jax.ShapeDtypeStruct((rows, total), jnp.float32),
        jax.ShapeDtypeStruct((rows, 1), jnp.float32),
        jax.ShapeDtypeStruct((rows, 1), jnp.float32),
    )
    operands = [limits, q_rows]
    specs = [smem_spec(), vmem_spec()]
    aliases = {}
    if number > 0:
        operands += [state[2], state[3], state[4], state[0], state[1]]
        specs += [vmem_spec()] * 3 + [any_spec()] * 2
        aliases = {5: 0, 6: 1}
    operands.append(gathered)
    specs.append(any_spec())
    work = n_head * block_keys * rows
    return pl.pallas_call(
        functools.partial(score_kernel, shape, number),
        out_shape=out_shape,
        in_specs=specs,
        out_specs=(any_spec(), any_spec(), vmem_spec(), vmem_spec(), vmem_spec()),
        scratch_shapes=[
            pltpu.VMEM((n_head, n_seq, chunk, half_pairs, pair_width), jnp.bfloat16),
            pltpu.VMEM((n_head, block_keys, key_width), jnp.bfloat16),
            pltpu.VMEM((n_head, rows, block_keys), jnp.float32),
            pltpu.SemaphoreType.DMA((n_head,)),
            pltpu.SemaphoreType.DMA((n_head,)),
            pltpu.SemaphoreType.DMA((n_head,)),
        ],
        input_output_aliases=aliases,
        compiler_params=pltpu.CompilerParams(vmem_limit_bytes=VMEM_LIMIT),
        cost_estimate=pl.CostEstimate(
            flops=2 * work * key_width, bytes_accessed=10**7, transcendentals=work
        ),
        name="score_part",
    )(*operands)


def finish_kernel(
    shape, depth, limit_ref, q_ref, marks, sum_in, high_in, weights_hbm, values_hbm, gathered,
    suffix_ref, earlier_ref, fresh_ref, up_ref, out_ref,
    weight_sum, highest, total, blocks, keys, last_weights, last_marks, near_keys, near_weights, near_mark,
    weights, values, load_sems, weight_sems, value_sems,
):
    rows, tile, scale, chunk, n_seq, n_head = shape
    n_blocks = weights_hbm.shape[0]
    block_keys, key_width = keys.shape[1:]
    latent_width = total.shape[1]
    half_pairs = blocks.shape[3]
    half_len = earlier_ref.shape[0]
    seq_idx = lax.axis_index("seq")
    live = suffix_ref[0]

    def load(head):
        return pltpu.make_async_copy(gathered.at[head], blocks.at[head], load_sems.at[head])

    def fetches(block):
        place = lax.rem(block, depth)
        return (
            pltpu.make_async_copy(weights_hbm.at[block], weights.at[place], weight_sems.at[place]),
            pltpu.make_async_copy(values_hbm.at[block], values.at[place], value_sems.at[place]),
        )

    def fetch(block):
        for copy in fetches(block):
            copy.start()

    for head in range(n_head):
        load(head).start()
    for block in range(min(depth, n_blocks)):
        fetch(block)
    weight_sum[...] = sum_in[...]
    highest[...] = high_in[...]
    near_keys[:half_len, :] = earlier_ref[...]
    near_keys[half_len:, :] = fresh_ref[...]

    def near(scores, start):
        row = lax.broadcasted_iota(jnp.int32, scores.shape, 0) + start
        place = lax.broadcasted_iota(jnp.int32, scores.shape, 1) + (seq_idx - 1) * half_len
        query = lax.rem(row, half_len) + seq_idx * half_len
        allowed = (place >= 0) & (place <= query) & (place < live)
        return jnp.where(allowed, scores, -jnp.inf)

    def near_note(part, new):
        near_mark[part, :] = new

    score_rows(
        q_ref, near_keys, near_weights, near_note, highest, weight_sum, rows, tile, scale, near
    )
    last_base = n_blocks

    def one_score(head, carry):
        load(head).wait()

        @pl.when(any_token(limit_ref, last_base + head, chunk))
        def _():
            load_block(blocks.at[head], keys.at[head], key_width)
            bias = block_bias(limit_ref, last_base + head, chunk, n_seq, half_pairs, block_keys)
            score_rows(
                q_ref, keys.at[head], last_weights.at[head],
                lambda part, new: set_mark(last_marks, part, head, new),
                highest, weight_sum, rows, tile, scale, lambda scores, start: scores + bias,
            )

        return carry

    last_marks[...] = jnp.zeros_like(last_marks)
    lax.fori_loop(0, n_head, one_score, 0)

    def add_block(weight_block, value_block, mark_of):
        for start in range(0, rows, tile):
            part = slice(start, start + tile)
            factor = jnp.exp2(mark_of(part) - highest[part, :]) / weight_sum[part, :]
            total[part, :] += jnp.dot(
                (weight_block[part, :] * factor).astype(jnp.bfloat16),
                value_block,
                preferred_element_type=jnp.float32,
            )

    def mark_column(table, block):
        def mark_of(part):
            chosen = table[part, :]
            column = lax.broadcasted_iota(jnp.int32, chosen.shape, 1)
            return jnp.sum(jnp.where(column == block, chosen, 0.0), axis=1, keepdims=True)

        return mark_of

    total[...] = jnp.zeros_like(total)
    add_block(near_weights, near_keys[:, :latent_width], lambda part: near_mark[part, :])

    def one_add(block, carry):
        for copy in fetches(block):
            copy.wait()

        @pl.when(any_token(limit_ref, block, chunk))
        def _():
            place = lax.rem(block, depth)
            add_block(weights.at[place], values[place], mark_column(marks, block))

        @pl.when(block + depth < n_blocks)
        def _():
            fetch(block + depth)

        return carry

    lax.fori_loop(0, n_blocks, one_add, 0)

    def one_last(head, carry):
        @pl.when(any_token(limit_ref, last_base + head, chunk))
        def _():
            add_block(
                last_weights.at[head], keys[head, :, :latent_width], mark_column(last_marks, head)
            )

        return carry

    lax.fori_loop(0, n_head, one_last, 0)
    heads, _, value_width = up_ref.shape
    steps = lax.broadcasted_iota(jnp.int32, (half_len, value_width), 0) + seq_idx * half_len
    for head in range(heads):
        latent = total[head * half_len : (head + 1) * half_len, :].astype(jnp.bfloat16)
        raised = jnp.dot(latent, up_ref[head], preferred_element_type=jnp.float32)
        out_ref[:, head * value_width : (head + 1) * value_width] = jnp.where(
            steps < live, raised, 0.0
        ).astype(jnp.bfloat16)


def finish(limits, q_rows, state, gathered, suffix, earlier, fresh, up_weight, shape):
    rows, tile, scale, chunk, n_seq, n_head = shape
    weights, values, marks, weight_sum, highest = state
    key_width = q_rows.shape[1]
    n_blocks, block_keys, latent_width = values.shape
    half_len = fresh.shape[0]
    heads, _, value_width = up_weight.shape
    depth = min(4, n_blocks)
    column = pltpu.VMEM((rows, 1), jnp.float32)
    work = (n_blocks + n_head) * block_keys * rows
    return pl.pallas_call(
        functools.partial(finish_kernel, shape, depth),
        out_shape=jax.ShapeDtypeStruct((half_len, heads * value_width), jnp.bfloat16),
        in_specs=[smem_spec()] + [vmem_spec()] * 4 + [any_spec()] * 3 + [smem_spec()] + [vmem_spec()] * 3,
        out_specs=vmem_spec(),
        scratch_shapes=[
            column,
            column,
            pltpu.VMEM((rows, latent_width), jnp.float32),
            pltpu.VMEM(gathered.shape, jnp.bfloat16),
            pltpu.VMEM((n_head, block_keys, key_width), jnp.bfloat16),
            pltpu.VMEM((n_head, rows, block_keys), jnp.float32),
            pltpu.VMEM((rows, n_head), jnp.float32),
            pltpu.VMEM((2 * half_len, key_width), jnp.bfloat16),
            pltpu.VMEM((rows, 2 * half_len), jnp.float32),
            column,
            pltpu.VMEM((depth, rows, block_keys), jnp.float32),
            pltpu.VMEM((depth, block_keys, latent_width), jnp.bfloat16),
            pltpu.SemaphoreType.DMA((n_head,)),
            pltpu.SemaphoreType.DMA((depth,)),
            pltpu.SemaphoreType.DMA((depth,)),
        ],
        compiler_params=pltpu.CompilerParams(vmem_limit_bytes=VMEM_LIMIT),
        cost_estimate=pl.CostEstimate(
            flops=2 * work * latent_width, bytes_accessed=3 * 10**7, transcendentals=work // 4
        ),
        name="finish",
    )(
        limits, q_rows, marks, weight_sum, highest, weights, values, gathered,
        suffix, earlier, fresh, up_weight,
    )


def local(
    queries,
    hidden,
    w_dkv,
    kv_gain,
    w_uk,
    value_up_weight,
    page_pool,
    page_owner,
    page_slot,
    prefix_len,
    suffix_len,
):
    n_head = lax.axis_size("head")
    n_req = lax.axis_size("req")
    n_seq = lax.axis_size("seq")
    req_idx = lax.axis_index("req")
    seq_idx = lax.axis_index("seq")
    _, half_len, d_local = hidden.shape
    heads_dev, nope_width, latent_width = w_uk.shape
    lat_width = w_dkv.shape[1]
    rope_width = lat_width - latent_width
    query_width = queries.shape[2] // heads_dev
    page_width = page_pool.shape[1]
    page_len = page_width // lat_width
    pairs = page_len // 2
    pages_req = page_slot.shape[1]
    cap = max(2, 2 * pages_req // (n_head * n_req))
    parts = 4
    chunk = n_req * cap // parts
    score_scale = float(query_width) ** (-0.5)

    owner_rows = page_owner[:, :, 0]
    counts, first, rest, foreign = pick_pages(
        owner_rows, page_slot, page_pool, cap, chunk, n_req, n_seq, pairs
    )
    gather = functools.partial(lax.all_gather, axis_name=("head", "seq"), axis=0, tiled=False)
    gathered = [gather(first)]
    arrived = [
        lax.ppermute(foreign[s - 1], "req", [(i, (i + s) % n_req) for i in range(n_req)])
        for s in range(1, n_req)
    ]
    joined = join_pages(counts, rest, arrived, chunk, cap, parts - 1)
    gathered += [gather(part) for part in joined]
    gathered = [g.reshape(n_head, n_seq, *g.shape[1:]) for g in gathered]

    my_prefix = lax.dynamic_index_in_dim(prefix_len, req_idx, 0, keepdims=False)
    my_suffix = lax.dynamic_index_in_dim(suffix_len, req_idx, 0, keepdims=False)
    own_owners = lax.dynamic_index_in_dim(owner_rows, req_idx, 0, keepdims=False)
    limits = token_limits(own_owners, my_prefix, req_idx, n_head, n_req, chunk, parts, page_len)
    local_t = jnp.arange(half_len, dtype=jnp.int32)
    glob_t = seq_idx * half_len + local_t
    positions = my_prefix + glob_t
    live_rows = glob_t < my_suffix

    partial_value = jnp.dot(hidden[0], w_dkv, preferred_element_type=jnp.float32)
    summed = lax.psum(partial_value, "head")
    fresh = finish_latent(summed, positions, live_rows, kv_gain, latent_width)
    new_pages = fresh.reshape(1, half_len // page_len, page_len * lat_width)
    earlier = from_behind(fresh, "seq", 1)

    query_rows = queries[0].reshape(half_len, heads_dev, query_width)
    q_latent = jnp.einsum(
        "thn,hnk->htk", query_rows[..., :nope_width], w_uk, preferred_element_type=jnp.float32
    ).astype(jnp.bfloat16)
    cosine_table, sine_table = angles(positions, rope_width)
    q_rotated = rotate(
        jnp.swapaxes(query_rows[..., nope_width:], 0, 1).astype(jnp.float32), cosine_table, sine_table
    ).astype(jnp.bfloat16)
    rows = heads_dev * half_len
    q_rows = jnp.concatenate([q_latent, q_rotated], axis=-1).reshape(rows, lat_width)

    tile = 256 if rows % 256 == 0 else rows
    shape = (rows, tile, score_scale * math.log2(math.e), chunk, n_seq, n_head)
    state = None
    part_slots = n_head * chunk
    for number in range(parts - 1):
        part_limits = limits[number * part_slots : (number + 1) * part_slots]
        state = score_part(
            number, parts, part_limits, q_rows, gathered[number], state, shape, latent_width
        )
    attn_out = finish(
        limits, q_rows, state, gathered[-1], my_suffix.reshape(1), earlier, fresh, value_up_weight, shape
    )
    return (attn_out[None], new_pages)


def solution(mesh):
    placed = (
        P(("groups", "req"), "seq", "head"),
        P(("groups", "req"), "seq", "head"),
        P("head", None),
        P(),
        P("head", None, None),
        P("head", None, None),
        P(("groups", "head", "req"), None),
        P("groups", None, None),
        P("groups", None),
        P("groups"),
        P("groups"),
    )
    return jax.shard_map(
        local,
        mesh=mesh,
        in_specs=placed,
        out_specs=(P(("groups", "req"), "seq", "head"), P(("groups", "req"), "seq", None)),
        check_vma=False,
    )
```

```python
import functools
import math

import jax
import jax.numpy as jnp
from jax import lax
from jax.experimental import pallas as pl
from jax.experimental.pallas import tpu as pltpu
from jax.sharding import PartitionSpec as P

LOWEST = -1e30
MASKED = -1e38
VMEM_LIMIT = 48 * 1024 * 1024


def from_behind(block, axis, distance):
    devices = range(lax.axis_size(axis))
    route = [(i - distance, i) for i in devices if i - distance in devices]
    return lax.ppermute(block, axis, route)


def rotate(vector, cosine_table, sine_table):
    half_width = vector.shape[-1] // 2
    first_half = vector[..., :half_width]
    second_half = vector[..., half_width:]
    return jnp.concatenate(
        [
            first_half * cosine_table - second_half * sine_table,
            first_half * sine_table + second_half * cosine_table,
        ],
        axis=-1,
    )


def angles(positions, rope_width):
    half_width = rope_width // 2
    frequency = 10000.0 ** (-2.0 * jnp.arange(half_width, dtype=jnp.float32) / rope_width)
    phases = positions.astype(jnp.float32)[:, None] * frequency[None, :]
    return (jnp.cos(phases), jnp.sin(phases))


def finish_latent(summed, positions, live_rows, kv_gain, latent_width):
    latent_part = summed[:, :latent_width]
    mean_square = jnp.mean(latent_part * latent_part, axis=-1, keepdims=True)
    normed = latent_part * lax.rsqrt(mean_square + 1e-06) * kv_gain
    cosine_table, sine_table = angles(positions, summed.shape[1] - latent_width)
    rotated = rotate(summed[:, latent_width:], cosine_table, sine_table)
    joined = jnp.concatenate([normed, rotated], axis=-1).astype(jnp.bfloat16)
    return jnp.where(live_rows[:, None], joined, jnp.zeros_like(joined))


def any_spec():
    return pl.BlockSpec(memory_space=pl.ANY)


def smem_spec():
    return pl.BlockSpec(memory_space=pltpu.SMEM)


def vmem_spec():
    return pl.BlockSpec(memory_space=pltpu.VMEM)


def hbm_spec():
    return pl.BlockSpec(memory_space=pltpu.HBM)


def pick_kernel(
    cap, owner_hbm, slot_hbm, pool_hbm, count_ref, first_ref, rest_ref, foreign_ref,
    owner_ref, slot_ref, pool_ref, pages, lists, sems,
):
    n_req = lax.axis_size("req")
    head_idx = lax.axis_index("head")
    req_idx = lax.axis_index("req")
    seq_idx = lax.axis_index("seq")
    n_pages = owner_ref.shape[1]
    pool_pages, pairs, pair_width = pages.shape
    chunk = first_ref.shape[0]
    loads = [
        pltpu.make_async_copy(owner_hbm, owner_ref, sems.at[0]),
        pltpu.make_async_copy(slot_hbm, slot_ref, sems.at[1]),
        pltpu.make_async_copy(pool_hbm, pool_ref, sems.at[2]),
    ]
    for load in loads:
        load.start()
    loads[0].wait()
    loads[1].wait()
    self_owner = head_idx * n_req + req_idx
    founds = []
    for shift in range(n_req):
        request = lax.rem(req_idx + shift, n_req)

        def note(page, found, shift=shift, request=request):
            lists[shift, found] = slot_ref[request, page]
            return found + (owner_ref[request, page] == self_owner).astype(jnp.int32)

        founds.append(lax.fori_loop(0, n_pages, note, jnp.int32(0), unroll=8))

    def tally(page, counts):
        owner = owner_ref[req_idx, page]
        return tuple(
            counts[shift]
            + (owner == head_idx * n_req + lax.rem(req_idx + n_req - shift, n_req)).astype(jnp.int32)
            for shift in range(n_req)
        )

    counts = lax.fori_loop(0, n_pages, tally, (jnp.int32(0),) * n_req, unroll=8)
    for shift in range(n_req):
        count_ref[shift] = counts[shift]
    loads[2].wait()
    step = 16
    row = lax.broadcasted_iota(jnp.int32, (step * step, step * step), 0)
    column = lax.broadcasted_iota(jnp.int32, (step * step, step * step), 1)
    swap = ((row // step == column % step) & (row % step == column // step)).astype(jnp.bfloat16)
    for page in range(0, pool_pages, step):
        for pair in range(0, pairs, step):
            rows = jnp.concatenate(
                [
                    pool_ref[page : page + step, (pair + i) * pair_width : (pair + i + 1) * pair_width]
                    for i in range(step)
                ],
                axis=0,
            )
            turned = jnp.dot(swap, rows, preferred_element_type=jnp.float32).astype(jnp.bfloat16)
            pages[page : page + step, pair : pair + step, :] = turned.reshape(step, step, pair_width)

    def send(shift, rank, target, sem):
        slot = jnp.where(rank < founds[shift], lists[shift, rank], 0)
        pltpu.make_async_copy(pages.at[slot], target, sem).start()

    for rank in range(cap):
        if rank < chunk:
            send(0, rank, first_ref.at[rank], sems.at[3])
        else:
            send(0, rank, rest_ref.at[rank - chunk], sems.at[4])
    half_cap = foreign_ref.shape[1]
    for shift in range(1, n_req):
        for j in range(half_cap):
            send(shift, seq_idx * half_cap + j, foreign_ref.at[shift - 1, j], sems.at[5])
    pltpu.make_async_copy(first_ref, first_ref, sems.at[3]).wait()
    if cap > chunk:
        pltpu.make_async_copy(rest_ref, rest_ref, sems.at[4]).wait()
    pltpu.make_async_copy(foreign_ref, foreign_ref, sems.at[5]).wait()


def pick_pages(page_owner, page_slot, page_pool, cap, chunk, n_req, n_seq, pairs):
    pool_pages, page_width = page_pool.shape
    page = (pairs, page_width // pairs)
    return pl.pallas_call(
        functools.partial(pick_kernel, cap),
        out_shape=(
            jax.ShapeDtypeStruct((n_req,), jnp.int32),
            jax.ShapeDtypeStruct((chunk, *page), jnp.bfloat16),
            jax.ShapeDtypeStruct((max(1, cap - chunk), *page), jnp.bfloat16),
            jax.ShapeDtypeStruct((n_req - 1, cap // n_seq, *page), jnp.bfloat16),
        ),
        in_specs=[any_spec(), any_spec(), hbm_spec()],
        out_specs=(smem_spec(), hbm_spec(), hbm_spec(), hbm_spec()),
        scratch_shapes=[
            pltpu.SMEM(page_owner.shape, jnp.int32),
            pltpu.SMEM(page_slot.shape, jnp.int32),
            pltpu.VMEM((pool_pages, page_width), jnp.bfloat16),
            pltpu.VMEM((pool_pages, *page), jnp.bfloat16),
            pltpu.SMEM((n_req, cap + 1), jnp.int32),
            pltpu.SemaphoreType.DMA((6,)),
        ],
        compiler_params=pltpu.CompilerParams(vmem_limit_bytes=VMEM_LIMIT),
        cost_estimate=pl.CostEstimate(flops=10**9, bytes_accessed=6 * 10**6, transcendentals=0),
        name="pick_pages",
    )(page_owner, page_slot, page_pool)


def join_kernel(chunk, cap, count_ref, rest_ref, mine_ref, other_ref, *refs):
    n_req = count_ref.shape[0]
    targets, sems = refs[:-1], refs[-1]
    seq_idx = lax.axis_index("seq")
    half_cap = mine_ref.shape[1]
    excess = jnp.maximum(count_ref[0] - chunk, 0)
    j = 0
    for part, target in enumerate(targets):
        for place in range(target.shape[0]):

            def fetch(condition, source, target=target, place=place, part=part):
                @pl.when(condition)
                def _():
                    pltpu.make_async_copy(source, target.at[place], sems.at[part]).start()

            rank = jnp.int32(j)
            taken = rank < excess
            if cap > chunk:
                fetch(taken, rest_ref.at[jnp.minimum(rank, cap - chunk - 1)])
            rank = rank - excess
            for shift in range(1, n_req):
                here = jnp.logical_not(taken) & (rank < count_ref[shift])
                half = rank // half_cap
                slot = jnp.clip(rank - half * half_cap, 0, half_cap - 1)
                fetch(here & (half == seq_idx), mine_ref.at[shift - 1, slot])
                fetch(here & (half != seq_idx), other_ref.at[shift - 1, slot])
                taken = taken | here
                rank = rank - count_ref[shift]
            fetch(jnp.logical_not(taken), mine_ref.at[0, 0])
            j += 1
    for part, target in enumerate(targets):
        pltpu.make_async_copy(target, target, sems.at[part]).wait()


def join_pages(counts, rest, mine, other, chunk, cap, sizes):
    return pl.pallas_call(
        functools.partial(join_kernel, chunk, cap),
        out_shape=tuple(jax.ShapeDtypeStruct((size, *rest.shape[1:]), jnp.bfloat16) for size in sizes),
        in_specs=[smem_spec()] + [hbm_spec()] * 3,
        out_specs=(vmem_spec(),) * len(sizes),
        scratch_shapes=[pltpu.SemaphoreType.DMA((len(sizes),))],
        compiler_params=pltpu.CompilerParams(vmem_limit_bytes=VMEM_LIMIT),
        cost_estimate=pl.CostEstimate(flops=0, bytes_accessed=3 * 10**6, transcendentals=0),
        name="join_pages",
    )(counts, rest, mine, other)


def token_limits(owners, prefix, req_idx, n_head, n_req, chunk, slots, page_len):
    pages = owners.shape[0]
    order = jnp.arange(pages, dtype=jnp.int32)
    place = owners // n_req
    shift = lax.rem(req_idx + n_req - lax.rem(owners, n_req), n_req)
    key = shift * pages + order
    together = place[None, :] == place[:, None]
    rank = jnp.sum((together & (key[None, :] < key[:, None])).astype(jnp.int32), axis=1)
    held = jnp.sum((together & (shift[None, :] == 0)).astype(jnp.int32), axis=1)
    early = (shift == 0) & (rank < chunk)
    within = jnp.where(early, rank, chunk + rank - jnp.minimum(held, chunk))
    slot = place * slots + within
    tokens = jnp.clip(prefix - order * page_len, 0, page_len)
    all_slots = jnp.arange(n_head * slots, dtype=jnp.int32)
    limits = jnp.sum(jnp.where(slot[None, :] == all_slots[:, None], tokens[None, :], 0), axis=1)
    return limits.reshape(n_head, slots)


def most_later(owner_rows, n_head, n_req, chunk):
    owners = jnp.arange(n_head * n_req, dtype=jnp.int32)
    held = jnp.sum((owner_rows[:, None, :] == owners[None, :, None]).astype(jnp.int32), axis=2)
    held = held.reshape(-1, n_head, n_req)
    own = jnp.arange(n_req)[None, None, :] == jnp.arange(held.shape[0])[:, None, None]
    early = jnp.minimum(jnp.sum(jnp.where(own, held, 0), axis=2), chunk)
    most = jnp.max(jnp.sum(held, axis=2) - early).reshape(1)
    n_groups = lax.axis_size("groups")
    passed = most
    for _ in range(n_groups - 1):
        passed = lax.ppermute(passed, "groups", [(i, (i + 1) % n_groups) for i in range(n_groups)])
        most = jnp.maximum(most, passed)
    return most[0]


def score_block(keys, queries_ref, target, note, highest, weight_sum, tile, scale, bias=None):
    rows = queries_ref.shape[1]
    for start in range(0, rows, tile):
        part = slice(start, start + tile)
        scores = jnp.dot(keys[...], queries_ref[:, part], preferred_element_type=jnp.float32) * scale
        if bias is not None:
            scores = scores + bias
        old = highest[:, part]
        new = jnp.maximum(old, jnp.max(scores, axis=0, keepdims=True))
        weights = jnp.exp2(scores - new)
        highest[:, part] = new
        weight_sum[:, part] = weight_sum[:, part] * jnp.exp2(old - new) + jnp.sum(
            weights, axis=0, keepdims=True
        )
        target[:, part] = weights
        note(part, new)


def block_limits(limit_ref, block, chunk):
    return [limit_ref[block * chunk + j] for j in range(chunk)]


def any_token(limit_ref, block, chunk):
    return functools.reduce(jnp.maximum, block_limits(limit_ref, block, chunk)) > 0


def load_block(block_ref, keys, limits, key_width):
    chunk, pairs, pair_width = block_ref.shape
    pair_rows = chunk * pairs
    page_rows = block_ref[...].reshape(pair_rows, pair_width)
    keys[:pair_rows, :key_width] = page_rows[:, :key_width]
    keys[pair_rows:, :key_width] = page_rows[:, key_width:]
    shape = (2 * pair_rows, keys.shape[1] - key_width)
    row = lax.broadcasted_iota(jnp.int32, shape, 0)
    pair_row = lax.rem(row, pair_rows)
    token = 2 * lax.rem(pair_row, pairs) + row // pair_rows
    limit = jnp.zeros_like(row)
    for j, value in enumerate(limits):
        limit = jnp.where(pair_row // pairs == j, value, limit)
    masked = (lax.broadcasted_iota(jnp.int32, shape, 1) == 0) & (token >= limit)
    keys[:, key_width:] = jnp.where(masked, MASKED, 0.0).astype(jnp.bfloat16)


def turn_values(keys, latent_width):
    return keys[:, :latent_width].T


def near_bias(n_keys, half_len, tile, live):
    seq_idx = lax.axis_index("seq")
    place = lax.broadcasted_iota(jnp.int32, (n_keys, tile), 0) + (seq_idx - 1) * half_len
    query = lax.rem(lax.broadcasted_iota(jnp.int32, (n_keys, tile), 1), half_len) + seq_idx * half_len
    allowed = (place >= 0) & (place <= query) & (place < live)
    return jnp.where(allowed, 0.0, -jnp.inf)


def score_kernel(shape, base, n_sources, first, near, limit_ref, queries_ref, *refs):
    tile, scale, chunk, key_width = shape
    refs = list(refs)
    if not first:
        marks_in, sum_in, high_in = [refs.pop(0) for _ in range(3)]
        refs.pop(0), refs.pop(0)
    if near:
        live_ref, earlier_ref, fresh_ref = [refs.pop(0) for _ in range(3)]
    sources = [refs.pop(0) for _ in range(n_sources)]
    weights_hbm, values_hbm, marks, weight_sum, highest = [refs.pop(0) for _ in range(5)]
    if near:
        near_weights, near_values, near_mark = [refs.pop(0) for _ in range(3)]
    blocks, keys, weights, values, load_sems, weight_sems, value_sems = [refs.pop(0) for _ in range(7)]
    n_blocks = blocks.shape[0]
    latent_width = values.shape[1]
    index = 0
    for source in sources:
        for i in range(source.shape[0] // chunk):
            pltpu.make_async_copy(
                source.at[i * chunk : (i + 1) * chunk], blocks.at[index], load_sems.at[index]
            ).start()
            index += 1
    if first:
        marks[...] = jnp.zeros_like(marks)
        weight_sum[...] = jnp.zeros_like(weight_sum)
        highest[...] = jnp.full_like(highest, LOWEST)
    else:
        marks[...] = marks_in[...]
        weight_sum[...] = sum_in[...]
        highest[...] = high_in[...]

    def stores(block):
        return (
            pltpu.make_async_copy(weights.at[block], weights_hbm.at[base + block], weight_sems.at[block]),
            pltpu.make_async_copy(values.at[block], values_hbm.at[base + block], value_sems.at[block]),
        )

    def one_block(block, carry):
        pltpu.make_async_copy(blocks.at[block], blocks.at[block], load_sems.at[block]).wait()

        @pl.when(any_token(limit_ref, block, chunk))
        def _():
            load_block(blocks.at[block], keys, block_limits(limit_ref, block, chunk), key_width)

            def note(part, new):
                marks[pl.ds(base + block, 1), part] = new

            score_block(
                keys, queries_ref, weights.at[block], note, highest, weight_sum, tile, scale
            )
            values[block] = turn_values(keys, latent_width)
            for copy in stores(block):
                copy.start()

        return carry

    lax.fori_loop(0, n_blocks, one_block, 0)
    if near:
        near_keys = refs.pop(0)
        half_len = fresh_ref.shape[0]
        near_keys[:, key_width:] = jnp.zeros_like(near_keys[:, key_width:])
        near_keys[:half_len, :key_width] = earlier_ref[...]
        near_keys[half_len:, :key_width] = fresh_ref[...]

        def note_near(part, new):
            near_mark[:, part] = new

        score_block(
            near_keys, queries_ref, near_weights, note_near, highest, weight_sum, tile, scale,
            near_bias(2 * half_len, half_len, tile, live_ref[0]),
        )
        near_values[...] = turn_values(near_keys, latent_width)

    def one_wait(block, carry):
        @pl.when(any_token(limit_ref, block, chunk))
        def _():
            for copy in stores(block):
                copy.wait()

        return carry

    lax.fori_loop(0, n_blocks, one_wait, 0)


def score_part(base, total, limits, queries, sources, state, shape, latent_width, near=None):
    tile, scale, chunk, key_width = shape
    width, rows = queries.shape
    _, pairs, pair_width = sources[0].shape
    block_keys = 2 * chunk * pairs
    n_blocks = sum(s.shape[0] for s in sources) // chunk
    row = jax.ShapeDtypeStruct((1, rows), jnp.float32)
    out_shape = [
        jax.ShapeDtypeStruct((total, block_keys, rows), jnp.float32),
        jax.ShapeDtypeStruct((total, latent_width, block_keys), jnp.bfloat16),
        jax.ShapeDtypeStruct((total, rows), jnp.float32),
        row,
        row,
    ]
    out_specs = [hbm_spec(), hbm_spec(), vmem_spec(), vmem_spec(), vmem_spec()]
    operands = [limits, queries]
    specs = [smem_spec(), vmem_spec()]
    aliases = {}
    if state is not None:
        operands += [state[2], state[3], state[4], state[0], state[1]]
        specs += [vmem_spec()] * 3 + [hbm_spec()] * 2
        aliases = {5: 0, 6: 1}
    scratch = [
        pltpu.VMEM((n_blocks, chunk, pairs, pair_width), jnp.bfloat16),
        pltpu.VMEM((block_keys, width), jnp.bfloat16),
        pltpu.VMEM((n_blocks, block_keys, rows), jnp.float32),
        pltpu.VMEM((n_blocks, latent_width, block_keys), jnp.bfloat16),
        pltpu.SemaphoreType.DMA((n_blocks,)),
        pltpu.SemaphoreType.DMA((n_blocks,)),
        pltpu.SemaphoreType.DMA((n_blocks,)),
    ]
    if near is not None:
        near_keys = 2 * near[-1].shape[0]
        operands += list(near)
        specs += [smem_spec(), vmem_spec(), vmem_spec()]
        out_shape += [
            jax.ShapeDtypeStruct((near_keys, rows), jnp.float32),
            jax.ShapeDtypeStruct((latent_width, near_keys), jnp.bfloat16),
            row,
        ]
        out_specs += [vmem_spec()] * 3
        scratch.append(pltpu.VMEM((near_keys, width), jnp.bfloat16))
    operands += list(sources)
    specs += [hbm_spec()] * len(sources)
    work = n_blocks * block_keys * rows // 2
    return pl.pallas_call(
        functools.partial(score_kernel, shape, base, len(sources), state is None, near is not None),
        out_shape=tuple(out_shape),
        in_specs=specs,
        out_specs=tuple(out_specs),
        scratch_shapes=scratch,
        input_output_aliases=aliases,
        compiler_params=pltpu.CompilerParams(vmem_limit_bytes=VMEM_LIMIT),
        cost_estimate=pl.CostEstimate(
            flops=2 * work * key_width, bytes_accessed=10**7, transcendentals=work
        ),
        name="score_part",
    )(*operands)


def finish_kernel(
    shape, depth, n_blocks, n_sources, limit_ref, last_limit_ref, queries_ref, marks, sum_in, high_in,
    near_weights, near_values, near_mark, live_ref, up_ref, weights_hbm, values_hbm, *refs,
):
    tile, scale, chunk, key_width = shape
    sources, refs = refs[:n_sources], refs[n_sources:]
    (
        out_ref, weight_sum, highest, total, blocks, keys, last_weights, last_values, last_marks,
        weights, values, used, load_sems, weight_sems, value_sems,
    ) = refs
    rows = queries_ref.shape[1]
    latent_width = total.shape[0]
    n_last = blocks.shape[0]
    index = 0
    for source in sources:
        for i in range(source.shape[0] // chunk):
            pltpu.make_async_copy(
                source.at[i * chunk : (i + 1) * chunk], blocks.at[index], load_sems.at[index]
            ).start()
            index += 1

    def list_block(block, count):
        used[count] = block
        return count + any_token(limit_ref, block, chunk).astype(jnp.int32)

    n_used = lax.fori_loop(0, n_blocks, list_block, jnp.int32(0))

    def fetches(number):
        place = lax.rem(number, depth)
        return (
            pltpu.make_async_copy(weights_hbm.at[used[number]], weights.at[place], weight_sems.at[place]),
            pltpu.make_async_copy(values_hbm.at[used[number]], values.at[place], value_sems.at[place]),
        )

    def fetch(number):
        @pl.when(number < n_used)
        def _():
            for copy in fetches(number):
                copy.start()

    for number in range(depth):
        fetch(jnp.int32(number))
    weight_sum[...] = sum_in[...]
    highest[...] = high_in[...]
    last_marks[...] = jnp.zeros_like(last_marks)

    def one_score(block, carry):
        pltpu.make_async_copy(blocks.at[block], blocks.at[block], load_sems.at[block]).wait()

        @pl.when(any_token(last_limit_ref, block, chunk))
        def _():
            load_block(blocks.at[block], keys, block_limits(last_limit_ref, block, chunk), key_width)

            def note(part, new):
                last_marks[pl.ds(block, 1), part] = new

            score_block(
                keys, queries_ref, last_weights.at[block], note, highest, weight_sum, tile, scale
            )
            last_values[block] = turn_values(keys, latent_width)

        return carry

    lax.fori_loop(0, n_last, one_score, 0)

    def add_block(weight_block, value_block, mark, begin=False):
        for start in range(0, rows, tile):
            part = slice(start, start + tile)
            factor = jnp.exp2(mark[:, part] - highest[:, part]) / weight_sum[:, part]
            added = jnp.dot(
                value_block[...],
                (weight_block[:, part] * factor).astype(jnp.bfloat16),
                preferred_element_type=jnp.float32,
            )
            total[:, part] = added if begin else total[:, part] + added

    add_block(near_weights, near_values, near_mark, begin=True)

    def one_add(number, carry):
        for copy in fetches(number):
            copy.wait()
        place = lax.rem(number, depth)
        add_block(weights.at[place], values.at[place], marks.at[pl.ds(used[number], 1)])
        fetch(number + depth)
        return carry

    lax.fori_loop(0, n_used, one_add, 0)

    def one_last(block, carry):
        @pl.when(any_token(last_limit_ref, block, chunk))
        def _():
            add_block(last_weights.at[block], last_values.at[block], last_marks.at[pl.ds(block, 1)])

        return carry

    lax.fori_loop(0, n_last, one_last, 0)
    heads, _, value_width = up_ref.shape
    half_len = out_ref.shape[0]
    steps = lax.broadcasted_iota(jnp.int32, (half_len, value_width), 0)
    steps = steps + lax.axis_index("seq") * half_len
    for head in range(heads):
        latent = total[:, head * half_len : (head + 1) * half_len].astype(jnp.bfloat16)
        raised = lax.dot_general(
            latent, up_ref[head], (((0,), (0,)), ((), ())), preferred_element_type=jnp.float32
        )
        out_ref[:, head * value_width : (head + 1) * value_width] = jnp.where(
            steps < live_ref[0], raised, 0.0
        ).astype(jnp.bfloat16)


def finish(n_blocks, limits, last_limits, queries, state, near_state, sources, live, up_weight, half_len, shape):
    tile, scale, chunk, key_width = shape
    weights, values, marks, weight_sum, highest = state
    width, rows = queries.shape
    _, latent_width, block_keys = values.shape
    _, pairs, pair_width = sources[0].shape
    heads, _, value_width = up_weight.shape
    depth = 4
    n_last = sum(s.shape[0] for s in sources) // chunk
    row = pltpu.VMEM((1, rows), jnp.float32)
    work = (n_blocks // 2 + n_last) * block_keys * rows
    return pl.pallas_call(
        functools.partial(finish_kernel, shape, depth, n_blocks, len(sources)),
        out_shape=jax.ShapeDtypeStruct((half_len, heads * value_width), jnp.bfloat16),
        in_specs=[smem_spec()] * 2
        + [vmem_spec()] * 7
        + [smem_spec(), vmem_spec()]
        + [hbm_spec()] * (2 + len(sources)),
        out_specs=vmem_spec(),
        scratch_shapes=[
            row,
            row,
            pltpu.VMEM((latent_width, rows), jnp.float32),
            pltpu.VMEM((n_last, chunk, pairs, pair_width), jnp.bfloat16),
            pltpu.VMEM((block_keys, width), jnp.bfloat16),
            pltpu.VMEM((n_last, block_keys, rows), jnp.float32),
            pltpu.VMEM((n_last, latent_width, block_keys), jnp.bfloat16),
            pltpu.VMEM((n_last, rows), jnp.float32),
            pltpu.VMEM((depth, block_keys, rows), jnp.float32),
            pltpu.VMEM((depth, latent_width, block_keys), jnp.bfloat16),
            pltpu.SMEM((n_blocks + depth + 1,), jnp.int32),
            pltpu.SemaphoreType.DMA((n_last,)),
            pltpu.SemaphoreType.DMA((depth,)),
            pltpu.SemaphoreType.DMA((depth,)),
        ],
        compiler_params=pltpu.CompilerParams(vmem_limit_bytes=VMEM_LIMIT),
        cost_estimate=pl.CostEstimate(
            flops=2 * work * latent_width, bytes_accessed=3 * 10**7, transcendentals=work // 4
        ),
        name="finish",
    )(
        limits, last_limits, queries, marks, weight_sum, highest, *near_state, live, up_weight,
        weights, values, *sources,
    )


def local(
    queries,
    hidden,
    w_dkv,
    kv_gain,
    w_uk,
    value_up_weight,
    page_pool,
    page_owner,
    page_slot,
    prefix_len,
    suffix_len,
):
    n_head = lax.axis_size("head")
    n_req = lax.axis_size("req")
    n_seq = lax.axis_size("seq")
    head_idx = lax.axis_index("head")
    req_idx = lax.axis_index("req")
    seq_idx = lax.axis_index("seq")
    _, half_len, d_local = hidden.shape
    heads_dev, nope_width, latent_width = w_uk.shape
    lat_width = w_dkv.shape[1]
    rope_width = lat_width - latent_width
    query_width = queries.shape[2] // heads_dev
    page_width = page_pool.shape[1]
    page_len = page_width // lat_width
    pairs = page_len // 2
    pages_req = page_slot.shape[1]
    cap = max(2, 2 * pages_req // (n_head * n_req))
    chunk = n_req * cap // 4
    slots = 4 * chunk
    score_scale = float(query_width) ** (-0.5)

    owner_rows = page_owner[:, :, 0]
    counts, first, rest, foreign = pick_pages(
        owner_rows, page_slot, page_pool, cap, chunk, n_req, n_seq, pairs
    )
    swap_route = [(i, n_seq - 1 - i) for i in range(n_seq)]
    stream_route = []
    for i in range(n_head - 1):
        stream_route.append((i * n_seq, (i + 1) * n_seq))
        stream_route.append(((i + 1) * n_seq + 1, i * n_seq + 1))

    def swap(block):
        return lax.ppermute(block, "seq", swap_route)

    def ring(block):
        steps = []
        for _ in range(n_head - 1):
            block = lax.ppermute(block, ("head", "seq"), stream_route)
            steps.append([block, swap(block)])
        return steps

    early_steps = ring(first)
    arrived = [
        lax.ppermute(foreign[s - 1], "req", [(i, (i + s) % n_req) for i in range(n_req)])
        for s in range(1, n_req)
    ]
    mine = arrived[0][None] if n_req == 2 else jnp.stack(arrived)
    other = swap(mine)
    middle, late = join_pages(counts, rest, mine, other, chunk, cap, (2 * chunk, chunk))
    middle_steps = ring(middle)
    most = most_later(owner_rows, n_head, n_req, chunk)

    my_prefix = lax.dynamic_index_in_dim(prefix_len, req_idx, 0, keepdims=False)
    my_suffix = lax.dynamic_index_in_dim(suffix_len, req_idx, 0, keepdims=False)
    own_owners = lax.dynamic_index_in_dim(owner_rows, req_idx, 0, keepdims=False)
    place_limits = token_limits(own_owners, my_prefix, req_idx, n_head, n_req, chunk, slots, page_len)
    upward = 2 * seq_idx - 1
    origins = [head_idx]
    for step in range(1, n_head):
        origins += [head_idx + upward * step, head_idx - upward * step]
    origins = jnp.stack(origins)
    heads = jnp.arange(n_head, dtype=jnp.int32)
    limits = jnp.sum(
        jnp.where((origins[:, None] == heads[None, :])[:, :, None], place_limits[None], 0), axis=1
    )

    local_t = jnp.arange(half_len, dtype=jnp.int32)
    glob_t = seq_idx * half_len + local_t
    positions = my_prefix + glob_t
    live_rows = glob_t < my_suffix
    partial_value = jnp.dot(hidden[0], w_dkv, preferred_element_type=jnp.float32)
    summed = lax.psum(partial_value, "head")
    fresh = finish_latent(summed, positions, live_rows, kv_gain, latent_width)
    new_pages = fresh.reshape(1, half_len // page_len, page_len * lat_width)
    earlier = from_behind(fresh, "seq", 1)

    rows = heads_dev * half_len
    query_rows = queries[0].reshape(half_len, heads_dev, query_width)
    q_latent = jnp.einsum(
        "thn,hnk->kht", query_rows[..., :nope_width], w_uk, preferred_element_type=jnp.float32
    ).astype(jnp.bfloat16)
    cosine_table, sine_table = angles(positions, rope_width)
    q_rotated = rotate(
        query_rows[..., nope_width:].astype(jnp.float32), cosine_table[:, None, :], sine_table[:, None, :]
    ).astype(jnp.bfloat16)
    q_rotated = jnp.transpose(q_rotated, (2, 1, 0))
    q_turned = jnp.concatenate(
        [
            q_latent.reshape(latent_width, rows),
            q_rotated.reshape(rope_width, rows),
            jnp.ones((1, rows), jnp.bfloat16),
            jnp.zeros((63, rows), jnp.bfloat16),
        ],
        axis=0,
    )

    tile = 256 if rows % 256 == 0 and 256 % half_len == 0 else half_len
    shape = (tile, score_scale * math.log2(math.e), chunk, lat_width)
    parts = {"early": (0, chunk), "middle": (chunk, 3 * chunk), "late": (3 * chunk, 4 * chunk)}

    def limits_of(pieces):
        return jnp.concatenate(
            [limits[origin, parts[name][0] : parts[name][1]] for name, origin in pieces]
        )

    def pieces_of(name, steps):
        return [(name, 2 * step + side + 1) for step in steps for side in range(2)]

    def arrays_of(arrived_steps, steps):
        return [arrived_steps[step][side] for step in steps for side in range(2)]

    last = n_head - 2
    cut = (last + 1) // 2
    calls = [
        (
            [("early", 0)] + pieces_of("early", range(last + 1)) + [("middle", 0)],
            [first] + arrays_of(early_steps, range(last + 1)) + [middle],
        ),
        (pieces_of("middle", range(cut)), arrays_of(middle_steps, range(cut))),
        (pieces_of("middle", range(cut, last)), arrays_of(middle_steps, range(cut, last))),
    ]
    n_blocks = 0
    state = None
    used_limits = []
    extra = (2 * 2 + 1 + 2 * last) if last >= 0 else 0
    total = sum(sum(a.shape[0] for a in arrays) // chunk for _, arrays in calls) + extra
    live = my_suffix.reshape(1)
    near_state = None
    for number, (pieces, arrays) in enumerate(calls):
        near = (live, earlier, fresh) if number == len(calls) - 1 else None
        used_limits.append(limits_of(pieces))
        state = score_part(
            n_blocks, total, used_limits[-1], q_turned, arrays, state, shape, latent_width, near
        )
        state, near_state = state[:5], state[5:]
        n_blocks += sum(a.shape[0] for a in arrays) // chunk

    last_pieces = pieces_of("middle", [last])
    last_arrays = arrays_of(middle_steps, [last])

    def end(blocks, limit_list, final_pieces, final_arrays, current):
        return finish(
            blocks, jnp.concatenate(limit_list), limits_of(final_pieces), q_turned, current, near_state,
            final_arrays, live, value_up_weight, half_len, shape,
        )

    def with_late(_):
        late_steps = ring(late)
        pieces = last_pieces + [("late", 0)] + pieces_of("late", range(last))
        arrays = last_arrays + [late] + arrays_of(late_steps, range(last))
        more = limits_of(pieces)
        current = score_part(
            n_blocks, total, more, q_turned, arrays, state, shape, latent_width
        )
        return end(
            n_blocks + sum(a.shape[0] for a in arrays) // chunk,
            used_limits + [more],
            pieces_of("late", [last]),
            arrays_of(late_steps, [last]),
            current,
        )

    def without_late(_):
        return end(n_blocks, used_limits, last_pieces, last_arrays, state)

    attn_out = lax.cond(most > 2 * chunk, with_late, without_late, 0)
    return (attn_out[None], new_pages)


def solution(mesh):
    placed = (
        P(("groups", "req"), "seq", "head"),
        P(("groups", "req"), "seq", "head"),
        P("head", None),
        P(),
        P("head", None, None),
        P("head", None, None),
        P(("groups", "head", "req"), None),
        P("groups", None, None),
        P("groups", None),
        P("groups"),
        P("groups"),
    )
    return jax.shard_map(
        local,
        mesh=mesh,
        in_specs=placed,
        out_specs=(P(("groups", "req"), "seq", "head"), P(("groups", "req"), "seq", None)),
        check_vma=False,
    )
```

```python
import functools
import math

import jax
import jax.numpy as jnp
from jax import lax
from jax.experimental import pallas as pl
from jax.experimental.pallas import tpu as pltpu
from jax.sharding import PartitionSpec as P

LOWEST = -1e30
MASKED = -1e38
VMEM_LIMIT = 60 * 1024 * 1024


def rotate(vector, cosine_table, sine_table):
    half_width = vector.shape[-1] // 2
    first_half = vector[..., :half_width]
    second_half = vector[..., half_width:]
    return jnp.concatenate(
        [
            first_half * cosine_table - second_half * sine_table,
            first_half * sine_table + second_half * cosine_table,
        ],
        axis=-1,
    )


def angles(positions, rope_width):
    half_width = rope_width // 2
    frequency = 10000.0 ** (-2.0 * jnp.arange(half_width, dtype=jnp.float32) / rope_width)
    phases = positions.astype(jnp.float32)[:, None] * frequency[None, :]
    return (jnp.cos(phases), jnp.sin(phases))


def finish_latent(summed, positions, live_rows, kv_gain, latent_width):
    latent_part = summed[:, :latent_width]
    mean_square = jnp.mean(latent_part * latent_part, axis=-1, keepdims=True)
    normed = latent_part * lax.rsqrt(mean_square + 1e-06) * kv_gain
    cosine_table, sine_table = angles(positions, summed.shape[1] - latent_width)
    rotated = rotate(summed[:, latent_width:], cosine_table, sine_table)
    joined = jnp.concatenate([normed, rotated], axis=-1).astype(jnp.bfloat16)
    return jnp.where(live_rows[:, None], joined, jnp.zeros_like(joined))


def any_spec():
    return pl.BlockSpec(memory_space=pl.ANY)


def smem_spec():
    return pl.BlockSpec(memory_space=pltpu.SMEM)


def vmem_spec():
    return pl.BlockSpec(memory_space=pltpu.VMEM)


def hbm_spec():
    return pl.BlockSpec(memory_space=pltpu.HBM)


def pick_kernel(
    cap, owner_hbm, slot_hbm, pool_hbm, count_ref, first_ref, rest_ref, foreign_ref,
    owner_ref, slot_ref, pool_ref, pages, lists, sems,
):
    n_req = lax.axis_size("req")
    head_idx = lax.axis_index("head")
    req_idx = lax.axis_index("req")
    seq_idx = lax.axis_index("seq")
    n_pages = owner_ref.shape[1]
    pool_pages, pairs, pair_width = pages.shape
    chunk = first_ref.shape[0]
    loads = [
        pltpu.make_async_copy(owner_hbm, owner_ref, sems.at[0]),
        pltpu.make_async_copy(slot_hbm, slot_ref, sems.at[1]),
        pltpu.make_async_copy(pool_hbm, pool_ref, sems.at[2]),
    ]
    for load in loads:
        load.start()
    loads[0].wait()
    loads[1].wait()
    self_owner = head_idx * n_req + req_idx
    founds = []
    for shift in range(n_req):
        request = lax.rem(req_idx + shift, n_req)

        def note(page, found, shift=shift, request=request):
            lists[shift, found] = slot_ref[request, page]
            return found + (owner_ref[request, page] == self_owner).astype(jnp.int32)

        founds.append(lax.fori_loop(0, n_pages, note, jnp.int32(0), unroll=8))

    def tally(page, counts):
        owner = owner_ref[req_idx, page]
        return tuple(
            counts[shift]
            + (owner == head_idx * n_req + lax.rem(req_idx + n_req - shift, n_req)).astype(jnp.int32)
            for shift in range(n_req)
        )

    counts = lax.fori_loop(0, n_pages, tally, (jnp.int32(0),) * n_req, unroll=8)
    for shift in range(n_req):
        count_ref[shift] = counts[shift]
    loads[2].wait()
    step = 16
    row = lax.broadcasted_iota(jnp.int32, (step * step, step * step), 0)
    column = lax.broadcasted_iota(jnp.int32, (step * step, step * step), 1)
    swap = ((row // step == column % step) & (row % step == column // step)).astype(jnp.bfloat16)
    for page in range(0, pool_pages, step):
        for pair in range(0, pairs, step):
            rows = jnp.concatenate(
                [
                    pool_ref[page : page + step, (pair + i) * pair_width : (pair + i + 1) * pair_width]
                    for i in range(step)
                ],
                axis=0,
            )
            turned = jnp.dot(swap, rows, preferred_element_type=jnp.float32).astype(jnp.bfloat16)
            pages[page : page + step, pair : pair + step, :] = turned.reshape(step, step, pair_width)

    def send(shift, rank, target, sem):
        slot = jnp.where(rank < founds[shift], lists[shift, rank], 0)
        pltpu.make_async_copy(pages.at[slot], target, sem).start()

    for rank in range(cap):
        if rank < chunk:
            send(0, rank, first_ref.at[rank], sems.at[3])
        else:
            send(0, rank, rest_ref.at[rank - chunk], sems.at[4])
    half_cap = foreign_ref.shape[1]
    for shift in range(1, n_req):
        for j in range(half_cap):
            send(shift, seq_idx * half_cap + j, foreign_ref.at[shift - 1, j], sems.at[5])
    pltpu.make_async_copy(first_ref, first_ref, sems.at[3]).wait()
    if cap > chunk:
        pltpu.make_async_copy(rest_ref, rest_ref, sems.at[4]).wait()
    pltpu.make_async_copy(foreign_ref, foreign_ref, sems.at[5]).wait()


def pick_pages(page_owner, page_slot, page_pool, cap, chunk, n_req, n_seq, pairs):
    pool_pages, page_width = page_pool.shape
    page = (pairs, page_width // pairs)
    return pl.pallas_call(
        functools.partial(pick_kernel, cap),
        out_shape=(
            jax.ShapeDtypeStruct((n_req,), jnp.int32),
            jax.ShapeDtypeStruct((chunk, *page), jnp.bfloat16),
            jax.ShapeDtypeStruct((max(1, cap - chunk), *page), jnp.bfloat16),
            jax.ShapeDtypeStruct((n_req - 1, cap // n_seq, *page), jnp.bfloat16),
        ),
        in_specs=[any_spec(), any_spec(), hbm_spec()],
        out_specs=(smem_spec(), hbm_spec(), hbm_spec(), hbm_spec()),
        scratch_shapes=[
            pltpu.SMEM(page_owner.shape, jnp.int32),
            pltpu.SMEM(page_slot.shape, jnp.int32),
            pltpu.VMEM((pool_pages, page_width), jnp.bfloat16),
            pltpu.VMEM((pool_pages, *page), jnp.bfloat16),
            pltpu.SMEM((n_req, cap + 1), jnp.int32),
            pltpu.SemaphoreType.DMA((6,)),
        ],
        compiler_params=pltpu.CompilerParams(vmem_limit_bytes=VMEM_LIMIT),
        cost_estimate=pl.CostEstimate(flops=10**9, bytes_accessed=6 * 10**6, transcendentals=0),
        name="pick_pages",
    )(page_owner, page_slot, page_pool)


def join_kernel(chunk, cap, count_ref, rest_ref, mine_ref, other_ref, *refs):
    n_req = count_ref.shape[0]
    targets, sems = refs[:-1], refs[-1]
    seq_idx = lax.axis_index("seq")
    half_cap = mine_ref.shape[1]
    excess = jnp.maximum(count_ref[0] - chunk, 0)
    j = 0
    for part, target in enumerate(targets):
        for place in range(target.shape[0]):

            def fetch(condition, source, target=target, place=place, part=part):
                @pl.when(condition)
                def _():
                    pltpu.make_async_copy(source, target.at[place], sems.at[part]).start()

            rank = jnp.int32(j)
            taken = rank < excess
            if cap > chunk:
                fetch(taken, rest_ref.at[jnp.minimum(rank, cap - chunk - 1)])
            rank = rank - excess
            for shift in range(1, n_req):
                here = jnp.logical_not(taken) & (rank < count_ref[shift])
                half = rank // half_cap
                slot = jnp.clip(rank - half * half_cap, 0, half_cap - 1)
                fetch(here & (half == seq_idx), mine_ref.at[shift - 1, slot])
                fetch(here & (half != seq_idx), other_ref.at[shift - 1, slot])
                taken = taken | here
                rank = rank - count_ref[shift]
            fetch(jnp.logical_not(taken), mine_ref.at[0, 0])
            j += 1
    for part, target in enumerate(targets):
        pltpu.make_async_copy(target, target, sems.at[part]).wait()


def join_pages(counts, rest, mine, other, chunk, cap, sizes):
    return pl.pallas_call(
        functools.partial(join_kernel, chunk, cap),
        out_shape=tuple(jax.ShapeDtypeStruct((size, *rest.shape[1:]), jnp.bfloat16) for size in sizes),
        in_specs=[smem_spec()] + [hbm_spec()] * 3,
        out_specs=(vmem_spec(),) * len(sizes),
        scratch_shapes=[pltpu.SemaphoreType.DMA((len(sizes),))],
        compiler_params=pltpu.CompilerParams(vmem_limit_bytes=VMEM_LIMIT),
        cost_estimate=pl.CostEstimate(flops=0, bytes_accessed=3 * 10**6, transcendentals=0),
        name="join_pages",
    )(counts, rest, mine, other)


def token_limits(owners, prefix, req_idx, n_head, n_req, chunk, slots, page_len):
    pages = owners.shape[0]
    order = jnp.arange(pages, dtype=jnp.int32)
    place = owners // n_req
    shift = lax.rem(req_idx + n_req - lax.rem(owners, n_req), n_req)
    key = shift * pages + order
    together = place[None, :] == place[:, None]
    rank = jnp.sum((together & (key[None, :] < key[:, None])).astype(jnp.int32), axis=1)
    held = jnp.sum((together & (shift[None, :] == 0)).astype(jnp.int32), axis=1)
    early = (shift == 0) & (rank < chunk)
    within = jnp.where(early, rank, chunk + rank - jnp.minimum(held, chunk))
    slot = place * slots + within
    tokens = jnp.clip(prefix - order * page_len, 0, page_len)
    all_slots = jnp.arange(n_head * slots, dtype=jnp.int32)
    limits = jnp.sum(jnp.where(slot[None, :] == all_slots[:, None], tokens[None, :], 0), axis=1)
    return limits.reshape(n_head, slots)


def most_later(owner_rows, n_head, n_req, chunk):
    owners = jnp.arange(n_head * n_req, dtype=jnp.int32)
    held = jnp.sum((owner_rows[:, None, :] == owners[None, :, None]).astype(jnp.int32), axis=2)
    held = held.reshape(-1, n_head, n_req)
    own = jnp.arange(n_req)[None, None, :] == jnp.arange(held.shape[0])[:, None, None]
    early = jnp.minimum(jnp.sum(jnp.where(own, held, 0), axis=2), chunk)
    most = jnp.max(jnp.sum(held, axis=2) - early).reshape(1)
    n_groups = lax.axis_size("groups")
    passed = most
    for _ in range(n_groups - 1):
        passed = lax.ppermute(passed, "groups", [(i, (i + 1) % n_groups) for i in range(n_groups)])
        most = jnp.maximum(most, passed)
    return most[0]


def score_block(keys, queries_ref, target, note, highest, weight_sum, tile, scale, bias=None):
    rows = queries_ref.shape[1]
    for start in range(0, rows, tile):
        part = slice(start, start + tile)
        scores = jnp.dot(keys[...], queries_ref[:, part], preferred_element_type=jnp.float32) * scale
        if bias is not None:
            scores = scores + bias
        old = highest[:, part]
        new = jnp.maximum(old, jnp.max(scores, axis=0, keepdims=True))
        weights = jnp.exp2(scores - new)
        highest[:, part] = new
        weight_sum[:, part] = weight_sum[:, part] * jnp.exp2(old - new) + jnp.sum(
            weights, axis=0, keepdims=True
        )
        target[:, part] = weights
        note(part, new)


def block_limits(limit_ref, block, chunk):
    return [limit_ref[block * chunk + j] for j in range(chunk)]


def any_token(limit_ref, block, chunk):
    return functools.reduce(jnp.maximum, block_limits(limit_ref, block, chunk)) > 0


def load_block(block_ref, keys, limits, key_width):
    chunk, pairs, pair_width = block_ref.shape
    pair_rows = chunk * pairs
    page_rows = block_ref[...].reshape(pair_rows, pair_width)
    keys[:pair_rows, :key_width] = page_rows[:, :key_width]
    keys[pair_rows:, :key_width] = page_rows[:, key_width:]
    shape = (2 * pair_rows, keys.shape[1] - key_width)
    row = lax.broadcasted_iota(jnp.int32, shape, 0)
    pair_row = lax.rem(row, pair_rows)
    token = 2 * lax.rem(pair_row, pairs) + row // pair_rows
    limit = jnp.zeros_like(row)
    for j, value in enumerate(limits):
        limit = jnp.where(pair_row // pairs == j, value, limit)
    masked = (lax.broadcasted_iota(jnp.int32, shape, 1) == 0) & (token >= limit)
    keys[:, key_width:] = jnp.where(masked, MASKED, 0.0).astype(jnp.bfloat16)


def turn_values(keys, latent_width):
    return keys[:, :latent_width].T


def near_bias(n_keys, half_len, tile, live):
    seq_idx = lax.axis_index("seq")
    place = lax.broadcasted_iota(jnp.int32, (n_keys, tile), 0)
    query = lax.rem(lax.broadcasted_iota(jnp.int32, (n_keys, tile), 1), half_len) + seq_idx * half_len
    allowed = (place <= query) & (place < live)
    return jnp.where(allowed, 0.0, -jnp.inf)


def score_kernel(shape, base, n_sources, first, near, limit_ref, queries_ref, *refs):
    tile, scale, chunk, key_width = shape
    refs = list(refs)
    if not first:
        marks_in, sum_in, high_in = [refs.pop(0) for _ in range(3)]
        refs.pop(0), refs.pop(0)
    if near:
        live_ref, suffix_ref = refs.pop(0), refs.pop(0)
    sources = [refs.pop(0) for _ in range(n_sources)]
    weights_hbm, values_hbm, marks, weight_sum, highest = [refs.pop(0) for _ in range(5)]
    if near:
        near_weights, near_values, near_mark = [refs.pop(0) for _ in range(3)]
    blocks, keys, weights, values, load_sems, weight_sems, value_sems = [refs.pop(0) for _ in range(7)]
    n_blocks = blocks.shape[0]
    latent_width = values.shape[1]
    index = 0
    for source in sources:
        for i in range(source.shape[0] // chunk):
            pltpu.make_async_copy(
                source.at[i * chunk : (i + 1) * chunk], blocks.at[index], load_sems.at[index]
            ).start()
            index += 1
    if first:
        marks[...] = jnp.zeros_like(marks)
        weight_sum[...] = jnp.zeros_like(weight_sum)
        highest[...] = jnp.full_like(highest, LOWEST)
    else:
        marks[...] = marks_in[...]
        weight_sum[...] = sum_in[...]
        highest[...] = high_in[...]

    def stores(block):
        return (
            pltpu.make_async_copy(weights.at[block], weights_hbm.at[base + block], weight_sems.at[block]),
            pltpu.make_async_copy(values.at[block], values_hbm.at[base + block], value_sems.at[block]),
        )

    def one_block(block, carry):
        pltpu.make_async_copy(blocks.at[block], blocks.at[block], load_sems.at[block]).wait()

        @pl.when(any_token(limit_ref, block, chunk))
        def _():
            load_block(blocks.at[block], keys, block_limits(limit_ref, block, chunk), key_width)

            def note(part, new):
                marks[pl.ds(base + block, 1), part] = new

            score_block(
                keys, queries_ref, weights.at[block], note, highest, weight_sum, tile, scale
            )
            values[block] = turn_values(keys, latent_width)
            for copy in stores(block):
                copy.start()

        return carry

    lax.fori_loop(0, n_blocks, one_block, 0)
    if near:
        near_keys = refs.pop(0)
        n_near = suffix_ref.shape[0]
        near_keys[:, key_width:] = jnp.zeros_like(near_keys[:, key_width:])
        near_keys[:, :key_width] = suffix_ref[...]

        def note_near(part, new):
            near_mark[:, part] = new

        score_block(
            near_keys, queries_ref, near_weights, note_near, highest, weight_sum, tile, scale,
            near_bias(n_near, n_near // lax.axis_size("seq"), tile, live_ref[0]),
        )
        near_values[...] = turn_values(near_keys, latent_width)

    def one_wait(block, carry):
        @pl.when(any_token(limit_ref, block, chunk))
        def _():
            for copy in stores(block):
                copy.wait()

        return carry

    lax.fori_loop(0, n_blocks, one_wait, 0)


def score_part(base, total, limits, queries, sources, state, shape, latent_width, near=None):
    tile, scale, chunk, key_width = shape
    width, rows = queries.shape
    _, pairs, pair_width = sources[0].shape
    block_keys = 2 * chunk * pairs
    n_blocks = sum(s.shape[0] for s in sources) // chunk
    row = jax.ShapeDtypeStruct((1, rows), jnp.float32)
    out_shape = [
        jax.ShapeDtypeStruct((total, block_keys, rows), jnp.float32),
        jax.ShapeDtypeStruct((total, latent_width, block_keys), jnp.bfloat16),
        jax.ShapeDtypeStruct((total, rows), jnp.float32),
        row,
        row,
    ]
    out_specs = [hbm_spec(), hbm_spec(), vmem_spec(), vmem_spec(), vmem_spec()]
    operands = [limits, queries]
    specs = [smem_spec(), vmem_spec()]
    aliases = {}
    if state is not None:
        operands += [state[2], state[3], state[4], state[0], state[1]]
        specs += [vmem_spec()] * 3 + [hbm_spec()] * 2
        aliases = {5: 0, 6: 1}
    scratch = [
        pltpu.VMEM((n_blocks, chunk, pairs, pair_width), jnp.bfloat16),
        pltpu.VMEM((block_keys, width), jnp.bfloat16),
        pltpu.VMEM((n_blocks, block_keys, rows), jnp.float32),
        pltpu.VMEM((n_blocks, latent_width, block_keys), jnp.bfloat16),
        pltpu.SemaphoreType.DMA((n_blocks,)),
        pltpu.SemaphoreType.DMA((n_blocks,)),
        pltpu.SemaphoreType.DMA((n_blocks,)),
    ]
    if near is not None:
        near_keys = near[-1].shape[0]
        operands += list(near)
        specs += [smem_spec(), vmem_spec()]
        out_shape += [
            jax.ShapeDtypeStruct((near_keys, rows), jnp.float32),
            jax.ShapeDtypeStruct((latent_width, near_keys), jnp.bfloat16),
            row,
        ]
        out_specs += [vmem_spec()] * 3
        scratch.append(pltpu.VMEM((near_keys, width), jnp.bfloat16))
    operands += list(sources)
    specs += [hbm_spec()] * len(sources)
    work = n_blocks * block_keys * rows // 2
    return pl.pallas_call(
        functools.partial(score_kernel, shape, base, len(sources), state is None, near is not None),
        out_shape=tuple(out_shape),
        in_specs=specs,
        out_specs=tuple(out_specs),
        scratch_shapes=scratch,
        input_output_aliases=aliases,
        compiler_params=pltpu.CompilerParams(vmem_limit_bytes=VMEM_LIMIT),
        cost_estimate=pl.CostEstimate(
            flops=work, bytes_accessed=10**5, transcendentals=0
        ),
        name="score_part",
    )(*operands)


def finish_kernel(
    shape, depth, n_blocks, n_sources, limit_ref, last_limit_ref, queries_ref, marks, sum_in, high_in,
    near_weights, near_values, near_mark, live_ref, up_ref, weights_hbm, values_hbm, *refs,
):
    tile, scale, chunk, key_width = shape
    sources, refs = refs[:n_sources], refs[n_sources:]
    (
        out_ref, weight_sum, highest, total, blocks, keys, last_weights, last_values, last_marks,
        weights, values, used, load_sems, weight_sems, value_sems,
    ) = refs
    rows = queries_ref.shape[1]
    latent_width = total.shape[0]
    n_last = blocks.shape[0]
    index = 0
    for source in sources:
        for i in range(source.shape[0] // chunk):
            pltpu.make_async_copy(
                source.at[i * chunk : (i + 1) * chunk], blocks.at[index], load_sems.at[index]
            ).start()
            index += 1

    def list_block(block, count):
        used[count] = block
        return count + any_token(limit_ref, block, chunk).astype(jnp.int32)

    n_used = lax.fori_loop(0, n_blocks, list_block, jnp.int32(0))

    def fetches(number):
        place = lax.rem(number, depth)
        return (
            pltpu.make_async_copy(weights_hbm.at[used[number]], weights.at[place], weight_sems.at[place]),
            pltpu.make_async_copy(values_hbm.at[used[number]], values.at[place], value_sems.at[place]),
        )

    def fetch(number):
        @pl.when(number < n_used)
        def _():
            for copy in fetches(number):
                copy.start()

    for number in range(depth):
        fetch(jnp.int32(number))
    weight_sum[...] = sum_in[...]
    highest[...] = high_in[...]
    last_marks[...] = jnp.zeros_like(last_marks)

    def one_score(block, carry):
        pltpu.make_async_copy(blocks.at[block], blocks.at[block], load_sems.at[block]).wait()

        @pl.when(any_token(last_limit_ref, block, chunk))
        def _():
            load_block(blocks.at[block], keys, block_limits(last_limit_ref, block, chunk), key_width)

            def note(part, new):
                last_marks[pl.ds(block, 1), part] = new

            score_block(
                keys, queries_ref, last_weights.at[block], note, highest, weight_sum, tile, scale
            )
            last_values[block] = turn_values(keys, latent_width)

        return carry

    lax.fori_loop(0, n_last, one_score, 0)

    def add_block(weight_block, value_block, mark, begin=False):
        for start in range(0, rows, tile):
            part = slice(start, start + tile)
            factor = jnp.exp2(mark[:, part] - highest[:, part]) / weight_sum[:, part]
            added = jnp.dot(
                value_block[...],
                (weight_block[:, part] * factor).astype(jnp.bfloat16),
                preferred_element_type=jnp.float32,
            )
            total[:, part] = added if begin else total[:, part] + added

    add_block(near_weights, near_values, near_mark, begin=True)

    def one_add(number, carry):
        for copy in fetches(number):
            copy.wait()
        place = lax.rem(number, depth)
        add_block(weights.at[place], values.at[place], marks.at[pl.ds(used[number], 1)])
        fetch(number + depth)
        return carry

    lax.fori_loop(0, n_used, one_add, 0)

    def one_last(block, carry):
        @pl.when(any_token(last_limit_ref, block, chunk))
        def _():
            add_block(last_weights.at[block], last_values.at[block], last_marks.at[pl.ds(block, 1)])

        return carry

    lax.fori_loop(0, n_last, one_last, 0)
    heads, _, value_width = up_ref.shape
    half_len = out_ref.shape[0]
    steps = lax.broadcasted_iota(jnp.int32, (half_len, value_width), 0)
    steps = steps + lax.axis_index("seq") * half_len
    for head in range(heads):
        latent = total[:, head * half_len : (head + 1) * half_len].astype(jnp.bfloat16)
        raised = lax.dot_general(
            latent, up_ref[head], (((0,), (0,)), ((), ())), preferred_element_type=jnp.float32
        )
        out_ref[:, head * value_width : (head + 1) * value_width] = jnp.where(
            steps < live_ref[0], raised, 0.0
        ).astype(jnp.bfloat16)


def finish(n_blocks, limits, last_limits, queries, state, near_state, sources, live, up_weight, half_len, shape):
    tile, scale, chunk, key_width = shape
    weights, values, marks, weight_sum, highest = state
    width, rows = queries.shape
    _, latent_width, block_keys = values.shape
    _, pairs, pair_width = sources[0].shape
    heads, _, value_width = up_weight.shape
    depth = 4
    n_last = sum(s.shape[0] for s in sources) // chunk
    row = pltpu.VMEM((1, rows), jnp.float32)
    work = (n_blocks // 2 + n_last) * block_keys * rows
    return pl.pallas_call(
        functools.partial(finish_kernel, shape, depth, n_blocks, len(sources)),
        out_shape=jax.ShapeDtypeStruct((half_len, heads * value_width), jnp.bfloat16),
        in_specs=[smem_spec()] * 2
        + [vmem_spec()] * 7
        + [smem_spec(), vmem_spec()]
        + [hbm_spec()] * (2 + len(sources)),
        out_specs=vmem_spec(),
        scratch_shapes=[
            row,
            row,
            pltpu.VMEM((latent_width, rows), jnp.float32),
            pltpu.VMEM((n_last, chunk, pairs, pair_width), jnp.bfloat16),
            pltpu.VMEM((block_keys, width), jnp.bfloat16),
            pltpu.VMEM((n_last, block_keys, rows), jnp.float32),
            pltpu.VMEM((n_last, latent_width, block_keys), jnp.bfloat16),
            pltpu.VMEM((n_last, rows), jnp.float32),
            pltpu.VMEM((depth, block_keys, rows), jnp.float32),
            pltpu.VMEM((depth, latent_width, block_keys), jnp.bfloat16),
            pltpu.SMEM((n_blocks + depth + 1,), jnp.int32),
            pltpu.SemaphoreType.DMA((n_last,)),
            pltpu.SemaphoreType.DMA((depth,)),
            pltpu.SemaphoreType.DMA((depth,)),
        ],
        compiler_params=pltpu.CompilerParams(vmem_limit_bytes=VMEM_LIMIT),
        cost_estimate=pl.CostEstimate(
            flops=2 * work * latent_width, bytes_accessed=3 * 10**7, transcendentals=work // 4
        ),
        name="finish",
    )(
        limits, last_limits, queries, marks, weight_sum, highest, *near_state, live, up_weight,
        weights, values, *sources,
    )


def local(
    queries,
    hidden,
    w_dkv,
    kv_gain,
    w_uk,
    value_up_weight,
    page_pool,
    page_owner,
    page_slot,
    prefix_len,
    suffix_len,
):
    n_head = lax.axis_size("head")
    n_req = lax.axis_size("req")
    n_seq = lax.axis_size("seq")
    head_idx = lax.axis_index("head")
    req_idx = lax.axis_index("req")
    seq_idx = lax.axis_index("seq")
    _, half_len, d_local = hidden.shape
    heads_dev, nope_width, latent_width = w_uk.shape
    lat_width = w_dkv.shape[1]
    rope_width = lat_width - latent_width
    query_width = queries.shape[2] // heads_dev
    page_width = page_pool.shape[1]
    page_len = page_width // lat_width
    pairs = page_len // 2
    pages_req = page_slot.shape[1]
    cap = max(2, 2 * pages_req // (n_head * n_req))
    chunk = n_req * cap // 4
    slots = 4 * chunk
    score_scale = float(query_width) ** (-0.5)

    owner_rows = page_owner[:, :, 0]
    counts, first, rest, foreign = pick_pages(
        owner_rows, page_slot, page_pool, cap, chunk, n_req, n_seq, pairs
    )
    swap_route = [(i, n_seq - 1 - i) for i in range(n_seq)]
    stream_route = []
    for i in range(n_head - 1):
        stream_route.append((i * n_seq, (i + 1) * n_seq))
        stream_route.append(((i + 1) * n_seq + 1, i * n_seq + 1))

    def swap(block):
        return lax.ppermute(block, "seq", swap_route)

    def stream(block):
        return lax.ppermute(block, ("head", "seq"), stream_route)

    def ring(block):
        steps = []
        for _ in range(n_head - 1):
            block = stream(block)
            steps.append([block, swap(block)])
        return steps

    my_prefix = lax.dynamic_index_in_dim(prefix_len, req_idx, 0, keepdims=False)
    my_suffix = lax.dynamic_index_in_dim(suffix_len, req_idx, 0, keepdims=False)
    own_owners = lax.dynamic_index_in_dim(owner_rows, req_idx, 0, keepdims=False)
    place_limits = token_limits(own_owners, my_prefix, req_idx, n_head, n_req, chunk, slots, page_len)
    upward = 2 * seq_idx - 1
    origins = [head_idx]
    for step in range(1, n_head):
        origins += [head_idx + upward * step, head_idx - upward * step]
    origins = jnp.stack(origins)
    heads = jnp.arange(n_head, dtype=jnp.int32)
    limits = jnp.sum(
        jnp.where((origins[:, None] == heads[None, :])[:, :, None], place_limits[None], 0), axis=1
    )

    positions = my_prefix + seq_idx * half_len + jnp.arange(half_len, dtype=jnp.int32)
    partial_value = jnp.dot(hidden[0], w_dkv, preferred_element_type=jnp.float32)
    rows = heads_dev * half_len
    query_rows = queries[0].reshape(half_len, heads_dev, query_width)
    q_latent = jnp.einsum(
        "thn,hnk->kht", query_rows[..., :nope_width], w_uk, preferred_element_type=jnp.float32
    ).astype(jnp.bfloat16)
    cosine_table, sine_table = angles(positions, rope_width)
    q_rotated = rotate(
        query_rows[..., nope_width:].astype(jnp.float32), cosine_table[:, None, :], sine_table[:, None, :]
    ).astype(jnp.bfloat16)
    q_rotated = jnp.transpose(q_rotated, (2, 1, 0))
    q_turned = jnp.concatenate(
        [
            q_latent.reshape(latent_width, rows),
            q_rotated.reshape(rope_width, rows),
            jnp.ones((1, rows), jnp.bfloat16),
            jnp.zeros((63, rows), jnp.bfloat16),
        ],
        axis=0,
    )

    early_steps = ring(first)
    arrived = [
        lax.ppermute(foreign[s - 1], "req", [(i, (i + s) % n_req) for i in range(n_req)])
        for s in range(1, n_req)
    ]
    mine = arrived[0][None] if n_req == 2 else jnp.stack(arrived)
    mine, q_turned = lax.optimization_barrier((mine, q_turned))
    other = swap(mine)
    middle, late = join_pages(counts, rest, mine, other, chunk, cap, (2 * chunk, chunk))
    owner_rows, counts = lax.optimization_barrier((owner_rows, counts))
    most = most_later(owner_rows, n_head, n_req, chunk)

    share = half_len // n_head
    partials = lax.all_to_all(partial_value, "head", split_axis=0, concat_axis=0, tiled=True)
    summed = jnp.sum(partials.reshape(n_head, share, lat_width), axis=0)
    share_t = seq_idx * half_len + head_idx * share + jnp.arange(share, dtype=jnp.int32)
    latent = finish_latent(summed, my_prefix + share_t, share_t < my_suffix, kv_gain, latent_width)

    tile = 256 if rows % 256 == 0 and 256 % half_len == 0 else half_len
    shape = (tile, score_scale * math.log2(math.e), chunk, lat_width)
    parts = {"early": (0, chunk), "middle": (chunk, 3 * chunk), "late": (3 * chunk, 4 * chunk)}

    def limits_of(pieces):
        return jnp.concatenate(
            [limits[origin, parts[name][0] : parts[name][1]] for name, origin in pieces]
        )

    def pieces_of(name, steps):
        return [(name, 2 * step + side + 1) for step in steps for side in range(2)]

    def arrays_of(arrived_steps, steps):
        return [arrived_steps[step][side] for step in steps for side in range(2)]

    last = n_head - 2
    live = my_suffix.reshape(1)
    near_state = ()
    extra = 4 + 1 + 2 * last
    total = 1 + 2 * (last + 1) + 2 + 4 * last + extra
    used_limits = []
    n_blocks = 0
    state = None

    def score(pieces, arrays, near=None):
        nonlocal n_blocks, state, near_state
        used_limits.append(limits_of(pieces))
        result = score_part(
            n_blocks, total, used_limits[-1], q_turned, arrays, state, shape, latent_width, near
        )
        state = result[:5]
        near_state = result[5:] or near_state
        n_blocks += sum(a.shape[0] for a in arrays) // chunk

    def tie(block):
        nonlocal state
        block, mark = lax.optimization_barrier((block, state[4]))
        state = (*state[:4], mark)
        return block

    middle, early_steps[last - 1][0] = lax.optimization_barrier((middle, early_steps[last - 1][0]))
    middle_steps = []
    block = stream(middle)
    for step in range(last + 1):
        received = block
        if step == 0:
            score(
                [("early", 0)] + pieces_of("early", range(last)),
                [first] + arrays_of(early_steps, range(last)),
            )
        elif step == 1:
            score(
                pieces_of("early", [last]) + [("middle", 0)] + pieces_of("middle", [0]),
                arrays_of(early_steps, [last]) + [middle] + arrays_of(middle_steps, [0]),
            )
        else:
            score(
                pieces_of("middle", [step - 1]),
                arrays_of(middle_steps, [step - 1]),
                (live, suffix_latent) if step == last else None,
            )
        received = tie(received)
        if step == 0:
            received, latent, most = lax.optimization_barrier((received, latent, most))
            copies = jnp.concatenate([latent] * n_head, axis=0)
            fresh = lax.all_to_all(copies, "head", split_axis=0, concat_axis=0, tiled=True)
            opposite = swap(fresh)
            suffix_latent = jnp.where(
                seq_idx == 0,
                jnp.concatenate([fresh, opposite], axis=0),
                jnp.concatenate([opposite, fresh], axis=0),
            )
        elif step == last - 1:
            received, suffix_latent = lax.optimization_barrier((received, suffix_latent))
        if step < last:
            block = stream(received)
        middle_steps.append([received, swap(received)])

    last_pieces = pieces_of("middle", [last])
    last_arrays = arrays_of(middle_steps, [last])

    def end(blocks, limit_list, final_pieces, final_arrays, current):
        return finish(
            blocks, jnp.concatenate(limit_list), limits_of(final_pieces), q_turned, current, near_state,
            final_arrays, live, value_up_weight, half_len, shape,
        )

    def with_late(_):
        block = stream(late)
        pieces = last_pieces + [("late", 0)]
        arrays = last_arrays + [late]
        current, blocks, limit_list = state, n_blocks, list(used_limits)
        for step in range(last + 1):
            received = block
            more = limits_of(pieces)
            limit_list.append(more)
            current = score_part(
                blocks, total, more, q_turned, arrays, current, shape, latent_width
            )[:5]
            blocks += sum(a.shape[0] for a in arrays) // chunk
            received, mark = lax.optimization_barrier((received, current[4]))
            current = (*current[:4], mark)
            if step < last:
                block = stream(received)
            arrays = [received, swap(received)]
            pieces = pieces_of("late", [step])
        return end(blocks, limit_list, pieces, arrays, current)

    def without_late(_):
        return end(n_blocks, used_limits, last_pieces, last_arrays, state)

    attn_out = lax.cond(most > 2 * chunk, with_late, without_late, 0)
    new_pages = fresh.reshape(1, half_len // page_len, page_len * lat_width)
    return (attn_out[None], new_pages)


def solution(mesh):
    placed = (
        P(("groups", "req"), "seq", "head"),
        P(("groups", "req"), "seq", "head"),
        P("head", None),
        P(),
        P("head", None, None),
        P("head", None, None),
        P(("groups", "head", "req"), None),
        P("groups", None, None),
        P("groups", None),
        P("groups"),
        P("groups"),
    )
    return jax.shard_map(
        local,
        mesh=mesh,
        in_specs=placed,
        out_specs=(P(("groups", "req"), "seq", "head"), P(("groups", "req"), "seq", None)),
        check_vma=False,
    )
```

```python
import functools
import math

import jax
import jax.numpy as jnp
from jax import lax
from jax.experimental import pallas as pl
from jax.experimental.pallas import tpu as pltpu
from jax.sharding import PartitionSpec as P

LOWEST = -1e30
MASKED = -1e38
MIB = 1024 * 1024


def rotate(vector, cosine_table, sine_table):
    half_width = vector.shape[-1] // 2
    first_half = vector[..., :half_width]
    second_half = vector[..., half_width:]
    return jnp.concatenate(
        [
            first_half * cosine_table - second_half * sine_table,
            first_half * sine_table + second_half * cosine_table,
        ],
        axis=-1,
    )


def angles(positions, rope_width):
    half_width = rope_width // 2
    frequency = 10000.0 ** (-2.0 * jnp.arange(half_width, dtype=jnp.float32) / rope_width)
    phases = positions.astype(jnp.float32)[:, None] * frequency[None, :]
    return (jnp.cos(phases), jnp.sin(phases))


def finish_latent(summed, positions, live_rows, kv_gain, latent_width):
    latent_part = summed[:, :latent_width]
    mean_square = jnp.mean(latent_part * latent_part, axis=-1, keepdims=True)
    normed = latent_part * lax.rsqrt(mean_square + 1e-06) * kv_gain
    cosine_table, sine_table = angles(positions, summed.shape[1] - latent_width)
    rotated = rotate(summed[:, latent_width:], cosine_table, sine_table)
    joined = jnp.concatenate([normed, rotated], axis=-1).astype(jnp.bfloat16)
    return jnp.where(live_rows[:, None], joined, jnp.zeros_like(joined))


def any_spec():
    return pl.BlockSpec(memory_space=pl.ANY)


def smem_spec():
    return pl.BlockSpec(memory_space=pltpu.SMEM)


def vmem_spec():
    return pl.BlockSpec(memory_space=pltpu.VMEM)


def hbm_spec():
    return pl.BlockSpec(memory_space=pltpu.HBM)


def pick_kernel(
    cap, owner_hbm, slot_hbm, pool_hbm, hidden_hbm, down_hbm, count_ref, first_ref, rest_ref,
    foreign_ref, partial_ref, owner_ref, slot_ref, pool_ref, hidden_ref, down_ref, pages, lists, sems,
):
    n_req = lax.axis_size("req")
    head_idx = lax.axis_index("head")
    req_idx = lax.axis_index("req")
    seq_idx = lax.axis_index("seq")
    n_pages = owner_ref.shape[1]
    pool_pages, pairs, pair_width = pages.shape
    chunk = first_ref.shape[0]
    loads = [
        pltpu.make_async_copy(owner_hbm, owner_ref, sems.at[0]),
        pltpu.make_async_copy(slot_hbm, slot_ref, sems.at[1]),
        pltpu.make_async_copy(pool_hbm, pool_ref, sems.at[2]),
        pltpu.make_async_copy(hidden_hbm, hidden_ref, sems.at[6]),
        pltpu.make_async_copy(down_hbm, down_ref, sems.at[7]),
    ]
    for load in loads:
        load.start()
    loads[0].wait()
    loads[1].wait()
    self_owner = head_idx * n_req + req_idx
    founds = []
    for shift in range(n_req):
        request = lax.rem(req_idx + shift, n_req)

        def note(page, found, shift=shift, request=request):
            lists[shift, found] = slot_ref[request, page]
            return found + (owner_ref[request, page] == self_owner).astype(jnp.int32)

        founds.append(lax.fori_loop(0, n_pages, note, jnp.int32(0), unroll=8))

    def tally(page, counts):
        owner = owner_ref[req_idx, page]
        return tuple(
            counts[shift]
            + (owner == head_idx * n_req + lax.rem(req_idx + n_req - shift, n_req)).astype(jnp.int32)
            for shift in range(n_req)
        )

    counts = lax.fori_loop(0, n_pages, tally, (jnp.int32(0),) * n_req, unroll=8)
    for shift in range(n_req):
        count_ref[shift] = counts[shift]
    loads[2].wait()
    step = 16
    row = lax.broadcasted_iota(jnp.int32, (step * step, step * step), 0)
    column = lax.broadcasted_iota(jnp.int32, (step * step, step * step), 1)
    swap = ((row // step == column % step) & (row % step == column // step)).astype(jnp.bfloat16)
    for page in range(0, pool_pages, step):
        for pair in range(0, pairs, step):
            rows = jnp.concatenate(
                [
                    pool_ref[page : page + step, (pair + i) * pair_width : (pair + i + 1) * pair_width]
                    for i in range(step)
                ],
                axis=0,
            )
            turned = jnp.dot(swap, rows, preferred_element_type=jnp.float32).astype(jnp.bfloat16)
            pages[page : page + step, pair : pair + step, :] = turned.reshape(step, step, pair_width)

    def send(shift, rank, target, sem):
        slot = jnp.where(rank < founds[shift], lists[shift, rank], 0)
        pltpu.make_async_copy(pages.at[slot], target, sem).start()

    for rank in range(cap):
        if rank < chunk:
            send(0, rank, first_ref.at[rank], sems.at[3])
        else:
            send(0, rank, rest_ref.at[rank - chunk], sems.at[4])
    half_cap = foreign_ref.shape[1]
    for shift in range(1, n_req):
        for j in range(half_cap):
            send(shift, seq_idx * half_cap + j, foreign_ref.at[shift - 1, j], sems.at[5])
    loads[3].wait()
    loads[4].wait()
    partial_ref[...] = lax.dot_general(
        down_ref[...], hidden_ref[...], (((1,), (1,)), ((), ())), preferred_element_type=jnp.float32
    )
    pltpu.make_async_copy(first_ref, first_ref, sems.at[3]).wait()
    if cap > chunk:
        pltpu.make_async_copy(rest_ref, rest_ref, sems.at[4]).wait()
    pltpu.make_async_copy(foreign_ref, foreign_ref, sems.at[5]).wait()


def pick_pages(page_owner, page_slot, page_pool, hidden, down, cap, chunk, n_req, n_seq, pairs):
    pool_pages, page_width = page_pool.shape
    page = (pairs, page_width // pairs)
    return pl.pallas_call(
        functools.partial(pick_kernel, cap),
        out_shape=(
            jax.ShapeDtypeStruct((n_req,), jnp.int32),
            jax.ShapeDtypeStruct((chunk, *page), jnp.bfloat16),
            jax.ShapeDtypeStruct((max(1, cap - chunk), *page), jnp.bfloat16),
            jax.ShapeDtypeStruct((n_req - 1, cap // n_seq, *page), jnp.bfloat16),
            jax.ShapeDtypeStruct((down.shape[0], hidden.shape[0]), jnp.float32),
        ),
        in_specs=[any_spec(), any_spec(), hbm_spec(), hbm_spec(), hbm_spec()],
        out_specs=(smem_spec(), hbm_spec(), hbm_spec(), hbm_spec(), vmem_spec()),
        scratch_shapes=[
            pltpu.SMEM(page_owner.shape, jnp.int32),
            pltpu.SMEM(page_slot.shape, jnp.int32),
            pltpu.VMEM((pool_pages, page_width), jnp.bfloat16),
            pltpu.VMEM(hidden.shape, jnp.bfloat16),
            pltpu.VMEM(down.shape, jnp.bfloat16),
            pltpu.VMEM((pool_pages, *page), jnp.bfloat16),
            pltpu.SMEM((n_req, cap + 1), jnp.int32),
            pltpu.SemaphoreType.DMA((8,)),
        ],
        compiler_params=pltpu.CompilerParams(vmem_limit_bytes=60 * MIB),
        cost_estimate=pl.CostEstimate(flops=10**9, bytes_accessed=6 * 10**6, transcendentals=0),
        name="pick_pages",
    )(page_owner, page_slot, page_pool, hidden, down)


def join_kernel(chunk, cap, count_ref, rest_ref, mine_ref, other_ref, *refs):
    n_req = count_ref.shape[0]
    targets, sems = refs[:-1], refs[-1]
    seq_idx = lax.axis_index("seq")
    half_cap = mine_ref.shape[1]
    excess = jnp.maximum(count_ref[0] - chunk, 0)
    j = 0
    for part, target in enumerate(targets):
        for place in range(target.shape[0]):

            def fetch(condition, source, target=target, place=place, part=part):
                @pl.when(condition)
                def _():
                    pltpu.make_async_copy(source, target.at[place], sems.at[part]).start()

            rank = jnp.int32(j)
            taken = rank < excess
            if cap > chunk:
                fetch(taken, rest_ref.at[jnp.minimum(rank, cap - chunk - 1)])
            rank = rank - excess
            for shift in range(1, n_req):
                here = jnp.logical_not(taken) & (rank < count_ref[shift])
                half = rank // half_cap
                slot = jnp.clip(rank - half * half_cap, 0, half_cap - 1)
                fetch(here & (half == seq_idx), mine_ref.at[shift - 1, slot])
                fetch(here & (half != seq_idx), other_ref.at[shift - 1, slot])
                taken = taken | here
                rank = rank - count_ref[shift]
            fetch(jnp.logical_not(taken), mine_ref.at[0, 0])
            j += 1
    for part, target in enumerate(targets):
        pltpu.make_async_copy(target, target, sems.at[part]).wait()


def join_pages(counts, rest, mine, other, chunk, cap, sizes):
    return pl.pallas_call(
        functools.partial(join_kernel, chunk, cap),
        out_shape=tuple(jax.ShapeDtypeStruct((size, *rest.shape[1:]), jnp.bfloat16) for size in sizes),
        in_specs=[smem_spec()] + [hbm_spec()] * 3,
        out_specs=(vmem_spec(),) * len(sizes),
        scratch_shapes=[pltpu.SemaphoreType.DMA((len(sizes),))],
        compiler_params=pltpu.CompilerParams(vmem_limit_bytes=10 * MIB),
        cost_estimate=pl.CostEstimate(flops=0, bytes_accessed=3 * 10**6, transcendentals=0),
        name="join_pages",
    )(counts, rest, mine, other)


def token_limits(owners, prefix, req_idx, n_head, n_req, chunk, slots, page_len):
    pages = owners.shape[0]
    order = jnp.arange(pages, dtype=jnp.int32)
    place = owners // n_req
    shift = lax.rem(req_idx + n_req - lax.rem(owners, n_req), n_req)
    key = shift * pages + order
    together = place[None, :] == place[:, None]
    rank = jnp.sum((together & (key[None, :] < key[:, None])).astype(jnp.int32), axis=1)
    held = jnp.sum((together & (shift[None, :] == 0)).astype(jnp.int32), axis=1)
    early = (shift == 0) & (rank < chunk)
    within = jnp.where(early, rank, chunk + rank - jnp.minimum(held, chunk))
    slot = place * slots + within
    tokens = jnp.clip(prefix - order * page_len, 0, page_len)
    all_slots = jnp.arange(n_head * slots, dtype=jnp.int32)
    limits = jnp.sum(jnp.where(slot[None, :] == all_slots[:, None], tokens[None, :], 0), axis=1)
    return limits.reshape(n_head, slots)


def most_later(owner_rows, n_head, n_req, chunk):
    owners = jnp.arange(n_head * n_req, dtype=jnp.int32)
    held = jnp.sum((owner_rows[:, None, :] == owners[None, :, None]).astype(jnp.int32), axis=2)
    held = held.reshape(-1, n_head, n_req)
    own = jnp.arange(n_req)[None, None, :] == jnp.arange(held.shape[0])[:, None, None]
    early = jnp.minimum(jnp.sum(jnp.where(own, held, 0), axis=2), chunk)
    most = jnp.max(jnp.sum(held, axis=2) - early).reshape(1)
    n_groups = lax.axis_size("groups")
    passed = most
    for _ in range(n_groups - 1):
        passed = lax.ppermute(passed, "groups", [(i, (i + 1) % n_groups) for i in range(n_groups)])
        most = jnp.maximum(most, passed)
    return most[0]


def score_block(keys, queries_ref, target, note, highest, weight_sum, tile, scale, bias=None):
    rows = queries_ref.shape[1]
    for start in range(0, rows, tile):
        part = slice(start, start + tile)
        scores = jnp.dot(keys[...], queries_ref[:, part], preferred_element_type=jnp.float32) * scale
        if bias is not None:
            scores = scores + bias
        old = highest[:, part]
        new = jnp.maximum(old, jnp.max(scores, axis=0, keepdims=True))
        weights = jnp.exp2(scores - new)
        highest[:, part] = new
        weight_sum[:, part] = weight_sum[:, part] * jnp.exp2(old - new) + jnp.sum(
            weights, axis=0, keepdims=True
        )
        target[:, part] = weights
        note(part, new)


def block_limits(limit_ref, block, chunk):
    return [limit_ref[block * chunk + j] for j in range(chunk)]


def any_token(limit_ref, block, chunk):
    return functools.reduce(jnp.maximum, block_limits(limit_ref, block, chunk)) > 0


def load_block(block_ref, keys, limits, key_width):
    chunk, pairs, pair_width = block_ref.shape
    pair_rows = chunk * pairs
    page_rows = block_ref[...].reshape(pair_rows, pair_width)
    keys[:pair_rows, :key_width] = page_rows[:, :key_width]
    keys[pair_rows:, :key_width] = page_rows[:, key_width:]
    shape = (2 * pair_rows, keys.shape[1] - key_width)
    row = lax.broadcasted_iota(jnp.int32, shape, 0)
    pair_row = lax.rem(row, pair_rows)
    token = 2 * lax.rem(pair_row, pairs) + row // pair_rows
    limit = jnp.zeros_like(row)
    for j, value in enumerate(limits):
        limit = jnp.where(pair_row // pairs == j, value, limit)
    masked = (lax.broadcasted_iota(jnp.int32, shape, 1) == 0) & (token >= limit)
    keys[:, key_width:] = jnp.where(masked, MASKED, 0.0).astype(jnp.bfloat16)


def turn_values(keys, latent_width):
    return keys[:, :latent_width].T


def near_bias(n_keys, half_len, tile, live):
    seq_idx = lax.axis_index("seq")
    place = lax.broadcasted_iota(jnp.int32, (n_keys, tile), 0)
    query = lax.rem(lax.broadcasted_iota(jnp.int32, (n_keys, tile), 1), half_len) + seq_idx * half_len
    allowed = (place <= query) & (place < live)
    return jnp.where(allowed, 0.0, -jnp.inf)


def score_kernel(shape, base, n_sources, first, near, limit_ref, queries_ref, *refs):
    tile, scale, chunk, key_width = shape
    refs = list(refs)
    if not first:
        marks_in, sum_in, high_in = [refs.pop(0) for _ in range(3)]
        refs.pop(0), refs.pop(0)
    if near:
        live_ref, suffix_ref = refs.pop(0), refs.pop(0)
    sources = [refs.pop(0) for _ in range(n_sources)]
    weights_hbm, values_hbm, marks, weight_sum, highest = [refs.pop(0) for _ in range(5)]
    if near:
        near_weights, near_values, near_mark = [refs.pop(0) for _ in range(3)]
    blocks, keys, weights, values, load_sems, weight_sems, value_sems = [refs.pop(0) for _ in range(7)]
    n_blocks = blocks.shape[0]
    latent_width = values.shape[1]
    index = 0
    for source in sources:
        for i in range(source.shape[0] // chunk):
            pltpu.make_async_copy(
                source.at[i * chunk : (i + 1) * chunk], blocks.at[index], load_sems.at[index]
            ).start()
            index += 1
    if first:
        marks[...] = jnp.zeros_like(marks)
        weight_sum[...] = jnp.zeros_like(weight_sum)
        highest[...] = jnp.full_like(highest, LOWEST)
    else:
        marks[...] = marks_in[...]
        weight_sum[...] = sum_in[...]
        highest[...] = high_in[...]

    def stores(block):
        return (
            pltpu.make_async_copy(weights.at[block], weights_hbm.at[base + block], weight_sems.at[block]),
            pltpu.make_async_copy(values.at[block], values_hbm.at[base + block], value_sems.at[block]),
        )

    def one_block(block, carry):
        pltpu.make_async_copy(blocks.at[block], blocks.at[block], load_sems.at[block]).wait()

        @pl.when(any_token(limit_ref, block, chunk))
        def _():
            load_block(blocks.at[block], keys, block_limits(limit_ref, block, chunk), key_width)

            def note(part, new):
                marks[pl.ds(base + block, 1), part] = new

            score_block(
                keys, queries_ref, weights.at[block], note, highest, weight_sum, tile, scale
            )
            values[block] = turn_values(keys, latent_width)
            for copy in stores(block):
                copy.start()

        return carry

    lax.fori_loop(0, n_blocks, one_block, 0)
    if near:
        near_keys = refs.pop(0)
        n_near = suffix_ref.shape[0]
        near_keys[:, key_width:] = jnp.zeros_like(near_keys[:, key_width:])
        near_keys[:, :key_width] = suffix_ref[...]

        def note_near(part, new):
            near_mark[:, part] = new

        score_block(
            near_keys, queries_ref, near_weights, note_near, highest, weight_sum, tile, scale,
            near_bias(n_near, n_near // lax.axis_size("seq"), tile, live_ref[0]),
        )
        near_values[...] = turn_values(near_keys, latent_width)

    def one_wait(block, carry):
        @pl.when(any_token(limit_ref, block, chunk))
        def _():
            for copy in stores(block):
                copy.wait()

        return carry

    lax.fori_loop(0, n_blocks, one_wait, 0)


def score_part(base, total, limits, queries, sources, state, shape, latent_width, near=None):
    tile, scale, chunk, key_width = shape
    width, rows = queries.shape
    _, pairs, pair_width = sources[0].shape
    block_keys = 2 * chunk * pairs
    n_blocks = sum(s.shape[0] for s in sources) // chunk
    row = jax.ShapeDtypeStruct((1, rows), jnp.float32)
    out_shape = [
        jax.ShapeDtypeStruct((total, block_keys, rows), jnp.float32),
        jax.ShapeDtypeStruct((total, latent_width, block_keys), jnp.bfloat16),
        jax.ShapeDtypeStruct((total, rows), jnp.float32),
        row,
        row,
    ]
    out_specs = [hbm_spec(), hbm_spec(), vmem_spec(), vmem_spec(), vmem_spec()]
    operands = [limits, queries]
    specs = [smem_spec(), vmem_spec()]
    aliases = {}
    if state is not None:
        operands += [state[2], state[3], state[4], state[0], state[1]]
        specs += [vmem_spec()] * 3 + [hbm_spec()] * 2
        aliases = {5: 0, 6: 1}
    scratch = [
        pltpu.VMEM((n_blocks, chunk, pairs, pair_width), jnp.bfloat16),
        pltpu.VMEM((block_keys, width), jnp.bfloat16),
        pltpu.VMEM((n_blocks, block_keys, rows), jnp.float32),
        pltpu.VMEM((n_blocks, latent_width, block_keys), jnp.bfloat16),
        pltpu.SemaphoreType.DMA((n_blocks,)),
        pltpu.SemaphoreType.DMA((n_blocks,)),
        pltpu.SemaphoreType.DMA((n_blocks,)),
    ]
    if near is not None:
        near_keys = near[-1].shape[0]
        operands += list(near)
        specs += [smem_spec(), vmem_spec()]
        out_shape += [
            jax.ShapeDtypeStruct((near_keys, rows), jnp.float32),
            jax.ShapeDtypeStruct((latent_width, near_keys), jnp.bfloat16),
            row,
        ]
        out_specs += [vmem_spec()] * 3
        scratch.append(pltpu.VMEM((near_keys, width), jnp.bfloat16))
    operands += list(sources)
    specs += [hbm_spec()] * len(sources)
    work = n_blocks * block_keys * rows // 2
    return pl.pallas_call(
        functools.partial(score_kernel, shape, base, len(sources), state is None, near is not None),
        out_shape=tuple(out_shape),
        in_specs=specs,
        out_specs=tuple(out_specs),
        scratch_shapes=scratch,
        input_output_aliases=aliases,
        compiler_params=pltpu.CompilerParams(vmem_limit_bytes=40 * MIB),
        cost_estimate=pl.CostEstimate(
            flops=work, bytes_accessed=10**5, transcendentals=0
        ),
        name="score_part",
    )(*operands)


def finish_kernel(
    shape, depth, n_blocks, n_sources, limit_ref, last_limit_ref, queries_ref, marks, sum_in, high_in,
    near_weights, near_values, near_mark, live_ref, up_ref, weights_hbm, values_hbm, *refs,
):
    tile, scale, chunk, key_width = shape
    sources, refs = refs[:n_sources], refs[n_sources:]
    (
        out_ref, weight_sum, highest, total, blocks, keys, last_weights, last_values, last_marks,
        weights, values, used, load_sems, weight_sems, value_sems,
    ) = refs
    rows = queries_ref.shape[1]
    latent_width = total.shape[0]
    n_last = blocks.shape[0]
    index = 0
    for source in sources:
        for i in range(source.shape[0] // chunk):
            pltpu.make_async_copy(
                source.at[i * chunk : (i + 1) * chunk], blocks.at[index], load_sems.at[index]
            ).start()
            index += 1

    def list_block(block, count):
        used[count] = block
        return count + any_token(limit_ref, block, chunk).astype(jnp.int32)

    n_used = lax.fori_loop(0, n_blocks, list_block, jnp.int32(0))

    def fetches(number):
        place = lax.rem(number, depth)
        return (
            pltpu.make_async_copy(weights_hbm.at[used[number]], weights.at[place], weight_sems.at[place]),
            pltpu.make_async_copy(values_hbm.at[used[number]], values.at[place], value_sems.at[place]),
        )

    def fetch(number):
        @pl.when(number < n_used)
        def _():
            for copy in fetches(number):
                copy.start()

    for number in range(depth):
        fetch(jnp.int32(number))
    weight_sum[...] = sum_in[...]
    highest[...] = high_in[...]
    last_marks[...] = jnp.zeros_like(last_marks)

    def one_score(block, carry):
        pltpu.make_async_copy(blocks.at[block], blocks.at[block], load_sems.at[block]).wait()

        @pl.when(any_token(last_limit_ref, block, chunk))
        def _():
            load_block(blocks.at[block], keys, block_limits(last_limit_ref, block, chunk), key_width)

            def note(part, new):
                last_marks[pl.ds(block, 1), part] = new

            score_block(
                keys, queries_ref, last_weights.at[block], note, highest, weight_sum, tile, scale
            )
            last_values[block] = turn_values(keys, latent_width)

        return carry

    lax.fori_loop(0, n_last, one_score, 0)

    def add_block(weight_block, value_block, mark, begin=False):
        for start in range(0, rows, tile):
            part = slice(start, start + tile)
            factor = jnp.exp2(mark[:, part] - highest[:, part]) / weight_sum[:, part]
            added = jnp.dot(
                value_block[...],
                (weight_block[:, part] * factor).astype(jnp.bfloat16),
                preferred_element_type=jnp.float32,
            )
            total[:, part] = added if begin else total[:, part] + added

    add_block(near_weights, near_values, near_mark, begin=True)

    def one_add(number, carry):
        for copy in fetches(number):
            copy.wait()
        place = lax.rem(number, depth)
        add_block(weights.at[place], values.at[place], marks.at[pl.ds(used[number], 1)])
        fetch(number + depth)
        return carry

    lax.fori_loop(0, n_used, one_add, 0)

    def one_last(block, carry):
        @pl.when(any_token(last_limit_ref, block, chunk))
        def _():
            add_block(last_weights.at[block], last_values.at[block], last_marks.at[pl.ds(block, 1)])

        return carry

    lax.fori_loop(0, n_last, one_last, 0)
    heads, _, value_width = up_ref.shape
    half_len = out_ref.shape[0]
    steps = lax.broadcasted_iota(jnp.int32, (half_len, value_width), 0)
    steps = steps + lax.axis_index("seq") * half_len
    for head in range(heads):
        latent = total[:, head * half_len : (head + 1) * half_len].astype(jnp.bfloat16)
        raised = lax.dot_general(
            latent, up_ref[head], (((0,), (0,)), ((), ())), preferred_element_type=jnp.float32
        )
        out_ref[:, head * value_width : (head + 1) * value_width] = jnp.where(
            steps < live_ref[0], raised, 0.0
        ).astype(jnp.bfloat16)


def finish(n_blocks, limits, last_limits, queries, state, near_state, sources, live, up_weight, half_len, shape):
    tile, scale, chunk, key_width = shape
    weights, values, marks, weight_sum, highest = state
    width, rows = queries.shape
    _, latent_width, block_keys = values.shape
    _, pairs, pair_width = sources[0].shape
    heads, _, value_width = up_weight.shape
    depth = 4
    n_last = sum(s.shape[0] for s in sources) // chunk
    row = pltpu.VMEM((1, rows), jnp.float32)
    work = (n_blocks // 2 + n_last) * block_keys * rows
    return pl.pallas_call(
        functools.partial(finish_kernel, shape, depth, n_blocks, len(sources)),
        out_shape=jax.ShapeDtypeStruct((half_len, heads * value_width), jnp.bfloat16),
        in_specs=[smem_spec()] * 2
        + [vmem_spec()] * 7
        + [smem_spec(), vmem_spec()]
        + [hbm_spec()] * (2 + len(sources)),
        out_specs=vmem_spec(),
        scratch_shapes=[
            row,
            row,
            pltpu.VMEM((latent_width, rows), jnp.float32),
            pltpu.VMEM((n_last, chunk, pairs, pair_width), jnp.bfloat16),
            pltpu.VMEM((block_keys, width), jnp.bfloat16),
            pltpu.VMEM((n_last, block_keys, rows), jnp.float32),
            pltpu.VMEM((n_last, latent_width, block_keys), jnp.bfloat16),
            pltpu.VMEM((n_last, rows), jnp.float32),
            pltpu.VMEM((depth, block_keys, rows), jnp.float32),
            pltpu.VMEM((depth, latent_width, block_keys), jnp.bfloat16),
            pltpu.SMEM((n_blocks + depth + 1,), jnp.int32),
            pltpu.SemaphoreType.DMA((n_last,)),
            pltpu.SemaphoreType.DMA((depth,)),
            pltpu.SemaphoreType.DMA((depth,)),
        ],
        compiler_params=pltpu.CompilerParams(vmem_limit_bytes=40 * MIB),
        cost_estimate=pl.CostEstimate(
            flops=2 * work * latent_width, bytes_accessed=3 * 10**7, transcendentals=work // 4
        ),
        name="finish",
    )(
        limits, last_limits, queries, marks, weight_sum, highest, *near_state, live, up_weight,
        weights, values, *sources,
    )


def local(
    queries,
    hidden,
    w_dkv,
    kv_gain,
    w_uk,
    value_up_weight,
    page_pool,
    page_owner,
    page_slot,
    prefix_len,
    suffix_len,
):
    n_head = lax.axis_size("head")
    n_req = lax.axis_size("req")
    n_seq = lax.axis_size("seq")
    head_idx = lax.axis_index("head")
    req_idx = lax.axis_index("req")
    seq_idx = lax.axis_index("seq")
    _, half_len, d_local = hidden.shape
    heads_dev, nope_width, latent_width = w_uk.shape
    lat_width = w_dkv.shape[1]
    rope_width = lat_width - latent_width
    query_width = queries.shape[2] // heads_dev
    page_width = page_pool.shape[1]
    page_len = page_width // lat_width
    pairs = page_len // 2
    pages_req = page_slot.shape[1]
    cap = max(2, 2 * pages_req // (n_head * n_req))
    chunk = n_req * cap // 4
    slots = 4 * chunk
    score_scale = float(query_width) ** (-0.5)

    owner_rows = page_owner[:, :, 0]
    counts, first, rest, foreign, partial_turned = pick_pages(
        owner_rows, page_slot, page_pool, hidden[0], w_dkv.T, cap, chunk, n_req, n_seq, pairs
    )
    swap_route = [(i, n_seq - 1 - i) for i in range(n_seq)]
    stream_route = []
    for i in range(n_head - 1):
        stream_route.append((i * n_seq, (i + 1) * n_seq))
        stream_route.append(((i + 1) * n_seq + 1, i * n_seq + 1))

    def swap(block):
        return lax.ppermute(block, "seq", swap_route)

    def stream(block):
        return lax.ppermute(block, ("head", "seq"), stream_route)

    def ring(block):
        steps = []
        for _ in range(n_head - 1):
            block = stream(block)
            steps.append([block, swap(block)])
        return steps

    my_prefix = lax.dynamic_index_in_dim(prefix_len, req_idx, 0, keepdims=False)
    my_suffix = lax.dynamic_index_in_dim(suffix_len, req_idx, 0, keepdims=False)
    own_owners = lax.dynamic_index_in_dim(owner_rows, req_idx, 0, keepdims=False)
    place_limits = token_limits(own_owners, my_prefix, req_idx, n_head, n_req, chunk, slots, page_len)
    upward = 2 * seq_idx - 1
    origins = [head_idx]
    for step in range(1, n_head):
        origins += [head_idx + upward * step, head_idx - upward * step]
    origins = jnp.stack(origins)
    heads = jnp.arange(n_head, dtype=jnp.int32)
    limits = jnp.sum(
        jnp.where((origins[:, None] == heads[None, :])[:, :, None], place_limits[None], 0), axis=1
    )

    positions = my_prefix + seq_idx * half_len + jnp.arange(half_len, dtype=jnp.int32)
    rows = heads_dev * half_len
    query_rows = queries[0].reshape(half_len, heads_dev, query_width)
    q_latent = jnp.einsum(
        "thn,hnk->kht", query_rows[..., :nope_width], w_uk, preferred_element_type=jnp.float32
    ).astype(jnp.bfloat16)
    cosine_table, sine_table = angles(positions, rope_width)
    q_rotated = rotate(
        query_rows[..., nope_width:].astype(jnp.float32), cosine_table[:, None, :], sine_table[:, None, :]
    ).astype(jnp.bfloat16)
    q_rotated = jnp.transpose(q_rotated, (2, 1, 0))
    q_turned = jnp.concatenate(
        [
            q_latent.reshape(latent_width, rows),
            q_rotated.reshape(rope_width, rows),
            jnp.ones((1, rows), jnp.bfloat16),
            jnp.zeros((63, rows), jnp.bfloat16),
        ],
        axis=0,
    )

    early_steps = ring(first)
    arrived = [
        lax.ppermute(foreign[s - 1], "req", [(i, (i + s) % n_req) for i in range(n_req)])
        for s in range(1, n_req)
    ]
    mine = arrived[0][None] if n_req == 2 else jnp.stack(arrived)
    mine, q_turned = lax.optimization_barrier((mine, q_turned))
    other = swap(mine)
    middle, late = join_pages(counts, rest, mine, other, chunk, cap, (2 * chunk, chunk))
    owner_rows, middle = lax.optimization_barrier((owner_rows, middle))
    most = most_later(owner_rows, n_head, n_req, chunk)

    summed = lax.psum(partial_turned, "head").T
    live_rows = seq_idx * half_len + jnp.arange(half_len, dtype=jnp.int32) < my_suffix
    tile = 256 if rows % 256 == 0 and 256 % half_len == 0 else half_len
    shape = (tile, score_scale * math.log2(math.e), chunk, lat_width)
    parts = {"early": (0, chunk), "middle": (chunk, 3 * chunk), "late": (3 * chunk, 4 * chunk)}

    def limits_of(pieces):
        return jnp.concatenate(
            [limits[origin, parts[name][0] : parts[name][1]] for name, origin in pieces]
        )

    def pieces_of(name, steps):
        return [(name, 2 * step + side + 1) for step in steps for side in range(2)]

    def arrays_of(arrived_steps, steps):
        return [arrived_steps[step][side] for step in steps for side in range(2)]

    last = n_head - 2
    live = my_suffix.reshape(1)
    near_state = ()
    extra = 4 + 1 + 2 * last
    total = 1 + 2 * (last + 1) + 2 + 4 * last + extra
    used_limits = []
    n_blocks = 0
    state = None

    def score(pieces, arrays, near=None):
        nonlocal n_blocks, state, near_state
        used_limits.append(limits_of(pieces))
        result = score_part(
            n_blocks, total, used_limits[-1], q_turned, arrays, state, shape, latent_width, near
        )
        state = result[:5]
        near_state = result[5:] or near_state
        n_blocks += sum(a.shape[0] for a in arrays) // chunk

    def tie(block):
        nonlocal state
        block, mark = lax.optimization_barrier((block, state[4]))
        state = (*state[:4], mark)
        return block

    middle, early_steps[last - 1][0] = lax.optimization_barrier((middle, early_steps[last - 1][0]))
    middle_steps = []
    block = stream(middle)
    for step in range(last + 1):
        received = block
        if step == 0:
            score(
                [("early", 0)] + pieces_of("early", range(last)),
                [first] + arrays_of(early_steps, range(last)),
            )
        elif step == 1:
            score(
                pieces_of("early", [last]) + [("middle", 0)] + pieces_of("middle", [0]),
                arrays_of(early_steps, [last]) + [middle] + arrays_of(middle_steps, [0]),
            )
        else:
            score(
                pieces_of("middle", [step - 1]),
                arrays_of(middle_steps, [step - 1]),
                (live, suffix_latent) if step == last else None,
            )
        received = tie(received)
        if step == 0:
            received, summed, most = lax.optimization_barrier((received, summed, most))
            fresh = finish_latent(summed, positions, live_rows, kv_gain, latent_width)
            opposite = swap(fresh)
            suffix_latent = jnp.where(
                seq_idx == 0,
                jnp.concatenate([fresh, opposite], axis=0),
                jnp.concatenate([opposite, fresh], axis=0),
            )
        elif step == last - 1:
            received, suffix_latent = lax.optimization_barrier((received, suffix_latent))
        if step < last:
            block = stream(received)
        middle_steps.append([received, swap(received)])

    last_pieces = pieces_of("middle", [last])
    last_arrays = arrays_of(middle_steps, [last])

    known = jnp.concatenate(used_limits)
    final = limits_of(last_pieces)

    def end(blocks, blocks_limits, final_limits, final_arrays, current):
        return finish(
            blocks, blocks_limits, final_limits, q_turned, current, near_state,
            final_arrays, live, value_up_weight, half_len, shape,
        )

    def with_late(_):
        block = stream(late)
        pieces = last_pieces + [("late", 0)]
        arrays = last_arrays + [late]
        current, blocks, limit_list = state, n_blocks, list(used_limits)
        for step in range(last + 1):
            received = block
            more = limits_of(pieces)
            limit_list.append(more)
            current = score_part(
                blocks, total, more, q_turned, arrays, current, shape, latent_width
            )[:5]
            blocks += sum(a.shape[0] for a in arrays) // chunk
            received, mark = lax.optimization_barrier((received, current[4]))
            current = (*current[:4], mark)
            if step < last:
                block = stream(received)
            arrays = [received, swap(received)]
            pieces = pieces_of("late", [step])
        return end(blocks, jnp.concatenate(limit_list), limits_of(pieces), arrays, current)

    def without_late(_):
        return end(n_blocks, known, final, last_arrays, state)

    attn_out = lax.cond(most > 2 * chunk, with_late, without_late, 0)
    new_pages = fresh.reshape(1, half_len // page_len, page_len * lat_width)
    return (attn_out[None], new_pages)


def solution(mesh):
    placed = (
        P(("groups", "req"), "seq", "head"),
        P(("groups", "req"), "seq", "head"),
        P("head", None),
        P(),
        P("head", None, None),
        P("head", None, None),
        P(("groups", "head", "req"), None),
        P("groups", None, None),
        P("groups", None),
        P("groups"),
        P("groups"),
    )
    return jax.shard_map(
        local,
        mesh=mesh,
        in_specs=placed,
        out_specs=(P(("groups", "req"), "seq", "head"), P(("groups", "req"), "seq", None)),
        check_vma=False,
    )
```

```python
import functools
import math

import jax
import jax.numpy as jnp
from jax import lax
from jax.experimental import pallas as pl
from jax.experimental.pallas import tpu as pltpu
from jax.sharding import PartitionSpec as P

LOWEST = -1e30
MASKED = -1e38
MIB = 1024 * 1024


def rotate(vector, cosine_table, sine_table):
    half_width = vector.shape[-1] // 2
    first_half = vector[..., :half_width]
    second_half = vector[..., half_width:]
    return jnp.concatenate(
        [
            first_half * cosine_table - second_half * sine_table,
            first_half * sine_table + second_half * cosine_table,
        ],
        axis=-1,
    )


def angles(positions, rope_width):
    half_width = rope_width // 2
    frequency = 10000.0 ** (-2.0 * jnp.arange(half_width, dtype=jnp.float32) / rope_width)
    phases = positions.astype(jnp.float32)[:, None] * frequency[None, :]
    return (jnp.cos(phases), jnp.sin(phases))


def finish_latent(summed, positions, live_rows, kv_gain, latent_width):
    latent_part = summed[:, :latent_width]
    mean_square = jnp.mean(latent_part * latent_part, axis=-1, keepdims=True)
    normed = latent_part * lax.rsqrt(mean_square + 1e-06) * kv_gain
    cosine_table, sine_table = angles(positions, summed.shape[1] - latent_width)
    rotated = rotate(summed[:, latent_width:], cosine_table, sine_table)
    joined = jnp.concatenate([normed, rotated], axis=-1).astype(jnp.bfloat16)
    return jnp.where(live_rows[:, None], joined, jnp.zeros_like(joined))


def any_spec():
    return pl.BlockSpec(memory_space=pl.ANY)


def smem_spec():
    return pl.BlockSpec(memory_space=pltpu.SMEM)


def vmem_spec():
    return pl.BlockSpec(memory_space=pltpu.VMEM)


def hbm_spec():
    return pl.BlockSpec(memory_space=pltpu.HBM)


def pick_kernel(
    cap, page_len, owner_hbm, slot_hbm, prefix_hbm, pool_hbm, hidden_hbm, down_hbm, count_ref, most_ref,
    first_ref, rest_ref, foreign_ref, partial_ref, owner_ref, slot_ref, prefix_ref, pool_ref, hidden_ref,
    down_ref, pages, lists, table, sems,
):
    n_req = lax.axis_size("req")
    head_idx = lax.axis_index("head")
    req_idx = lax.axis_index("req")
    seq_idx = lax.axis_index("seq")
    n_pages = owner_ref.shape[1]
    pool_pages, pairs, pair_width = pages.shape
    chunk = first_ref.shape[0]
    loads = [
        pltpu.make_async_copy(owner_hbm, owner_ref, sems.at[0]),
        pltpu.make_async_copy(slot_hbm, slot_ref, sems.at[1]),
        pltpu.make_async_copy(pool_hbm, pool_ref, sems.at[2]),
        pltpu.make_async_copy(hidden_hbm, hidden_ref, sems.at[6]),
        pltpu.make_async_copy(down_hbm, down_ref, sems.at[7]),
        pltpu.make_async_copy(prefix_hbm, prefix_ref, sems.at[8]),
    ]
    for load in loads:
        load.start()
    loads[0].wait()
    loads[1].wait()
    loads[5].wait()
    self_owner = head_idx * n_req + req_idx
    n_owners = table.shape[1]
    for shift in range(n_req):
        for owner in range(n_owners):
            table[shift, owner] = 0
    founds = []
    most = jnp.int32(0)
    for shift in range(n_req):
        request = lax.rem(req_idx + shift, n_req)

        def note(page, found, shift=shift, request=request):
            owner = owner_ref[request, page]
            needed = page * page_len < prefix_ref[request]
            table[shift, owner] += needed.astype(jnp.int32)
            lists[shift, found] = slot_ref[request, page]
            return found + (needed & (owner == self_owner)).astype(jnp.int32)

        founds.append(lax.fori_loop(0, n_pages, note, jnp.int32(0), unroll=8))
        for place in range(n_owners // n_req):
            held = functools.reduce(jnp.add, [table[shift, place * n_req + i] for i in range(n_req)])
            early = jnp.minimum(table[shift, place * n_req + request], chunk)
            most = jnp.maximum(most, held - early)
    for shift in range(n_req):
        count_ref[shift] = table[0, head_idx * n_req + lax.rem(req_idx + n_req - shift, n_req)]
    most_ref[0] = most
    loads[2].wait()
    step = 16
    row = lax.broadcasted_iota(jnp.int32, (step * step, step * step), 0)
    column = lax.broadcasted_iota(jnp.int32, (step * step, step * step), 1)
    swap = ((row // step == column % step) & (row % step == column // step)).astype(jnp.bfloat16)
    for page in range(0, pool_pages, step):
        for pair in range(0, pairs, step):
            rows = jnp.concatenate(
                [
                    pool_ref[page : page + step, (pair + i) * pair_width : (pair + i + 1) * pair_width]
                    for i in range(step)
                ],
                axis=0,
            )
            turned = jnp.dot(swap, rows, preferred_element_type=jnp.float32).astype(jnp.bfloat16)
            pages[page : page + step, pair : pair + step, :] = turned.reshape(step, step, pair_width)

    def send(shift, rank, target, sem):
        slot = jnp.where(rank < founds[shift], lists[shift, rank], 0)
        pltpu.make_async_copy(pages.at[slot], target, sem).start()

    for rank in range(cap):
        if rank < chunk:
            send(0, rank, first_ref.at[rank], sems.at[3])
        else:
            send(0, rank, rest_ref.at[rank - chunk], sems.at[4])
    half_cap = foreign_ref.shape[1]
    for shift in range(1, n_req):
        for j in range(half_cap):
            send(shift, seq_idx * half_cap + j, foreign_ref.at[shift - 1, j], sems.at[5])
    loads[3].wait()
    loads[4].wait()
    partial_ref[...] = lax.dot_general(
        hidden_ref[...], down_ref[...], (((1,), (1,)), ((), ())), preferred_element_type=jnp.float32
    )
    pltpu.make_async_copy(first_ref, first_ref, sems.at[3]).wait()
    if cap > chunk:
        pltpu.make_async_copy(rest_ref, rest_ref, sems.at[4]).wait()
    pltpu.make_async_copy(foreign_ref, foreign_ref, sems.at[5]).wait()


def pick_pages(
    page_owner, page_slot, prefix_len, page_pool, hidden, down, cap, chunk, n_head, n_req, n_seq, pairs
):
    pool_pages, page_width = page_pool.shape
    page = (pairs, page_width // pairs)
    return pl.pallas_call(
        functools.partial(pick_kernel, cap, 2 * pairs),
        out_shape=(
            jax.ShapeDtypeStruct((n_req,), jnp.int32),
            jax.ShapeDtypeStruct((1,), jnp.int32),
            jax.ShapeDtypeStruct((chunk, *page), jnp.bfloat16),
            jax.ShapeDtypeStruct((max(1, cap - chunk), *page), jnp.bfloat16),
            jax.ShapeDtypeStruct((n_req - 1, cap // n_seq, *page), jnp.bfloat16),
            jax.ShapeDtypeStruct((hidden.shape[0], down.shape[0]), jnp.float32),
        ),
        in_specs=[any_spec(), any_spec(), any_spec(), hbm_spec(), hbm_spec(), hbm_spec()],
        out_specs=(smem_spec(), smem_spec(), hbm_spec(), hbm_spec(), hbm_spec(), vmem_spec()),
        scratch_shapes=[
            pltpu.SMEM(page_owner.shape, jnp.int32),
            pltpu.SMEM(page_slot.shape, jnp.int32),
            pltpu.SMEM(prefix_len.shape, jnp.int32),
            pltpu.VMEM((pool_pages, page_width), jnp.bfloat16),
            pltpu.VMEM(hidden.shape, jnp.bfloat16),
            pltpu.VMEM(down.shape, jnp.bfloat16),
            pltpu.VMEM((pool_pages, *page), jnp.bfloat16),
            pltpu.SMEM((n_req, cap + 1), jnp.int32),
            pltpu.SMEM((n_req, n_head * n_req), jnp.int32),
            pltpu.SemaphoreType.DMA((9,)),
        ],
        compiler_params=pltpu.CompilerParams(vmem_limit_bytes=60 * MIB),
        cost_estimate=pl.CostEstimate(flops=10**9, bytes_accessed=6 * 10**6, transcendentals=0),
        name="pick_pages",
    )(page_owner, page_slot, prefix_len, page_pool, hidden, down)


def join_kernel(chunk, cap, count_ref, rest_ref, mine_ref, other_ref, *refs):
    n_req = count_ref.shape[0]
    targets, sems = refs[:-1], refs[-1]
    seq_idx = lax.axis_index("seq")
    half_cap = mine_ref.shape[1]
    excess = jnp.maximum(count_ref[0] - chunk, 0)
    j = 0
    for part, target in enumerate(targets):
        for place in range(target.shape[0]):

            def fetch(condition, source, target=target, place=place, part=part):
                @pl.when(condition)
                def _():
                    pltpu.make_async_copy(source, target.at[place], sems.at[part]).start()

            rank = jnp.int32(j)
            taken = rank < excess
            if cap > chunk:
                fetch(taken, rest_ref.at[jnp.minimum(rank, cap - chunk - 1)])
            rank = rank - excess
            for shift in range(1, n_req):
                here = jnp.logical_not(taken) & (rank < count_ref[shift])
                half = rank // half_cap
                slot = jnp.clip(rank - half * half_cap, 0, half_cap - 1)
                fetch(here & (half == seq_idx), mine_ref.at[shift - 1, slot])
                fetch(here & (half != seq_idx), other_ref.at[shift - 1, slot])
                taken = taken | here
                rank = rank - count_ref[shift]
            fetch(jnp.logical_not(taken), mine_ref.at[0, 0])
            j += 1
    for part, target in enumerate(targets):
        pltpu.make_async_copy(target, target, sems.at[part]).wait()


def join_pages(counts, rest, mine, other, chunk, cap, sizes):
    return pl.pallas_call(
        functools.partial(join_kernel, chunk, cap),
        out_shape=tuple(jax.ShapeDtypeStruct((size, *rest.shape[1:]), jnp.bfloat16) for size in sizes),
        in_specs=[smem_spec()] + [hbm_spec()] * 3,
        out_specs=(vmem_spec(),) * len(sizes),
        scratch_shapes=[pltpu.SemaphoreType.DMA((len(sizes),))],
        compiler_params=pltpu.CompilerParams(vmem_limit_bytes=10 * MIB),
        cost_estimate=pl.CostEstimate(flops=0, bytes_accessed=3 * 10**6, transcendentals=0),
        name="join_pages",
    )(counts, rest, mine, other)


def token_limits(owners, prefix, req_idx, n_head, n_req, chunk, slots, page_len):
    pages = owners.shape[0]
    order = jnp.arange(pages, dtype=jnp.int32)
    place = owners // n_req
    shift = lax.rem(req_idx + n_req - lax.rem(owners, n_req), n_req)
    key = shift * pages + order
    together = (place[None, :] == place[:, None]) & (order * page_len < prefix)[None, :]
    rank = jnp.sum((together & (key[None, :] < key[:, None])).astype(jnp.int32), axis=1)
    held = jnp.sum((together & (shift[None, :] == 0)).astype(jnp.int32), axis=1)
    early = (shift == 0) & (rank < chunk)
    within = jnp.where(early, rank, chunk + rank - jnp.minimum(held, chunk))
    slot = place * slots + within
    tokens = jnp.clip(prefix - order * page_len, 0, page_len)
    all_slots = jnp.arange(n_head * slots, dtype=jnp.int32)
    limits = jnp.sum(jnp.where(slot[None, :] == all_slots[:, None], tokens[None, :], 0), axis=1)
    return limits.reshape(n_head, slots)


def over_groups(most):
    n_groups = lax.axis_size("groups")
    passed = most
    for _ in range(n_groups - 1):
        passed = lax.ppermute(passed, "groups", [(i, (i + 1) % n_groups) for i in range(n_groups)])
        most = jnp.maximum(most, passed)
    return most[0]


def query_kernel(query_ref, up_ref, cosine_ref, sine_ref, out_ref):
    heads, nope_width, latent_width = up_ref.shape
    half_len, width = query_ref.shape
    query_width = width // heads
    half_rope = cosine_ref.shape[0]
    key_width = latent_width + 2 * half_rope
    for head in range(heads):
        part = slice(head * half_len, (head + 1) * half_len)
        both = query_ref[:, head * query_width : (head + 1) * query_width]
        latent = lax.dot_general(
            up_ref[head], both[:, :nope_width], (((0,), (1,)), ((), ())), preferred_element_type=jnp.float32
        )
        out_ref[:latent_width, part] = latent.astype(jnp.bfloat16)
        turned = both[:, nope_width:].astype(jnp.float32).T
        low, high = turned[:half_rope], turned[half_rope:]
        out_ref[latent_width : latent_width + half_rope, part] = (
            low * cosine_ref[...] - high * sine_ref[...]
        ).astype(jnp.bfloat16)
        out_ref[latent_width + half_rope : key_width, part] = (
            low * sine_ref[...] + high * cosine_ref[...]
        ).astype(jnp.bfloat16)
    rest = out_ref.shape[0] - key_width
    row = lax.broadcasted_iota(jnp.int32, (rest, out_ref.shape[1]), 0)
    out_ref[key_width:, :] = (row == 0).astype(jnp.bfloat16)


def turn_queries(queries, w_uk, cosine_table, sine_table, key_rows):
    heads, nope_width, latent_width = w_uk.shape
    rows = heads * queries.shape[0]
    return pl.pallas_call(
        query_kernel,
        out_shape=jax.ShapeDtypeStruct((key_rows, rows), jnp.bfloat16),
        in_specs=[vmem_spec()] * 4,
        out_specs=vmem_spec(),
        compiler_params=pltpu.CompilerParams(vmem_limit_bytes=20 * MIB),
        cost_estimate=pl.CostEstimate(
            flops=2 * rows * nope_width * latent_width, bytes_accessed=3 * 10**6, transcendentals=0
        ),
        name="turn_queries",
    )(queries, w_uk, cosine_table, sine_table)


def score_block(keys, queries_ref, target, note, highest, weight_sum, tile, scale, bias=None):
    rows = queries_ref.shape[1]
    for start in range(0, rows, tile):
        part = slice(start, start + tile)
        scores = jnp.dot(keys[...], queries_ref[:, part], preferred_element_type=jnp.float32) * scale
        if bias is not None:
            scores = scores + bias
        old = highest[:, part]
        new = jnp.maximum(old, jnp.max(scores, axis=0, keepdims=True))
        weights = jnp.exp2(scores - new)
        highest[:, part] = new
        weight_sum[:, part] = weight_sum[:, part] * jnp.exp2(old - new) + jnp.sum(
            weights, axis=0, keepdims=True
        )
        target[:, part] = weights
        note(part, new)


def block_limits(limit_ref, block, chunk):
    return [limit_ref[block * chunk + j] for j in range(chunk)]


def any_token(limit_ref, block, chunk):
    return functools.reduce(jnp.maximum, block_limits(limit_ref, block, chunk)) > 0


def load_block(block_ref, keys, limits, key_width):
    chunk, pairs, pair_width = block_ref.shape
    pair_rows = chunk * pairs
    page_rows = block_ref[...].reshape(pair_rows, pair_width)
    keys[:pair_rows, :key_width] = page_rows[:, :key_width]
    keys[pair_rows:, :key_width] = page_rows[:, key_width:]
    shape = (2 * pair_rows, keys.shape[1] - key_width)
    row = lax.broadcasted_iota(jnp.int32, shape, 0)
    pair_row = lax.rem(row, pair_rows)
    token = 2 * lax.rem(pair_row, pairs) + row // pair_rows
    limit = jnp.zeros_like(row)
    for j, value in enumerate(limits):
        limit = jnp.where(pair_row // pairs == j, value, limit)
    masked = (lax.broadcasted_iota(jnp.int32, shape, 1) == 0) & (token >= limit)
    keys[:, key_width:] = jnp.where(masked, MASKED, 0.0).astype(jnp.bfloat16)


def turn_values(keys, latent_width):
    return keys[:, :latent_width].T


def near_bias(n_keys, half_len, tile, live):
    seq_idx = lax.axis_index("seq")
    place = lax.broadcasted_iota(jnp.int32, (n_keys, tile), 0)
    query = lax.rem(lax.broadcasted_iota(jnp.int32, (n_keys, tile), 1), half_len) + seq_idx * half_len
    allowed = (place <= query) & (place < live)
    return jnp.where(allowed, 0.0, -jnp.inf)


def score_kernel(shape, base, n_sources, first, near, limit_ref, queries_ref, *refs):
    tile, scale, chunk, key_width = shape
    refs = list(refs)
    if not first:
        marks_in, sum_in, high_in = [refs.pop(0) for _ in range(3)]
        refs.pop(0), refs.pop(0)
    if near:
        live_ref, suffix_ref = refs.pop(0), refs.pop(0)
    sources = [refs.pop(0) for _ in range(n_sources)]
    weights_hbm, values_hbm, marks, weight_sum, highest = [refs.pop(0) for _ in range(5)]
    if near:
        near_weights, near_values, near_mark = [refs.pop(0) for _ in range(3)]
    blocks, keys, weights, values, load_sems, weight_sems, value_sems = [refs.pop(0) for _ in range(7)]
    n_blocks = blocks.shape[0]
    latent_width = values.shape[1]
    index = 0
    for source in sources:
        for i in range(source.shape[0] // chunk):
            pltpu.make_async_copy(
                source.at[i * chunk : (i + 1) * chunk], blocks.at[index], load_sems.at[index]
            ).start()
            index += 1
    if first:
        marks[...] = jnp.zeros_like(marks)
        weight_sum[...] = jnp.zeros_like(weight_sum)
        highest[...] = jnp.full_like(highest, LOWEST)
    else:
        marks[...] = marks_in[...]
        weight_sum[...] = sum_in[...]
        highest[...] = high_in[...]

    def stores(block):
        return (
            pltpu.make_async_copy(weights.at[block], weights_hbm.at[base + block], weight_sems.at[block]),
            pltpu.make_async_copy(values.at[block], values_hbm.at[base + block], value_sems.at[block]),
        )

    def one_block(block, carry):
        pltpu.make_async_copy(blocks.at[block], blocks.at[block], load_sems.at[block]).wait()

        @pl.when(any_token(limit_ref, block, chunk))
        def _():
            load_block(blocks.at[block], keys, block_limits(limit_ref, block, chunk), key_width)

            def note(part, new):
                marks[pl.ds(base + block, 1), part] = new

            score_block(
                keys, queries_ref, weights.at[block], note, highest, weight_sum, tile, scale
            )
            values[block] = turn_values(keys, latent_width)
            for copy in stores(block):
                copy.start()

        return carry

    lax.fori_loop(0, n_blocks, one_block, 0)
    if near:
        near_keys = refs.pop(0)
        n_near = suffix_ref.shape[0]
        near_keys[:, key_width:] = jnp.zeros_like(near_keys[:, key_width:])
        near_keys[:, :key_width] = suffix_ref[...]

        def note_near(part, new):
            near_mark[:, part] = new

        score_block(
            near_keys, queries_ref, near_weights, note_near, highest, weight_sum, tile, scale,
            near_bias(n_near, n_near // lax.axis_size("seq"), tile, live_ref[0]),
        )
        near_values[...] = turn_values(near_keys, latent_width)

    def one_wait(block, carry):
        @pl.when(any_token(limit_ref, block, chunk))
        def _():
            for copy in stores(block):
                copy.wait()

        return carry

    lax.fori_loop(0, n_blocks, one_wait, 0)


def score_part(base, total, limits, queries, sources, state, shape, latent_width, near=None):
    tile, scale, chunk, key_width = shape
    width, rows = queries.shape
    _, pairs, pair_width = sources[0].shape
    block_keys = 2 * chunk * pairs
    n_blocks = sum(s.shape[0] for s in sources) // chunk
    row = jax.ShapeDtypeStruct((1, rows), jnp.float32)
    out_shape = [
        jax.ShapeDtypeStruct((total, block_keys, rows), jnp.float32),
        jax.ShapeDtypeStruct((total, latent_width, block_keys), jnp.bfloat16),
        jax.ShapeDtypeStruct((total, rows), jnp.float32),
        row,
        row,
    ]
    out_specs = [hbm_spec(), hbm_spec(), vmem_spec(), vmem_spec(), vmem_spec()]
    operands = [limits, queries]
    specs = [smem_spec(), vmem_spec()]
    aliases = {}
    if state is not None:
        operands += [state[2], state[3], state[4], state[0], state[1]]
        specs += [vmem_spec()] * 3 + [hbm_spec()] * 2
        aliases = {5: 0, 6: 1}
    scratch = [
        pltpu.VMEM((n_blocks, chunk, pairs, pair_width), jnp.bfloat16),
        pltpu.VMEM((block_keys, width), jnp.bfloat16),
        pltpu.VMEM((n_blocks, block_keys, rows), jnp.float32),
        pltpu.VMEM((n_blocks, latent_width, block_keys), jnp.bfloat16),
        pltpu.SemaphoreType.DMA((n_blocks,)),
        pltpu.SemaphoreType.DMA((n_blocks,)),
        pltpu.SemaphoreType.DMA((n_blocks,)),
    ]
    if near is not None:
        near_keys = near[-1].shape[0]
        operands += list(near)
        specs += [smem_spec(), vmem_spec()]
        out_shape += [
            jax.ShapeDtypeStruct((near_keys, rows), jnp.float32),
            jax.ShapeDtypeStruct((latent_width, near_keys), jnp.bfloat16),
            row,
        ]
        out_specs += [vmem_spec()] * 3
        scratch.append(pltpu.VMEM((near_keys, width), jnp.bfloat16))
    operands += list(sources)
    specs += [hbm_spec()] * len(sources)
    work = n_blocks * block_keys * rows // 2
    return pl.pallas_call(
        functools.partial(score_kernel, shape, base, len(sources), state is None, near is not None),
        out_shape=tuple(out_shape),
        in_specs=specs,
        out_specs=tuple(out_specs),
        scratch_shapes=scratch,
        input_output_aliases=aliases,
        compiler_params=pltpu.CompilerParams(vmem_limit_bytes=40 * MIB),
        cost_estimate=pl.CostEstimate(
            flops=work, bytes_accessed=10**5, transcendentals=0
        ),
        name="score_part",
    )(*operands)


def finish_kernel(
    shape, depth, n_blocks, n_sources, limit_ref, last_limit_ref, queries_ref, marks, sum_in, high_in,
    near_weights, near_values, near_mark, live_ref, up_ref, weights_hbm, values_hbm, *refs,
):
    tile, scale, chunk, key_width = shape
    sources, refs = refs[:n_sources], refs[n_sources:]
    (
        out_ref, weight_sum, highest, total, blocks, keys, last_weights, last_values, last_marks,
        weights, values, used, load_sems, weight_sems, value_sems,
    ) = refs
    rows = queries_ref.shape[1]
    latent_width = total.shape[0]
    n_last = blocks.shape[0]
    index = 0
    for source in sources:
        for i in range(source.shape[0] // chunk):
            pltpu.make_async_copy(
                source.at[i * chunk : (i + 1) * chunk], blocks.at[index], load_sems.at[index]
            ).start()
            index += 1

    def list_block(block, count):
        used[count] = block
        return count + any_token(limit_ref, block, chunk).astype(jnp.int32)

    n_used = lax.fori_loop(0, n_blocks, list_block, jnp.int32(0))

    def fetches(number):
        place = lax.rem(number, depth)
        return (
            pltpu.make_async_copy(weights_hbm.at[used[number]], weights.at[place], weight_sems.at[place]),
            pltpu.make_async_copy(values_hbm.at[used[number]], values.at[place], value_sems.at[place]),
        )

    def fetch(number):
        @pl.when(number < n_used)
        def _():
            for copy in fetches(number):
                copy.start()

    for number in range(depth):
        fetch(jnp.int32(number))
    weight_sum[...] = sum_in[...]
    highest[...] = high_in[...]
    last_marks[...] = jnp.zeros_like(last_marks)

    def one_score(block, carry):
        pltpu.make_async_copy(blocks.at[block], blocks.at[block], load_sems.at[block]).wait()

        @pl.when(any_token(last_limit_ref, block, chunk))
        def _():
            load_block(blocks.at[block], keys, block_limits(last_limit_ref, block, chunk), key_width)

            def note(part, new):
                last_marks[pl.ds(block, 1), part] = new

            score_block(
                keys, queries_ref, last_weights.at[block], note, highest, weight_sum, tile, scale
            )
            last_values[block] = turn_values(keys, latent_width)

        return carry

    lax.fori_loop(0, n_last, one_score, 0)

    def add_block(weight_block, value_block, mark, begin=False):
        for start in range(0, rows, tile):
            part = slice(start, start + tile)
            factor = jnp.exp2(mark[:, part] - highest[:, part]) / weight_sum[:, part]
            added = jnp.dot(
                value_block[...],
                (weight_block[:, part] * factor).astype(jnp.bfloat16),
                preferred_element_type=jnp.float32,
            )
            total[:, part] = added if begin else total[:, part] + added

    add_block(near_weights, near_values, near_mark, begin=True)

    def one_add(number, carry):
        for copy in fetches(number):
            copy.wait()
        place = lax.rem(number, depth)
        add_block(weights.at[place], values.at[place], marks.at[pl.ds(used[number], 1)])
        fetch(number + depth)
        return carry

    lax.fori_loop(0, n_used, one_add, 0)

    def one_last(block, carry):
        @pl.when(any_token(last_limit_ref, block, chunk))
        def _():
            add_block(last_weights.at[block], last_values.at[block], last_marks.at[pl.ds(block, 1)])

        return carry

    lax.fori_loop(0, n_last, one_last, 0)
    heads, _, value_width = up_ref.shape
    half_len = out_ref.shape[0]
    steps = lax.broadcasted_iota(jnp.int32, (half_len, value_width), 0)
    steps = steps + lax.axis_index("seq") * half_len
    for head in range(heads):
        latent = total[:, head * half_len : (head + 1) * half_len].astype(jnp.bfloat16)
        raised = lax.dot_general(
            latent, up_ref[head], (((0,), (0,)), ((), ())), preferred_element_type=jnp.float32
        )
        out_ref[:, head * value_width : (head + 1) * value_width] = jnp.where(
            steps < live_ref[0], raised, 0.0
        ).astype(jnp.bfloat16)


def finish(n_blocks, limits, last_limits, queries, state, near_state, sources, live, up_weight, half_len, shape):
    tile, scale, chunk, key_width = shape
    weights, values, marks, weight_sum, highest = state
    width, rows = queries.shape
    _, latent_width, block_keys = values.shape
    _, pairs, pair_width = sources[0].shape
    heads, _, value_width = up_weight.shape
    depth = 4
    n_last = sum(s.shape[0] for s in sources) // chunk
    row = pltpu.VMEM((1, rows), jnp.float32)
    work = (n_blocks // 2 + n_last) * block_keys * rows
    return pl.pallas_call(
        functools.partial(finish_kernel, shape, depth, n_blocks, len(sources)),
        out_shape=jax.ShapeDtypeStruct((half_len, heads * value_width), jnp.bfloat16),
        in_specs=[smem_spec()] * 2
        + [vmem_spec()] * 7
        + [smem_spec(), vmem_spec()]
        + [hbm_spec()] * (2 + len(sources)),
        out_specs=vmem_spec(),
        scratch_shapes=[
            row,
            row,
            pltpu.VMEM((latent_width, rows), jnp.float32),
            pltpu.VMEM((n_last, chunk, pairs, pair_width), jnp.bfloat16),
            pltpu.VMEM((block_keys, width), jnp.bfloat16),
            pltpu.VMEM((n_last, block_keys, rows), jnp.float32),
            pltpu.VMEM((n_last, latent_width, block_keys), jnp.bfloat16),
            pltpu.VMEM((n_last, rows), jnp.float32),
            pltpu.VMEM((depth, block_keys, rows), jnp.float32),
            pltpu.VMEM((depth, latent_width, block_keys), jnp.bfloat16),
            pltpu.SMEM((n_blocks + depth + 1,), jnp.int32),
            pltpu.SemaphoreType.DMA((n_last,)),
            pltpu.SemaphoreType.DMA((depth,)),
            pltpu.SemaphoreType.DMA((depth,)),
        ],
        compiler_params=pltpu.CompilerParams(vmem_limit_bytes=40 * MIB),
        cost_estimate=pl.CostEstimate(
            flops=2 * work * latent_width, bytes_accessed=3 * 10**7, transcendentals=work // 4
        ),
        name="finish",
    )(
        limits, last_limits, queries, marks, weight_sum, highest, *near_state, live, up_weight,
        weights, values, *sources,
    )


def local(
    queries,
    hidden,
    w_dkv,
    kv_gain,
    w_uk,
    value_up_weight,
    page_pool,
    page_owner,
    page_slot,
    prefix_len,
    suffix_len,
):
    n_head = lax.axis_size("head")
    n_req = lax.axis_size("req")
    n_seq = lax.axis_size("seq")
    head_idx = lax.axis_index("head")
    req_idx = lax.axis_index("req")
    seq_idx = lax.axis_index("seq")
    _, half_len, d_local = hidden.shape
    heads_dev, nope_width, latent_width = w_uk.shape
    lat_width = w_dkv.shape[1]
    rope_width = lat_width - latent_width
    query_width = queries.shape[2] // heads_dev
    page_width = page_pool.shape[1]
    page_len = page_width // lat_width
    pairs = page_len // 2
    pages_req = page_slot.shape[1]
    cap = max(2, 2 * pages_req // (n_head * n_req))
    chunk = n_req * cap // 4
    slots = 4 * chunk
    score_scale = float(query_width) ** (-0.5)

    owner_rows = page_owner[:, :, 0]
    counts, most, first, rest, foreign, partial_value = pick_pages(
        owner_rows, page_slot, prefix_len, page_pool, hidden[0], w_dkv.T,
        cap, chunk, n_head, n_req, n_seq, pairs,
    )
    swap_route = [(i, n_seq - 1 - i) for i in range(n_seq)]
    stream_route = []
    for i in range(n_head - 1):
        stream_route.append((i * n_seq, (i + 1) * n_seq))
        stream_route.append(((i + 1) * n_seq + 1, i * n_seq + 1))

    def swap(block):
        return lax.ppermute(block, "seq", swap_route)

    def stream(block):
        return lax.ppermute(block, ("head", "seq"), stream_route)

    my_prefix = lax.dynamic_index_in_dim(prefix_len, req_idx, 0, keepdims=False)
    my_suffix = lax.dynamic_index_in_dim(suffix_len, req_idx, 0, keepdims=False)
    own_owners = lax.dynamic_index_in_dim(owner_rows, req_idx, 0, keepdims=False)
    place_limits = token_limits(own_owners, my_prefix, req_idx, n_head, n_req, chunk, slots, page_len)
    upward = 2 * seq_idx - 1
    origins = [head_idx]
    for step in range(1, n_head):
        origins += [head_idx + upward * step, head_idx - upward * step]
    origins = jnp.stack(origins)
    heads = jnp.arange(n_head, dtype=jnp.int32)
    limits = jnp.sum(
        jnp.where((origins[:, None] == heads[None, :])[:, :, None], place_limits[None], 0), axis=1
    )

    positions = my_prefix + seq_idx * half_len + jnp.arange(half_len, dtype=jnp.int32)
    rows = heads_dev * half_len
    half_rope = rope_width // 2
    frequency = 10000.0 ** (-2.0 * jnp.arange(half_rope, dtype=jnp.float32) / rope_width)
    phases = frequency[:, None] * positions.astype(jnp.float32)[None, :]
    q_turned = turn_queries(queries[0], w_uk, jnp.cos(phases), jnp.sin(phases), lat_width + 64)

    arrived = [
        lax.ppermute(foreign[s - 1], "req", [(i, (i + s) % n_req) for i in range(n_req)])
        for s in range(1, n_req)
    ]
    early_steps = [stream(first)]
    share = half_len // n_head
    partials = lax.all_to_all(partial_value, "head", split_axis=0, concat_axis=0, tiled=True)
    summed = jnp.sum(partials.reshape(n_head, share, lat_width), axis=0)
    share_t = seq_idx * half_len + head_idx * share + jnp.arange(share, dtype=jnp.int32)
    latent = finish_latent(summed, my_prefix + share_t, share_t < my_suffix, kv_gain, latent_width)
    copies = jnp.concatenate([latent] * n_head, axis=0)
    fresh = lax.all_to_all(copies, "head", split_axis=0, concat_axis=0, tiled=True)
    early_steps[0], fresh = lax.optimization_barrier((early_steps[0], fresh))
    for step in range(1, n_head - 1):
        early_steps.append(stream(early_steps[-1]))
    early_steps = [[block, None] for block in early_steps]
    for step in range(n_head - 2):
        early_steps[step][1] = swap(early_steps[step][0])
    mine = arrived[0][None] if n_req == 2 else jnp.stack(arrived)
    mine, fresh = lax.optimization_barrier((mine, fresh))
    other = swap(mine)
    middle, late = join_pages(counts, rest, mine, other, chunk, cap, (2 * chunk, chunk))

    tile = 256 if rows % 256 == 0 and 256 % half_len == 0 else half_len
    shape = (tile, score_scale * math.log2(math.e), chunk, lat_width)
    parts = {"early": (0, chunk), "middle": (chunk, 3 * chunk), "late": (3 * chunk, 4 * chunk)}

    def limits_of(pieces):
        return jnp.concatenate(
            [limits[origin, parts[name][0] : parts[name][1]] for name, origin in pieces]
        )

    def pieces_of(name, steps):
        return [(name, 2 * step + side + 1) for step in steps for side in range(2)]

    def arrays_of(arrived_steps, steps):
        return [arrived_steps[step][side] for step in steps for side in range(2)]

    last = n_head - 2
    live = my_suffix.reshape(1)
    near_state = ()
    extra = 4 + 1 + 2 * last
    total = 1 + 2 * (last + 1) + 2 + 4 * last + extra
    used_limits = []
    n_blocks = 0
    state = None

    def score(pieces, arrays, near=None):
        nonlocal n_blocks, state, near_state
        used_limits.append(limits_of(pieces))
        result = score_part(
            n_blocks, total, used_limits[-1], q_turned, arrays, state, shape, latent_width, near
        )
        state = result[:5]
        near_state = result[5:] or near_state
        n_blocks += sum(a.shape[0] for a in arrays) // chunk

    def tie(block):
        nonlocal state
        block, mark = lax.optimization_barrier((block, state[4]))
        state = (*state[:4], mark)
        return block

    middle, early_steps[last - 1][0] = lax.optimization_barrier((middle, early_steps[last - 1][0]))
    middle_steps = []
    block = stream(middle)
    for step in range(last + 1):
        received = block
        if step == 0:
            score(
                [("early", 0)] + pieces_of("early", range(last)),
                [first] + arrays_of(early_steps, range(last)),
            )
        elif step == 1:
            score(
                pieces_of("early", [last]) + [("middle", 0)] + pieces_of("middle", [0]),
                arrays_of(early_steps, [last]) + [middle] + arrays_of(middle_steps, [0]),
            )
        else:
            score(
                pieces_of("middle", [step - 1]),
                arrays_of(middle_steps, [step - 1]),
                (live, suffix_latent) if step == last else None,
            )
        received = tie(received)
        if step == 0:
            early_steps[last][0] = tie(early_steps[last][0])
            early_steps[last][1] = swap(early_steps[last][0])
            opposite = swap(fresh)
            suffix_latent = jnp.where(
                seq_idx == 0,
                jnp.concatenate([fresh, opposite], axis=0),
                jnp.concatenate([opposite, fresh], axis=0),
            )
            most = over_groups(most)
            received, most = lax.optimization_barrier((received, most))
        elif step == last - 1:
            received, suffix_latent = lax.optimization_barrier((received, suffix_latent))
        if step < last:
            block = stream(received)
        middle_steps.append([received, swap(received)])

    last_pieces = pieces_of("middle", [last])
    last_arrays = arrays_of(middle_steps, [last])

    known = jnp.concatenate(used_limits)
    final = limits_of(last_pieces)

    def end(blocks, blocks_limits, final_limits, final_arrays, current):
        return finish(
            blocks, blocks_limits, final_limits, q_turned, current, near_state,
            final_arrays, live, value_up_weight, half_len, shape,
        )

    def with_late(_):
        block = stream(late)
        pieces = last_pieces + [("late", 0)]
        arrays = last_arrays + [late]
        current, blocks, limit_list = state, n_blocks, list(used_limits)
        for step in range(last + 1):
            received = block
            more = limits_of(pieces)
            limit_list.append(more)
            current = score_part(
                blocks, total, more, q_turned, arrays, current, shape, latent_width
            )[:5]
            blocks += sum(a.shape[0] for a in arrays) // chunk
            received, mark = lax.optimization_barrier((received, current[4]))
            current = (*current[:4], mark)
            if step < last:
                block = stream(received)
            arrays = [received, swap(received)]
            pieces = pieces_of("late", [step])
        return end(blocks, jnp.concatenate(limit_list), limits_of(pieces), arrays, current)

    def without_late(_):
        return end(n_blocks, known, final, last_arrays, state)

    attn_out = lax.cond(most > 2 * chunk, with_late, without_late, 0)
    new_pages = fresh.reshape(1, half_len // page_len, page_len * lat_width)
    return (attn_out[None], new_pages)


def solution(mesh):
    placed = (
        P(("groups", "req"), "seq", "head"),
        P(("groups", "req"), "seq", "head"),
        P("head", None),
        P(),
        P("head", None, None),
        P("head", None, None),
        P(("groups", "head", "req"), None),
        P("groups", None, None),
        P("groups", None),
        P("groups"),
        P("groups"),
    )
    return jax.shard_map(
        local,
        mesh=mesh,
        in_specs=placed,
        out_specs=(P(("groups", "req"), "seq", "head"), P(("groups", "req"), "seq", None)),
        check_vma=False,
    )
```

```python
import functools
import math

import jax
import jax.numpy as jnp
from jax import lax
from jax.experimental import pallas as pl
from jax.experimental.pallas import tpu as pltpu
from jax.sharding import PartitionSpec as P

LOWEST = -1e30
MASKED = -1e38
MIB = 1024 * 1024


def rotate(vector, cosine_table, sine_table):
    half_width = vector.shape[-1] // 2
    first_half = vector[..., :half_width]
    second_half = vector[..., half_width:]
    return jnp.concatenate(
        [
            first_half * cosine_table - second_half * sine_table,
            first_half * sine_table + second_half * cosine_table,
        ],
        axis=-1,
    )


def angles(positions, rope_width):
    half_width = rope_width // 2
    frequency = 10000.0 ** (-2.0 * jnp.arange(half_width, dtype=jnp.float32) / rope_width)
    phases = positions.astype(jnp.float32)[:, None] * frequency[None, :]
    return (jnp.cos(phases), jnp.sin(phases))


def finish_latent(summed, positions, live_rows, kv_gain, latent_width):
    latent_part = summed[:, :latent_width]
    mean_square = jnp.mean(latent_part * latent_part, axis=-1, keepdims=True)
    normed = latent_part * lax.rsqrt(mean_square + 1e-06) * kv_gain
    cosine_table, sine_table = angles(positions, summed.shape[1] - latent_width)
    rotated = rotate(summed[:, latent_width:], cosine_table, sine_table)
    joined = jnp.concatenate([normed, rotated], axis=-1).astype(jnp.bfloat16)
    return jnp.where(live_rows[:, None], joined, jnp.zeros_like(joined))


def any_spec():
    return pl.BlockSpec(memory_space=pl.ANY)


def smem_spec():
    return pl.BlockSpec(memory_space=pltpu.SMEM)


def vmem_spec():
    return pl.BlockSpec(memory_space=pltpu.VMEM)


def hbm_spec():
    return pl.BlockSpec(memory_space=pltpu.HBM)


def pick_kernel(
    cap, page_len, owner_hbm, slot_hbm, prefix_hbm, suffix_hbm, pool_hbm, hidden_hbm, down_hbm, count_ref,
    most_ref, length_ref, live_ref, first_ref, rest_ref, foreign_ref, partial_ref, owner_ref, slot_ref,
    prefix_ref, suffix_ref, pool_ref, hidden_ref, down_ref, pages, lists, table, sems,
):
    n_req = lax.axis_size("req")
    head_idx = lax.axis_index("head")
    req_idx = lax.axis_index("req")
    seq_idx = lax.axis_index("seq")
    n_pages = owner_ref.shape[1]
    pool_pages, pairs, pair_width = pages.shape
    chunk = first_ref.shape[0]
    loads = [
        pltpu.make_async_copy(owner_hbm, owner_ref, sems.at[0]),
        pltpu.make_async_copy(slot_hbm, slot_ref, sems.at[1]),
        pltpu.make_async_copy(pool_hbm, pool_ref, sems.at[2]),
        pltpu.make_async_copy(hidden_hbm, hidden_ref, sems.at[6]),
        pltpu.make_async_copy(down_hbm, down_ref, sems.at[7]),
        pltpu.make_async_copy(prefix_hbm, prefix_ref, sems.at[8]),
        pltpu.make_async_copy(suffix_hbm, suffix_ref, sems.at[9]),
    ]
    for load in loads:
        load.start()
    loads[0].wait()
    loads[1].wait()
    loads[5].wait()
    loads[6].wait()
    length_ref[0] = prefix_ref[req_idx]
    live_ref[0] = suffix_ref[req_idx]
    self_owner = head_idx * n_req + req_idx
    n_owners = table.shape[1]
    for shift in range(n_req):
        for owner in range(n_owners):
            table[shift, owner] = 0
    founds = []
    most = jnp.int32(0)
    for shift in range(n_req):
        request = lax.rem(req_idx + shift, n_req)

        def note(page, found, shift=shift, request=request):
            owner = owner_ref[request, page]
            needed = page * page_len < prefix_ref[request]
            table[shift, owner] += needed.astype(jnp.int32)
            lists[shift, found] = slot_ref[request, page]
            return found + (needed & (owner == self_owner)).astype(jnp.int32)

        founds.append(lax.fori_loop(0, n_pages, note, jnp.int32(0), unroll=8))
        for place in range(n_owners // n_req):
            held = functools.reduce(jnp.add, [table[shift, place * n_req + i] for i in range(n_req)])
            early = jnp.minimum(table[shift, place * n_req + request], chunk)
            most = jnp.maximum(most, held - early)
    for shift in range(n_req):
        count_ref[shift] = table[0, head_idx * n_req + lax.rem(req_idx + n_req - shift, n_req)]
    most_ref[0] = most
    loads[2].wait()
    step = 16
    row = lax.broadcasted_iota(jnp.int32, (step * step, step * step), 0)
    column = lax.broadcasted_iota(jnp.int32, (step * step, step * step), 1)
    swap = ((row // step == column % step) & (row % step == column // step)).astype(jnp.bfloat16)
    for page in range(0, pool_pages, step):
        for pair in range(0, pairs, step):
            rows = jnp.concatenate(
                [
                    pool_ref[page : page + step, (pair + i) * pair_width : (pair + i + 1) * pair_width]
                    for i in range(step)
                ],
                axis=0,
            )
            turned = jnp.dot(swap, rows, preferred_element_type=jnp.float32).astype(jnp.bfloat16)
            pages[page : page + step, pair : pair + step, :] = turned.reshape(step, step, pair_width)

    def send(shift, rank, target, sem):
        slot = jnp.where(rank < founds[shift], lists[shift, rank], 0)
        pltpu.make_async_copy(pages.at[slot], target, sem).start()

    for rank in range(cap):
        if rank < chunk:
            send(0, rank, first_ref.at[rank], sems.at[3])
        else:
            send(0, rank, rest_ref.at[rank - chunk], sems.at[4])
    half_cap = foreign_ref.shape[1]
    for shift in range(1, n_req):
        for j in range(half_cap):
            send(shift, seq_idx * half_cap + j, foreign_ref.at[shift - 1, j], sems.at[5])
    loads[3].wait()
    loads[4].wait()
    partial_ref[...] = lax.dot_general(
        hidden_ref[...], down_ref[...], (((1,), (1,)), ((), ())), preferred_element_type=jnp.float32
    )
    pltpu.make_async_copy(first_ref, first_ref, sems.at[3]).wait()
    if cap > chunk:
        pltpu.make_async_copy(rest_ref, rest_ref, sems.at[4]).wait()
    pltpu.make_async_copy(foreign_ref, foreign_ref, sems.at[5]).wait()


def pick_pages(
    page_owner, page_slot, prefix_len, suffix_len, page_pool, hidden, down,
    cap, chunk, n_head, n_req, n_seq, pairs,
):
    pool_pages, page_width = page_pool.shape
    page = (pairs, page_width // pairs)
    return pl.pallas_call(
        functools.partial(pick_kernel, cap, 2 * pairs),
        out_shape=(
            jax.ShapeDtypeStruct((n_req,), jnp.int32),
            jax.ShapeDtypeStruct((1,), jnp.int32),
            jax.ShapeDtypeStruct((1,), jnp.int32),
            jax.ShapeDtypeStruct((1,), jnp.int32),
            jax.ShapeDtypeStruct((chunk, *page), jnp.bfloat16),
            jax.ShapeDtypeStruct((max(1, cap - chunk), *page), jnp.bfloat16),
            jax.ShapeDtypeStruct((n_req - 1, cap // n_seq, *page), jnp.bfloat16),
            jax.ShapeDtypeStruct((hidden.shape[0], down.shape[0]), jnp.float32),
        ),
        in_specs=[any_spec()] * 4 + [hbm_spec()] * 3,
        out_specs=(smem_spec(), smem_spec(), smem_spec(), smem_spec(), hbm_spec(), hbm_spec(), hbm_spec(), vmem_spec()),
        scratch_shapes=[
            pltpu.SMEM(page_owner.shape, jnp.int32),
            pltpu.SMEM(page_slot.shape, jnp.int32),
            pltpu.SMEM(prefix_len.shape, jnp.int32),
            pltpu.SMEM(suffix_len.shape, jnp.int32),
            pltpu.VMEM((pool_pages, page_width), jnp.bfloat16),
            pltpu.VMEM(hidden.shape, jnp.bfloat16),
            pltpu.VMEM(down.shape, jnp.bfloat16),
            pltpu.VMEM((pool_pages, *page), jnp.bfloat16),
            pltpu.SMEM((n_req, cap + 1), jnp.int32),
            pltpu.SMEM((n_req, n_head * n_req), jnp.int32),
            pltpu.SemaphoreType.DMA((10,)),
        ],
        compiler_params=pltpu.CompilerParams(vmem_limit_bytes=60 * MIB),
        cost_estimate=pl.CostEstimate(flops=10**9, bytes_accessed=6 * 10**6, transcendentals=0),
        name="pick_pages",
    )(page_owner, page_slot, prefix_len, suffix_len, page_pool, hidden, down)


def join_kernel(chunk, cap, count_ref, rest_ref, mine_ref, other_ref, *refs):
    n_req = count_ref.shape[0]
    targets, sems = refs[:-1], refs[-1]
    seq_idx = lax.axis_index("seq")
    half_cap = mine_ref.shape[1]
    excess = jnp.maximum(count_ref[0] - chunk, 0)
    j = 0
    for part, target in enumerate(targets):
        for place in range(target.shape[0]):

            def fetch(condition, source, target=target, place=place, part=part):
                @pl.when(condition)
                def _():
                    pltpu.make_async_copy(source, target.at[place], sems.at[part]).start()

            rank = jnp.int32(j)
            taken = rank < excess
            if cap > chunk:
                fetch(taken, rest_ref.at[jnp.minimum(rank, cap - chunk - 1)])
            rank = rank - excess
            for shift in range(1, n_req):
                here = jnp.logical_not(taken) & (rank < count_ref[shift])
                half = rank // half_cap
                slot = jnp.clip(rank - half * half_cap, 0, half_cap - 1)
                fetch(here & (half == seq_idx), mine_ref.at[shift - 1, slot])
                fetch(here & (half != seq_idx), other_ref.at[shift - 1, slot])
                taken = taken | here
                rank = rank - count_ref[shift]
            fetch(jnp.logical_not(taken), mine_ref.at[0, 0])
            j += 1
    for part, target in enumerate(targets):
        pltpu.make_async_copy(target, target, sems.at[part]).wait()


def join_pages(counts, rest, mine, other, chunk, cap, sizes):
    return pl.pallas_call(
        functools.partial(join_kernel, chunk, cap),
        out_shape=tuple(jax.ShapeDtypeStruct((size, *rest.shape[1:]), jnp.bfloat16) for size in sizes),
        in_specs=[smem_spec()] + [hbm_spec()] * 3,
        out_specs=(vmem_spec(),) * len(sizes),
        scratch_shapes=[pltpu.SemaphoreType.DMA((len(sizes),))],
        compiler_params=pltpu.CompilerParams(vmem_limit_bytes=10 * MIB),
        cost_estimate=pl.CostEstimate(flops=0, bytes_accessed=3 * 10**6, transcendentals=0),
        name="join_pages",
    )(counts, rest, mine, other)


def plan_kernel(pieces, page_len, chunk, owner_ref, prefix_ref, limit_ref, places, counts, running):
    n_req = lax.axis_size("req")
    head_idx = lax.axis_index("head")
    req_idx = lax.axis_index("req")
    n_head, width = places.shape
    n_pages = owner_ref.shape[1]
    prefix = prefix_ref[req_idx]
    for place in range(n_head):
        for shift in range(n_req):
            counts[place, shift] = 0
            running[place, shift] = 0
        for slot in range(width):
            places[place, slot] = 0

    def where_from(page):
        owner = owner_ref[req_idx, page]
        place = owner // n_req
        shift = lax.rem(req_idx + n_req - (owner - place * n_req), n_req)
        return place, shift, (page * page_len < prefix).astype(jnp.int32)

    def count(page, carry):
        place, shift, needed = where_from(page)
        counts[place, shift] += needed
        return carry

    def note(page, carry):
        place, shift, needed = where_from(page)
        rank = running[place, shift]
        running[place, shift] = rank + needed
        for earlier in range(n_req - 1):
            rank = rank + jnp.where(earlier < shift, counts[place, earlier], 0)
        early = (shift == 0) & (rank < chunk)
        slot = jnp.where(early, rank, chunk + rank - jnp.minimum(counts[place, 0], chunk))
        slot = jnp.where(needed > 0, slot, width - 1)
        places[place, slot] = jnp.clip(prefix - page * page_len, 0, page_len)
        return carry

    lax.fori_loop(0, n_pages, count, 0, unroll=4)
    lax.fori_loop(0, n_pages, note, 0, unroll=4)
    upward = 2 * lax.axis_index("seq") - 1
    for block, (first, origin) in enumerate(pieces):
        step, side = (origin + 1) // 2, 2 * (origin % 2) - 1
        place = head_idx + upward * side * step
        inside = (place >= 0) & (place < n_head)
        place = jnp.clip(place, 0, n_head - 1)
        for j in range(chunk):
            limit_ref[block * chunk + j] = jnp.where(inside, places[place, first + j], 0)


def plan_blocks(page_owner, prefix_len, pieces, n_head, n_req, chunk, page_len):
    return pl.pallas_call(
        functools.partial(plan_kernel, pieces, page_len, chunk),
        out_shape=jax.ShapeDtypeStruct((len(pieces) * chunk,), jnp.int32),
        in_specs=[smem_spec()] * 2,
        out_specs=smem_spec(),
        scratch_shapes=[
            pltpu.SMEM((n_head, 4 * chunk + 1), jnp.int32),
            pltpu.SMEM((n_head, n_req), jnp.int32),
            pltpu.SMEM((n_head, n_req), jnp.int32),
        ],
        cost_estimate=pl.CostEstimate(flops=10**4, bytes_accessed=10**4, transcendentals=0),
        name="plan_blocks",
    )(page_owner, prefix_len)


def over_groups(most):
    n_groups = lax.axis_size("groups")
    passed = most
    for _ in range(n_groups - 1):
        passed = lax.ppermute(passed, "groups", [(i, (i + 1) % n_groups) for i in range(n_groups)])
        most = jnp.maximum(most, passed)
    return most[0]


def query_kernel(query_ref, up_ref, cosine_ref, sine_ref, out_ref):
    heads, nope_width, latent_width = up_ref.shape
    half_len, width = query_ref.shape
    query_width = width // heads
    half_rope = cosine_ref.shape[0]
    key_width = latent_width + 2 * half_rope
    for head in range(heads):
        part = slice(head * half_len, (head + 1) * half_len)
        both = query_ref[:, head * query_width : (head + 1) * query_width]
        latent = lax.dot_general(
            up_ref[head], both[:, :nope_width], (((0,), (1,)), ((), ())), preferred_element_type=jnp.float32
        )
        out_ref[:latent_width, part] = latent.astype(jnp.bfloat16)
        turned = both[:, nope_width:].astype(jnp.float32).T
        low, high = turned[:half_rope], turned[half_rope:]
        out_ref[latent_width : latent_width + half_rope, part] = (
            low * cosine_ref[...] - high * sine_ref[...]
        ).astype(jnp.bfloat16)
        out_ref[latent_width + half_rope : key_width, part] = (
            low * sine_ref[...] + high * cosine_ref[...]
        ).astype(jnp.bfloat16)
    rest = out_ref.shape[0] - key_width
    row = lax.broadcasted_iota(jnp.int32, (rest, out_ref.shape[1]), 0)
    out_ref[key_width:, :] = (row == 0).astype(jnp.bfloat16)


def turn_queries(queries, w_uk, cosine_table, sine_table, key_rows):
    heads, nope_width, latent_width = w_uk.shape
    rows = heads * queries.shape[0]
    return pl.pallas_call(
        query_kernel,
        out_shape=jax.ShapeDtypeStruct((key_rows, rows), jnp.bfloat16),
        in_specs=[vmem_spec()] * 4,
        out_specs=vmem_spec(),
        compiler_params=pltpu.CompilerParams(vmem_limit_bytes=20 * MIB),
        cost_estimate=pl.CostEstimate(
            flops=2 * rows * nope_width * latent_width, bytes_accessed=3 * 10**6, transcendentals=0
        ),
        name="turn_queries",
    )(queries, w_uk, cosine_table, sine_table)


def score_block(keys, queries_ref, target, note, highest, weight_sum, tile, scale, bias=None):
    rows = queries_ref.shape[1]
    for start in range(0, rows, tile):
        part = slice(start, start + tile)
        scores = jnp.dot(keys[...], queries_ref[:, part], preferred_element_type=jnp.float32) * scale
        if bias is not None:
            scores = scores + bias
        old = highest[:, part]
        new = jnp.maximum(old, jnp.max(scores, axis=0, keepdims=True))
        weights = jnp.exp2(scores - new)
        highest[:, part] = new
        weight_sum[:, part] = weight_sum[:, part] * jnp.exp2(old - new) + jnp.sum(
            weights, axis=0, keepdims=True
        )
        target[:, part] = weights
        note(part, new)


def block_limits(limit_ref, block, chunk):
    return [limit_ref[block * chunk + j] for j in range(chunk)]


def any_token(limit_ref, block, chunk):
    return functools.reduce(jnp.maximum, block_limits(limit_ref, block, chunk)) > 0


def load_block(block_ref, keys, limits, key_width):
    chunk, pairs, pair_width = block_ref.shape
    pair_rows = chunk * pairs
    page_rows = block_ref[...].reshape(pair_rows, pair_width)
    keys[:pair_rows, :key_width] = page_rows[:, :key_width]
    keys[pair_rows:, :key_width] = page_rows[:, key_width:]
    shape = (2 * pair_rows, keys.shape[1] - key_width)
    row = lax.broadcasted_iota(jnp.int32, shape, 0)
    pair_row = lax.rem(row, pair_rows)
    token = 2 * lax.rem(pair_row, pairs) + row // pair_rows
    limit = jnp.zeros_like(row)
    for j, value in enumerate(limits):
        limit = jnp.where(pair_row // pairs == j, value, limit)
    masked = (lax.broadcasted_iota(jnp.int32, shape, 1) == 0) & (token >= limit)
    keys[:, key_width:] = jnp.where(masked, MASKED, 0.0).astype(jnp.bfloat16)


def turn_values(keys, latent_width):
    return keys[:, :latent_width].T


def near_bias(n_keys, half_len, tile, live):
    seq_idx = lax.axis_index("seq")
    place = lax.broadcasted_iota(jnp.int32, (n_keys, tile), 0)
    query = lax.rem(lax.broadcasted_iota(jnp.int32, (n_keys, tile), 1), half_len) + seq_idx * half_len
    allowed = (place <= query) & (place < live)
    return jnp.where(allowed, 0.0, -jnp.inf)


def score_kernel(shape, base, n_sources, first, near, limit_ref, queries_ref, *refs):
    tile, scale, chunk, key_width = shape
    refs = list(refs)
    if not first:
        marks_in, sum_in, high_in = [refs.pop(0) for _ in range(3)]
        refs.pop(0), refs.pop(0)
    if near:
        live_ref, suffix_ref = refs.pop(0), refs.pop(0)
    sources = [refs.pop(0) for _ in range(n_sources)]
    weights_hbm, values_hbm, marks, weight_sum, highest = [refs.pop(0) for _ in range(5)]
    if near:
        near_weights, near_values, near_mark = [refs.pop(0) for _ in range(3)]
    blocks, keys, weights, values, load_sems, weight_sems, value_sems = [refs.pop(0) for _ in range(7)]
    n_blocks = blocks.shape[0]
    latent_width = values.shape[1]
    index = 0
    for source in sources:
        for i in range(source.shape[0] // chunk):
            pltpu.make_async_copy(
                source.at[i * chunk : (i + 1) * chunk], blocks.at[index], load_sems.at[index]
            ).start()
            index += 1
    if first:
        marks[...] = jnp.zeros_like(marks)
        weight_sum[...] = jnp.zeros_like(weight_sum)
        highest[...] = jnp.full_like(highest, LOWEST)
    else:
        marks[...] = marks_in[...]
        weight_sum[...] = sum_in[...]
        highest[...] = high_in[...]

    def stores(block):
        return (
            pltpu.make_async_copy(weights.at[block], weights_hbm.at[base + block], weight_sems.at[block]),
            pltpu.make_async_copy(values.at[block], values_hbm.at[base + block], value_sems.at[block]),
        )

    def one_block(block, carry):
        pltpu.make_async_copy(blocks.at[block], blocks.at[block], load_sems.at[block]).wait()

        @pl.when(any_token(limit_ref, base + block, chunk))
        def _():
            load_block(blocks.at[block], keys, block_limits(limit_ref, base + block, chunk), key_width)

            def note(part, new):
                marks[pl.ds(base + block, 1), part] = new

            score_block(
                keys, queries_ref, weights.at[block], note, highest, weight_sum, tile, scale
            )
            values[block] = turn_values(keys, latent_width)
            for copy in stores(block):
                copy.start()

        return carry

    lax.fori_loop(0, n_blocks, one_block, 0)
    if near:
        near_keys = refs.pop(0)
        n_near = suffix_ref.shape[0]
        near_keys[:, key_width:] = jnp.zeros_like(near_keys[:, key_width:])
        near_keys[:, :key_width] = suffix_ref[...]

        def note_near(part, new):
            near_mark[:, part] = new

        score_block(
            near_keys, queries_ref, near_weights, note_near, highest, weight_sum, tile, scale,
            near_bias(n_near, n_near // lax.axis_size("seq"), tile, live_ref[0]),
        )
        near_values[...] = turn_values(near_keys, latent_width)

    def one_wait(block, carry):
        @pl.when(any_token(limit_ref, base + block, chunk))
        def _():
            for copy in stores(block):
                copy.wait()

        return carry

    lax.fori_loop(0, n_blocks, one_wait, 0)


def score_part(base, total, limits, queries, sources, state, shape, latent_width, near=None):
    tile, scale, chunk, key_width = shape
    width, rows = queries.shape
    _, pairs, pair_width = sources[0].shape
    block_keys = 2 * chunk * pairs
    n_blocks = sum(s.shape[0] for s in sources) // chunk
    row = jax.ShapeDtypeStruct((1, rows), jnp.float32)
    out_shape = [
        jax.ShapeDtypeStruct((total, block_keys, rows), jnp.float32),
        jax.ShapeDtypeStruct((total, latent_width, block_keys), jnp.bfloat16),
        jax.ShapeDtypeStruct((total, rows), jnp.float32),
        row,
        row,
    ]
    out_specs = [hbm_spec(), hbm_spec(), vmem_spec(), vmem_spec(), vmem_spec()]
    operands = [limits, queries]
    specs = [smem_spec(), vmem_spec()]
    aliases = {}
    if state is not None:
        operands += [state[2], state[3], state[4], state[0], state[1]]
        specs += [vmem_spec()] * 3 + [hbm_spec()] * 2
        aliases = {5: 0, 6: 1}
    scratch = [
        pltpu.VMEM((n_blocks, chunk, pairs, pair_width), jnp.bfloat16),
        pltpu.VMEM((block_keys, width), jnp.bfloat16),
        pltpu.VMEM((n_blocks, block_keys, rows), jnp.float32),
        pltpu.VMEM((n_blocks, latent_width, block_keys), jnp.bfloat16),
        pltpu.SemaphoreType.DMA((n_blocks,)),
        pltpu.SemaphoreType.DMA((n_blocks,)),
        pltpu.SemaphoreType.DMA((n_blocks,)),
    ]
    if near is not None:
        near_keys = near[-1].shape[0]
        operands += list(near)
        specs += [smem_spec(), vmem_spec()]
        out_shape += [
            jax.ShapeDtypeStruct((near_keys, rows), jnp.float32),
            jax.ShapeDtypeStruct((latent_width, near_keys), jnp.bfloat16),
            row,
        ]
        out_specs += [vmem_spec()] * 3
        scratch.append(pltpu.VMEM((near_keys, width), jnp.bfloat16))
    operands += list(sources)
    specs += [hbm_spec()] * len(sources)
    work = n_blocks * block_keys * rows // 2
    return pl.pallas_call(
        functools.partial(score_kernel, shape, base, len(sources), state is None, near is not None),
        out_shape=tuple(out_shape),
        in_specs=specs,
        out_specs=tuple(out_specs),
        scratch_shapes=scratch,
        input_output_aliases=aliases,
        compiler_params=pltpu.CompilerParams(vmem_limit_bytes=40 * MIB),
        cost_estimate=pl.CostEstimate(
            flops=work, bytes_accessed=10**5, transcendentals=0
        ),
        name="score_part",
    )(*operands)


def finish_kernel(
    shape, depth, n_blocks, n_sources, limit_ref, queries_ref, marks, sum_in, high_in,
    near_weights, near_values, near_mark, live_ref, up_ref, weights_hbm, values_hbm, *refs,
):
    tile, scale, chunk, key_width = shape
    sources, refs = refs[:n_sources], refs[n_sources:]
    (
        out_ref, weight_sum, highest, total, blocks, keys, last_weights, last_values, last_marks,
        weights, values, used, load_sems, weight_sems, value_sems,
    ) = refs
    rows = queries_ref.shape[1]
    latent_width = total.shape[0]
    n_last = blocks.shape[0]
    index = 0
    for source in sources:
        for i in range(source.shape[0] // chunk):
            pltpu.make_async_copy(
                source.at[i * chunk : (i + 1) * chunk], blocks.at[index], load_sems.at[index]
            ).start()
            index += 1

    def list_block(block, count):
        used[count] = block
        return count + any_token(limit_ref, block, chunk).astype(jnp.int32)

    n_used = lax.fori_loop(0, n_blocks, list_block, jnp.int32(0))

    def fetches(number):
        place = lax.rem(number, depth)
        return (
            pltpu.make_async_copy(weights_hbm.at[used[number]], weights.at[place], weight_sems.at[place]),
            pltpu.make_async_copy(values_hbm.at[used[number]], values.at[place], value_sems.at[place]),
        )

    def fetch(number):
        @pl.when(number < n_used)
        def _():
            for copy in fetches(number):
                copy.start()

    for number in range(depth):
        fetch(jnp.int32(number))
    weight_sum[...] = sum_in[...]
    highest[...] = high_in[...]
    last_marks[...] = jnp.zeros_like(last_marks)

    def one_score(block, carry):
        pltpu.make_async_copy(blocks.at[block], blocks.at[block], load_sems.at[block]).wait()

        @pl.when(any_token(limit_ref, n_blocks + block, chunk))
        def _():
            load_block(blocks.at[block], keys, block_limits(limit_ref, n_blocks + block, chunk), key_width)

            def note(part, new):
                last_marks[pl.ds(block, 1), part] = new

            score_block(
                keys, queries_ref, last_weights.at[block], note, highest, weight_sum, tile, scale
            )
            last_values[block] = turn_values(keys, latent_width)

        return carry

    lax.fori_loop(0, n_last, one_score, 0)

    def add_block(weight_block, value_block, mark, begin=False):
        for start in range(0, rows, tile):
            part = slice(start, start + tile)
            factor = jnp.exp2(mark[:, part] - highest[:, part]) / weight_sum[:, part]
            added = jnp.dot(
                value_block[...],
                (weight_block[:, part] * factor).astype(jnp.bfloat16),
                preferred_element_type=jnp.float32,
            )
            total[:, part] = added if begin else total[:, part] + added

    add_block(near_weights, near_values, near_mark, begin=True)

    def one_add(number, carry):
        for copy in fetches(number):
            copy.wait()
        place = lax.rem(number, depth)
        add_block(weights.at[place], values.at[place], marks.at[pl.ds(used[number], 1)])
        fetch(number + depth)
        return carry

    lax.fori_loop(0, n_used, one_add, 0)

    def one_last(block, carry):
        @pl.when(any_token(limit_ref, n_blocks + block, chunk))
        def _():
            add_block(last_weights.at[block], last_values.at[block], last_marks.at[pl.ds(block, 1)])

        return carry

    lax.fori_loop(0, n_last, one_last, 0)
    heads, _, value_width = up_ref.shape
    half_len = out_ref.shape[0]
    steps = lax.broadcasted_iota(jnp.int32, (half_len, value_width), 0)
    steps = steps + lax.axis_index("seq") * half_len
    for head in range(heads):
        latent = total[:, head * half_len : (head + 1) * half_len].astype(jnp.bfloat16)
        raised = lax.dot_general(
            latent, up_ref[head], (((0,), (0,)), ((), ())), preferred_element_type=jnp.float32
        )
        out_ref[:, head * value_width : (head + 1) * value_width] = jnp.where(
            steps < live_ref[0], raised, 0.0
        ).astype(jnp.bfloat16)


def finish(n_blocks, limits, queries, state, near_state, sources, live, up_weight, half_len, shape):
    tile, scale, chunk, key_width = shape
    weights, values, marks, weight_sum, highest = state
    width, rows = queries.shape
    _, latent_width, block_keys = values.shape
    _, pairs, pair_width = sources[0].shape
    heads, _, value_width = up_weight.shape
    depth = 4
    n_last = sum(s.shape[0] for s in sources) // chunk
    row = pltpu.VMEM((1, rows), jnp.float32)
    work = (n_blocks // 2 + n_last) * block_keys * rows
    return pl.pallas_call(
        functools.partial(finish_kernel, shape, depth, n_blocks, len(sources)),
        out_shape=jax.ShapeDtypeStruct((half_len, heads * value_width), jnp.bfloat16),
        in_specs=[smem_spec()]
        + [vmem_spec()] * 7
        + [smem_spec(), vmem_spec()]
        + [hbm_spec()] * (2 + len(sources)),
        out_specs=vmem_spec(),
        scratch_shapes=[
            row,
            row,
            pltpu.VMEM((latent_width, rows), jnp.float32),
            pltpu.VMEM((n_last, chunk, pairs, pair_width), jnp.bfloat16),
            pltpu.VMEM((block_keys, width), jnp.bfloat16),
            pltpu.VMEM((n_last, block_keys, rows), jnp.float32),
            pltpu.VMEM((n_last, latent_width, block_keys), jnp.bfloat16),
            pltpu.VMEM((n_last, rows), jnp.float32),
            pltpu.VMEM((depth, block_keys, rows), jnp.float32),
            pltpu.VMEM((depth, latent_width, block_keys), jnp.bfloat16),
            pltpu.SMEM((n_blocks + depth + 1,), jnp.int32),
            pltpu.SemaphoreType.DMA((n_last,)),
            pltpu.SemaphoreType.DMA((depth,)),
            pltpu.SemaphoreType.DMA((depth,)),
        ],
        compiler_params=pltpu.CompilerParams(vmem_limit_bytes=40 * MIB),
        cost_estimate=pl.CostEstimate(
            flops=2 * work * latent_width, bytes_accessed=3 * 10**7, transcendentals=work // 4
        ),
        name="finish",
    )(
        limits, queries, marks, weight_sum, highest, *near_state, live, up_weight,
        weights, values, *sources,
    )


def local(
    queries,
    hidden,
    w_dkv,
    kv_gain,
    w_uk,
    value_up_weight,
    page_pool,
    page_owner,
    page_slot,
    prefix_len,
    suffix_len,
):
    n_head = lax.axis_size("head")
    n_req = lax.axis_size("req")
    n_seq = lax.axis_size("seq")
    head_idx = lax.axis_index("head")
    req_idx = lax.axis_index("req")
    seq_idx = lax.axis_index("seq")
    _, half_len, d_local = hidden.shape
    heads_dev, nope_width, latent_width = w_uk.shape
    lat_width = w_dkv.shape[1]
    rope_width = lat_width - latent_width
    query_width = queries.shape[2] // heads_dev
    page_width = page_pool.shape[1]
    page_len = page_width // lat_width
    pairs = page_len // 2
    pages_req = page_slot.shape[1]
    cap = max(2, 2 * pages_req // (n_head * n_req))
    chunk = n_req * cap // 4
    score_scale = float(query_width) ** (-0.5)

    owner_rows = page_owner[:, :, 0]
    counts, most, my_prefix, live, first, rest, foreign, partial_value = pick_pages(
        owner_rows, page_slot, prefix_len, suffix_len, page_pool, hidden[0], w_dkv.T,
        cap, chunk, n_head, n_req, n_seq, pairs,
    )
    swap_route = [(i, n_seq - 1 - i) for i in range(n_seq)]
    stream_route = []
    for i in range(n_head - 1):
        stream_route.append((i * n_seq, (i + 1) * n_seq))
        stream_route.append(((i + 1) * n_seq + 1, i * n_seq + 1))

    def swap(block):
        return lax.ppermute(block, "seq", swap_route)

    def stream(block):
        return lax.ppermute(block, ("head", "seq"), stream_route)

    positions = my_prefix + seq_idx * half_len + jnp.arange(half_len, dtype=jnp.int32)
    rows = heads_dev * half_len
    half_rope = rope_width // 2
    frequency = 10000.0 ** (-2.0 * jnp.arange(half_rope, dtype=jnp.float32) / rope_width)
    phases = frequency[:, None] * positions.astype(jnp.float32)[None, :]
    q_turned = turn_queries(queries[0], w_uk, jnp.cos(phases), jnp.sin(phases), lat_width + 64)

    arrived = [
        lax.ppermute(foreign[s - 1], "req", [(i, (i + s) % n_req) for i in range(n_req)])
        for s in range(1, n_req)
    ]
    early_steps = [stream(first)]
    share = half_len // n_head
    partial_value, q_turned = lax.optimization_barrier((partial_value, q_turned))
    partials = lax.all_to_all(partial_value, "head", split_axis=0, concat_axis=0, tiled=True)
    for step in range(1, n_head - 1):
        early_steps.append(stream(early_steps[-1]))
    early_steps = [[block, None] for block in early_steps]
    for step in range(n_head - 2):
        early_steps[step][1] = swap(early_steps[step][0])
    mine = arrived[0][None] if n_req == 2 else jnp.stack(arrived)
    other = swap(mine)
    middle, late = join_pages(counts, rest, mine, other, chunk, cap, (2 * chunk, chunk))
    middle, partials = lax.optimization_barrier((middle, partials))
    summed = jnp.sum(partials.reshape(n_head, share, lat_width), axis=0)
    share_t = seq_idx * half_len + head_idx * share + jnp.arange(share, dtype=jnp.int32)
    latent = finish_latent(summed, my_prefix + share_t, share_t < live, kv_gain, latent_width)

    tile = 256 if rows % 256 == 0 and 256 % half_len == 0 else half_len
    shape = (tile, score_scale * math.log2(math.e), chunk, lat_width)
    last = n_head - 2
    near_state = ()
    extra = 4 + 1 + 2 * last
    total = 1 + 2 * (last + 1) + 2 + 4 * last + extra
    firsts = {"early": [0], "middle": [chunk, 2 * chunk], "late": [3 * chunk]}
    pieces = []

    def piece(name, origin):
        pieces.extend((place, origin) for place in firsts[name])

    def step_pieces(name, step):
        piece(name, 2 * step + 1)
        piece(name, 2 * step + 2)

    piece("early", 0)
    for step in range(last + 1):
        step_pieces("early", step)
    piece("middle", 0)
    for step in range(last + 1):
        step_pieces("middle", step)
    piece("late", 0)
    for step in range(last + 1):
        step_pieces("late", step)
    limits = plan_blocks(
        owner_rows, prefix_len, tuple(pieces), n_head, n_req, chunk, page_len
    )
    n_blocks = 0
    state = None

    def arrays_of(arrived_steps, steps):
        return [arrived_steps[step][side] for step in steps for side in range(2)]

    def score(arrays, near=None):
        nonlocal n_blocks, state, near_state
        result = score_part(
            n_blocks, total, limits, q_turned, arrays, state, shape, latent_width, near
        )
        state = result[:5]
        near_state = result[5:] or near_state
        n_blocks += sum(a.shape[0] for a in arrays) // chunk

    def tie(block):
        nonlocal state
        block, mark = lax.optimization_barrier((block, state[4]))
        state = (*state[:4], mark)
        return block

    middle, early_steps[last - 1][0] = lax.optimization_barrier((middle, early_steps[last - 1][0]))
    middle_steps = []
    block = stream(middle)
    for step in range(last + 1):
        received = block
        if step == 0:
            score([first] + arrays_of(early_steps, range(last)))
        elif step == 1:
            score(arrays_of(early_steps, [last]) + [middle] + arrays_of(middle_steps, [0]))
        else:
            score(
                arrays_of(middle_steps, [step - 1]), (live, suffix_latent) if step == last else None
            )
        received = tie(received)
        if step == 0:
            early_steps[last][0] = tie(early_steps[last][0])
            early_steps[last][1] = swap(early_steps[last][0])
            most = over_groups(most)
            received, most, latent = lax.optimization_barrier((received, most, latent))
            copies = jnp.concatenate([latent] * n_head, axis=0)
            fresh = lax.all_to_all(copies, "head", split_axis=0, concat_axis=0, tiled=True)
            opposite = swap(fresh)
            suffix_latent = jnp.where(
                seq_idx == 0,
                jnp.concatenate([fresh, opposite], axis=0),
                jnp.concatenate([opposite, fresh], axis=0),
            )
        if step < last:
            block = stream(received)
        middle_steps.append([received, swap(received)])

    last_arrays = arrays_of(middle_steps, [last])

    def end(blocks, final_arrays, current):
        return finish(
            blocks, limits, q_turned, current, near_state, final_arrays, live, value_up_weight, half_len, shape
        )

    def with_late(_):
        block = stream(late)
        arrays = last_arrays + [late]
        current, blocks = state, n_blocks
        for step in range(last + 1):
            received = block
            current = score_part(
                blocks, total, limits, q_turned, arrays, current, shape, latent_width
            )[:5]
            blocks += sum(a.shape[0] for a in arrays) // chunk
            received, mark = lax.optimization_barrier((received, current[4]))
            current = (*current[:4], mark)
            if step < last:
                block = stream(received)
            arrays = [received, swap(received)]
        return end(blocks, arrays, current)

    def without_late(_):
        return end(n_blocks, last_arrays, state)

    attn_out = lax.cond(most > 2 * chunk, with_late, without_late, 0)
    new_pages = fresh.reshape(1, half_len // page_len, page_len * lat_width)
    return (attn_out[None], new_pages)


def solution(mesh):
    placed = (
        P(("groups", "req"), "seq", "head"),
        P(("groups", "req"), "seq", "head"),
        P("head", None),
        P(),
        P("head", None, None),
        P("head", None, None),
        P(("groups", "head", "req"), None),
        P("groups", None, None),
        P("groups", None),
        P("groups"),
        P("groups"),
    )
    return jax.shard_map(
        local,
        mesh=mesh,
        in_specs=placed,
        out_specs=(P(("groups", "req"), "seq", "head"), P(("groups", "req"), "seq", None)),
        check_vma=False,
    )
```

```python
import functools
import math

import jax
import jax.numpy as jnp
from jax import lax
from jax.experimental import pallas as pl
from jax.experimental.pallas import tpu as pltpu
from jax.sharding import PartitionSpec as P

LOWEST = -1e30
MASKED = -1e38
MIB = 1024 * 1024


def rotate(vector, cosine_table, sine_table):
    half_width = vector.shape[-1] // 2
    first_half = vector[..., :half_width]
    second_half = vector[..., half_width:]
    return jnp.concatenate(
        [
            first_half * cosine_table - second_half * sine_table,
            first_half * sine_table + second_half * cosine_table,
        ],
        axis=-1,
    )


def angles(positions, rope_width):
    half_width = rope_width // 2
    frequency = 10000.0 ** (-2.0 * jnp.arange(half_width, dtype=jnp.float32) / rope_width)
    phases = positions.astype(jnp.float32)[:, None] * frequency[None, :]
    return (jnp.cos(phases), jnp.sin(phases))


def finish_latent(summed, positions, live_rows, kv_gain, latent_width):
    latent_part = summed[:, :latent_width]
    mean_square = jnp.mean(latent_part * latent_part, axis=-1, keepdims=True)
    normed = latent_part * lax.rsqrt(mean_square + 1e-06) * kv_gain
    cosine_table, sine_table = angles(positions, summed.shape[1] - latent_width)
    rotated = rotate(summed[:, latent_width:], cosine_table, sine_table)
    joined = jnp.concatenate([normed, rotated], axis=-1).astype(jnp.bfloat16)
    return jnp.where(live_rows[:, None], joined, jnp.zeros_like(joined))


def any_spec():
    return pl.BlockSpec(memory_space=pl.ANY)


def smem_spec():
    return pl.BlockSpec(memory_space=pltpu.SMEM)


def vmem_spec():
    return pl.BlockSpec(memory_space=pltpu.VMEM)


def hbm_spec():
    return pl.BlockSpec(memory_space=pltpu.HBM)


def pick_kernel(
    cap, page_len, owner_hbm, slot_hbm, prefix_hbm, suffix_hbm, pool_hbm, hidden_hbm, down_hbm, count_ref,
    most_ref, length_ref, live_ref, first_ref, rest_ref, foreign_ref, partial_ref, owner_ref, slot_ref,
    prefix_ref, suffix_ref, pool_ref, hidden_ref, down_ref, pages, lists, table, sems,
):
    n_req = lax.axis_size("req")
    head_idx = lax.axis_index("head")
    req_idx = lax.axis_index("req")
    seq_idx = lax.axis_index("seq")
    n_pages = owner_ref.shape[1]
    pool_pages, pairs, pair_width = pages.shape
    chunk = first_ref.shape[0]
    loads = [
        pltpu.make_async_copy(owner_hbm, owner_ref, sems.at[0]),
        pltpu.make_async_copy(slot_hbm, slot_ref, sems.at[1]),
        pltpu.make_async_copy(pool_hbm, pool_ref, sems.at[2]),
        pltpu.make_async_copy(hidden_hbm, hidden_ref, sems.at[6]),
        pltpu.make_async_copy(down_hbm, down_ref, sems.at[7]),
        pltpu.make_async_copy(prefix_hbm, prefix_ref, sems.at[8]),
        pltpu.make_async_copy(suffix_hbm, suffix_ref, sems.at[9]),
    ]
    for load in loads:
        load.start()
    loads[0].wait()
    loads[1].wait()
    loads[5].wait()
    loads[6].wait()
    length_ref[0] = prefix_ref[req_idx]
    live_ref[0] = suffix_ref[req_idx]
    self_owner = head_idx * n_req + req_idx
    n_owners = table.shape[1]
    for shift in range(n_req):
        for owner in range(n_owners):
            table[shift, owner] = 0
    founds = []
    most = jnp.int32(0)
    for shift in range(n_req):
        request = lax.rem(req_idx + shift, n_req)

        def note(page, found, shift=shift, request=request):
            owner = owner_ref[request, page]
            needed = page * page_len < prefix_ref[request]
            table[shift, owner] += needed.astype(jnp.int32)
            lists[shift, found] = slot_ref[request, page]
            return found + (needed & (owner == self_owner)).astype(jnp.int32)

        founds.append(lax.fori_loop(0, n_pages, note, jnp.int32(0), unroll=8))
        for place in range(n_owners // n_req):
            held = functools.reduce(jnp.add, [table[shift, place * n_req + i] for i in range(n_req)])
            early = jnp.minimum(table[shift, place * n_req + request], chunk)
            most = jnp.maximum(most, held - early)
    for shift in range(n_req):
        count_ref[shift] = table[0, head_idx * n_req + lax.rem(req_idx + n_req - shift, n_req)]
    most_ref[0] = most
    loads[2].wait()
    step = 16
    row = lax.broadcasted_iota(jnp.int32, (step * step, step * step), 0)
    column = lax.broadcasted_iota(jnp.int32, (step * step, step * step), 1)
    swap = ((row // step == column % step) & (row % step == column // step)).astype(jnp.bfloat16)
    for page in range(0, pool_pages, step):
        for pair in range(0, pairs, step):
            rows = jnp.concatenate(
                [
                    pool_ref[page : page + step, (pair + i) * pair_width : (pair + i + 1) * pair_width]
                    for i in range(step)
                ],
                axis=0,
            )
            turned = jnp.dot(swap, rows, preferred_element_type=jnp.float32).astype(jnp.bfloat16)
            pages[page : page + step, pair : pair + step, :] = turned.reshape(step, step, pair_width)

    def send(shift, rank, target, sem):
        slot = jnp.where(rank < founds[shift], lists[shift, rank], 0)
        pltpu.make_async_copy(pages.at[slot], target, sem).start()

    for rank in range(cap):
        if rank < chunk:
            send(0, rank, first_ref.at[rank], sems.at[3])
        else:
            send(0, rank, rest_ref.at[rank - chunk], sems.at[4])
    half_cap = foreign_ref.shape[1]
    for shift in range(1, n_req):
        for j in range(half_cap):
            send(shift, seq_idx * half_cap + j, foreign_ref.at[shift - 1, j], sems.at[5])
    loads[3].wait()
    loads[4].wait()
    partial_ref[...] = lax.dot_general(
        hidden_ref[...], down_ref[...], (((1,), (1,)), ((), ())), preferred_element_type=jnp.float32
    )
    pltpu.make_async_copy(first_ref, first_ref, sems.at[3]).wait()
    if cap > chunk:
        pltpu.make_async_copy(rest_ref, rest_ref, sems.at[4]).wait()
    pltpu.make_async_copy(foreign_ref, foreign_ref, sems.at[5]).wait()


def pick_pages(
    page_owner, page_slot, prefix_len, suffix_len, page_pool, hidden, down,
    cap, chunk, n_head, n_req, n_seq, pairs,
):
    pool_pages, page_width = page_pool.shape
    page = (pairs, page_width // pairs)
    return pl.pallas_call(
        functools.partial(pick_kernel, cap, 2 * pairs),
        out_shape=(
            jax.ShapeDtypeStruct((n_req,), jnp.int32),
            jax.ShapeDtypeStruct((1,), jnp.int32),
            jax.ShapeDtypeStruct((1,), jnp.int32),
            jax.ShapeDtypeStruct((1,), jnp.int32),
            jax.ShapeDtypeStruct((chunk, *page), jnp.bfloat16),
            jax.ShapeDtypeStruct((max(1, cap - chunk), *page), jnp.bfloat16),
            jax.ShapeDtypeStruct((n_req - 1, cap // n_seq, *page), jnp.bfloat16),
            jax.ShapeDtypeStruct((hidden.shape[0], down.shape[0]), jnp.float32),
        ),
        in_specs=[any_spec()] * 4 + [hbm_spec()] * 3,
        out_specs=(smem_spec(), smem_spec(), smem_spec(), smem_spec(), hbm_spec(), hbm_spec(), hbm_spec(), vmem_spec()),
        scratch_shapes=[
            pltpu.SMEM(page_owner.shape, jnp.int32),
            pltpu.SMEM(page_slot.shape, jnp.int32),
            pltpu.SMEM(prefix_len.shape, jnp.int32),
            pltpu.SMEM(suffix_len.shape, jnp.int32),
            pltpu.VMEM((pool_pages, page_width), jnp.bfloat16),
            pltpu.VMEM(hidden.shape, jnp.bfloat16),
            pltpu.VMEM(down.shape, jnp.bfloat16),
            pltpu.VMEM((pool_pages, *page), jnp.bfloat16),
            pltpu.SMEM((n_req, cap + 1), jnp.int32),
            pltpu.SMEM((n_req, n_head * n_req), jnp.int32),
            pltpu.SemaphoreType.DMA((10,)),
        ],
        compiler_params=pltpu.CompilerParams(vmem_limit_bytes=60 * MIB),
        cost_estimate=pl.CostEstimate(flops=10**9, bytes_accessed=6 * 10**6, transcendentals=0),
        name="pick_pages",
    )(page_owner, page_slot, prefix_len, suffix_len, page_pool, hidden, down)


def join_kernel(chunk, cap, count_ref, rest_ref, mine_ref, other_ref, *refs):
    n_req = count_ref.shape[0]
    targets, sems = refs[:-1], refs[-1]
    seq_idx = lax.axis_index("seq")
    half_cap = mine_ref.shape[1]
    excess = jnp.maximum(count_ref[0] - chunk, 0)
    j = 0
    for part, target in enumerate(targets):
        for place in range(target.shape[0]):

            def fetch(condition, source, target=target, place=place, part=part):
                @pl.when(condition)
                def _():
                    pltpu.make_async_copy(source, target.at[place], sems.at[part]).start()

            rank = jnp.int32(j)
            taken = rank < excess
            if cap > chunk:
                fetch(taken, rest_ref.at[jnp.minimum(rank, cap - chunk - 1)])
            rank = rank - excess
            for shift in range(1, n_req):
                here = jnp.logical_not(taken) & (rank < count_ref[shift])
                half = rank // half_cap
                slot = jnp.clip(rank - half * half_cap, 0, half_cap - 1)
                fetch(here & (half == seq_idx), mine_ref.at[shift - 1, slot])
                fetch(here & (half != seq_idx), other_ref.at[shift - 1, slot])
                taken = taken | here
                rank = rank - count_ref[shift]
            fetch(jnp.logical_not(taken), mine_ref.at[0, 0])
            j += 1
    for part, target in enumerate(targets):
        pltpu.make_async_copy(target, target, sems.at[part]).wait()


def join_pages(counts, rest, mine, other, chunk, cap, sizes):
    return pl.pallas_call(
        functools.partial(join_kernel, chunk, cap),
        out_shape=tuple(jax.ShapeDtypeStruct((size, *rest.shape[1:]), jnp.bfloat16) for size in sizes),
        in_specs=[smem_spec()] + [hbm_spec()] * 3,
        out_specs=(vmem_spec(),) * len(sizes),
        scratch_shapes=[pltpu.SemaphoreType.DMA((len(sizes),))],
        compiler_params=pltpu.CompilerParams(vmem_limit_bytes=10 * MIB),
        cost_estimate=pl.CostEstimate(flops=0, bytes_accessed=3 * 10**6, transcendentals=0),
        name="join_pages",
    )(counts, rest, mine, other)


def plan_kernel(pieces, page_len, chunk, owner_ref, prefix_ref, limit_ref, places, counts, running):
    n_req = lax.axis_size("req")
    head_idx = lax.axis_index("head")
    req_idx = lax.axis_index("req")
    n_head, width = places.shape
    n_pages = owner_ref.shape[1]
    prefix = prefix_ref[req_idx]
    for place in range(n_head):
        for shift in range(n_req):
            counts[place, shift] = 0
            running[place, shift] = 0
        for slot in range(width):
            places[place, slot] = 0

    def where_from(page):
        owner = owner_ref[req_idx, page]
        place = owner // n_req
        shift = lax.rem(req_idx + n_req - (owner - place * n_req), n_req)
        return place, shift, (page * page_len < prefix).astype(jnp.int32)

    def count(page, carry):
        place, shift, needed = where_from(page)
        counts[place, shift] += needed
        return carry

    def note(page, carry):
        place, shift, needed = where_from(page)
        rank = running[place, shift]
        running[place, shift] = rank + needed
        for earlier in range(n_req - 1):
            rank = rank + jnp.where(earlier < shift, counts[place, earlier], 0)
        early = (shift == 0) & (rank < chunk)
        slot = jnp.where(early, rank, chunk + rank - jnp.minimum(counts[place, 0], chunk))
        slot = jnp.where(needed > 0, slot, width - 1)
        places[place, slot] = jnp.clip(prefix - page * page_len, 0, page_len)
        return carry

    lax.fori_loop(0, n_pages, count, 0, unroll=4)
    lax.fori_loop(0, n_pages, note, 0, unroll=4)
    upward = 2 * lax.axis_index("seq") - 1
    for block, (first, origin) in enumerate(pieces):
        step, side = (origin + 1) // 2, 2 * (origin % 2) - 1
        place = head_idx + upward * side * step
        inside = (place >= 0) & (place < n_head)
        place = jnp.clip(place, 0, n_head - 1)
        for j in range(chunk):
            limit_ref[block * chunk + j] = jnp.where(inside, places[place, first + j], 0)


def plan_blocks(page_owner, prefix_len, pieces, n_head, n_req, chunk, page_len):
    return pl.pallas_call(
        functools.partial(plan_kernel, pieces, page_len, chunk),
        out_shape=jax.ShapeDtypeStruct((len(pieces) * chunk,), jnp.int32),
        in_specs=[smem_spec()] * 2,
        out_specs=smem_spec(),
        scratch_shapes=[
            pltpu.SMEM((n_head, 4 * chunk + 1), jnp.int32),
            pltpu.SMEM((n_head, n_req), jnp.int32),
            pltpu.SMEM((n_head, n_req), jnp.int32),
        ],
        cost_estimate=pl.CostEstimate(flops=10**4, bytes_accessed=10**4, transcendentals=0),
        name="plan_blocks",
    )(page_owner, prefix_len)


def over_groups(most):
    n_groups = lax.axis_size("groups")
    passed = most
    for _ in range(n_groups - 1):
        passed = lax.ppermute(passed, "groups", [(i, (i + 1) % n_groups) for i in range(n_groups)])
        most = jnp.maximum(most, passed)
    return most[0]


def query_kernel(query_hbm, up_hbm, cosine_ref, sine_ref, out_ref, query_ref, up_ref, sems):
    loads = [
        pltpu.make_async_copy(query_hbm, query_ref, sems.at[0]),
        pltpu.make_async_copy(up_hbm, up_ref, sems.at[1]),
    ]
    for load in loads:
        load.start()
    for load in loads:
        load.wait()
    heads, nope_width, latent_width = up_ref.shape
    half_len, width = query_ref.shape
    query_width = width // heads
    half_rope = cosine_ref.shape[0]
    key_width = latent_width + 2 * half_rope
    for head in range(heads):
        part = slice(head * half_len, (head + 1) * half_len)
        both = query_ref[:, head * query_width : (head + 1) * query_width]
        latent = lax.dot_general(
            up_ref[head], both[:, :nope_width], (((0,), (1,)), ((), ())), preferred_element_type=jnp.float32
        )
        out_ref[:latent_width, part] = latent.astype(jnp.bfloat16)
        turned = both[:, nope_width:].astype(jnp.float32).T
        low, high = turned[:half_rope], turned[half_rope:]
        out_ref[latent_width : latent_width + half_rope, part] = (
            low * cosine_ref[...] - high * sine_ref[...]
        ).astype(jnp.bfloat16)
        out_ref[latent_width + half_rope : key_width, part] = (
            low * sine_ref[...] + high * cosine_ref[...]
        ).astype(jnp.bfloat16)
    rest = out_ref.shape[0] - key_width
    row = lax.broadcasted_iota(jnp.int32, (rest, out_ref.shape[1]), 0)
    out_ref[key_width:, :] = (row == 0).astype(jnp.bfloat16)


def turn_queries(queries, w_uk, cosine_table, sine_table, key_rows):
    heads, nope_width, latent_width = w_uk.shape
    rows = heads * queries.shape[0]
    return pl.pallas_call(
        query_kernel,
        out_shape=jax.ShapeDtypeStruct((key_rows, rows), jnp.bfloat16),
        in_specs=[any_spec()] * 2 + [vmem_spec()] * 2,
        out_specs=vmem_spec(),
        scratch_shapes=[
            pltpu.VMEM(queries.shape, jnp.bfloat16),
            pltpu.VMEM(w_uk.shape, jnp.bfloat16),
            pltpu.SemaphoreType.DMA((2,)),
        ],
        compiler_params=pltpu.CompilerParams(vmem_limit_bytes=60 * MIB),
        cost_estimate=pl.CostEstimate(
            flops=2 * rows * nope_width * latent_width, bytes_accessed=3 * 10**6, transcendentals=0
        ),
        name="turn_queries",
    )(queries, w_uk, cosine_table, sine_table)


def score_block(keys, queries_ref, target, note, highest, weight_sum, tile, scale, bias=None):
    rows = queries_ref.shape[1]
    for start in range(0, rows, tile):
        part = slice(start, start + tile)
        scores = jnp.dot(keys[...], queries_ref[:, part], preferred_element_type=jnp.float32) * scale
        if bias is not None:
            scores = scores + bias
        old = highest[:, part]
        new = jnp.maximum(old, jnp.max(scores, axis=0, keepdims=True))
        weights = jnp.exp2(scores - new)
        highest[:, part] = new
        weight_sum[:, part] = weight_sum[:, part] * jnp.exp2(old - new) + jnp.sum(
            weights, axis=0, keepdims=True
        )
        target[:, part] = weights
        note(part, new)


def block_limits(limit_ref, block, chunk):
    return [limit_ref[block * chunk + j] for j in range(chunk)]


def any_token(limit_ref, block, chunk):
    return functools.reduce(jnp.maximum, block_limits(limit_ref, block, chunk)) > 0


def load_block(block_ref, keys, limits, key_width):
    chunk, pairs, pair_width = block_ref.shape
    pair_rows = chunk * pairs
    page_rows = block_ref[...].reshape(pair_rows, pair_width)
    keys[:pair_rows, :key_width] = page_rows[:, :key_width]
    keys[pair_rows:, :key_width] = page_rows[:, key_width:]
    shape = (2 * pair_rows, keys.shape[1] - key_width)
    row = lax.broadcasted_iota(jnp.int32, shape, 0)
    pair_row = lax.rem(row, pair_rows)
    token = 2 * lax.rem(pair_row, pairs) + row // pair_rows
    limit = jnp.zeros_like(row)
    for j, value in enumerate(limits):
        limit = jnp.where(pair_row // pairs == j, value, limit)
    masked = (lax.broadcasted_iota(jnp.int32, shape, 1) == 0) & (token >= limit)
    keys[:, key_width:] = jnp.where(masked, MASKED, 0.0).astype(jnp.bfloat16)


def turn_values(keys, latent_width):
    return keys[:, :latent_width].T


def near_bias(n_keys, half_len, tile, live):
    seq_idx = lax.axis_index("seq")
    place = lax.broadcasted_iota(jnp.int32, (n_keys, tile), 0)
    query = lax.rem(lax.broadcasted_iota(jnp.int32, (n_keys, tile), 1), half_len) + seq_idx * half_len
    allowed = (place <= query) & (place < live)
    return jnp.where(allowed, 0.0, -jnp.inf)


def score_kernel(shape, base, n_sources, first, near, limit_ref, queries_ref, *refs):
    tile, scale, chunk, key_width = shape
    refs = list(refs)
    if not first:
        marks_in, sum_in, high_in = [refs.pop(0) for _ in range(3)]
        refs.pop(0), refs.pop(0)
    if near:
        live_ref, suffix_ref = refs.pop(0), refs.pop(0)
    sources = [refs.pop(0) for _ in range(n_sources)]
    weights_hbm, values_hbm, marks, weight_sum, highest = [refs.pop(0) for _ in range(5)]
    if near:
        near_weights, near_values, near_mark = [refs.pop(0) for _ in range(3)]
    blocks, keys, weights, values, load_sems, weight_sems, value_sems = [refs.pop(0) for _ in range(7)]
    n_blocks = blocks.shape[0]
    latent_width = values.shape[1]
    index = 0
    for source in sources:
        for i in range(source.shape[0] // chunk):
            pltpu.make_async_copy(
                source.at[i * chunk : (i + 1) * chunk], blocks.at[index], load_sems.at[index]
            ).start()
            index += 1
    if first:
        marks[...] = jnp.zeros_like(marks)
        weight_sum[...] = jnp.zeros_like(weight_sum)
        highest[...] = jnp.full_like(highest, LOWEST)
    else:
        marks[...] = marks_in[...]
        weight_sum[...] = sum_in[...]
        highest[...] = high_in[...]

    def stores(block):
        return (
            pltpu.make_async_copy(weights.at[block], weights_hbm.at[base + block], weight_sems.at[block]),
            pltpu.make_async_copy(values.at[block], values_hbm.at[base + block], value_sems.at[block]),
        )

    def one_block(block, carry):
        pltpu.make_async_copy(blocks.at[block], blocks.at[block], load_sems.at[block]).wait()

        @pl.when(any_token(limit_ref, base + block, chunk))
        def _():
            load_block(blocks.at[block], keys, block_limits(limit_ref, base + block, chunk), key_width)

            def note(part, new):
                marks[pl.ds(base + block, 1), part] = new

            score_block(
                keys, queries_ref, weights.at[block], note, highest, weight_sum, tile, scale
            )
            values[block] = turn_values(keys, latent_width)
            for copy in stores(block):
                copy.start()

        return carry

    lax.fori_loop(0, n_blocks, one_block, 0)
    if near:
        near_keys = refs.pop(0)
        n_near = suffix_ref.shape[0]
        near_keys[:, key_width:] = jnp.zeros_like(near_keys[:, key_width:])
        near_keys[:, :key_width] = suffix_ref[...]

        def note_near(part, new):
            near_mark[:, part] = new

        score_block(
            near_keys, queries_ref, near_weights, note_near, highest, weight_sum, tile, scale,
            near_bias(n_near, n_near // lax.axis_size("seq"), tile, live_ref[0]),
        )
        near_values[...] = turn_values(near_keys, latent_width)

    def one_wait(block, carry):
        @pl.when(any_token(limit_ref, base + block, chunk))
        def _():
            for copy in stores(block):
                copy.wait()

        return carry

    lax.fori_loop(0, n_blocks, one_wait, 0)


def score_part(base, total, limits, queries, sources, state, shape, latent_width, near=None):
    tile, scale, chunk, key_width = shape
    width, rows = queries.shape
    _, pairs, pair_width = sources[0].shape
    block_keys = 2 * chunk * pairs
    n_blocks = sum(s.shape[0] for s in sources) // chunk
    row = jax.ShapeDtypeStruct((1, rows), jnp.float32)
    out_shape = [
        jax.ShapeDtypeStruct((total, block_keys, rows), jnp.float32),
        jax.ShapeDtypeStruct((total, latent_width, block_keys), jnp.bfloat16),
        jax.ShapeDtypeStruct((total, rows), jnp.float32),
        row,
        row,
    ]
    out_specs = [hbm_spec(), hbm_spec(), vmem_spec(), vmem_spec(), vmem_spec()]
    operands = [limits, queries]
    specs = [smem_spec(), vmem_spec()]
    aliases = {}
    if state is not None:
        operands += [state[2], state[3], state[4], state[0], state[1]]
        specs += [vmem_spec()] * 3 + [hbm_spec()] * 2
        aliases = {5: 0, 6: 1}
    scratch = [
        pltpu.VMEM((n_blocks, chunk, pairs, pair_width), jnp.bfloat16),
        pltpu.VMEM((block_keys, width), jnp.bfloat16),
        pltpu.VMEM((n_blocks, block_keys, rows), jnp.float32),
        pltpu.VMEM((n_blocks, latent_width, block_keys), jnp.bfloat16),
        pltpu.SemaphoreType.DMA((n_blocks,)),
        pltpu.SemaphoreType.DMA((n_blocks,)),
        pltpu.SemaphoreType.DMA((n_blocks,)),
    ]
    if near is not None:
        near_keys = near[-1].shape[0]
        operands += list(near)
        specs += [smem_spec(), vmem_spec()]
        out_shape += [
            jax.ShapeDtypeStruct((near_keys, rows), jnp.float32),
            jax.ShapeDtypeStruct((latent_width, near_keys), jnp.bfloat16),
            row,
        ]
        out_specs += [vmem_spec()] * 3
        scratch.append(pltpu.VMEM((near_keys, width), jnp.bfloat16))
    operands += list(sources)
    specs += [hbm_spec()] * len(sources)
    work = n_blocks * block_keys * rows // 2
    return pl.pallas_call(
        functools.partial(score_kernel, shape, base, len(sources), state is None, near is not None),
        out_shape=tuple(out_shape),
        in_specs=specs,
        out_specs=tuple(out_specs),
        scratch_shapes=scratch,
        input_output_aliases=aliases,
        compiler_params=pltpu.CompilerParams(vmem_limit_bytes=40 * MIB),
        cost_estimate=pl.CostEstimate(
            flops=work, bytes_accessed=10**5, transcendentals=0
        ),
        name="score_part",
    )(*operands)


def finish_kernel(
    shape, depth, n_blocks, n_sources, limit_ref, queries_ref, marks, sum_in, high_in,
    near_weights, near_values, near_mark, live_ref, up_ref, weights_hbm, values_hbm, *refs,
):
    tile, scale, chunk, key_width = shape
    sources, refs = refs[:n_sources], refs[n_sources:]
    (
        out_ref, weight_sum, highest, total, blocks, keys, last_weights, last_values, last_marks,
        weights, values, used, load_sems, weight_sems, value_sems,
    ) = refs
    rows = queries_ref.shape[1]
    latent_width = total.shape[0]
    n_last = blocks.shape[0]
    index = 0
    for source in sources:
        for i in range(source.shape[0] // chunk):
            pltpu.make_async_copy(
                source.at[i * chunk : (i + 1) * chunk], blocks.at[index], load_sems.at[index]
            ).start()
            index += 1

    def list_block(block, count):
        used[count] = block
        return count + any_token(limit_ref, block, chunk).astype(jnp.int32)

    n_used = lax.fori_loop(0, n_blocks, list_block, jnp.int32(0))

    def fetches(number):
        place = lax.rem(number, depth)
        return (
            pltpu.make_async_copy(weights_hbm.at[used[number]], weights.at[place], weight_sems.at[place]),
            pltpu.make_async_copy(values_hbm.at[used[number]], values.at[place], value_sems.at[place]),
        )

    def fetch(number):
        @pl.when(number < n_used)
        def _():
            for copy in fetches(number):
                copy.start()

    for number in range(depth):
        fetch(jnp.int32(number))
    weight_sum[...] = sum_in[...]
    highest[...] = high_in[...]
    last_marks[...] = jnp.zeros_like(last_marks)

    def one_score(block, carry):
        pltpu.make_async_copy(blocks.at[block], blocks.at[block], load_sems.at[block]).wait()

        @pl.when(any_token(limit_ref, n_blocks + block, chunk))
        def _():
            load_block(blocks.at[block], keys, block_limits(limit_ref, n_blocks + block, chunk), key_width)

            def note(part, new):
                last_marks[pl.ds(block, 1), part] = new

            score_block(
                keys, queries_ref, last_weights.at[block], note, highest, weight_sum, tile, scale
            )
            last_values[block] = turn_values(keys, latent_width)

        return carry

    lax.fori_loop(0, n_last, one_score, 0)

    def add_block(weight_block, value_block, mark, begin=False):
        for start in range(0, rows, tile):
            part = slice(start, start + tile)
            factor = jnp.exp2(mark[:, part] - highest[:, part]) / weight_sum[:, part]
            added = jnp.dot(
                value_block[...],
                (weight_block[:, part] * factor).astype(jnp.bfloat16),
                preferred_element_type=jnp.float32,
            )
            total[:, part] = added if begin else total[:, part] + added

    add_block(near_weights, near_values, near_mark, begin=True)

    def one_add(number, carry):
        for copy in fetches(number):
            copy.wait()
        place = lax.rem(number, depth)
        add_block(weights.at[place], values.at[place], marks.at[pl.ds(used[number], 1)])
        fetch(number + depth)
        return carry

    lax.fori_loop(0, n_used, one_add, 0)

    def one_last(block, carry):
        @pl.when(any_token(limit_ref, n_blocks + block, chunk))
        def _():
            add_block(last_weights.at[block], last_values.at[block], last_marks.at[pl.ds(block, 1)])

        return carry

    lax.fori_loop(0, n_last, one_last, 0)
    heads, _, value_width = up_ref.shape
    half_len = out_ref.shape[0]
    steps = lax.broadcasted_iota(jnp.int32, (half_len, value_width), 0)
    steps = steps + lax.axis_index("seq") * half_len
    for head in range(heads):
        latent = total[:, head * half_len : (head + 1) * half_len].astype(jnp.bfloat16)
        raised = lax.dot_general(
            latent, up_ref[head], (((0,), (0,)), ((), ())), preferred_element_type=jnp.float32
        )
        out_ref[:, head * value_width : (head + 1) * value_width] = jnp.where(
            steps < live_ref[0], raised, 0.0
        ).astype(jnp.bfloat16)


def finish(n_blocks, limits, queries, state, near_state, sources, live, up_weight, half_len, shape):
    tile, scale, chunk, key_width = shape
    weights, values, marks, weight_sum, highest = state
    width, rows = queries.shape
    _, latent_width, block_keys = values.shape
    _, pairs, pair_width = sources[0].shape
    heads, _, value_width = up_weight.shape
    depth = 4
    n_last = sum(s.shape[0] for s in sources) // chunk
    row = pltpu.VMEM((1, rows), jnp.float32)
    work = (n_blocks // 2 + n_last) * block_keys * rows
    return pl.pallas_call(
        functools.partial(finish_kernel, shape, depth, n_blocks, len(sources)),
        out_shape=jax.ShapeDtypeStruct((half_len, heads * value_width), jnp.bfloat16),
        in_specs=[smem_spec()]
        + [vmem_spec()] * 7
        + [smem_spec(), vmem_spec()]
        + [hbm_spec()] * (2 + len(sources)),
        out_specs=vmem_spec(),
        scratch_shapes=[
            row,
            row,
            pltpu.VMEM((latent_width, rows), jnp.float32),
            pltpu.VMEM((n_last, chunk, pairs, pair_width), jnp.bfloat16),
            pltpu.VMEM((block_keys, width), jnp.bfloat16),
            pltpu.VMEM((n_last, block_keys, rows), jnp.float32),
            pltpu.VMEM((n_last, latent_width, block_keys), jnp.bfloat16),
            pltpu.VMEM((n_last, rows), jnp.float32),
            pltpu.VMEM((depth, block_keys, rows), jnp.float32),
            pltpu.VMEM((depth, latent_width, block_keys), jnp.bfloat16),
            pltpu.SMEM((n_blocks + depth + 1,), jnp.int32),
            pltpu.SemaphoreType.DMA((n_last,)),
            pltpu.SemaphoreType.DMA((depth,)),
            pltpu.SemaphoreType.DMA((depth,)),
        ],
        compiler_params=pltpu.CompilerParams(vmem_limit_bytes=40 * MIB),
        cost_estimate=pl.CostEstimate(
            flops=2 * work * latent_width, bytes_accessed=3 * 10**7, transcendentals=work // 4
        ),
        name="finish",
    )(
        limits, queries, marks, weight_sum, highest, *near_state, live, up_weight,
        weights, values, *sources,
    )


def local(
    queries,
    hidden,
    w_dkv,
    kv_gain,
    w_uk,
    value_up_weight,
    page_pool,
    page_owner,
    page_slot,
    prefix_len,
    suffix_len,
):
    n_head = lax.axis_size("head")
    n_req = lax.axis_size("req")
    n_seq = lax.axis_size("seq")
    head_idx = lax.axis_index("head")
    req_idx = lax.axis_index("req")
    seq_idx = lax.axis_index("seq")
    _, half_len, d_local = hidden.shape
    heads_dev, nope_width, latent_width = w_uk.shape
    lat_width = w_dkv.shape[1]
    rope_width = lat_width - latent_width
    query_width = queries.shape[2] // heads_dev
    page_width = page_pool.shape[1]
    page_len = page_width // lat_width
    pairs = page_len // 2
    pages_req = page_slot.shape[1]
    cap = max(2, 2 * pages_req // (n_head * n_req))
    chunk = n_req * cap // 4
    score_scale = float(query_width) ** (-0.5)

    owner_rows = page_owner[:, :, 0]
    counts, most, my_prefix, live, first, rest, foreign, partial_value = pick_pages(
        owner_rows, page_slot, prefix_len, suffix_len, page_pool, hidden[0], w_dkv.T,
        cap, chunk, n_head, n_req, n_seq, pairs,
    )
    swap_route = [(i, n_seq - 1 - i) for i in range(n_seq)]
    stream_route = []
    for i in range(n_head - 1):
        stream_route.append((i * n_seq, (i + 1) * n_seq))
        stream_route.append(((i + 1) * n_seq + 1, i * n_seq + 1))

    def swap(block):
        return lax.ppermute(block, "seq", swap_route)

    def stream(block):
        return lax.ppermute(block, ("head", "seq"), stream_route)

    positions = my_prefix + seq_idx * half_len + jnp.arange(half_len, dtype=jnp.int32)
    rows = heads_dev * half_len
    half_rope = rope_width // 2
    frequency = 10000.0 ** (-2.0 * jnp.arange(half_rope, dtype=jnp.float32) / rope_width)
    phases = frequency[:, None] * positions.astype(jnp.float32)[None, :]
    q_turned = turn_queries(queries[0], w_uk, jnp.cos(phases), jnp.sin(phases), lat_width + 64)

    arrived = [
        lax.ppermute(foreign[s - 1], "req", [(i, (i + s) % n_req) for i in range(n_req)])
        for s in range(1, n_req)
    ]
    early_steps = [stream(first)]
    share = half_len // n_head
    partial_value, q_turned = lax.optimization_barrier((partial_value, q_turned))
    partials = lax.all_to_all(partial_value, "head", split_axis=0, concat_axis=0, tiled=True)
    mine = arrived[0][None] if n_req == 2 else jnp.stack(arrived)
    other = swap(mine)
    middle, late = join_pages(counts, rest, mine, other, chunk, cap, (2 * chunk, chunk))
    partials, early_steps[0] = lax.optimization_barrier((partials, early_steps[0]))
    for step in range(1, n_head - 1):
        early_steps.append(stream(early_steps[-1]))
    early_steps = [[block, None] for block in early_steps]
    for step in range(n_head - 2):
        early_steps[step][1] = swap(early_steps[step][0])
    summed = jnp.sum(partials.reshape(n_head, share, lat_width), axis=0)
    share_t = seq_idx * half_len + head_idx * share + jnp.arange(share, dtype=jnp.int32)
    latent = finish_latent(summed, my_prefix + share_t, share_t < live, kv_gain, latent_width)
    copies = jnp.concatenate([latent] * n_head, axis=0)
    fresh = lax.all_to_all(copies, "head", split_axis=0, concat_axis=0, tiled=True)
    middle, fresh, most = lax.optimization_barrier((middle, fresh, most))

    tile = 256 if rows % 256 == 0 and 256 % half_len == 0 else half_len
    shape = (tile, score_scale * math.log2(math.e), chunk, lat_width)
    last = n_head - 2
    near_state = ()
    extra = 4 + 1 + 2 * last
    total = 1 + 2 * (last + 1) + 2 + 4 * last + extra
    firsts = {"early": [0], "middle": [chunk, 2 * chunk], "late": [3 * chunk]}
    pieces = []

    def piece(name, origin):
        pieces.extend((place, origin) for place in firsts[name])

    def step_pieces(name, step):
        piece(name, 2 * step + 1)
        piece(name, 2 * step + 2)

    piece("early", 0)
    for step in range(last + 1):
        step_pieces("early", step)
    piece("middle", 0)
    for step in range(last + 1):
        step_pieces("middle", step)
    piece("late", 0)
    for step in range(last + 1):
        step_pieces("late", step)
    limits = plan_blocks(
        owner_rows, prefix_len, tuple(pieces), n_head, n_req, chunk, page_len
    )
    n_blocks = 0
    state = None

    def arrays_of(arrived_steps, steps):
        return [arrived_steps[step][side] for step in steps for side in range(2)]

    def score(arrays, near=None):
        nonlocal n_blocks, state, near_state
        result = score_part(
            n_blocks, total, limits, q_turned, arrays, state, shape, latent_width, near
        )
        state = result[:5]
        near_state = result[5:] or near_state
        n_blocks += sum(a.shape[0] for a in arrays) // chunk

    def tie(block):
        nonlocal state
        block, mark = lax.optimization_barrier((block, state[4]))
        state = (*state[:4], mark)
        return block

    middle_steps = []
    block = stream(middle)
    for step in range(last + 1):
        received = block
        if step == 0:
            score([first] + arrays_of(early_steps, range(last)))
        elif step == 1:
            score(arrays_of(early_steps, [last]) + [middle] + arrays_of(middle_steps, [0]))
        else:
            score(
                arrays_of(middle_steps, [step - 1]), (live, suffix_latent) if step == last else None
            )
        received = tie(received)
        if step == 0:
            early_steps[last][0] = tie(early_steps[last][0])
            early_steps[last][1] = swap(early_steps[last][0])
            most = over_groups(most)
            received, most = lax.optimization_barrier((received, most))
            opposite = swap(fresh)
            suffix_latent = jnp.where(
                seq_idx == 0,
                jnp.concatenate([fresh, opposite], axis=0),
                jnp.concatenate([opposite, fresh], axis=0),
            )
        if step < last:
            block = stream(received)
        middle_steps.append([received, swap(received)])

    last_arrays = arrays_of(middle_steps, [last])

    def end(blocks, final_arrays, current):
        return finish(
            blocks, limits, q_turned, current, near_state, final_arrays, live, value_up_weight, half_len, shape
        )

    def with_late(_):
        block = stream(late)
        arrays = last_arrays + [late]
        current, blocks = state, n_blocks
        for step in range(last + 1):
            received = block
            current = score_part(
                blocks, total, limits, q_turned, arrays, current, shape, latent_width
            )[:5]
            blocks += sum(a.shape[0] for a in arrays) // chunk
            received, mark = lax.optimization_barrier((received, current[4]))
            current = (*current[:4], mark)
            if step < last:
                block = stream(received)
            arrays = [received, swap(received)]
        return end(blocks, arrays, current)

    def without_late(_):
        return end(n_blocks, last_arrays, state)

    attn_out = lax.cond(most > 2 * chunk, with_late, without_late, 0)
    new_pages = fresh.reshape(1, half_len // page_len, page_len * lat_width)
    return (attn_out[None], new_pages)


def solution(mesh):
    placed = (
        P(("groups", "req"), "seq", "head"),
        P(("groups", "req"), "seq", "head"),
        P("head", None),
        P(),
        P("head", None, None),
        P("head", None, None),
        P(("groups", "head", "req"), None),
        P("groups", None, None),
        P("groups", None),
        P("groups"),
        P("groups"),
    )
    return jax.shard_map(
        local,
        mesh=mesh,
        in_specs=placed,
        out_specs=(P(("groups", "req"), "seq", "head"), P(("groups", "req"), "seq", None)),
        check_vma=False,
    )
```

```python
import functools
import math

import jax
import jax.numpy as jnp
from jax import lax
from jax.experimental import pallas as pl
from jax.experimental.pallas import tpu as pltpu
from jax.sharding import PartitionSpec as P

LOWEST = -1e30
MASKED = -1e38
MIB = 1024 * 1024


def rotate(vector, cosine_table, sine_table):
    half_width = vector.shape[-1] // 2
    first_half = vector[..., :half_width]
    second_half = vector[..., half_width:]
    return jnp.concatenate(
        [
            first_half * cosine_table - second_half * sine_table,
            first_half * sine_table + second_half * cosine_table,
        ],
        axis=-1,
    )


def angles(positions, rope_width):
    half_width = rope_width // 2
    frequency = 10000.0 ** (-2.0 * jnp.arange(half_width, dtype=jnp.float32) / rope_width)
    phases = positions.astype(jnp.float32)[:, None] * frequency[None, :]
    return (jnp.cos(phases), jnp.sin(phases))


def finish_latent(summed, positions, live_rows, kv_gain, latent_width):
    latent_part = summed[:, :latent_width]
    mean_square = jnp.mean(latent_part * latent_part, axis=-1, keepdims=True)
    normed = latent_part * lax.rsqrt(mean_square + 1e-06) * kv_gain
    cosine_table, sine_table = angles(positions, summed.shape[1] - latent_width)
    rotated = rotate(summed[:, latent_width:], cosine_table, sine_table)
    joined = jnp.concatenate([normed, rotated], axis=-1).astype(jnp.bfloat16)
    return jnp.where(live_rows[:, None], joined, jnp.zeros_like(joined))


def any_spec():
    return pl.BlockSpec(memory_space=pl.ANY)


def smem_spec():
    return pl.BlockSpec(memory_space=pltpu.SMEM)


def vmem_spec():
    return pl.BlockSpec(memory_space=pltpu.VMEM)


def hbm_spec():
    return pl.BlockSpec(memory_space=pltpu.HBM)


def pick_kernel(
    cap, page_len, owner_hbm, slot_hbm, prefix_hbm, suffix_hbm, pool_hbm, hidden_hbm, down_hbm, count_ref,
    most_ref, length_ref, live_ref, first_ref, rest_ref, foreign_ref, partial_ref, owner_ref, slot_ref,
    prefix_ref, suffix_ref, pool_ref, hidden_ref, down_ref, pages, lists, table, sems,
):
    n_req = lax.axis_size("req")
    head_idx = lax.axis_index("head")
    req_idx = lax.axis_index("req")
    seq_idx = lax.axis_index("seq")
    n_pages = owner_ref.shape[1]
    pool_pages, pairs, pair_width = pages.shape
    chunk = first_ref.shape[0]
    loads = [
        pltpu.make_async_copy(owner_hbm, owner_ref, sems.at[0]),
        pltpu.make_async_copy(slot_hbm, slot_ref, sems.at[1]),
        pltpu.make_async_copy(pool_hbm, pool_ref, sems.at[2]),
        pltpu.make_async_copy(hidden_hbm, hidden_ref, sems.at[6]),
        pltpu.make_async_copy(down_hbm, down_ref, sems.at[7]),
        pltpu.make_async_copy(prefix_hbm, prefix_ref, sems.at[8]),
        pltpu.make_async_copy(suffix_hbm, suffix_ref, sems.at[9]),
    ]
    for load in loads:
        load.start()
    loads[0].wait()
    loads[1].wait()
    loads[5].wait()
    loads[6].wait()
    length_ref[0] = prefix_ref[req_idx]
    live_ref[0] = suffix_ref[req_idx]
    self_owner = head_idx * n_req + req_idx
    n_owners = table.shape[1]
    for shift in range(n_req):
        for owner in range(n_owners):
            table[shift, owner] = 0
    founds = []
    most = jnp.int32(0)
    for shift in range(n_req):
        request = lax.rem(req_idx + shift, n_req)

        def note(page, found, shift=shift, request=request):
            owner = owner_ref[request, page]
            needed = page * page_len < prefix_ref[request]
            table[shift, owner] += needed.astype(jnp.int32)
            lists[shift, found] = slot_ref[request, page]
            return found + (needed & (owner == self_owner)).astype(jnp.int32)

        founds.append(lax.fori_loop(0, n_pages, note, jnp.int32(0), unroll=8))
        for place in range(n_owners // n_req):
            held = functools.reduce(jnp.add, [table[shift, place * n_req + i] for i in range(n_req)])
            early = jnp.minimum(table[shift, place * n_req + request], chunk)
            most = jnp.maximum(most, held - early)
    for shift in range(n_req):
        count_ref[shift] = table[0, head_idx * n_req + lax.rem(req_idx + n_req - shift, n_req)]
    most_ref[0] = most
    loads[2].wait()
    step = 16
    row = lax.broadcasted_iota(jnp.int32, (step * step, step * step), 0)
    column = lax.broadcasted_iota(jnp.int32, (step * step, step * step), 1)
    swap = ((row // step == column % step) & (row % step == column // step)).astype(jnp.bfloat16)
    for page in range(0, pool_pages, step):
        for pair in range(0, pairs, step):
            rows = jnp.concatenate(
                [
                    pool_ref[page : page + step, (pair + i) * pair_width : (pair + i + 1) * pair_width]
                    for i in range(step)
                ],
                axis=0,
            )
            turned = jnp.dot(swap, rows, preferred_element_type=jnp.float32).astype(jnp.bfloat16)
            pages[page : page + step, pair : pair + step, :] = turned.reshape(step, step, pair_width)

    def send(shift, rank, target, sem):
        slot = jnp.where(rank < founds[shift], lists[shift, rank], 0)
        pltpu.make_async_copy(pages.at[slot], target, sem).start()

    for rank in range(cap):
        if rank < chunk:
            send(0, rank, first_ref.at[rank], sems.at[3])
        else:
            send(0, rank, rest_ref.at[rank - chunk], sems.at[4])
    half_cap = foreign_ref.shape[1]
    for shift in range(1, n_req):
        for j in range(half_cap):
            send(shift, seq_idx * half_cap + j, foreign_ref.at[shift - 1, j], sems.at[5])
    loads[3].wait()
    loads[4].wait()
    partial_ref[...] = lax.dot_general(
        hidden_ref[...], down_ref[...], (((1,), (1,)), ((), ())), preferred_element_type=jnp.float32
    )
    pltpu.make_async_copy(first_ref, first_ref, sems.at[3]).wait()
    if cap > chunk:
        pltpu.make_async_copy(rest_ref, rest_ref, sems.at[4]).wait()
    pltpu.make_async_copy(foreign_ref, foreign_ref, sems.at[5]).wait()


def pick_pages(
    page_owner, page_slot, prefix_len, suffix_len, page_pool, hidden, down,
    cap, chunk, n_head, n_req, n_seq, pairs,
):
    pool_pages, page_width = page_pool.shape
    page = (pairs, page_width // pairs)
    return pl.pallas_call(
        functools.partial(pick_kernel, cap, 2 * pairs),
        out_shape=(
            jax.ShapeDtypeStruct((n_req,), jnp.int32),
            jax.ShapeDtypeStruct((1,), jnp.int32),
            jax.ShapeDtypeStruct((1,), jnp.int32),
            jax.ShapeDtypeStruct((1,), jnp.int32),
            jax.ShapeDtypeStruct((chunk, *page), jnp.bfloat16),
            jax.ShapeDtypeStruct((max(1, cap - chunk), *page), jnp.bfloat16),
            jax.ShapeDtypeStruct((n_req - 1, cap // n_seq, *page), jnp.bfloat16),
            jax.ShapeDtypeStruct((hidden.shape[0], down.shape[0]), jnp.float32),
        ),
        in_specs=[any_spec()] * 4 + [hbm_spec()] * 3,
        out_specs=(smem_spec(), smem_spec(), smem_spec(), smem_spec(), hbm_spec(), hbm_spec(), hbm_spec(), vmem_spec()),
        scratch_shapes=[
            pltpu.SMEM(page_owner.shape, jnp.int32),
            pltpu.SMEM(page_slot.shape, jnp.int32),
            pltpu.SMEM(prefix_len.shape, jnp.int32),
            pltpu.SMEM(suffix_len.shape, jnp.int32),
            pltpu.VMEM((pool_pages, page_width), jnp.bfloat16),
            pltpu.VMEM(hidden.shape, jnp.bfloat16),
            pltpu.VMEM(down.shape, jnp.bfloat16),
            pltpu.VMEM((pool_pages, *page), jnp.bfloat16),
            pltpu.SMEM((n_req, cap + 1), jnp.int32),
            pltpu.SMEM((n_req, n_head * n_req), jnp.int32),
            pltpu.SemaphoreType.DMA((10,)),
        ],
        compiler_params=pltpu.CompilerParams(vmem_limit_bytes=60 * MIB),
        cost_estimate=pl.CostEstimate(flops=10**9, bytes_accessed=6 * 10**6, transcendentals=0),
        name="pick_pages",
    )(page_owner, page_slot, prefix_len, suffix_len, page_pool, hidden, down)


def join_kernel(chunk, cap, count_ref, rest_ref, mine_ref, other_ref, *refs):
    n_req = count_ref.shape[0]
    targets, sems = refs[:-1], refs[-1]
    seq_idx = lax.axis_index("seq")
    half_cap = mine_ref.shape[1]
    excess = jnp.maximum(count_ref[0] - chunk, 0)
    j = 0
    for part, target in enumerate(targets):
        for place in range(target.shape[0]):

            def fetch(condition, source, target=target, place=place, part=part):
                @pl.when(condition)
                def _():
                    pltpu.make_async_copy(source, target.at[place], sems.at[part]).start()

            rank = jnp.int32(j)
            taken = rank < excess
            if cap > chunk:
                fetch(taken, rest_ref.at[jnp.minimum(rank, cap - chunk - 1)])
            rank = rank - excess
            for shift in range(1, n_req):
                here = jnp.logical_not(taken) & (rank < count_ref[shift])
                half = rank // half_cap
                slot = jnp.clip(rank - half * half_cap, 0, half_cap - 1)
                fetch(here & (half == seq_idx), mine_ref.at[shift - 1, slot])
                fetch(here & (half != seq_idx), other_ref.at[shift - 1, slot])
                taken = taken | here
                rank = rank - count_ref[shift]
            fetch(jnp.logical_not(taken), mine_ref.at[0, 0])
            j += 1
    for part, target in enumerate(targets):
        pltpu.make_async_copy(target, target, sems.at[part]).wait()


def join_pages(counts, rest, mine, other, chunk, cap, sizes):
    return pl.pallas_call(
        functools.partial(join_kernel, chunk, cap),
        out_shape=tuple(jax.ShapeDtypeStruct((size, *rest.shape[1:]), jnp.bfloat16) for size in sizes),
        in_specs=[smem_spec()] + [hbm_spec()] * 3,
        out_specs=(vmem_spec(),) * len(sizes),
        scratch_shapes=[pltpu.SemaphoreType.DMA((len(sizes),))],
        compiler_params=pltpu.CompilerParams(vmem_limit_bytes=10 * MIB),
        cost_estimate=pl.CostEstimate(flops=0, bytes_accessed=3 * 10**6, transcendentals=0),
        name="join_pages",
    )(counts, rest, mine, other)


def plan_kernel(page_len, chunk, owner_ref, prefix_ref, limit_ref):
    n_head = lax.axis_size("head")
    n_req = lax.axis_size("req")
    head_idx = lax.axis_index("head")
    req_idx = lax.axis_index("req")
    upward = 2 * lax.axis_index("seq") - 1
    n = owner_ref.shape[1]
    prefix = prefix_ref[req_idx]
    diagonal = lax.broadcasted_iota(jnp.int32, (n, n), 0) == lax.broadcasted_iota(jnp.int32, (n, n), 1)

    def column(values):
        return jnp.sum(jnp.where(diagonal, values, 0), axis=1, keepdims=True)

    owner = owner_ref[pl.ds(req_idx, 1), :]
    place = jnp.zeros_like(owner)
    for head in range(1, n_head):
        place = place + (owner >= head * n_req).astype(jnp.int32)
    shift = req_idx - (owner - place * n_req)
    shift = jnp.where(shift < 0, shift + n_req, shift)
    order = lax.broadcasted_iota(jnp.int32, (1, n), 1)
    needed = (order * page_len < prefix).astype(jnp.int32)
    key = shift * n + order
    together = (column(place) == place) & (column(needed) > 0)
    rank = jnp.sum((together & (column(key) < key)).astype(jnp.int32), axis=0, keepdims=True)
    held = jnp.sum((together & (column(shift) == 0)).astype(jnp.int32), axis=0, keepdims=True)
    early = (shift == 0) & (rank < chunk)
    within = jnp.where(early, rank, chunk + rank - jnp.minimum(held, chunk))
    away = place - head_idx
    distance = jnp.abs(away)
    origin = jnp.where(away * upward > 0, 2 * distance - 1, 2 * distance)
    origins = 2 * n_head - 1
    slot = jnp.where(
        within < chunk,
        origin * chunk + within,
        jnp.where(
            within < 3 * chunk,
            (origins + 2 * origin) * chunk + within - chunk,
            (3 * origins + origin) * chunk + within - 3 * chunk,
        ),
    )
    slot = column(jnp.where(needed > 0, slot, -1))
    tokens = column(jnp.clip(prefix - order * page_len, 0, page_len))
    lane = lax.broadcasted_iota(jnp.int32, (n, limit_ref.shape[1]), 1)
    limit_ref[...] = jnp.sum(jnp.where(lane == slot, tokens, 0), axis=0, keepdims=True)


def plan_blocks(page_owner, prefix_len, n_head, chunk, page_len):
    return pl.pallas_call(
        functools.partial(plan_kernel, page_len, chunk),
        out_shape=jax.ShapeDtypeStruct((1, 4 * (2 * n_head - 1) * chunk), jnp.int32),
        in_specs=[vmem_spec(), smem_spec()],
        out_specs=vmem_spec(),
        cost_estimate=pl.CostEstimate(flops=10**4, bytes_accessed=10**4, transcendentals=0),
        name="plan_blocks",
    )(page_owner, prefix_len)


def over_groups(most):
    n_groups = lax.axis_size("groups")
    passed = most
    for _ in range(n_groups - 1):
        passed = lax.ppermute(passed, "groups", [(i, (i + 1) % n_groups) for i in range(n_groups)])
        most = jnp.maximum(most, passed)
    return most[0]


def query_kernel(query_hbm, up_hbm, cosine_ref, sine_ref, out_ref, query_ref, up_ref, sems):
    loads = [
        pltpu.make_async_copy(query_hbm, query_ref, sems.at[0]),
        pltpu.make_async_copy(up_hbm, up_ref, sems.at[1]),
    ]
    for load in loads:
        load.start()
    for load in loads:
        load.wait()
    heads, nope_width, latent_width = up_ref.shape
    half_len, width = query_ref.shape
    query_width = width // heads
    half_rope = cosine_ref.shape[0]
    key_width = latent_width + 2 * half_rope
    for head in range(heads):
        part = slice(head * half_len, (head + 1) * half_len)
        both = query_ref[:, head * query_width : (head + 1) * query_width]
        latent = lax.dot_general(
            up_ref[head], both[:, :nope_width], (((0,), (1,)), ((), ())), preferred_element_type=jnp.float32
        )
        out_ref[:latent_width, part] = latent.astype(jnp.bfloat16)
        turned = both[:, nope_width:].astype(jnp.float32).T
        low, high = turned[:half_rope], turned[half_rope:]
        out_ref[latent_width : latent_width + half_rope, part] = (
            low * cosine_ref[...] - high * sine_ref[...]
        ).astype(jnp.bfloat16)
        out_ref[latent_width + half_rope : key_width, part] = (
            low * sine_ref[...] + high * cosine_ref[...]
        ).astype(jnp.bfloat16)
    rest = out_ref.shape[0] - key_width
    row = lax.broadcasted_iota(jnp.int32, (rest, out_ref.shape[1]), 0)
    out_ref[key_width:, :] = (row == 0).astype(jnp.bfloat16)


def turn_queries(queries, w_uk, cosine_table, sine_table, key_rows):
    heads, nope_width, latent_width = w_uk.shape
    rows = heads * queries.shape[0]
    return pl.pallas_call(
        query_kernel,
        out_shape=jax.ShapeDtypeStruct((key_rows, rows), jnp.bfloat16),
        in_specs=[any_spec()] * 2 + [vmem_spec()] * 2,
        out_specs=vmem_spec(),
        scratch_shapes=[
            pltpu.VMEM(queries.shape, jnp.bfloat16),
            pltpu.VMEM(w_uk.shape, jnp.bfloat16),
            pltpu.SemaphoreType.DMA((2,)),
        ],
        compiler_params=pltpu.CompilerParams(vmem_limit_bytes=60 * MIB),
        cost_estimate=pl.CostEstimate(
            flops=2 * rows * nope_width * latent_width, bytes_accessed=3 * 10**6, transcendentals=0
        ),
        name="turn_queries",
    )(queries, w_uk, cosine_table, sine_table)


def score_block(keys, queries_ref, target, note, highest, weight_sum, tile, scale, bias=None):
    rows = queries_ref.shape[1]
    for start in range(0, rows, tile):
        part = slice(start, start + tile)
        scores = jnp.dot(keys[...], queries_ref[:, part], preferred_element_type=jnp.float32) * scale
        if bias is not None:
            scores = scores + bias
        old = highest[:, part]
        new = jnp.maximum(old, jnp.max(scores, axis=0, keepdims=True))
        weights = jnp.exp2(scores - new)
        highest[:, part] = new
        weight_sum[:, part] = weight_sum[:, part] * jnp.exp2(old - new) + jnp.sum(
            weights, axis=0, keepdims=True
        )
        target[:, part] = weights
        note(part, new)


def block_limits(limit_ref, block, chunk):
    return [limit_ref[0, block * chunk + j] for j in range(chunk)]


def any_token(limit_ref, block, chunk):
    return functools.reduce(jnp.maximum, block_limits(limit_ref, block, chunk)) > 0


def load_block(block_ref, keys, limits, key_width):
    chunk, pairs, pair_width = block_ref.shape
    pair_rows = chunk * pairs
    page_rows = block_ref[...].reshape(pair_rows, pair_width)
    keys[:pair_rows, :key_width] = page_rows[:, :key_width]
    keys[pair_rows:, :key_width] = page_rows[:, key_width:]
    shape = (2 * pair_rows, keys.shape[1] - key_width)
    row = lax.broadcasted_iota(jnp.int32, shape, 0)
    pair_row = lax.rem(row, pair_rows)
    token = 2 * lax.rem(pair_row, pairs) + row // pair_rows
    limit = jnp.zeros_like(row)
    for j, value in enumerate(limits):
        limit = jnp.where(pair_row // pairs == j, value, limit)
    masked = (lax.broadcasted_iota(jnp.int32, shape, 1) == 0) & (token >= limit)
    keys[:, key_width:] = jnp.where(masked, MASKED, 0.0).astype(jnp.bfloat16)


def turn_values(keys, latent_width):
    return keys[:, :latent_width].T


def near_bias(n_keys, half_len, tile, live):
    seq_idx = lax.axis_index("seq")
    place = lax.broadcasted_iota(jnp.int32, (n_keys, tile), 0)
    query = lax.rem(lax.broadcasted_iota(jnp.int32, (n_keys, tile), 1), half_len) + seq_idx * half_len
    allowed = (place <= query) & (place < live)
    return jnp.where(allowed, 0.0, -jnp.inf)


def score_kernel(shape, base, n_sources, first, near, limit_ref, queries_ref, *refs):
    tile, scale, chunk, key_width = shape
    refs = list(refs)
    if not first:
        marks_in, sum_in, high_in = [refs.pop(0) for _ in range(3)]
        refs.pop(0), refs.pop(0)
    if near:
        live_ref, suffix_ref = refs.pop(0), refs.pop(0)
    sources = [refs.pop(0) for _ in range(n_sources)]
    weights_hbm, values_hbm, marks, weight_sum, highest = [refs.pop(0) for _ in range(5)]
    if near:
        near_weights, near_values, near_mark = [refs.pop(0) for _ in range(3)]
    blocks, keys, weights, values, load_sems, weight_sems, value_sems = [refs.pop(0) for _ in range(7)]
    n_blocks = blocks.shape[0]
    latent_width = values.shape[1]
    index = 0
    for source in sources:
        for i in range(source.shape[0] // chunk):
            pltpu.make_async_copy(
                source.at[i * chunk : (i + 1) * chunk], blocks.at[index], load_sems.at[index]
            ).start()
            index += 1
    if first:
        marks[...] = jnp.zeros_like(marks)
        weight_sum[...] = jnp.zeros_like(weight_sum)
        highest[...] = jnp.full_like(highest, LOWEST)
    else:
        marks[...] = marks_in[...]
        weight_sum[...] = sum_in[...]
        highest[...] = high_in[...]

    def stores(block):
        return (
            pltpu.make_async_copy(weights.at[block], weights_hbm.at[base + block], weight_sems.at[block]),
            pltpu.make_async_copy(values.at[block], values_hbm.at[base + block], value_sems.at[block]),
        )

    def one_block(block, carry):
        pltpu.make_async_copy(blocks.at[block], blocks.at[block], load_sems.at[block]).wait()

        @pl.when(any_token(limit_ref, base + block, chunk))
        def _():
            load_block(blocks.at[block], keys, block_limits(limit_ref, base + block, chunk), key_width)

            def note(part, new):
                marks[pl.ds(base + block, 1), part] = new

            score_block(
                keys, queries_ref, weights.at[block], note, highest, weight_sum, tile, scale
            )
            values[block] = turn_values(keys, latent_width)
            for copy in stores(block):
                copy.start()

        return carry

    lax.fori_loop(0, n_blocks, one_block, 0)
    if near:
        near_keys = refs.pop(0)
        n_near = suffix_ref.shape[0]
        near_keys[:, key_width:] = jnp.zeros_like(near_keys[:, key_width:])
        near_keys[:, :key_width] = suffix_ref[...]

        def note_near(part, new):
            near_mark[:, part] = new

        score_block(
            near_keys, queries_ref, near_weights, note_near, highest, weight_sum, tile, scale,
            near_bias(n_near, n_near // lax.axis_size("seq"), tile, live_ref[0]),
        )
        near_values[...] = turn_values(near_keys, latent_width)

    def one_wait(block, carry):
        @pl.when(any_token(limit_ref, base + block, chunk))
        def _():
            for copy in stores(block):
                copy.wait()

        return carry

    lax.fori_loop(0, n_blocks, one_wait, 0)


def score_part(base, total, limits, queries, sources, state, shape, latent_width, near=None):
    tile, scale, chunk, key_width = shape
    width, rows = queries.shape
    _, pairs, pair_width = sources[0].shape
    block_keys = 2 * chunk * pairs
    n_blocks = sum(s.shape[0] for s in sources) // chunk
    row = jax.ShapeDtypeStruct((1, rows), jnp.float32)
    out_shape = [
        jax.ShapeDtypeStruct((total, block_keys, rows), jnp.float32),
        jax.ShapeDtypeStruct((total, latent_width, block_keys), jnp.bfloat16),
        jax.ShapeDtypeStruct((total, rows), jnp.float32),
        row,
        row,
    ]
    out_specs = [hbm_spec(), hbm_spec(), vmem_spec(), vmem_spec(), vmem_spec()]
    operands = [limits, queries]
    specs = [smem_spec(), vmem_spec()]
    aliases = {}
    if state is not None:
        operands += [state[2], state[3], state[4], state[0], state[1]]
        specs += [vmem_spec()] * 3 + [hbm_spec()] * 2
        aliases = {5: 0, 6: 1}
    scratch = [
        pltpu.VMEM((n_blocks, chunk, pairs, pair_width), jnp.bfloat16),
        pltpu.VMEM((block_keys, width), jnp.bfloat16),
        pltpu.VMEM((n_blocks, block_keys, rows), jnp.float32),
        pltpu.VMEM((n_blocks, latent_width, block_keys), jnp.bfloat16),
        pltpu.SemaphoreType.DMA((n_blocks,)),
        pltpu.SemaphoreType.DMA((n_blocks,)),
        pltpu.SemaphoreType.DMA((n_blocks,)),
    ]
    if near is not None:
        near_keys = near[-1].shape[0]
        operands += list(near)
        specs += [smem_spec(), vmem_spec()]
        out_shape += [
            jax.ShapeDtypeStruct((near_keys, rows), jnp.float32),
            jax.ShapeDtypeStruct((latent_width, near_keys), jnp.bfloat16),
            row,
        ]
        out_specs += [vmem_spec()] * 3
        scratch.append(pltpu.VMEM((near_keys, width), jnp.bfloat16))
    operands += list(sources)
    specs += [hbm_spec()] * len(sources)
    work = n_blocks * block_keys * rows // 2
    return pl.pallas_call(
        functools.partial(score_kernel, shape, base, len(sources), state is None, near is not None),
        out_shape=tuple(out_shape),
        in_specs=specs,
        out_specs=tuple(out_specs),
        scratch_shapes=scratch,
        input_output_aliases=aliases,
        compiler_params=pltpu.CompilerParams(vmem_limit_bytes=54 * MIB),
        cost_estimate=pl.CostEstimate(
            flops=work, bytes_accessed=10**5, transcendentals=0
        ),
        name="score_part",
    )(*operands)


def finish_kernel(
    shape, depth, n_blocks, n_sources, limit_ref, queries_ref, marks, sum_in, high_in,
    near_weights, near_values, near_mark, live_ref, up_ref, weights_hbm, values_hbm, *refs,
):
    tile, scale, chunk, key_width = shape
    sources, refs = refs[:n_sources], refs[n_sources:]
    (
        out_ref, weight_sum, highest, total, blocks, keys, last_weights, last_values, last_marks,
        weights, values, used, load_sems, weight_sems, value_sems,
    ) = refs
    rows = queries_ref.shape[1]
    latent_width = total.shape[0]
    n_last = blocks.shape[0]
    index = 0
    for source in sources:
        for i in range(source.shape[0] // chunk):
            pltpu.make_async_copy(
                source.at[i * chunk : (i + 1) * chunk], blocks.at[index], load_sems.at[index]
            ).start()
            index += 1

    def list_block(block, count):
        used[count] = block
        return count + any_token(limit_ref, block, chunk).astype(jnp.int32)

    n_used = lax.fori_loop(0, n_blocks, list_block, jnp.int32(0))

    def fetches(number):
        place = lax.rem(number, depth)
        return (
            pltpu.make_async_copy(weights_hbm.at[used[number]], weights.at[place], weight_sems.at[place]),
            pltpu.make_async_copy(values_hbm.at[used[number]], values.at[place], value_sems.at[place]),
        )

    def fetch(number):
        @pl.when(number < n_used)
        def _():
            for copy in fetches(number):
                copy.start()

    for number in range(depth):
        fetch(jnp.int32(number))
    weight_sum[...] = sum_in[...]
    highest[...] = high_in[...]
    last_marks[...] = jnp.zeros_like(last_marks)

    def one_score(block, carry):
        pltpu.make_async_copy(blocks.at[block], blocks.at[block], load_sems.at[block]).wait()

        @pl.when(any_token(limit_ref, n_blocks + block, chunk))
        def _():
            load_block(blocks.at[block], keys, block_limits(limit_ref, n_blocks + block, chunk), key_width)

            def note(part, new):
                last_marks[pl.ds(block, 1), part] = new

            score_block(
                keys, queries_ref, last_weights.at[block], note, highest, weight_sum, tile, scale
            )
            last_values[block] = turn_values(keys, latent_width)

        return carry

    lax.fori_loop(0, n_last, one_score, 0)

    def add_block(weight_block, value_block, mark, begin=False):
        for start in range(0, rows, tile):
            part = slice(start, start + tile)
            factor = jnp.exp2(mark[:, part] - highest[:, part]) / weight_sum[:, part]
            added = jnp.dot(
                value_block[...],
                (weight_block[:, part] * factor).astype(jnp.bfloat16),
                preferred_element_type=jnp.float32,
            )
            total[:, part] = added if begin else total[:, part] + added

    add_block(near_weights, near_values, near_mark, begin=True)

    def one_add(number, carry):
        for copy in fetches(number):
            copy.wait()
        place = lax.rem(number, depth)
        add_block(weights.at[place], values.at[place], marks.at[pl.ds(used[number], 1)])
        fetch(number + depth)
        return carry

    lax.fori_loop(0, n_used, one_add, 0)

    def one_last(block, carry):
        @pl.when(any_token(limit_ref, n_blocks + block, chunk))
        def _():
            add_block(last_weights.at[block], last_values.at[block], last_marks.at[pl.ds(block, 1)])

        return carry

    lax.fori_loop(0, n_last, one_last, 0)
    heads, _, value_width = up_ref.shape
    half_len = out_ref.shape[0]
    steps = lax.broadcasted_iota(jnp.int32, (half_len, value_width), 0)
    steps = steps + lax.axis_index("seq") * half_len
    for head in range(heads):
        latent = total[:, head * half_len : (head + 1) * half_len].astype(jnp.bfloat16)
        raised = lax.dot_general(
            latent, up_ref[head], (((0,), (0,)), ((), ())), preferred_element_type=jnp.float32
        )
        out_ref[:, head * value_width : (head + 1) * value_width] = jnp.where(
            steps < live_ref[0], raised, 0.0
        ).astype(jnp.bfloat16)


def finish(n_blocks, limits, queries, state, near_state, sources, live, up_weight, half_len, shape):
    tile, scale, chunk, key_width = shape
    weights, values, marks, weight_sum, highest = state
    width, rows = queries.shape
    _, latent_width, block_keys = values.shape
    _, pairs, pair_width = sources[0].shape
    heads, _, value_width = up_weight.shape
    depth = 4
    n_last = sum(s.shape[0] for s in sources) // chunk
    row = pltpu.VMEM((1, rows), jnp.float32)
    work = (n_blocks // 2 + n_last) * block_keys * rows
    return pl.pallas_call(
        functools.partial(finish_kernel, shape, depth, n_blocks, len(sources)),
        out_shape=jax.ShapeDtypeStruct((half_len, heads * value_width), jnp.bfloat16),
        in_specs=[smem_spec()]
        + [vmem_spec()] * 7
        + [smem_spec(), vmem_spec()]
        + [hbm_spec()] * (2 + len(sources)),
        out_specs=vmem_spec(),
        scratch_shapes=[
            row,
            row,
            pltpu.VMEM((latent_width, rows), jnp.float32),
            pltpu.VMEM((n_last, chunk, pairs, pair_width), jnp.bfloat16),
            pltpu.VMEM((block_keys, width), jnp.bfloat16),
            pltpu.VMEM((n_last, block_keys, rows), jnp.float32),
            pltpu.VMEM((n_last, latent_width, block_keys), jnp.bfloat16),
            pltpu.VMEM((n_last, rows), jnp.float32),
            pltpu.VMEM((depth, block_keys, rows), jnp.float32),
            pltpu.VMEM((depth, latent_width, block_keys), jnp.bfloat16),
            pltpu.SMEM((n_blocks + depth + 1,), jnp.int32),
            pltpu.SemaphoreType.DMA((n_last,)),
            pltpu.SemaphoreType.DMA((depth,)),
            pltpu.SemaphoreType.DMA((depth,)),
        ],
        compiler_params=pltpu.CompilerParams(vmem_limit_bytes=54 * MIB),
        cost_estimate=pl.CostEstimate(
            flops=2 * work * latent_width, bytes_accessed=3 * 10**7, transcendentals=work // 4
        ),
        name="finish",
    )(
        limits, queries, marks, weight_sum, highest, *near_state, live, up_weight,
        weights, values, *sources,
    )


def local(
    queries,
    hidden,
    w_dkv,
    kv_gain,
    w_uk,
    value_up_weight,
    page_pool,
    page_owner,
    page_slot,
    prefix_len,
    suffix_len,
):
    n_head = lax.axis_size("head")
    n_req = lax.axis_size("req")
    n_seq = lax.axis_size("seq")
    head_idx = lax.axis_index("head")
    req_idx = lax.axis_index("req")
    seq_idx = lax.axis_index("seq")
    _, half_len, d_local = hidden.shape
    heads_dev, nope_width, latent_width = w_uk.shape
    lat_width = w_dkv.shape[1]
    rope_width = lat_width - latent_width
    query_width = queries.shape[2] // heads_dev
    page_width = page_pool.shape[1]
    page_len = page_width // lat_width
    pairs = page_len // 2
    pages_req = page_slot.shape[1]
    cap = max(2, 2 * pages_req // (n_head * n_req))
    chunk = n_req * cap // 4
    score_scale = float(query_width) ** (-0.5)

    owner_rows = page_owner[:, :, 0]
    counts, most, my_prefix, live, first, rest, foreign, partial_value = pick_pages(
        owner_rows, page_slot, prefix_len, suffix_len, page_pool, hidden[0], w_dkv.T,
        cap, chunk, n_head, n_req, n_seq, pairs,
    )
    swap_route = [(i, n_seq - 1 - i) for i in range(n_seq)]
    stream_route = []
    for i in range(n_head - 1):
        stream_route.append((i * n_seq, (i + 1) * n_seq))
        stream_route.append(((i + 1) * n_seq + 1, i * n_seq + 1))

    def swap(block):
        return lax.ppermute(block, "seq", swap_route)

    def stream(block):
        return lax.ppermute(block, ("head", "seq"), stream_route)

    positions = my_prefix + seq_idx * half_len + jnp.arange(half_len, dtype=jnp.int32)
    rows = heads_dev * half_len
    half_rope = rope_width // 2
    frequency = 10000.0 ** (-2.0 * jnp.arange(half_rope, dtype=jnp.float32) / rope_width)
    phases = frequency[:, None] * positions.astype(jnp.float32)[None, :]
    q_turned = turn_queries(queries[0], w_uk, jnp.cos(phases), jnp.sin(phases), lat_width + 64)

    arrived = [
        lax.ppermute(foreign[s - 1], "req", [(i, (i + s) % n_req) for i in range(n_req)])
        for s in range(1, n_req)
    ]
    share = half_len // n_head
    first, partial_value, q_turned = lax.optimization_barrier((first, partial_value, q_turned))
    early_steps = [stream(first)]
    partials = lax.all_to_all(partial_value, "head", split_axis=0, concat_axis=0, tiled=True)
    mine = arrived[0][None] if n_req == 2 else jnp.stack(arrived)
    mine, q_turned, partials = lax.optimization_barrier((mine, q_turned, partials))
    other = swap(mine)
    middle, late = join_pages(counts, rest, mine, other, chunk, cap, (2 * chunk, chunk))
    partials, early_steps[0] = lax.optimization_barrier((partials, early_steps[0]))
    for step in range(1, n_head - 1):
        early_steps.append(stream(early_steps[-1]))
    early_steps = [[block, None] for block in early_steps]
    for step in range(n_head - 2):
        early_steps[step][1] = swap(early_steps[step][0])
    summed = jnp.sum(partials.reshape(n_head, share, lat_width), axis=0)
    share_t = seq_idx * half_len + head_idx * share + jnp.arange(share, dtype=jnp.int32)
    latent = finish_latent(summed, my_prefix + share_t, share_t < live, kv_gain, latent_width)
    copies = jnp.concatenate([latent] * n_head, axis=0)
    fresh = lax.all_to_all(copies, "head", split_axis=0, concat_axis=0, tiled=True)
    middle, fresh, most = lax.optimization_barrier((middle, fresh, most))

    tile = 256 if rows % 256 == 0 and 256 % half_len == 0 else half_len
    shape = (tile, score_scale * math.log2(math.e), chunk, lat_width)
    last = n_head - 2
    near_state = ()
    extra = 4 + 1 + 2 * last
    total = 1 + 2 * (last + 1) + 2 + 4 * last + extra
    limits = plan_blocks(owner_rows, prefix_len, n_head, chunk, page_len)
    n_blocks = 0
    state = None

    def arrays_of(arrived_steps, steps):
        return [arrived_steps[step][side] for step in steps for side in range(2)]

    def score(arrays, near=None):
        nonlocal n_blocks, state, near_state
        result = score_part(
            n_blocks, total, limits, q_turned, arrays, state, shape, latent_width, near
        )
        state = result[:5]
        near_state = result[5:] or near_state
        n_blocks += sum(a.shape[0] for a in arrays) // chunk

    def tie(block):
        nonlocal state
        block, mark = lax.optimization_barrier((block, state[4]))
        state = (*state[:4], mark)
        return block

    middle_steps = []
    block = stream(middle)
    for step in range(last + 1):
        received = block
        if step == 0:
            score([first] + arrays_of(early_steps, range(last)))
        elif step == 1:
            score(arrays_of(early_steps, [last]) + [middle] + arrays_of(middle_steps, [0]))
        else:
            score(
                arrays_of(middle_steps, [step - 1]), (live, suffix_latent) if step == last else None
            )
        received = tie(received)
        if step == 0:
            early_steps[last][0] = tie(early_steps[last][0])
            early_steps[last][1] = swap(early_steps[last][0])
            most = over_groups(most)
            received, most = lax.optimization_barrier((received, most))
            opposite = swap(fresh)
            suffix_latent = jnp.where(
                seq_idx == 0,
                jnp.concatenate([fresh, opposite], axis=0),
                jnp.concatenate([opposite, fresh], axis=0),
            )
        if step < last:
            block = stream(received)
        middle_steps.append([received, swap(received)])

    last_arrays = arrays_of(middle_steps, [last])

    def end(blocks, final_arrays, current):
        return finish(
            blocks, limits, q_turned, current, near_state, final_arrays, live, value_up_weight, half_len, shape
        )

    def with_late(_):
        block = stream(late)
        arrays = last_arrays + [late]
        current, blocks = state, n_blocks
        for step in range(last + 1):
            received = block
            current = score_part(
                blocks, total, limits, q_turned, arrays, current, shape, latent_width
            )[:5]
            blocks += sum(a.shape[0] for a in arrays) // chunk
            received, mark = lax.optimization_barrier((received, current[4]))
            current = (*current[:4], mark)
            if step < last:
                block = stream(received)
            arrays = [received, swap(received)]
        return end(blocks, arrays, current)

    def without_late(_):
        return end(n_blocks, last_arrays, state)

    attn_out = lax.cond(most > 2 * chunk, with_late, without_late, 0)
    new_pages = fresh.reshape(1, half_len // page_len, page_len * lat_width)
    return (attn_out[None], new_pages)


def solution(mesh):
    placed = (
        P(("groups", "req"), "seq", "head"),
        P(("groups", "req"), "seq", "head"),
        P("head", None),
        P(),
        P("head", None, None),
        P("head", None, None),
        P(("groups", "head", "req"), None),
        P("groups", None, None),
        P("groups", None),
        P("groups"),
        P("groups"),
    )
    return jax.shard_map(
        local,
        mesh=mesh,
        in_specs=placed,
        out_specs=(P(("groups", "req"), "seq", "head"), P(("groups", "req"), "seq", None)),
        check_vma=False,
    )
```

```python
import functools
import math

import jax
import jax.numpy as jnp
from jax import lax
from jax.experimental import pallas as pl
from jax.experimental.pallas import tpu as pltpu
from jax.sharding import PartitionSpec as P

LOWEST = -1e30
MASKED = -1e38
MIB = 1024 * 1024


def rotate(vector, cosine_table, sine_table):
    half_width = vector.shape[-1] // 2
    first_half = vector[..., :half_width]
    second_half = vector[..., half_width:]
    return jnp.concatenate(
        [
            first_half * cosine_table - second_half * sine_table,
            first_half * sine_table + second_half * cosine_table,
        ],
        axis=-1,
    )


def angles(positions, rope_width):
    half_width = rope_width // 2
    frequency = 10000.0 ** (-2.0 * jnp.arange(half_width, dtype=jnp.float32) / rope_width)
    phases = positions.astype(jnp.float32)[:, None] * frequency[None, :]
    return (jnp.cos(phases), jnp.sin(phases))


def finish_latent(summed, positions, live_rows, kv_gain, latent_width):
    latent_part = summed[:, :latent_width]
    mean_square = jnp.mean(latent_part * latent_part, axis=-1, keepdims=True)
    normed = latent_part * lax.rsqrt(mean_square + 1e-06) * kv_gain
    cosine_table, sine_table = angles(positions, summed.shape[1] - latent_width)
    rotated = rotate(summed[:, latent_width:], cosine_table, sine_table)
    joined = jnp.concatenate([normed, rotated], axis=-1).astype(jnp.bfloat16)
    return jnp.where(live_rows[:, None], joined, jnp.zeros_like(joined))


def any_spec():
    return pl.BlockSpec(memory_space=pl.ANY)


def smem_spec():
    return pl.BlockSpec(memory_space=pltpu.SMEM)


def vmem_spec():
    return pl.BlockSpec(memory_space=pltpu.VMEM)


def hbm_spec():
    return pl.BlockSpec(memory_space=pltpu.HBM)


def pick_kernel(
    cap, page_len, owner_hbm, slot_hbm, prefix_hbm, suffix_hbm, pool_hbm, hidden_hbm, down_hbm, count_ref,
    most_ref, length_ref, live_ref, first_ref, rest_ref, foreign_ref, partial_ref, owner_ref, slot_ref,
    prefix_ref, suffix_ref, pool_ref, hidden_ref, down_ref, pages, lists, table, sems,
):
    n_req = lax.axis_size("req")
    head_idx = lax.axis_index("head")
    req_idx = lax.axis_index("req")
    seq_idx = lax.axis_index("seq")
    n_pages = owner_ref.shape[1]
    pool_pages, pairs, pair_width = pages.shape
    chunk = first_ref.shape[0]
    loads = [
        pltpu.make_async_copy(owner_hbm, owner_ref, sems.at[0]),
        pltpu.make_async_copy(slot_hbm, slot_ref, sems.at[1]),
        pltpu.make_async_copy(pool_hbm, pool_ref, sems.at[2]),
        pltpu.make_async_copy(hidden_hbm, hidden_ref, sems.at[6]),
        pltpu.make_async_copy(down_hbm, down_ref, sems.at[7]),
        pltpu.make_async_copy(prefix_hbm, prefix_ref, sems.at[8]),
        pltpu.make_async_copy(suffix_hbm, suffix_ref, sems.at[9]),
    ]
    for load in loads:
        load.start()
    loads[0].wait()
    loads[1].wait()
    loads[5].wait()
    loads[6].wait()
    length_ref[0] = prefix_ref[req_idx]
    live_ref[0] = suffix_ref[req_idx]
    self_owner = head_idx * n_req + req_idx
    n_owners = table.shape[1]
    for shift in range(n_req):
        for owner in range(n_owners):
            table[shift, owner] = 0
    founds = []
    most = jnp.int32(0)
    for shift in range(n_req):
        request = lax.rem(req_idx + shift, n_req)

        def note(page, found, shift=shift, request=request):
            owner = owner_ref[request, page]
            needed = page * page_len < prefix_ref[request]
            table[shift, owner] += needed.astype(jnp.int32)
            lists[shift, found] = slot_ref[request, page]
            return found + (needed & (owner == self_owner)).astype(jnp.int32)

        founds.append(lax.fori_loop(0, n_pages, note, jnp.int32(0), unroll=8))
        for place in range(n_owners // n_req):
            held = functools.reduce(jnp.add, [table[shift, place * n_req + i] for i in range(n_req)])
            early = jnp.minimum(table[shift, place * n_req + request], chunk)
            most = jnp.maximum(most, held - early)
    for shift in range(n_req):
        count_ref[shift] = table[0, head_idx * n_req + lax.rem(req_idx + n_req - shift, n_req)]
    most_ref[0] = most
    loads[2].wait()
    step = 16
    row = lax.broadcasted_iota(jnp.int32, (step * step, step * step), 0)
    column = lax.broadcasted_iota(jnp.int32, (step * step, step * step), 1)
    swap = ((row // step == column % step) & (row % step == column // step)).astype(jnp.bfloat16)
    for page in range(0, pool_pages, step):
        for pair in range(0, pairs, step):
            rows = jnp.concatenate(
                [
                    pool_ref[page : page + step, (pair + i) * pair_width : (pair + i + 1) * pair_width]
                    for i in range(step)
                ],
                axis=0,
            )
            turned = jnp.dot(swap, rows, preferred_element_type=jnp.float32).astype(jnp.bfloat16)
            pages[page : page + step, pair : pair + step, :] = turned.reshape(step, step, pair_width)

    def send(shift, rank, target, sem):
        slot = jnp.where(rank < founds[shift], lists[shift, rank], 0)
        pltpu.make_async_copy(pages.at[slot], target, sem).start()

    for rank in range(cap):
        if rank < chunk:
            send(0, rank, first_ref.at[rank], sems.at[3])
        else:
            send(0, rank, rest_ref.at[rank - chunk], sems.at[4])
    half_cap = foreign_ref.shape[1]
    for shift in range(1, n_req):
        for j in range(half_cap):
            send(shift, seq_idx * half_cap + j, foreign_ref.at[shift - 1, j], sems.at[5])
    loads[3].wait()
    loads[4].wait()
    partial_ref[...] = lax.dot_general(
        hidden_ref[...], down_ref[...], (((1,), (1,)), ((), ())), preferred_element_type=jnp.float32
    )
    pltpu.make_async_copy(first_ref, first_ref, sems.at[3]).wait()
    if cap > chunk:
        pltpu.make_async_copy(rest_ref, rest_ref, sems.at[4]).wait()
    pltpu.make_async_copy(foreign_ref, foreign_ref, sems.at[5]).wait()


def pick_pages(
    page_owner, page_slot, prefix_len, suffix_len, page_pool, hidden, down,
    cap, chunk, n_head, n_req, n_seq, pairs,
):
    pool_pages, page_width = page_pool.shape
    page = (pairs, page_width // pairs)
    return pl.pallas_call(
        functools.partial(pick_kernel, cap, 2 * pairs),
        out_shape=(
            jax.ShapeDtypeStruct((n_req,), jnp.int32),
            jax.ShapeDtypeStruct((1,), jnp.int32),
            jax.ShapeDtypeStruct((1,), jnp.int32),
            jax.ShapeDtypeStruct((1,), jnp.int32),
            jax.ShapeDtypeStruct((chunk, *page), jnp.bfloat16),
            jax.ShapeDtypeStruct((max(1, cap - chunk), *page), jnp.bfloat16),
            jax.ShapeDtypeStruct((n_req - 1, cap // n_seq, *page), jnp.bfloat16),
            jax.ShapeDtypeStruct((hidden.shape[0], down.shape[0]), jnp.float32),
        ),
        in_specs=[any_spec()] * 4 + [hbm_spec()] * 3,
        out_specs=(smem_spec(), smem_spec(), smem_spec(), smem_spec(), hbm_spec(), hbm_spec(), hbm_spec(), vmem_spec()),
        scratch_shapes=[
            pltpu.SMEM(page_owner.shape, jnp.int32),
            pltpu.SMEM(page_slot.shape, jnp.int32),
            pltpu.SMEM(prefix_len.shape, jnp.int32),
            pltpu.SMEM(suffix_len.shape, jnp.int32),
            pltpu.VMEM((pool_pages, page_width), jnp.bfloat16),
            pltpu.VMEM(hidden.shape, jnp.bfloat16),
            pltpu.VMEM(down.shape, jnp.bfloat16),
            pltpu.VMEM((pool_pages, *page), jnp.bfloat16),
            pltpu.SMEM((n_req, cap + 1), jnp.int32),
            pltpu.SMEM((n_req, n_head * n_req), jnp.int32),
            pltpu.SemaphoreType.DMA((10,)),
        ],
        compiler_params=pltpu.CompilerParams(vmem_limit_bytes=60 * MIB),
        cost_estimate=pl.CostEstimate(flops=10**9, bytes_accessed=6 * 10**6, transcendentals=0),
        name="pick_pages",
    )(page_owner, page_slot, prefix_len, suffix_len, page_pool, hidden, down)


def join_kernel(chunk, cap, count_ref, rest_ref, mine_ref, other_ref, *refs):
    n_req = count_ref.shape[0]
    targets, sems = refs[:-1], refs[-1]
    seq_idx = lax.axis_index("seq")
    half_cap = mine_ref.shape[1]
    excess = jnp.maximum(count_ref[0] - chunk, 0)
    j = 0
    for part, target in enumerate(targets):
        for place in range(target.shape[0]):

            def fetch(condition, source, target=target, place=place, part=part):
                @pl.when(condition)
                def _():
                    pltpu.make_async_copy(source, target.at[place], sems.at[part]).start()

            rank = jnp.int32(j)
            taken = rank < excess
            if cap > chunk:
                fetch(taken, rest_ref.at[jnp.minimum(rank, cap - chunk - 1)])
            rank = rank - excess
            for shift in range(1, n_req):
                here = jnp.logical_not(taken) & (rank < count_ref[shift])
                half = rank // half_cap
                slot = jnp.clip(rank - half * half_cap, 0, half_cap - 1)
                fetch(here & (half == seq_idx), mine_ref.at[shift - 1, slot])
                fetch(here & (half != seq_idx), other_ref.at[shift - 1, slot])
                taken = taken | here
                rank = rank - count_ref[shift]
            fetch(jnp.logical_not(taken), mine_ref.at[0, 0])
            j += 1
    for part, target in enumerate(targets):
        pltpu.make_async_copy(target, target, sems.at[part]).wait()


def join_pages(counts, rest, mine, other, chunk, cap, sizes):
    return pl.pallas_call(
        functools.partial(join_kernel, chunk, cap),
        out_shape=tuple(jax.ShapeDtypeStruct((size, *rest.shape[1:]), jnp.bfloat16) for size in sizes),
        in_specs=[smem_spec()] + [hbm_spec()] * 3,
        out_specs=(vmem_spec(),) * len(sizes),
        scratch_shapes=[pltpu.SemaphoreType.DMA((len(sizes),))],
        compiler_params=pltpu.CompilerParams(vmem_limit_bytes=10 * MIB),
        cost_estimate=pl.CostEstimate(flops=0, bytes_accessed=3 * 10**6, transcendentals=0),
        name="join_pages",
    )(counts, rest, mine, other)


def plan_kernel(page_len, chunk, owner_ref, prefix_ref, limit_ref):
    n_head = lax.axis_size("head")
    n_req = lax.axis_size("req")
    head_idx = lax.axis_index("head")
    req_idx = lax.axis_index("req")
    upward = 2 * lax.axis_index("seq") - 1
    n = owner_ref.shape[1]
    prefix = prefix_ref[req_idx]
    diagonal = lax.broadcasted_iota(jnp.int32, (n, n), 0) == lax.broadcasted_iota(jnp.int32, (n, n), 1)

    def column(values):
        return jnp.sum(jnp.where(diagonal, values, 0), axis=1, keepdims=True)

    owner = owner_ref[pl.ds(req_idx, 1), :]
    place = jnp.zeros_like(owner)
    for head in range(1, n_head):
        place = place + (owner >= head * n_req).astype(jnp.int32)
    shift = req_idx - (owner - place * n_req)
    shift = jnp.where(shift < 0, shift + n_req, shift)
    order = lax.broadcasted_iota(jnp.int32, (1, n), 1)
    needed = (order * page_len < prefix).astype(jnp.int32)
    key = shift * n + order
    together = (column(place) == place) & (column(needed) > 0)
    rank = jnp.sum((together & (column(key) < key)).astype(jnp.int32), axis=0, keepdims=True)
    held = jnp.sum((together & (column(shift) == 0)).astype(jnp.int32), axis=0, keepdims=True)
    early = (shift == 0) & (rank < chunk)
    within = jnp.where(early, rank, chunk + rank - jnp.minimum(held, chunk))
    away = place - head_idx
    distance = jnp.abs(away)
    origin = jnp.where(away * upward > 0, 2 * distance - 1, 2 * distance)
    origins = 2 * n_head - 1
    slot = jnp.where(
        within < chunk,
        origin * chunk + within,
        jnp.where(
            within < 3 * chunk,
            (origins + 2 * origin) * chunk + within - chunk,
            (3 * origins + origin) * chunk + within - 3 * chunk,
        ),
    )
    slot = column(jnp.where(needed > 0, slot, -1))
    tokens = column(jnp.clip(prefix - order * page_len, 0, page_len))
    lane = lax.broadcasted_iota(jnp.int32, (n, limit_ref.shape[1]), 1)
    limit_ref[...] = jnp.sum(jnp.where(lane == slot, tokens, 0), axis=0, keepdims=True)


def plan_blocks(page_owner, prefix_len, n_head, chunk, page_len):
    return pl.pallas_call(
        functools.partial(plan_kernel, page_len, chunk),
        out_shape=jax.ShapeDtypeStruct((1, 4 * (2 * n_head - 1) * chunk), jnp.int32),
        in_specs=[vmem_spec(), smem_spec()],
        out_specs=vmem_spec(),
        cost_estimate=pl.CostEstimate(flops=10**4, bytes_accessed=10**4, transcendentals=0),
        name="plan_blocks",
    )(page_owner, prefix_len)


def over_groups(most):
    n_groups = lax.axis_size("groups")
    passed = most
    for _ in range(n_groups - 1):
        passed = lax.ppermute(passed, "groups", [(i, (i + 1) % n_groups) for i in range(n_groups)])
        most = jnp.maximum(most, passed)
    return most[0]


def query_kernel(query_hbm, up_hbm, cosine_ref, sine_ref, out_ref, query_ref, up_ref, sems):
    loads = [
        pltpu.make_async_copy(query_hbm, query_ref, sems.at[0]),
        pltpu.make_async_copy(up_hbm, up_ref, sems.at[1]),
    ]
    for load in loads:
        load.start()
    for load in loads:
        load.wait()
    heads, nope_width, latent_width = up_ref.shape
    half_len, width = query_ref.shape
    query_width = width // heads
    half_rope = cosine_ref.shape[0]
    key_width = latent_width + 2 * half_rope
    for head in range(heads):
        part = slice(head * half_len, (head + 1) * half_len)
        both = query_ref[:, head * query_width : (head + 1) * query_width]
        latent = lax.dot_general(
            up_ref[head], both[:, :nope_width], (((0,), (1,)), ((), ())), preferred_element_type=jnp.float32
        )
        out_ref[:latent_width, part] = latent.astype(jnp.bfloat16)
        turned = both[:, nope_width:].astype(jnp.float32).T
        low, high = turned[:half_rope], turned[half_rope:]
        out_ref[latent_width : latent_width + half_rope, part] = (
            low * cosine_ref[...] - high * sine_ref[...]
        ).astype(jnp.bfloat16)
        out_ref[latent_width + half_rope : key_width, part] = (
            low * sine_ref[...] + high * cosine_ref[...]
        ).astype(jnp.bfloat16)
    rest = out_ref.shape[0] - key_width
    row = lax.broadcasted_iota(jnp.int32, (rest, out_ref.shape[1]), 0)
    out_ref[key_width:, :] = (row == 0).astype(jnp.bfloat16)


def turn_queries(queries, w_uk, cosine_table, sine_table, key_rows):
    heads, nope_width, latent_width = w_uk.shape
    rows = heads * queries.shape[0]
    return pl.pallas_call(
        query_kernel,
        out_shape=jax.ShapeDtypeStruct((key_rows, rows), jnp.bfloat16),
        in_specs=[any_spec()] * 2 + [vmem_spec()] * 2,
        out_specs=vmem_spec(),
        scratch_shapes=[
            pltpu.VMEM(queries.shape, jnp.bfloat16),
            pltpu.VMEM(w_uk.shape, jnp.bfloat16),
            pltpu.SemaphoreType.DMA((2,)),
        ],
        compiler_params=pltpu.CompilerParams(vmem_limit_bytes=60 * MIB),
        cost_estimate=pl.CostEstimate(
            flops=2 * rows * nope_width * latent_width, bytes_accessed=3 * 10**6, transcendentals=0
        ),
        name="turn_queries",
    )(queries, w_uk, cosine_table, sine_table)


def score_block(keys, queries_ref, target, note, highest, weight_sum, tile, scale, bias=None):
    rows = queries_ref.shape[1]
    for start in range(0, rows, tile):
        part = slice(start, start + tile)
        scores = jnp.dot(keys[...], queries_ref[:, part], preferred_element_type=jnp.float32) * scale
        if bias is not None:
            scores = scores + bias
        old = highest[:, part]
        new = jnp.maximum(old, jnp.max(scores, axis=0, keepdims=True))
        weights = jnp.exp2(scores - new)
        highest[:, part] = new
        weight_sum[:, part] = weight_sum[:, part] * jnp.exp2(old - new) + jnp.sum(
            weights, axis=0, keepdims=True
        )
        target[:, part] = weights
        note(part, new)


def block_limits(limit_ref, block, chunk):
    return [limit_ref[0, block * chunk + j] for j in range(chunk)]


def any_token(limit_ref, block, chunk):
    return functools.reduce(jnp.maximum, block_limits(limit_ref, block, chunk)) > 0


def load_block(block_ref, keys, limits, key_width):
    chunk, pairs, pair_width = block_ref.shape
    pair_rows = chunk * pairs
    page_rows = block_ref[...].reshape(pair_rows, pair_width)
    keys[:pair_rows, :key_width] = page_rows[:, :key_width]
    keys[pair_rows:, :key_width] = page_rows[:, key_width:]
    shape = (2 * pair_rows, keys.shape[1] - key_width)
    row = lax.broadcasted_iota(jnp.int32, shape, 0)
    pair_row = lax.rem(row, pair_rows)
    token = 2 * lax.rem(pair_row, pairs) + row // pair_rows
    limit = jnp.zeros_like(row)
    for j, value in enumerate(limits):
        limit = jnp.where(pair_row // pairs == j, value, limit)
    masked = (lax.broadcasted_iota(jnp.int32, shape, 1) == 0) & (token >= limit)
    keys[:, key_width:] = jnp.where(masked, MASKED, 0.0).astype(jnp.bfloat16)


def turn_values(keys, latent_width):
    return keys[:, :latent_width].T


def near_bias(n_keys, half_len, tile, live):
    seq_idx = lax.axis_index("seq")
    place = lax.broadcasted_iota(jnp.int32, (n_keys, tile), 0)
    query = lax.rem(lax.broadcasted_iota(jnp.int32, (n_keys, tile), 1), half_len) + seq_idx * half_len
    allowed = (place <= query) & (place < live)
    return jnp.where(allowed, 0.0, -jnp.inf)


def score_kernel(shape, base, n_sources, first, near, limit_ref, queries_ref, *refs):
    tile, scale, chunk, key_width = shape
    refs = list(refs)
    if not first:
        marks_in, sum_in, high_in = [refs.pop(0) for _ in range(3)]
        refs.pop(0), refs.pop(0)
    if near:
        live_ref, suffix_ref = refs.pop(0), refs.pop(0)
    sources = [refs.pop(0) for _ in range(n_sources)]
    weights_hbm, values_hbm, marks, weight_sum, highest = [refs.pop(0) for _ in range(5)]
    if near:
        near_weights, near_values, near_mark = [refs.pop(0) for _ in range(3)]
    blocks, keys, weights, values, load_sems, weight_sems, value_sems = [refs.pop(0) for _ in range(7)]
    n_blocks = blocks.shape[0]
    latent_width = values.shape[1]
    index = 0
    for source in sources:
        for i in range(source.shape[0] // chunk):
            pltpu.make_async_copy(
                source.at[i * chunk : (i + 1) * chunk], blocks.at[index], load_sems.at[index]
            ).start()
            index += 1
    if first:
        marks[...] = jnp.zeros_like(marks)
        weight_sum[...] = jnp.zeros_like(weight_sum)
        highest[...] = jnp.full_like(highest, LOWEST)
    else:
        marks[...] = marks_in[...]
        weight_sum[...] = sum_in[...]
        highest[...] = high_in[...]

    def stores(block):
        return (
            pltpu.make_async_copy(weights.at[block], weights_hbm.at[base + block], weight_sems.at[block]),
            pltpu.make_async_copy(values.at[block], values_hbm.at[base + block], value_sems.at[block]),
        )

    def one_block(block, carry):
        pltpu.make_async_copy(blocks.at[block], blocks.at[block], load_sems.at[block]).wait()

        @pl.when(any_token(limit_ref, base + block, chunk))
        def _():
            load_block(blocks.at[block], keys, block_limits(limit_ref, base + block, chunk), key_width)

            def note(part, new):
                marks[pl.ds(base + block, 1), part] = new

            score_block(
                keys, queries_ref, weights.at[block], note, highest, weight_sum, tile, scale
            )
            values[block] = turn_values(keys, latent_width)
            for copy in stores(block):
                copy.start()

        return carry

    lax.fori_loop(0, n_blocks, one_block, 0)
    if near:
        near_keys = refs.pop(0)
        n_near = suffix_ref.shape[0]
        near_keys[:, key_width:] = jnp.zeros_like(near_keys[:, key_width:])
        near_keys[:, :key_width] = suffix_ref[...]

        def note_near(part, new):
            near_mark[:, part] = new

        score_block(
            near_keys, queries_ref, near_weights, note_near, highest, weight_sum, tile, scale,
            near_bias(n_near, n_near // lax.axis_size("seq"), tile, live_ref[0]),
        )
        near_values[...] = turn_values(near_keys, latent_width)

    def one_wait(block, carry):
        @pl.when(any_token(limit_ref, base + block, chunk))
        def _():
            for copy in stores(block):
                copy.wait()

        return carry

    lax.fori_loop(0, n_blocks, one_wait, 0)


def score_part(base, total, limits, queries, sources, state, shape, latent_width, near=None):
    tile, scale, chunk, key_width = shape
    width, rows = queries.shape
    _, pairs, pair_width = sources[0].shape
    block_keys = 2 * chunk * pairs
    n_blocks = sum(s.shape[0] for s in sources) // chunk
    row = jax.ShapeDtypeStruct((1, rows), jnp.float32)
    out_shape = [
        jax.ShapeDtypeStruct((total, block_keys, rows), jnp.float32),
        jax.ShapeDtypeStruct((total, latent_width, block_keys), jnp.bfloat16),
        jax.ShapeDtypeStruct((total, rows), jnp.float32),
        row,
        row,
    ]
    out_specs = [hbm_spec(), hbm_spec(), vmem_spec(), vmem_spec(), vmem_spec()]
    operands = [limits, queries]
    specs = [smem_spec(), vmem_spec()]
    aliases = {}
    if state is not None:
        operands += [state[2], state[3], state[4], state[0], state[1]]
        specs += [vmem_spec()] * 3 + [hbm_spec()] * 2
        aliases = {5: 0, 6: 1}
    scratch = [
        pltpu.VMEM((n_blocks, chunk, pairs, pair_width), jnp.bfloat16),
        pltpu.VMEM((block_keys, width), jnp.bfloat16),
        pltpu.VMEM((n_blocks, block_keys, rows), jnp.float32),
        pltpu.VMEM((n_blocks, latent_width, block_keys), jnp.bfloat16),
        pltpu.SemaphoreType.DMA((n_blocks,)),
        pltpu.SemaphoreType.DMA((n_blocks,)),
        pltpu.SemaphoreType.DMA((n_blocks,)),
    ]
    if near is not None:
        near_keys = near[-1].shape[0]
        operands += list(near)
        specs += [smem_spec(), vmem_spec()]
        out_shape += [
            jax.ShapeDtypeStruct((near_keys, rows), jnp.float32),
            jax.ShapeDtypeStruct((latent_width, near_keys), jnp.bfloat16),
            row,
        ]
        out_specs += [vmem_spec()] * 3
        scratch.append(pltpu.VMEM((near_keys, width), jnp.bfloat16))
    operands += list(sources)
    specs += [hbm_spec()] * len(sources)
    work = n_blocks * block_keys * rows // 2
    return pl.pallas_call(
        functools.partial(score_kernel, shape, base, len(sources), state is None, near is not None),
        out_shape=tuple(out_shape),
        in_specs=specs,
        out_specs=tuple(out_specs),
        scratch_shapes=scratch,
        input_output_aliases=aliases,
        compiler_params=pltpu.CompilerParams(vmem_limit_bytes=54 * MIB),
        cost_estimate=pl.CostEstimate(
            flops=work, bytes_accessed=10**5, transcendentals=0
        ),
        name="score_part",
    )(*operands)


def finish_kernel(
    shape, depth, n_blocks, n_sources, limit_ref, queries_ref, marks, sum_in, high_in,
    near_weights, near_values, near_mark, live_ref, up_ref, weights_hbm, values_hbm, *refs,
):
    tile, scale, chunk, key_width = shape
    sources, refs = refs[:n_sources], refs[n_sources:]
    (
        out_ref, weight_sum, highest, total, blocks, keys, last_weights, last_values, last_marks,
        weights, values, used, load_sems, weight_sems, value_sems,
    ) = refs
    rows = queries_ref.shape[1]
    latent_width = total.shape[0]
    n_last = blocks.shape[0]
    index = 0
    for source in sources:
        for i in range(source.shape[0] // chunk):
            pltpu.make_async_copy(
                source.at[i * chunk : (i + 1) * chunk], blocks.at[index], load_sems.at[index]
            ).start()
            index += 1

    def list_block(block, count):
        used[count] = block
        return count + any_token(limit_ref, block, chunk).astype(jnp.int32)

    n_used = lax.fori_loop(0, n_blocks, list_block, jnp.int32(0))

    def fetches(number):
        place = lax.rem(number, depth)
        return (
            pltpu.make_async_copy(weights_hbm.at[used[number]], weights.at[place], weight_sems.at[place]),
            pltpu.make_async_copy(values_hbm.at[used[number]], values.at[place], value_sems.at[place]),
        )

    def fetch(number):
        @pl.when(number < n_used)
        def _():
            for copy in fetches(number):
                copy.start()

    for number in range(depth):
        fetch(jnp.int32(number))
    weight_sum[...] = sum_in[...]
    highest[...] = high_in[...]
    last_marks[...] = jnp.zeros_like(last_marks)

    def one_score(block, carry):
        pltpu.make_async_copy(blocks.at[block], blocks.at[block], load_sems.at[block]).wait()

        @pl.when(any_token(limit_ref, n_blocks + block, chunk))
        def _():
            load_block(blocks.at[block], keys, block_limits(limit_ref, n_blocks + block, chunk), key_width)

            def note(part, new):
                last_marks[pl.ds(block, 1), part] = new

            score_block(
                keys, queries_ref, last_weights.at[block], note, highest, weight_sum, tile, scale
            )
            last_values[block] = turn_values(keys, latent_width)

        return carry

    lax.fori_loop(0, n_last, one_score, 0)

    def add_block(weight_block, value_block, mark, begin=False):
        for start in range(0, rows, tile):
            part = slice(start, start + tile)
            factor = jnp.exp2(mark[:, part] - highest[:, part]) / weight_sum[:, part]
            added = jnp.dot(
                value_block[...],
                (weight_block[:, part] * factor).astype(jnp.bfloat16),
                preferred_element_type=jnp.float32,
            )
            total[:, part] = added if begin else total[:, part] + added

    add_block(near_weights, near_values, near_mark, begin=True)

    def one_add(number, carry):
        for copy in fetches(number):
            copy.wait()
        place = lax.rem(number, depth)
        add_block(weights.at[place], values.at[place], marks.at[pl.ds(used[number], 1)])
        fetch(number + depth)
        return carry

    lax.fori_loop(0, n_used, one_add, 0)

    def one_last(block, carry):
        @pl.when(any_token(limit_ref, n_blocks + block, chunk))
        def _():
            add_block(last_weights.at[block], last_values.at[block], last_marks.at[pl.ds(block, 1)])

        return carry

    lax.fori_loop(0, n_last, one_last, 0)
    heads, _, value_width = up_ref.shape
    half_len = out_ref.shape[0]
    steps = lax.broadcasted_iota(jnp.int32, (half_len, value_width), 0)
    steps = steps + lax.axis_index("seq") * half_len
    for head in range(heads):
        latent = total[:, head * half_len : (head + 1) * half_len].astype(jnp.bfloat16)
        raised = lax.dot_general(
            latent, up_ref[head], (((0,), (0,)), ((), ())), preferred_element_type=jnp.float32
        )
        out_ref[:, head * value_width : (head + 1) * value_width] = jnp.where(
            steps < live_ref[0], raised, 0.0
        ).astype(jnp.bfloat16)


def finish(n_blocks, limits, queries, state, near_state, sources, live, up_weight, half_len, shape):
    tile, scale, chunk, key_width = shape
    weights, values, marks, weight_sum, highest = state
    width, rows = queries.shape
    _, latent_width, block_keys = values.shape
    _, pairs, pair_width = sources[0].shape
    heads, _, value_width = up_weight.shape
    depth = 4
    n_last = sum(s.shape[0] for s in sources) // chunk
    row = pltpu.VMEM((1, rows), jnp.float32)
    work = (n_blocks // 2 + n_last) * block_keys * rows
    return pl.pallas_call(
        functools.partial(finish_kernel, shape, depth, n_blocks, len(sources)),
        out_shape=jax.ShapeDtypeStruct((half_len, heads * value_width), jnp.bfloat16),
        in_specs=[smem_spec()]
        + [vmem_spec()] * 7
        + [smem_spec(), vmem_spec()]
        + [hbm_spec()] * (2 + len(sources)),
        out_specs=vmem_spec(),
        scratch_shapes=[
            row,
            row,
            pltpu.VMEM((latent_width, rows), jnp.float32),
            pltpu.VMEM((n_last, chunk, pairs, pair_width), jnp.bfloat16),
            pltpu.VMEM((block_keys, width), jnp.bfloat16),
            pltpu.VMEM((n_last, block_keys, rows), jnp.float32),
            pltpu.VMEM((n_last, latent_width, block_keys), jnp.bfloat16),
            pltpu.VMEM((n_last, rows), jnp.float32),
            pltpu.VMEM((depth, block_keys, rows), jnp.float32),
            pltpu.VMEM((depth, latent_width, block_keys), jnp.bfloat16),
            pltpu.SMEM((n_blocks + depth + 1,), jnp.int32),
            pltpu.SemaphoreType.DMA((n_last,)),
            pltpu.SemaphoreType.DMA((depth,)),
            pltpu.SemaphoreType.DMA((depth,)),
        ],
        compiler_params=pltpu.CompilerParams(vmem_limit_bytes=54 * MIB),
        cost_estimate=pl.CostEstimate(
            flops=2 * work * latent_width, bytes_accessed=3 * 10**7, transcendentals=work // 4
        ),
        name="finish",
    )(
        limits, queries, marks, weight_sum, highest, *near_state, live, up_weight,
        weights, values, *sources,
    )


def local(
    queries,
    hidden,
    w_dkv,
    kv_gain,
    w_uk,
    value_up_weight,
    page_pool,
    page_owner,
    page_slot,
    prefix_len,
    suffix_len,
):
    n_head = lax.axis_size("head")
    n_req = lax.axis_size("req")
    n_seq = lax.axis_size("seq")
    head_idx = lax.axis_index("head")
    req_idx = lax.axis_index("req")
    seq_idx = lax.axis_index("seq")
    _, half_len, d_local = hidden.shape
    heads_dev, nope_width, latent_width = w_uk.shape
    lat_width = w_dkv.shape[1]
    rope_width = lat_width - latent_width
    query_width = queries.shape[2] // heads_dev
    page_width = page_pool.shape[1]
    page_len = page_width // lat_width
    pairs = page_len // 2
    pages_req = page_slot.shape[1]
    cap = max(2, 2 * pages_req // (n_head * n_req))
    chunk = n_req * cap // 4
    score_scale = float(query_width) ** (-0.5)

    owner_rows = page_owner[:, :, 0]
    counts, most, my_prefix, live, first, rest, foreign, partial_value = pick_pages(
        owner_rows, page_slot, prefix_len, suffix_len, page_pool, hidden[0], w_dkv.T,
        cap, chunk, n_head, n_req, n_seq, pairs,
    )
    swap_route = [(i, n_seq - 1 - i) for i in range(n_seq)]
    stream_route = []
    for i in range(n_head - 1):
        stream_route.append((i * n_seq, (i + 1) * n_seq))
        stream_route.append(((i + 1) * n_seq + 1, i * n_seq + 1))

    def swap(block):
        return lax.ppermute(block, "seq", swap_route)

    def stream(block):
        return lax.ppermute(block, ("head", "seq"), stream_route)

    positions = my_prefix + seq_idx * half_len + jnp.arange(half_len, dtype=jnp.int32)
    rows = heads_dev * half_len
    half_rope = rope_width // 2
    frequency = 10000.0 ** (-2.0 * jnp.arange(half_rope, dtype=jnp.float32) / rope_width)
    phases = frequency[:, None] * positions.astype(jnp.float32)[None, :]
    q_turned = turn_queries(queries[0], w_uk, jnp.cos(phases), jnp.sin(phases), lat_width + 64)

    arrived = [
        lax.ppermute(foreign[s - 1], "req", [(i, (i + s) % n_req) for i in range(n_req)])
        for s in range(1, n_req)
    ]
    share = half_len // n_head
    partials = lax.all_to_all(partial_value, "head", split_axis=0, concat_axis=0, tiled=True)
    first, partials = lax.optimization_barrier((first, partials))
    early_steps = [stream(first)]
    mine = arrived[0][None] if n_req == 2 else jnp.stack(arrived)
    mine, q_turned, partials = lax.optimization_barrier((mine, q_turned, partials))
    other = swap(mine)
    middle, late = join_pages(counts, rest, mine, other, chunk, cap, (2 * chunk, chunk))
    for step in range(1, n_head - 1):
        early_steps.append(stream(early_steps[-1]))
    early_steps = [[block, None] for block in early_steps]
    for step in range(n_head - 2):
        early_steps[step][1] = swap(early_steps[step][0])
    summed = jnp.sum(partials.reshape(n_head, share, lat_width), axis=0)
    share_t = seq_idx * half_len + head_idx * share + jnp.arange(share, dtype=jnp.int32)
    latent = finish_latent(summed, my_prefix + share_t, share_t < live, kv_gain, latent_width)
    middle, most = lax.optimization_barrier((middle, most))

    tile = 256 if rows % 256 == 0 and 256 % half_len == 0 else half_len
    shape = (tile, score_scale * math.log2(math.e), chunk, lat_width)
    last = n_head - 2
    near_state = ()
    extra = 4 + 1 + 2 * last
    total = 1 + 2 * (last + 1) + 2 + 4 * last + extra
    limits = plan_blocks(owner_rows, prefix_len, n_head, chunk, page_len)
    n_blocks = 0
    state = None

    def arrays_of(arrived_steps, steps):
        return [arrived_steps[step][side] for step in steps for side in range(2)]

    def score(arrays, near=None):
        nonlocal n_blocks, state, near_state
        result = score_part(
            n_blocks, total, limits, q_turned, arrays, state, shape, latent_width, near
        )
        state = result[:5]
        near_state = result[5:] or near_state
        n_blocks += sum(a.shape[0] for a in arrays) // chunk

    def tie(block):
        nonlocal state
        block, mark = lax.optimization_barrier((block, state[4]))
        state = (*state[:4], mark)
        return block

    middle_steps = []
    block = stream(middle)
    for step in range(last + 1):
        received = block
        if step == 0:
            score([first] + arrays_of(early_steps, range(last)))
        elif step == 1:
            score(arrays_of(early_steps, [last]) + [middle] + arrays_of(middle_steps, [0]))
        else:
            score(
                arrays_of(middle_steps, [step - 1]), (live, suffix_latent) if step == last else None
            )
        received = tie(received)
        if step == 0:
            early_steps[last][0] = tie(early_steps[last][0])
            early_steps[last][1] = swap(early_steps[last][0])
            most = over_groups(most)
            received, most, latent = lax.optimization_barrier((received, most, latent))
            copies = jnp.concatenate([latent] * n_head, axis=0)
            fresh = lax.all_to_all(copies, "head", split_axis=0, concat_axis=0, tiled=True)
            received, fresh = lax.optimization_barrier((received, fresh))
            opposite = swap(fresh)
            suffix_latent = jnp.where(
                seq_idx == 0,
                jnp.concatenate([fresh, opposite], axis=0),
                jnp.concatenate([opposite, fresh], axis=0),
            )
        if step < last:
            block = stream(received)
        middle_steps.append([received, swap(received)])

    last_arrays = arrays_of(middle_steps, [last])

    def end(blocks, final_arrays, current):
        return finish(
            blocks, limits, q_turned, current, near_state, final_arrays, live, value_up_weight, half_len, shape
        )

    def with_late(_):
        block = stream(late)
        arrays = last_arrays + [late]
        current, blocks = state, n_blocks
        for step in range(last + 1):
            received = block
            current = score_part(
                blocks, total, limits, q_turned, arrays, current, shape, latent_width
            )[:5]
            blocks += sum(a.shape[0] for a in arrays) // chunk
            received, mark = lax.optimization_barrier((received, current[4]))
            current = (*current[:4], mark)
            if step < last:
                block = stream(received)
            arrays = [received, swap(received)]
        return end(blocks, arrays, current)

    def without_late(_):
        return end(n_blocks, last_arrays, state)

    attn_out = lax.cond(most > 2 * chunk, with_late, without_late, 0)
    new_pages = fresh.reshape(1, half_len // page_len, page_len * lat_width)
    return (attn_out[None], new_pages)


def solution(mesh):
    placed = (
        P(("groups", "req"), "seq", "head"),
        P(("groups", "req"), "seq", "head"),
        P("head", None),
        P(),
        P("head", None, None),
        P("head", None, None),
        P(("groups", "head", "req"), None),
        P("groups", None, None),
        P("groups", None),
        P("groups"),
        P("groups"),
    )
    return jax.shard_map(
        local,
        mesh=mesh,
        in_specs=placed,
        out_specs=(P(("groups", "req"), "seq", "head"), P(("groups", "req"), "seq", None)),
        check_vma=False,
    )
```

```python
import functools
import math

import jax
import jax.numpy as jnp
from jax import lax
from jax.experimental import pallas as pl
from jax.experimental.pallas import tpu as pltpu
from jax.sharding import PartitionSpec as P

LOWEST = -1e30
MASKED = -1e38
MIB = 1024 * 1024


def rotate(vector, cosine_table, sine_table):
    half_width = vector.shape[-1] // 2
    first_half = vector[..., :half_width]
    second_half = vector[..., half_width:]
    return jnp.concatenate(
        [
            first_half * cosine_table - second_half * sine_table,
            first_half * sine_table + second_half * cosine_table,
        ],
        axis=-1,
    )


def angles(positions, rope_width):
    half_width = rope_width // 2
    frequency = 10000.0 ** (-2.0 * jnp.arange(half_width, dtype=jnp.float32) / rope_width)
    phases = positions.astype(jnp.float32)[:, None] * frequency[None, :]
    return (jnp.cos(phases), jnp.sin(phases))


def finish_latent(summed, positions, live_rows, kv_gain, latent_width):
    latent_part = summed[:, :latent_width]
    mean_square = jnp.mean(latent_part * latent_part, axis=-1, keepdims=True)
    normed = latent_part * lax.rsqrt(mean_square + 1e-06) * kv_gain
    cosine_table, sine_table = angles(positions, summed.shape[1] - latent_width)
    rotated = rotate(summed[:, latent_width:], cosine_table, sine_table)
    joined = jnp.concatenate([normed, rotated], axis=-1).astype(jnp.bfloat16)
    return jnp.where(live_rows[:, None], joined, jnp.zeros_like(joined))


def any_spec():
    return pl.BlockSpec(memory_space=pl.ANY)


def smem_spec():
    return pl.BlockSpec(memory_space=pltpu.SMEM)


def vmem_spec():
    return pl.BlockSpec(memory_space=pltpu.VMEM)


def hbm_spec():
    return pl.BlockSpec(memory_space=pltpu.HBM)


def pick_kernel(
    cap, page_len, owner_hbm, slot_hbm, prefix_hbm, suffix_hbm, pool_hbm, hidden_hbm, down_hbm, count_ref,
    most_ref, length_ref, live_ref, first_ref, rest_ref, foreign_ref, partial_ref, owner_ref, slot_ref,
    prefix_ref, suffix_ref, pool_ref, hidden_ref, down_ref, pages, lists, table, sems,
):
    n_req = lax.axis_size("req")
    head_idx = lax.axis_index("head")
    req_idx = lax.axis_index("req")
    seq_idx = lax.axis_index("seq")
    n_pages = owner_ref.shape[1]
    pool_pages, pairs, pair_width = pages.shape
    chunk = first_ref.shape[0]
    loads = [
        pltpu.make_async_copy(owner_hbm, owner_ref, sems.at[0]),
        pltpu.make_async_copy(slot_hbm, slot_ref, sems.at[1]),
        pltpu.make_async_copy(pool_hbm, pool_ref, sems.at[2]),
        pltpu.make_async_copy(hidden_hbm, hidden_ref, sems.at[6]),
        pltpu.make_async_copy(down_hbm, down_ref, sems.at[7]),
        pltpu.make_async_copy(prefix_hbm, prefix_ref, sems.at[8]),
        pltpu.make_async_copy(suffix_hbm, suffix_ref, sems.at[9]),
    ]
    for load in loads:
        load.start()
    loads[0].wait()
    loads[1].wait()
    loads[5].wait()
    loads[6].wait()
    length_ref[0] = prefix_ref[req_idx]
    live_ref[0] = suffix_ref[req_idx]
    self_owner = head_idx * n_req + req_idx
    n_owners = table.shape[1]
    for shift in range(n_req):
        for owner in range(n_owners):
            table[shift, owner] = 0
    founds = []
    most = jnp.int32(0)
    for shift in range(n_req):
        request = lax.rem(req_idx + shift, n_req)

        def note(page, found, shift=shift, request=request):
            owner = owner_ref[request, page]
            needed = page * page_len < prefix_ref[request]
            table[shift, owner] += needed.astype(jnp.int32)
            lists[shift, found] = slot_ref[request, page]
            return found + (needed & (owner == self_owner)).astype(jnp.int32)

        founds.append(lax.fori_loop(0, n_pages, note, jnp.int32(0), unroll=8))
        for place in range(n_owners // n_req):
            held = functools.reduce(jnp.add, [table[shift, place * n_req + i] for i in range(n_req)])
            early = jnp.minimum(table[shift, place * n_req + request], chunk)
            most = jnp.maximum(most, held - early)
    for shift in range(n_req):
        count_ref[shift] = table[0, head_idx * n_req + lax.rem(req_idx + n_req - shift, n_req)]
    most_ref[0] = most
    loads[2].wait()
    step = 16
    row = lax.broadcasted_iota(jnp.int32, (step * step, step * step), 0)
    column = lax.broadcasted_iota(jnp.int32, (step * step, step * step), 1)
    swap = ((row // step == column % step) & (row % step == column // step)).astype(jnp.bfloat16)
    for page in range(0, pool_pages, step):
        for pair in range(0, pairs, step):
            rows = jnp.concatenate(
                [
                    pool_ref[page : page + step, (pair + i) * pair_width : (pair + i + 1) * pair_width]
                    for i in range(step)
                ],
                axis=0,
            )
            turned = jnp.dot(swap, rows, preferred_element_type=jnp.float32).astype(jnp.bfloat16)
            pages[page : page + step, pair : pair + step, :] = turned.reshape(step, step, pair_width)

    def send(shift, rank, target, sem):
        slot = jnp.where(rank < founds[shift], lists[shift, rank], 0)
        pltpu.make_async_copy(pages.at[slot], target, sem).start()

    for rank in range(cap):
        if rank < chunk:
            send(0, rank, first_ref.at[rank], sems.at[3])
        else:
            send(0, rank, rest_ref.at[rank - chunk], sems.at[4])
    half_cap = foreign_ref.shape[1]
    for shift in range(1, n_req):
        for j in range(half_cap):
            send(shift, seq_idx * half_cap + j, foreign_ref.at[shift - 1, j], sems.at[5])
    loads[3].wait()
    loads[4].wait()
    partial_ref[...] = lax.dot_general(
        hidden_ref[...], down_ref[...], (((1,), (1,)), ((), ())), preferred_element_type=jnp.float32
    )
    pltpu.make_async_copy(first_ref, first_ref, sems.at[3]).wait()
    if cap > chunk:
        pltpu.make_async_copy(rest_ref, rest_ref, sems.at[4]).wait()
    pltpu.make_async_copy(foreign_ref, foreign_ref, sems.at[5]).wait()


def pick_pages(
    page_owner, page_slot, prefix_len, suffix_len, page_pool, hidden, down,
    cap, chunk, n_head, n_req, n_seq, pairs,
):
    pool_pages, page_width = page_pool.shape
    page = (pairs, page_width // pairs)
    return pl.pallas_call(
        functools.partial(pick_kernel, cap, 2 * pairs),
        out_shape=(
            jax.ShapeDtypeStruct((n_req,), jnp.int32),
            jax.ShapeDtypeStruct((1,), jnp.int32),
            jax.ShapeDtypeStruct((1,), jnp.int32),
            jax.ShapeDtypeStruct((1,), jnp.int32),
            jax.ShapeDtypeStruct((chunk, *page), jnp.bfloat16),
            jax.ShapeDtypeStruct((max(1, cap - chunk), *page), jnp.bfloat16),
            jax.ShapeDtypeStruct((n_req - 1, cap // n_seq, *page), jnp.bfloat16),
            jax.ShapeDtypeStruct((hidden.shape[0], down.shape[0]), jnp.float32),
        ),
        in_specs=[any_spec()] * 4 + [hbm_spec()] * 3,
        out_specs=(smem_spec(), smem_spec(), smem_spec(), smem_spec(), hbm_spec(), hbm_spec(), hbm_spec(), vmem_spec()),
        scratch_shapes=[
            pltpu.SMEM(page_owner.shape, jnp.int32),
            pltpu.SMEM(page_slot.shape, jnp.int32),
            pltpu.SMEM(prefix_len.shape, jnp.int32),
            pltpu.SMEM(suffix_len.shape, jnp.int32),
            pltpu.VMEM((pool_pages, page_width), jnp.bfloat16),
            pltpu.VMEM(hidden.shape, jnp.bfloat16),
            pltpu.VMEM(down.shape, jnp.bfloat16),
            pltpu.VMEM((pool_pages, *page), jnp.bfloat16),
            pltpu.SMEM((n_req, cap + 1), jnp.int32),
            pltpu.SMEM((n_req, n_head * n_req), jnp.int32),
            pltpu.SemaphoreType.DMA((10,)),
        ],
        compiler_params=pltpu.CompilerParams(vmem_limit_bytes=60 * MIB),
        cost_estimate=pl.CostEstimate(flops=10**9, bytes_accessed=6 * 10**6, transcendentals=0),
        name="pick_pages",
    )(page_owner, page_slot, prefix_len, suffix_len, page_pool, hidden, down)


def join_kernel(chunk, cap, count_ref, rest_ref, mine_ref, other_ref, *refs):
    n_req = count_ref.shape[0]
    targets, sems = refs[:-1], refs[-1]
    seq_idx = lax.axis_index("seq")
    half_cap = mine_ref.shape[1]
    excess = jnp.maximum(count_ref[0] - chunk, 0)
    j = 0
    for part, target in enumerate(targets):
        for place in range(target.shape[0]):

            def fetch(condition, source, target=target, place=place, part=part):
                @pl.when(condition)
                def _():
                    pltpu.make_async_copy(source, target.at[place], sems.at[part]).start()

            rank = jnp.int32(j)
            taken = rank < excess
            if cap > chunk:
                fetch(taken, rest_ref.at[jnp.minimum(rank, cap - chunk - 1)])
            rank = rank - excess
            for shift in range(1, n_req):
                here = jnp.logical_not(taken) & (rank < count_ref[shift])
                half = rank // half_cap
                slot = jnp.clip(rank - half * half_cap, 0, half_cap - 1)
                fetch(here & (half == seq_idx), mine_ref.at[shift - 1, slot])
                fetch(here & (half != seq_idx), other_ref.at[shift - 1, slot])
                taken = taken | here
                rank = rank - count_ref[shift]
            fetch(jnp.logical_not(taken), mine_ref.at[0, 0])
            j += 1
    for part, target in enumerate(targets):
        pltpu.make_async_copy(target, target, sems.at[part]).wait()


def join_pages(counts, rest, mine, other, chunk, cap, sizes):
    return pl.pallas_call(
        functools.partial(join_kernel, chunk, cap),
        out_shape=tuple(jax.ShapeDtypeStruct((size, *rest.shape[1:]), jnp.bfloat16) for size in sizes),
        in_specs=[smem_spec()] + [hbm_spec()] * 3,
        out_specs=(vmem_spec(),) * len(sizes),
        scratch_shapes=[pltpu.SemaphoreType.DMA((len(sizes),))],
        compiler_params=pltpu.CompilerParams(vmem_limit_bytes=10 * MIB),
        cost_estimate=pl.CostEstimate(flops=0, bytes_accessed=3 * 10**6, transcendentals=0),
        name="join_pages",
    )(counts, rest, mine, other)


def plan_kernel(page_len, chunk, owner_ref, prefix_ref, limit_ref):
    n_head = lax.axis_size("head")
    n_req = lax.axis_size("req")
    head_idx = lax.axis_index("head")
    req_idx = lax.axis_index("req")
    upward = 2 * lax.axis_index("seq") - 1
    n = owner_ref.shape[1]
    prefix = prefix_ref[req_idx]
    diagonal = lax.broadcasted_iota(jnp.int32, (n, n), 0) == lax.broadcasted_iota(jnp.int32, (n, n), 1)

    def column(values):
        return jnp.sum(jnp.where(diagonal, values, 0), axis=1, keepdims=True)

    owner = owner_ref[pl.ds(req_idx, 1), :]
    place = jnp.zeros_like(owner)
    for head in range(1, n_head):
        place = place + (owner >= head * n_req).astype(jnp.int32)
    shift = req_idx - (owner - place * n_req)
    shift = jnp.where(shift < 0, shift + n_req, shift)
    order = lax.broadcasted_iota(jnp.int32, (1, n), 1)
    needed = (order * page_len < prefix).astype(jnp.int32)
    key = shift * n + order
    together = (column(place) == place) & (column(needed) > 0)
    rank = jnp.sum((together & (column(key) < key)).astype(jnp.int32), axis=0, keepdims=True)
    held = jnp.sum((together & (column(shift) == 0)).astype(jnp.int32), axis=0, keepdims=True)
    early = (shift == 0) & (rank < chunk)
    within = jnp.where(early, rank, chunk + rank - jnp.minimum(held, chunk))
    away = place - head_idx
    distance = jnp.abs(away)
    origin = jnp.where(away * upward > 0, 2 * distance - 1, 2 * distance)
    origins = 2 * n_head - 1
    slot = jnp.where(
        within < chunk,
        origin * chunk + within,
        jnp.where(
            within < 3 * chunk,
            (origins + 2 * origin) * chunk + within - chunk,
            (3 * origins + origin) * chunk + within - 3 * chunk,
        ),
    )
    slot = column(jnp.where(needed > 0, slot, -1))
    tokens = column(jnp.clip(prefix - order * page_len, 0, page_len))
    lane = lax.broadcasted_iota(jnp.int32, (n, limit_ref.shape[1]), 1)
    limit_ref[...] = jnp.sum(jnp.where(lane == slot, tokens, 0), axis=0, keepdims=True)


def plan_blocks(page_owner, prefix_len, n_head, chunk, page_len):
    return pl.pallas_call(
        functools.partial(plan_kernel, page_len, chunk),
        out_shape=jax.ShapeDtypeStruct((1, 4 * (2 * n_head - 1) * chunk), jnp.int32),
        in_specs=[vmem_spec(), smem_spec()],
        out_specs=vmem_spec(),
        cost_estimate=pl.CostEstimate(flops=10**4, bytes_accessed=10**4, transcendentals=0),
        name="plan_blocks",
    )(page_owner, prefix_len)


def over_groups(most):
    n_groups = lax.axis_size("groups")
    passed = most
    for _ in range(n_groups - 1):
        passed = lax.ppermute(passed, "groups", [(i, (i + 1) % n_groups) for i in range(n_groups)])
        most = jnp.maximum(most, passed)
    return most[0]


def query_kernel(query_hbm, up_hbm, cosine_ref, sine_ref, out_ref, query_ref, up_ref, sems):
    loads = [
        pltpu.make_async_copy(query_hbm, query_ref, sems.at[0]),
        pltpu.make_async_copy(up_hbm, up_ref, sems.at[1]),
    ]
    for load in loads:
        load.start()
    for load in loads:
        load.wait()
    heads, nope_width, latent_width = up_ref.shape
    half_len, width = query_ref.shape
    query_width = width // heads
    half_rope = cosine_ref.shape[0]
    key_width = latent_width + 2 * half_rope
    for head in range(heads):
        part = slice(head * half_len, (head + 1) * half_len)
        both = query_ref[:, head * query_width : (head + 1) * query_width]
        latent = lax.dot_general(
            up_ref[head], both[:, :nope_width], (((0,), (1,)), ((), ())), preferred_element_type=jnp.float32
        )
        out_ref[:latent_width, part] = latent.astype(jnp.bfloat16)
        turned = both[:, nope_width:].astype(jnp.float32).T
        low, high = turned[:half_rope], turned[half_rope:]
        out_ref[latent_width : latent_width + half_rope, part] = (
            low * cosine_ref[...] - high * sine_ref[...]
        ).astype(jnp.bfloat16)
        out_ref[latent_width + half_rope : key_width, part] = (
            low * sine_ref[...] + high * cosine_ref[...]
        ).astype(jnp.bfloat16)
    rest = out_ref.shape[0] - key_width
    row = lax.broadcasted_iota(jnp.int32, (rest, out_ref.shape[1]), 0)
    out_ref[key_width:, :] = (row == 0).astype(jnp.bfloat16)


def turn_queries(queries, w_uk, cosine_table, sine_table, key_rows):
    heads, nope_width, latent_width = w_uk.shape
    rows = heads * queries.shape[0]
    return pl.pallas_call(
        query_kernel,
        out_shape=jax.ShapeDtypeStruct((key_rows, rows), jnp.bfloat16),
        in_specs=[any_spec()] * 2 + [vmem_spec()] * 2,
        out_specs=vmem_spec(),
        scratch_shapes=[
            pltpu.VMEM(queries.shape, jnp.bfloat16),
            pltpu.VMEM(w_uk.shape, jnp.bfloat16),
            pltpu.SemaphoreType.DMA((2,)),
        ],
        compiler_params=pltpu.CompilerParams(vmem_limit_bytes=60 * MIB),
        cost_estimate=pl.CostEstimate(
            flops=2 * rows * nope_width * latent_width, bytes_accessed=3 * 10**6, transcendentals=0
        ),
        name="turn_queries",
    )(queries, w_uk, cosine_table, sine_table)


def score_block(keys, queries_ref, target, note, highest, weight_sum, tile, scale, bias=None):
    rows = queries_ref.shape[1]
    for start in range(0, rows, tile):
        part = slice(start, start + tile)
        scores = jnp.dot(keys[...], queries_ref[:, part], preferred_element_type=jnp.float32) * scale
        if bias is not None:
            scores = scores + bias
        old = highest[:, part]
        new = jnp.maximum(old, jnp.max(scores, axis=0, keepdims=True))
        weights = jnp.exp2(scores - new)
        highest[:, part] = new
        weight_sum[:, part] = weight_sum[:, part] * jnp.exp2(old - new) + jnp.sum(
            weights, axis=0, keepdims=True
        )
        target[:, part] = weights
        note(part, new)


def block_limits(limit_ref, block, chunk):
    return [limit_ref[0, block * chunk + j] for j in range(chunk)]


def any_token(limit_ref, block, chunk):
    return functools.reduce(jnp.maximum, block_limits(limit_ref, block, chunk)) > 0


def load_block(block_ref, keys, limits, key_width):
    chunk, pairs, pair_width = block_ref.shape
    pair_rows = chunk * pairs
    page_rows = block_ref[...].reshape(pair_rows, pair_width)
    keys[:pair_rows, :key_width] = page_rows[:, :key_width]
    keys[pair_rows:, :key_width] = page_rows[:, key_width:]
    shape = (2 * pair_rows, keys.shape[1] - key_width)
    row = lax.broadcasted_iota(jnp.int32, shape, 0)
    pair_row = lax.rem(row, pair_rows)
    token = 2 * lax.rem(pair_row, pairs) + row // pair_rows
    limit = jnp.zeros_like(row)
    for j, value in enumerate(limits):
        limit = jnp.where(pair_row // pairs == j, value, limit)
    masked = (lax.broadcasted_iota(jnp.int32, shape, 1) == 0) & (token >= limit)
    keys[:, key_width:] = jnp.where(masked, MASKED, 0.0).astype(jnp.bfloat16)


def turn_values(keys, latent_width):
    return keys[:, :latent_width].T


def near_bias(n_keys, half_len, tile, live):
    seq_idx = lax.axis_index("seq")
    place = lax.broadcasted_iota(jnp.int32, (n_keys, tile), 0)
    query = lax.rem(lax.broadcasted_iota(jnp.int32, (n_keys, tile), 1), half_len) + seq_idx * half_len
    allowed = (place <= query) & (place < live)
    return jnp.where(allowed, 0.0, -jnp.inf)


def score_kernel(shape, base, n_sources, first, near, limit_ref, queries_ref, *refs):
    tile, scale, chunk, key_width = shape
    refs = list(refs)
    if not first:
        marks_in, sum_in, high_in = [refs.pop(0) for _ in range(3)]
        refs.pop(0), refs.pop(0)
    if near:
        live_ref, suffix_ref = refs.pop(0), refs.pop(0)
    sources = [refs.pop(0) for _ in range(n_sources)]
    weights_hbm, values_hbm, marks, weight_sum, highest = [refs.pop(0) for _ in range(5)]
    if near:
        near_weights, near_values, near_mark = [refs.pop(0) for _ in range(3)]
    blocks, keys, weights, values, load_sems, weight_sems, value_sems = [refs.pop(0) for _ in range(7)]
    n_blocks = blocks.shape[0]
    latent_width = values.shape[1]
    index = 0
    for source in sources:
        for i in range(source.shape[0] // chunk):
            pltpu.make_async_copy(
                source.at[i * chunk : (i + 1) * chunk], blocks.at[index], load_sems.at[index]
            ).start()
            index += 1
    if first:
        marks[...] = jnp.zeros_like(marks)
        weight_sum[...] = jnp.zeros_like(weight_sum)
        highest[...] = jnp.full_like(highest, LOWEST)
    else:
        marks[...] = marks_in[...]
        weight_sum[...] = sum_in[...]
        highest[...] = high_in[...]

    def stores(block):
        return (
            pltpu.make_async_copy(weights.at[block], weights_hbm.at[base + block], weight_sems.at[block]),
            pltpu.make_async_copy(values.at[block], values_hbm.at[base + block], value_sems.at[block]),
        )

    def one_block(block, carry):
        pltpu.make_async_copy(blocks.at[block], blocks.at[block], load_sems.at[block]).wait()

        @pl.when(any_token(limit_ref, base + block, chunk))
        def _():
            load_block(blocks.at[block], keys, block_limits(limit_ref, base + block, chunk), key_width)

            def note(part, new):
                marks[pl.ds(base + block, 1), part] = new

            score_block(
                keys, queries_ref, weights.at[block], note, highest, weight_sum, tile, scale
            )
            values[block] = turn_values(keys, latent_width)
            for copy in stores(block):
                copy.start()

        return carry

    lax.fori_loop(0, n_blocks, one_block, 0)
    if near:
        near_keys = refs.pop(0)
        n_near = suffix_ref.shape[0]
        near_keys[:, key_width:] = jnp.zeros_like(near_keys[:, key_width:])
        near_keys[:, :key_width] = suffix_ref[...]

        def note_near(part, new):
            near_mark[:, part] = new

        score_block(
            near_keys, queries_ref, near_weights, note_near, highest, weight_sum, tile, scale,
            near_bias(n_near, n_near // lax.axis_size("seq"), tile, live_ref[0]),
        )
        near_values[...] = turn_values(near_keys, latent_width)

    def one_wait(block, carry):
        @pl.when(any_token(limit_ref, base + block, chunk))
        def _():
            for copy in stores(block):
                copy.wait()

        return carry

    lax.fori_loop(0, n_blocks, one_wait, 0)


def score_part(base, total, limits, queries, sources, state, shape, latent_width, near=None):
    tile, scale, chunk, key_width = shape
    width, rows = queries.shape
    _, pairs, pair_width = sources[0].shape
    block_keys = 2 * chunk * pairs
    n_blocks = sum(s.shape[0] for s in sources) // chunk
    row = jax.ShapeDtypeStruct((1, rows), jnp.float32)
    out_shape = [
        jax.ShapeDtypeStruct((total, block_keys, rows), jnp.float32),
        jax.ShapeDtypeStruct((total, latent_width, block_keys), jnp.bfloat16),
        jax.ShapeDtypeStruct((total, rows), jnp.float32),
        row,
        row,
    ]
    out_specs = [hbm_spec(), hbm_spec(), vmem_spec(), vmem_spec(), vmem_spec()]
    operands = [limits, queries]
    specs = [smem_spec(), vmem_spec()]
    aliases = {}
    if state is not None:
        operands += [state[2], state[3], state[4], state[0], state[1]]
        specs += [vmem_spec()] * 3 + [hbm_spec()] * 2
        aliases = {5: 0, 6: 1}
    scratch = [
        pltpu.VMEM((n_blocks, chunk, pairs, pair_width), jnp.bfloat16),
        pltpu.VMEM((block_keys, width), jnp.bfloat16),
        pltpu.VMEM((n_blocks, block_keys, rows), jnp.float32),
        pltpu.VMEM((n_blocks, latent_width, block_keys), jnp.bfloat16),
        pltpu.SemaphoreType.DMA((n_blocks,)),
        pltpu.SemaphoreType.DMA((n_blocks,)),
        pltpu.SemaphoreType.DMA((n_blocks,)),
    ]
    if near is not None:
        near_keys = near[-1].shape[0]
        operands += list(near)
        specs += [smem_spec(), vmem_spec()]
        out_shape += [
            jax.ShapeDtypeStruct((near_keys, rows), jnp.float32),
            jax.ShapeDtypeStruct((latent_width, near_keys), jnp.bfloat16),
            row,
        ]
        out_specs += [vmem_spec()] * 3
        scratch.append(pltpu.VMEM((near_keys, width), jnp.bfloat16))
    operands += list(sources)
    specs += [hbm_spec()] * len(sources)
    work = n_blocks * block_keys * rows // 2
    return pl.pallas_call(
        functools.partial(score_kernel, shape, base, len(sources), state is None, near is not None),
        out_shape=tuple(out_shape),
        in_specs=specs,
        out_specs=tuple(out_specs),
        scratch_shapes=scratch,
        input_output_aliases=aliases,
        compiler_params=pltpu.CompilerParams(vmem_limit_bytes=54 * MIB),
        cost_estimate=pl.CostEstimate(
            flops=work, bytes_accessed=10**5, transcendentals=0
        ),
        name="score_part",
    )(*operands)


def finish_kernel(
    shape, depth, n_blocks, n_sources, limit_ref, queries_ref, marks, sum_in, high_in,
    near_weights, near_values, near_mark, live_ref, up_ref, weights_hbm, values_hbm, *refs,
):
    tile, scale, chunk, key_width = shape
    sources, refs = refs[:n_sources], refs[n_sources:]
    (
        out_ref, weight_sum, highest, total, blocks, keys, last_weights, last_values, last_marks,
        weights, values, used, load_sems, weight_sems, value_sems,
    ) = refs
    rows = queries_ref.shape[1]
    latent_width = total.shape[0]
    n_last = blocks.shape[0]
    index = 0
    for source in sources:
        for i in range(source.shape[0] // chunk):
            pltpu.make_async_copy(
                source.at[i * chunk : (i + 1) * chunk], blocks.at[index], load_sems.at[index]
            ).start()
            index += 1

    def list_block(block, count):
        used[count] = block
        return count + any_token(limit_ref, block, chunk).astype(jnp.int32)

    n_used = lax.fori_loop(0, n_blocks, list_block, jnp.int32(0))

    def fetches(number):
        place = lax.rem(number, depth)
        return (
            pltpu.make_async_copy(weights_hbm.at[used[number]], weights.at[place], weight_sems.at[place]),
            pltpu.make_async_copy(values_hbm.at[used[number]], values.at[place], value_sems.at[place]),
        )

    def fetch(number):
        @pl.when(number < n_used)
        def _():
            for copy in fetches(number):
                copy.start()

    for number in range(depth):
        fetch(jnp.int32(number))
    weight_sum[...] = sum_in[...]
    highest[...] = high_in[...]
    last_marks[...] = jnp.zeros_like(last_marks)

    def one_score(block, carry):
        pltpu.make_async_copy(blocks.at[block], blocks.at[block], load_sems.at[block]).wait()

        @pl.when(any_token(limit_ref, n_blocks + block, chunk))
        def _():
            load_block(blocks.at[block], keys, block_limits(limit_ref, n_blocks + block, chunk), key_width)

            def note(part, new):
                last_marks[pl.ds(block, 1), part] = new

            score_block(
                keys, queries_ref, last_weights.at[block], note, highest, weight_sum, tile, scale
            )
            last_values[block] = turn_values(keys, latent_width)

        return carry

    lax.fori_loop(0, n_last, one_score, 0)

    def add_block(weight_block, value_block, mark, begin=False):
        for start in range(0, rows, tile):
            part = slice(start, start + tile)
            factor = jnp.exp2(mark[:, part] - highest[:, part]) / weight_sum[:, part]
            added = jnp.dot(
                value_block[...],
                (weight_block[:, part] * factor).astype(jnp.bfloat16),
                preferred_element_type=jnp.float32,
            )
            total[:, part] = added if begin else total[:, part] + added

    add_block(near_weights, near_values, near_mark, begin=True)

    def one_add(number, carry):
        for copy in fetches(number):
            copy.wait()
        place = lax.rem(number, depth)
        add_block(weights.at[place], values.at[place], marks.at[pl.ds(used[number], 1)])
        fetch(number + depth)
        return carry

    lax.fori_loop(0, n_used, one_add, 0)

    def one_last(block, carry):
        @pl.when(any_token(limit_ref, n_blocks + block, chunk))
        def _():
            add_block(last_weights.at[block], last_values.at[block], last_marks.at[pl.ds(block, 1)])

        return carry

    lax.fori_loop(0, n_last, one_last, 0)
    heads, _, value_width = up_ref.shape
    half_len = out_ref.shape[0]
    steps = lax.broadcasted_iota(jnp.int32, (half_len, value_width), 0)
    steps = steps + lax.axis_index("seq") * half_len
    for head in range(heads):
        latent = total[:, head * half_len : (head + 1) * half_len].astype(jnp.bfloat16)
        raised = lax.dot_general(
            latent, up_ref[head], (((0,), (0,)), ((), ())), preferred_element_type=jnp.float32
        )
        out_ref[:, head * value_width : (head + 1) * value_width] = jnp.where(
            steps < live_ref[0], raised, 0.0
        ).astype(jnp.bfloat16)


def finish(n_blocks, limits, queries, state, near_state, sources, live, up_weight, half_len, shape):
    tile, scale, chunk, key_width = shape
    weights, values, marks, weight_sum, highest = state
    width, rows = queries.shape
    _, latent_width, block_keys = values.shape
    _, pairs, pair_width = sources[0].shape
    heads, _, value_width = up_weight.shape
    depth = 4
    n_last = sum(s.shape[0] for s in sources) // chunk
    row = pltpu.VMEM((1, rows), jnp.float32)
    work = (n_blocks // 2 + n_last) * block_keys * rows
    return pl.pallas_call(
        functools.partial(finish_kernel, shape, depth, n_blocks, len(sources)),
        out_shape=jax.ShapeDtypeStruct((half_len, heads * value_width), jnp.bfloat16),
        in_specs=[smem_spec()]
        + [vmem_spec()] * 7
        + [smem_spec(), vmem_spec()]
        + [hbm_spec()] * (2 + len(sources)),
        out_specs=vmem_spec(),
        scratch_shapes=[
            row,
            row,
            pltpu.VMEM((latent_width, rows), jnp.float32),
            pltpu.VMEM((n_last, chunk, pairs, pair_width), jnp.bfloat16),
            pltpu.VMEM((block_keys, width), jnp.bfloat16),
            pltpu.VMEM((n_last, block_keys, rows), jnp.float32),
            pltpu.VMEM((n_last, latent_width, block_keys), jnp.bfloat16),
            pltpu.VMEM((n_last, rows), jnp.float32),
            pltpu.VMEM((depth, block_keys, rows), jnp.float32),
            pltpu.VMEM((depth, latent_width, block_keys), jnp.bfloat16),
            pltpu.SMEM((n_blocks + depth + 1,), jnp.int32),
            pltpu.SemaphoreType.DMA((n_last,)),
            pltpu.SemaphoreType.DMA((depth,)),
            pltpu.SemaphoreType.DMA((depth,)),
        ],
        compiler_params=pltpu.CompilerParams(vmem_limit_bytes=54 * MIB),
        cost_estimate=pl.CostEstimate(
            flops=2 * work * latent_width, bytes_accessed=3 * 10**7, transcendentals=work // 4
        ),
        name="finish",
    )(
        limits, queries, marks, weight_sum, highest, *near_state, live, up_weight,
        weights, values, *sources,
    )


def local(
    queries,
    hidden,
    w_dkv,
    kv_gain,
    w_uk,
    value_up_weight,
    page_pool,
    page_owner,
    page_slot,
    prefix_len,
    suffix_len,
):
    n_head = lax.axis_size("head")
    n_req = lax.axis_size("req")
    n_seq = lax.axis_size("seq")
    head_idx = lax.axis_index("head")
    req_idx = lax.axis_index("req")
    seq_idx = lax.axis_index("seq")
    _, half_len, d_local = hidden.shape
    heads_dev, nope_width, latent_width = w_uk.shape
    lat_width = w_dkv.shape[1]
    rope_width = lat_width - latent_width
    query_width = queries.shape[2] // heads_dev
    page_width = page_pool.shape[1]
    page_len = page_width // lat_width
    pairs = page_len // 2
    pages_req = page_slot.shape[1]
    cap = max(2, 2 * pages_req // (n_head * n_req))
    chunk = n_req * cap // 4
    score_scale = float(query_width) ** (-0.5)

    owner_rows = page_owner[:, :, 0]
    counts, most, my_prefix, live, first, rest, foreign, partial_value = pick_pages(
        owner_rows, page_slot, prefix_len, suffix_len, page_pool, hidden[0], w_dkv.T,
        cap, chunk, n_head, n_req, n_seq, pairs,
    )
    swap_route = [(i, n_seq - 1 - i) for i in range(n_seq)]
    stream_route = []
    for i in range(n_head - 1):
        stream_route.append((i * n_seq, (i + 1) * n_seq))
        stream_route.append(((i + 1) * n_seq + 1, i * n_seq + 1))

    def swap(block):
        return lax.ppermute(block, "seq", swap_route)

    def stream(block):
        return lax.ppermute(block, ("head", "seq"), stream_route)

    positions = my_prefix + seq_idx * half_len + jnp.arange(half_len, dtype=jnp.int32)
    rows = heads_dev * half_len
    half_rope = rope_width // 2
    frequency = 10000.0 ** (-2.0 * jnp.arange(half_rope, dtype=jnp.float32) / rope_width)
    phases = frequency[:, None] * positions.astype(jnp.float32)[None, :]
    q_turned = turn_queries(queries[0], w_uk, jnp.cos(phases), jnp.sin(phases), lat_width + 64)

    arrived = [
        lax.ppermute(foreign[s - 1], "req", [(i, (i + s) % n_req) for i in range(n_req)])
        for s in range(1, n_req)
    ]
    early_steps = [stream(first)]
    share = half_len // n_head
    partials = lax.all_to_all(partial_value, "head", split_axis=0, concat_axis=0, tiled=True)
    summed = jnp.sum(partials.reshape(n_head, share, lat_width), axis=0)
    share_t = seq_idx * half_len + head_idx * share + jnp.arange(share, dtype=jnp.int32)
    latent = finish_latent(summed, my_prefix + share_t, share_t < live, kv_gain, latent_width)
    copies = jnp.concatenate([latent] * n_head, axis=0)
    fresh = lax.all_to_all(copies, "head", split_axis=0, concat_axis=0, tiled=True)
    early_steps[0], fresh = lax.optimization_barrier((early_steps[0], fresh))
    for step in range(1, n_head - 1):
        early_steps.append(stream(early_steps[-1]))
    early_steps = [[block, None] for block in early_steps]
    for step in range(n_head - 2):
        early_steps[step][1] = swap(early_steps[step][0])
    mine = arrived[0][None] if n_req == 2 else jnp.stack(arrived)
    most = over_groups(most)
    mine, fresh, most = lax.optimization_barrier((mine, fresh, most))
    other = swap(mine)
    middle, late = join_pages(counts, rest, mine, other, chunk, cap, (2 * chunk, chunk))

    tile = 256 if rows % 256 == 0 and 256 % half_len == 0 else half_len
    shape = (tile, score_scale * math.log2(math.e), chunk, lat_width)
    last = n_head - 2
    near_state = ()
    extra = 4 + 1 + 2 * last
    total = 1 + 2 * (last + 1) + 2 + 4 * last + extra
    limits = plan_blocks(owner_rows, prefix_len, n_head, chunk, page_len)
    n_blocks = 0
    state = None

    def arrays_of(arrived_steps, steps):
        return [arrived_steps[step][side] for step in steps for side in range(2)]

    def score(arrays, near=None):
        nonlocal n_blocks, state, near_state
        result = score_part(
            n_blocks, total, limits, q_turned, arrays, state, shape, latent_width, near
        )
        state = result[:5]
        near_state = result[5:] or near_state
        n_blocks += sum(a.shape[0] for a in arrays) // chunk

    def tie(block):
        nonlocal state
        block, mark = lax.optimization_barrier((block, state[4]))
        state = (*state[:4], mark)
        return block

    middle, early_steps[last - 1][0] = lax.optimization_barrier((middle, early_steps[last - 1][0]))
    middle_steps = []
    block = stream(middle)
    for step in range(last + 1):
        received = block
        if step == 0:
            score([first] + arrays_of(early_steps, range(last)))
        elif step == 1:
            score(arrays_of(early_steps, [last]) + [middle] + arrays_of(middle_steps, [0]))
        else:
            score(
                arrays_of(middle_steps, [step - 1]), (live, suffix_latent) if step == last else None
            )
        received = tie(received)
        if step == 0:
            early_steps[last][0] = tie(early_steps[last][0])
            early_steps[last][1] = swap(early_steps[last][0])
            opposite = swap(fresh)
            suffix_latent = jnp.where(
                seq_idx == 0,
                jnp.concatenate([fresh, opposite], axis=0),
                jnp.concatenate([opposite, fresh], axis=0),
            )
        if step < last:
            block = stream(received)
        middle_steps.append([received, swap(received)])

    last_arrays = arrays_of(middle_steps, [last])

    def end(blocks, final_arrays, current):
        return finish(
            blocks, limits, q_turned, current, near_state, final_arrays, live, value_up_weight, half_len, shape
        )

    def with_late(_):
        block = stream(late)
        arrays = last_arrays + [late]
        current, blocks = state, n_blocks
        for step in range(last + 1):
            received = block
            current = score_part(
                blocks, total, limits, q_turned, arrays, current, shape, latent_width
            )[:5]
            blocks += sum(a.shape[0] for a in arrays) // chunk
            received, mark = lax.optimization_barrier((received, current[4]))
            current = (*current[:4], mark)
            if step < last:
                block = stream(received)
            arrays = [received, swap(received)]
        return end(blocks, arrays, current)

    def without_late(_):
        return end(n_blocks, last_arrays, state)

    attn_out = lax.cond(most > 2 * chunk, with_late, without_late, 0)
    new_pages = fresh.reshape(1, half_len // page_len, page_len * lat_width)
    return (attn_out[None], new_pages)


def solution(mesh):
    placed = (
        P(("groups", "req"), "seq", "head"),
        P(("groups", "req"), "seq", "head"),
        P("head", None),
        P(),
        P("head", None, None),
        P("head", None, None),
        P(("groups", "head", "req"), None),
        P("groups", None, None),
        P("groups", None),
        P("groups"),
        P("groups"),
    )
    return jax.shard_map(
        local,
        mesh=mesh,
        in_specs=placed,
        out_specs=(P(("groups", "req"), "seq", "head"), P(("groups", "req"), "seq", None)),
        check_vma=False,
    )
```

```python
import functools
import math

import jax
import jax.numpy as jnp
from jax import lax
from jax.experimental import pallas as pl
from jax.experimental.pallas import tpu as pltpu
from jax.sharding import PartitionSpec as P

LOWEST = -1e30
MASKED = -1e38
MIB = 1024 * 1024


def rotate(vector, cosine_table, sine_table):
    half_width = vector.shape[-1] // 2
    first_half = vector[..., :half_width]
    second_half = vector[..., half_width:]
    return jnp.concatenate(
        [
            first_half * cosine_table - second_half * sine_table,
            first_half * sine_table + second_half * cosine_table,
        ],
        axis=-1,
    )


def angles(positions, rope_width):
    half_width = rope_width // 2
    frequency = 10000.0 ** (-2.0 * jnp.arange(half_width, dtype=jnp.float32) / rope_width)
    phases = positions.astype(jnp.float32)[:, None] * frequency[None, :]
    return (jnp.cos(phases), jnp.sin(phases))


def finish_latent(summed, positions, live_rows, kv_gain, latent_width):
    latent_part = summed[:, :latent_width]
    mean_square = jnp.mean(latent_part * latent_part, axis=-1, keepdims=True)
    normed = latent_part * lax.rsqrt(mean_square + 1e-06) * kv_gain
    cosine_table, sine_table = angles(positions, summed.shape[1] - latent_width)
    rotated = rotate(summed[:, latent_width:], cosine_table, sine_table)
    joined = jnp.concatenate([normed, rotated], axis=-1).astype(jnp.bfloat16)
    return jnp.where(live_rows[:, None], joined, jnp.zeros_like(joined))


def any_spec():
    return pl.BlockSpec(memory_space=pl.ANY)


def smem_spec():
    return pl.BlockSpec(memory_space=pltpu.SMEM)


def vmem_spec():
    return pl.BlockSpec(memory_space=pltpu.VMEM)


def hbm_spec():
    return pl.BlockSpec(memory_space=pltpu.HBM)


def pick_kernel(
    cap, page_len, owner_hbm, slot_hbm, prefix_hbm, suffix_hbm, pool_hbm, hidden_hbm, down_hbm, count_ref,
    most_ref, length_ref, live_ref, first_ref, rest_ref, foreign_ref, partial_ref, owner_ref, slot_ref,
    prefix_ref, suffix_ref, pool_ref, hidden_ref, down_ref, pages, lists, table, sems,
):
    n_req = lax.axis_size("req")
    head_idx = lax.axis_index("head")
    req_idx = lax.axis_index("req")
    seq_idx = lax.axis_index("seq")
    n_pages = owner_ref.shape[1]
    pool_pages, pairs, pair_width = pages.shape
    chunk = first_ref.shape[0]
    loads = [
        pltpu.make_async_copy(owner_hbm, owner_ref, sems.at[0]),
        pltpu.make_async_copy(slot_hbm, slot_ref, sems.at[1]),
        pltpu.make_async_copy(pool_hbm, pool_ref, sems.at[2]),
        pltpu.make_async_copy(hidden_hbm, hidden_ref, sems.at[6]),
        pltpu.make_async_copy(down_hbm, down_ref, sems.at[7]),
        pltpu.make_async_copy(prefix_hbm, prefix_ref, sems.at[8]),
        pltpu.make_async_copy(suffix_hbm, suffix_ref, sems.at[9]),
    ]
    for load in loads:
        load.start()
    loads[0].wait()
    loads[1].wait()
    loads[5].wait()
    loads[6].wait()
    length_ref[0] = prefix_ref[req_idx]
    live_ref[0] = suffix_ref[req_idx]
    self_owner = head_idx * n_req + req_idx
    n_owners = table.shape[1]
    for shift in range(n_req):
        for owner in range(n_owners):
            table[shift, owner] = 0
    founds = []
    most = jnp.int32(0)
    for shift in range(n_req):
        request = lax.rem(req_idx + shift, n_req)

        def note(page, found, shift=shift, request=request):
            owner = owner_ref[request, page]
            needed = page * page_len < prefix_ref[request]
            table[shift, owner] += needed.astype(jnp.int32)
            lists[shift, found] = slot_ref[request, page]
            return found + (needed & (owner == self_owner)).astype(jnp.int32)

        founds.append(lax.fori_loop(0, n_pages, note, jnp.int32(0), unroll=8))
        for place in range(n_owners // n_req):
            held = functools.reduce(jnp.add, [table[shift, place * n_req + i] for i in range(n_req)])
            early = jnp.minimum(table[shift, place * n_req + request], chunk)
            most = jnp.maximum(most, held - early)
    for shift in range(n_req):
        count_ref[shift] = table[0, head_idx * n_req + lax.rem(req_idx + n_req - shift, n_req)]
    most_ref[0] = most
    loads[2].wait()
    step = 16
    row = lax.broadcasted_iota(jnp.int32, (step * step, step * step), 0)
    column = lax.broadcasted_iota(jnp.int32, (step * step, step * step), 1)
    swap = ((row // step == column % step) & (row % step == column // step)).astype(jnp.bfloat16)
    for page in range(0, pool_pages, step):
        for pair in range(0, pairs, step):
            rows = jnp.concatenate(
                [
                    pool_ref[page : page + step, (pair + i) * pair_width : (pair + i + 1) * pair_width]
                    for i in range(step)
                ],
                axis=0,
            )
            turned = jnp.dot(swap, rows, preferred_element_type=jnp.float32).astype(jnp.bfloat16)
            pages[page : page + step, pair : pair + step, :] = turned.reshape(step, step, pair_width)

    def send(shift, rank, target, sem):
        slot = jnp.where(rank < founds[shift], lists[shift, rank], 0)
        pltpu.make_async_copy(pages.at[slot], target, sem).start()

    for rank in range(cap):
        if rank < chunk:
            send(0, rank, first_ref.at[rank], sems.at[3])
        else:
            send(0, rank, rest_ref.at[rank - chunk], sems.at[4])
    half_cap = foreign_ref.shape[1]
    for shift in range(1, n_req):
        for j in range(half_cap):
            send(shift, seq_idx * half_cap + j, foreign_ref.at[shift - 1, j], sems.at[5])
    loads[3].wait()
    loads[4].wait()
    partial_ref[...] = lax.dot_general(
        hidden_ref[...], down_ref[...], (((1,), (1,)), ((), ())), preferred_element_type=jnp.float32
    )
    pltpu.make_async_copy(first_ref, first_ref, sems.at[3]).wait()
    if cap > chunk:
        pltpu.make_async_copy(rest_ref, rest_ref, sems.at[4]).wait()
    pltpu.make_async_copy(foreign_ref, foreign_ref, sems.at[5]).wait()


def pick_pages(
    page_owner, page_slot, prefix_len, suffix_len, page_pool, hidden, down,
    cap, chunk, n_head, n_req, n_seq, pairs,
):
    pool_pages, page_width = page_pool.shape
    page = (pairs, page_width // pairs)
    return pl.pallas_call(
        functools.partial(pick_kernel, cap, 2 * pairs),
        out_shape=(
            jax.ShapeDtypeStruct((n_req,), jnp.int32),
            jax.ShapeDtypeStruct((1,), jnp.int32),
            jax.ShapeDtypeStruct((1,), jnp.int32),
            jax.ShapeDtypeStruct((1,), jnp.int32),
            jax.ShapeDtypeStruct((chunk, *page), jnp.bfloat16),
            jax.ShapeDtypeStruct((max(1, cap - chunk), *page), jnp.bfloat16),
            jax.ShapeDtypeStruct((n_req - 1, cap // n_seq, *page), jnp.bfloat16),
            jax.ShapeDtypeStruct((hidden.shape[0], down.shape[0]), jnp.float32),
        ),
        in_specs=[any_spec()] * 4 + [hbm_spec()] * 3,
        out_specs=(smem_spec(), smem_spec(), smem_spec(), smem_spec(), hbm_spec(), hbm_spec(), hbm_spec(), vmem_spec()),
        scratch_shapes=[
            pltpu.SMEM(page_owner.shape, jnp.int32),
            pltpu.SMEM(page_slot.shape, jnp.int32),
            pltpu.SMEM(prefix_len.shape, jnp.int32),
            pltpu.SMEM(suffix_len.shape, jnp.int32),
            pltpu.VMEM((pool_pages, page_width), jnp.bfloat16),
            pltpu.VMEM(hidden.shape, jnp.bfloat16),
            pltpu.VMEM(down.shape, jnp.bfloat16),
            pltpu.VMEM((pool_pages, *page), jnp.bfloat16),
            pltpu.SMEM((n_req, cap + 1), jnp.int32),
            pltpu.SMEM((n_req, n_head * n_req), jnp.int32),
            pltpu.SemaphoreType.DMA((10,)),
        ],
        compiler_params=pltpu.CompilerParams(vmem_limit_bytes=60 * MIB),
        cost_estimate=pl.CostEstimate(flops=10**9, bytes_accessed=6 * 10**6, transcendentals=0),
        name="pick_pages",
    )(page_owner, page_slot, prefix_len, suffix_len, page_pool, hidden, down)


def join_kernel(chunk, cap, count_ref, rest_ref, mine_ref, other_ref, *refs):
    n_req = count_ref.shape[0]
    targets, sems = refs[:-1], refs[-1]
    seq_idx = lax.axis_index("seq")
    half_cap = mine_ref.shape[1]
    excess = jnp.maximum(count_ref[0] - chunk, 0)
    j = 0
    for part, target in enumerate(targets):
        for place in range(target.shape[0]):

            def fetch(condition, source, target=target, place=place, part=part):
                @pl.when(condition)
                def _():
                    pltpu.make_async_copy(source, target.at[place], sems.at[part]).start()

            rank = jnp.int32(j)
            taken = rank < excess
            if cap > chunk:
                fetch(taken, rest_ref.at[jnp.minimum(rank, cap - chunk - 1)])
            rank = rank - excess
            for shift in range(1, n_req):
                here = jnp.logical_not(taken) & (rank < count_ref[shift])
                half = rank // half_cap
                slot = jnp.clip(rank - half * half_cap, 0, half_cap - 1)
                fetch(here & (half == seq_idx), mine_ref.at[shift - 1, slot])
                fetch(here & (half != seq_idx), other_ref.at[shift - 1, slot])
                taken = taken | here
                rank = rank - count_ref[shift]
            fetch(jnp.logical_not(taken), mine_ref.at[0, 0])
            j += 1
    for part, target in enumerate(targets):
        pltpu.make_async_copy(target, target, sems.at[part]).wait()


def join_pages(counts, rest, mine, other, chunk, cap, sizes):
    return pl.pallas_call(
        functools.partial(join_kernel, chunk, cap),
        out_shape=tuple(jax.ShapeDtypeStruct((size, *rest.shape[1:]), jnp.bfloat16) for size in sizes),
        in_specs=[smem_spec()] + [hbm_spec()] * 3,
        out_specs=(vmem_spec(),) * len(sizes),
        scratch_shapes=[pltpu.SemaphoreType.DMA((len(sizes),))],
        compiler_params=pltpu.CompilerParams(vmem_limit_bytes=10 * MIB),
        cost_estimate=pl.CostEstimate(flops=0, bytes_accessed=3 * 10**6, transcendentals=0),
        name="join_pages",
    )(counts, rest, mine, other)


def plan_kernel(page_len, chunk, owner_ref, prefix_ref, limit_ref):
    n_head = lax.axis_size("head")
    n_req = lax.axis_size("req")
    head_idx = lax.axis_index("head")
    req_idx = lax.axis_index("req")
    upward = 2 * lax.axis_index("seq") - 1
    n = owner_ref.shape[1]
    prefix = prefix_ref[req_idx]
    diagonal = lax.broadcasted_iota(jnp.int32, (n, n), 0) == lax.broadcasted_iota(jnp.int32, (n, n), 1)

    def column(values):
        return jnp.sum(jnp.where(diagonal, values, 0), axis=1, keepdims=True)

    owner = owner_ref[pl.ds(req_idx, 1), :]
    place = jnp.zeros_like(owner)
    for head in range(1, n_head):
        place = place + (owner >= head * n_req).astype(jnp.int32)
    shift = req_idx - (owner - place * n_req)
    shift = jnp.where(shift < 0, shift + n_req, shift)
    order = lax.broadcasted_iota(jnp.int32, (1, n), 1)
    needed = (order * page_len < prefix).astype(jnp.int32)
    key = shift * n + order
    together = (column(place) == place) & (column(needed) > 0)
    rank = jnp.sum((together & (column(key) < key)).astype(jnp.int32), axis=0, keepdims=True)
    held = jnp.sum((together & (column(shift) == 0)).astype(jnp.int32), axis=0, keepdims=True)
    early = (shift == 0) & (rank < chunk)
    within = jnp.where(early, rank, chunk + rank - jnp.minimum(held, chunk))
    away = place - head_idx
    distance = jnp.abs(away)
    origin = jnp.where(away * upward > 0, 2 * distance - 1, 2 * distance)
    origins = 2 * n_head - 1
    slot = jnp.where(
        within < chunk,
        origin * chunk + within,
        jnp.where(
            within < 3 * chunk,
            (origins + 2 * origin) * chunk + within - chunk,
            (3 * origins + origin) * chunk + within - 3 * chunk,
        ),
    )
    slot = column(jnp.where(needed > 0, slot, -1))
    tokens = column(jnp.clip(prefix - order * page_len, 0, page_len))
    lane = lax.broadcasted_iota(jnp.int32, (n, limit_ref.shape[1]), 1)
    limit_ref[...] = jnp.sum(jnp.where(lane == slot, tokens, 0), axis=0, keepdims=True)


def plan_blocks(page_owner, prefix_len, n_head, chunk, page_len):
    return pl.pallas_call(
        functools.partial(plan_kernel, page_len, chunk),
        out_shape=jax.ShapeDtypeStruct((1, 4 * (2 * n_head - 1) * chunk), jnp.int32),
        in_specs=[vmem_spec(), smem_spec()],
        out_specs=vmem_spec(),
        cost_estimate=pl.CostEstimate(flops=10**4, bytes_accessed=10**4, transcendentals=0),
        name="plan_blocks",
    )(page_owner, prefix_len)


def over_groups(most):
    n_groups = lax.axis_size("groups")
    passed = most
    for _ in range(n_groups - 1):
        passed = lax.ppermute(passed, "groups", [(i, (i + 1) % n_groups) for i in range(n_groups)])
        most = jnp.maximum(most, passed)
    return most[0]


def query_kernel(query_hbm, up_hbm, cosine_ref, sine_ref, out_ref, query_ref, up_ref, sems):
    loads = [
        pltpu.make_async_copy(query_hbm, query_ref, sems.at[0]),
        pltpu.make_async_copy(up_hbm, up_ref, sems.at[1]),
    ]
    for load in loads:
        load.start()
    for load in loads:
        load.wait()
    heads, nope_width, latent_width = up_ref.shape
    half_len, width = query_ref.shape
    query_width = width // heads
    half_rope = cosine_ref.shape[0]
    key_width = latent_width + 2 * half_rope
    for head in range(heads):
        part = slice(head * half_len, (head + 1) * half_len)
        both = query_ref[:, head * query_width : (head + 1) * query_width]
        latent = lax.dot_general(
            up_ref[head], both[:, :nope_width], (((0,), (1,)), ((), ())), preferred_element_type=jnp.float32
        )
        out_ref[:latent_width, part] = latent.astype(jnp.bfloat16)
        turned = both[:, nope_width:].astype(jnp.float32).T
        low, high = turned[:half_rope], turned[half_rope:]
        out_ref[latent_width : latent_width + half_rope, part] = (
            low * cosine_ref[...] - high * sine_ref[...]
        ).astype(jnp.bfloat16)
        out_ref[latent_width + half_rope : key_width, part] = (
            low * sine_ref[...] + high * cosine_ref[...]
        ).astype(jnp.bfloat16)
    rest = out_ref.shape[0] - key_width
    row = lax.broadcasted_iota(jnp.int32, (rest, out_ref.shape[1]), 0)
    out_ref[key_width:, :] = (row == 0).astype(jnp.bfloat16)


def turn_queries(queries, w_uk, cosine_table, sine_table, key_rows):
    heads, nope_width, latent_width = w_uk.shape
    rows = heads * queries.shape[0]
    return pl.pallas_call(
        query_kernel,
        out_shape=jax.ShapeDtypeStruct((key_rows, rows), jnp.bfloat16),
        in_specs=[any_spec()] * 2 + [vmem_spec()] * 2,
        out_specs=vmem_spec(),
        scratch_shapes=[
            pltpu.VMEM(queries.shape, jnp.bfloat16),
            pltpu.VMEM(w_uk.shape, jnp.bfloat16),
            pltpu.SemaphoreType.DMA((2,)),
        ],
        compiler_params=pltpu.CompilerParams(vmem_limit_bytes=60 * MIB),
        cost_estimate=pl.CostEstimate(
            flops=2 * rows * nope_width * latent_width, bytes_accessed=3 * 10**6, transcendentals=0
        ),
        name="turn_queries",
    )(queries, w_uk, cosine_table, sine_table)


def score_block(keys, queries_ref, target, note, highest, weight_sum, tile, scale, bias=None):
    rows = queries_ref.shape[1]
    for start in range(0, rows, tile):
        part = slice(start, start + tile)
        scores = jnp.dot(keys[...], queries_ref[:, part], preferred_element_type=jnp.float32) * scale
        if bias is not None:
            scores = scores + bias
        old = highest[:, part]
        new = jnp.maximum(old, jnp.max(scores, axis=0, keepdims=True))
        weights = jnp.exp2(scores - new)
        highest[:, part] = new
        weight_sum[:, part] = weight_sum[:, part] * jnp.exp2(old - new) + jnp.sum(
            weights, axis=0, keepdims=True
        )
        target[:, part] = weights
        note(part, new)


def block_limits(limit_ref, block, chunk):
    return [limit_ref[0, block * chunk + j] for j in range(chunk)]


def any_token(limit_ref, block, chunk):
    return functools.reduce(jnp.maximum, block_limits(limit_ref, block, chunk)) > 0


def load_block(block_ref, keys, limits, key_width):
    chunk, pairs, pair_width = block_ref.shape
    pair_rows = chunk * pairs
    page_rows = block_ref[...].reshape(pair_rows, pair_width)
    keys[:pair_rows, :key_width] = page_rows[:, :key_width]
    keys[pair_rows:, :key_width] = page_rows[:, key_width:]
    shape = (2 * pair_rows, keys.shape[1] - key_width)
    row = lax.broadcasted_iota(jnp.int32, shape, 0)
    pair_row = lax.rem(row, pair_rows)
    token = 2 * lax.rem(pair_row, pairs) + row // pair_rows
    limit = jnp.zeros_like(row)
    for j, value in enumerate(limits):
        limit = jnp.where(pair_row // pairs == j, value, limit)
    masked = (lax.broadcasted_iota(jnp.int32, shape, 1) == 0) & (token >= limit)
    keys[:, key_width:] = jnp.where(masked, MASKED, 0.0).astype(jnp.bfloat16)


def turn_values(keys, latent_width):
    return keys[:, :latent_width].T


def near_bias(n_keys, half_len, tile, live):
    seq_idx = lax.axis_index("seq")
    place = lax.broadcasted_iota(jnp.int32, (n_keys, tile), 0)
    query = lax.rem(lax.broadcasted_iota(jnp.int32, (n_keys, tile), 1), half_len) + seq_idx * half_len
    allowed = (place <= query) & (place < live)
    return jnp.where(allowed, 0.0, -jnp.inf)


def score_kernel(shape, base, n_sources, first, near, limit_ref, queries_ref, *refs):
    tile, scale, chunk, key_width = shape
    refs = list(refs)
    if not first:
        marks_in, sum_in, high_in = [refs.pop(0) for _ in range(3)]
        refs.pop(0), refs.pop(0)
    if near:
        live_ref, suffix_ref = refs.pop(0), refs.pop(0)
    sources = [refs.pop(0) for _ in range(n_sources)]
    weights_hbm, values_hbm, marks, weight_sum, highest = [refs.pop(0) for _ in range(5)]
    if near:
        near_weights, near_values, near_mark = [refs.pop(0) for _ in range(3)]
    blocks, keys, weights, values, load_sems, weight_sems, value_sems = [refs.pop(0) for _ in range(7)]
    n_blocks = blocks.shape[0]
    latent_width = values.shape[1]
    index = 0
    for source in sources:
        for i in range(source.shape[0] // chunk):
            pltpu.make_async_copy(
                source.at[i * chunk : (i + 1) * chunk], blocks.at[index], load_sems.at[index]
            ).start()
            index += 1
    if first:
        marks[...] = jnp.zeros_like(marks)
        weight_sum[...] = jnp.zeros_like(weight_sum)
        highest[...] = jnp.full_like(highest, LOWEST)
    else:
        marks[...] = marks_in[...]
        weight_sum[...] = sum_in[...]
        highest[...] = high_in[...]

    def stores(block):
        return (
            pltpu.make_async_copy(weights.at[block], weights_hbm.at[base + block], weight_sems.at[block]),
            pltpu.make_async_copy(values.at[block], values_hbm.at[base + block], value_sems.at[block]),
        )

    def one_block(block, carry):
        pltpu.make_async_copy(blocks.at[block], blocks.at[block], load_sems.at[block]).wait()

        @pl.when(any_token(limit_ref, base + block, chunk))
        def _():
            load_block(blocks.at[block], keys, block_limits(limit_ref, base + block, chunk), key_width)

            def note(part, new):
                marks[pl.ds(base + block, 1), part] = new

            score_block(
                keys, queries_ref, weights.at[block], note, highest, weight_sum, tile, scale
            )
            values[block] = turn_values(keys, latent_width)
            for copy in stores(block):
                copy.start()

        return carry

    lax.fori_loop(0, n_blocks, one_block, 0)
    if near:
        near_keys = refs.pop(0)
        n_near = suffix_ref.shape[0]
        near_keys[:, key_width:] = jnp.zeros_like(near_keys[:, key_width:])
        near_keys[:, :key_width] = suffix_ref[...]

        def note_near(part, new):
            near_mark[:, part] = new

        score_block(
            near_keys, queries_ref, near_weights, note_near, highest, weight_sum, tile, scale,
            near_bias(n_near, n_near // lax.axis_size("seq"), tile, live_ref[0]),
        )
        near_values[...] = turn_values(near_keys, latent_width)

    def one_wait(block, carry):
        @pl.when(any_token(limit_ref, base + block, chunk))
        def _():
            for copy in stores(block):
                copy.wait()

        return carry

    lax.fori_loop(0, n_blocks, one_wait, 0)


def score_part(base, total, limits, queries, sources, state, shape, latent_width, near=None):
    tile, scale, chunk, key_width = shape
    width, rows = queries.shape
    _, pairs, pair_width = sources[0].shape
    block_keys = 2 * chunk * pairs
    n_blocks = sum(s.shape[0] for s in sources) // chunk
    row = jax.ShapeDtypeStruct((1, rows), jnp.float32)
    out_shape = [
        jax.ShapeDtypeStruct((total, block_keys, rows), jnp.float32),
        jax.ShapeDtypeStruct((total, latent_width, block_keys), jnp.bfloat16),
        jax.ShapeDtypeStruct((total, rows), jnp.float32),
        row,
        row,
    ]
    out_specs = [hbm_spec(), hbm_spec(), vmem_spec(), vmem_spec(), vmem_spec()]
    operands = [limits, queries]
    specs = [smem_spec(), vmem_spec()]
    aliases = {}
    if state is not None:
        operands += [state[2], state[3], state[4], state[0], state[1]]
        specs += [vmem_spec()] * 3 + [hbm_spec()] * 2
        aliases = {5: 0, 6: 1}
    scratch = [
        pltpu.VMEM((n_blocks, chunk, pairs, pair_width), jnp.bfloat16),
        pltpu.VMEM((block_keys, width), jnp.bfloat16),
        pltpu.VMEM((n_blocks, block_keys, rows), jnp.float32),
        pltpu.VMEM((n_blocks, latent_width, block_keys), jnp.bfloat16),
        pltpu.SemaphoreType.DMA((n_blocks,)),
        pltpu.SemaphoreType.DMA((n_blocks,)),
        pltpu.SemaphoreType.DMA((n_blocks,)),
    ]
    if near is not None:
        near_keys = near[-1].shape[0]
        operands += list(near)
        specs += [smem_spec(), vmem_spec()]
        out_shape += [
            jax.ShapeDtypeStruct((near_keys, rows), jnp.float32),
            jax.ShapeDtypeStruct((latent_width, near_keys), jnp.bfloat16),
            row,
        ]
        out_specs += [vmem_spec()] * 3
        scratch.append(pltpu.VMEM((near_keys, width), jnp.bfloat16))
    operands += list(sources)
    specs += [hbm_spec()] * len(sources)
    work = n_blocks * block_keys * rows // 2
    return pl.pallas_call(
        functools.partial(score_kernel, shape, base, len(sources), state is None, near is not None),
        out_shape=tuple(out_shape),
        in_specs=specs,
        out_specs=tuple(out_specs),
        scratch_shapes=scratch,
        input_output_aliases=aliases,
        compiler_params=pltpu.CompilerParams(vmem_limit_bytes=54 * MIB),
        cost_estimate=pl.CostEstimate(
            flops=work, bytes_accessed=10**5, transcendentals=0
        ),
        name="score_part",
    )(*operands)


def finish_kernel(
    shape, depth, n_blocks, n_sources, limit_ref, queries_ref, marks, sum_in, high_in,
    near_weights, near_values, near_mark, live_ref, up_ref, weights_hbm, values_hbm, *refs,
):
    tile, scale, chunk, key_width = shape
    sources, refs = refs[:n_sources], refs[n_sources:]
    (
        out_ref, weight_sum, highest, total, blocks, keys, last_weights, last_values, last_marks,
        weights, values, used, load_sems, weight_sems, value_sems,
    ) = refs
    rows = queries_ref.shape[1]
    latent_width = total.shape[0]
    n_last = blocks.shape[0]
    index = 0
    for source in sources:
        for i in range(source.shape[0] // chunk):
            pltpu.make_async_copy(
                source.at[i * chunk : (i + 1) * chunk], blocks.at[index], load_sems.at[index]
            ).start()
            index += 1

    def list_block(block, count):
        used[count] = block
        return count + any_token(limit_ref, block, chunk).astype(jnp.int32)

    n_used = lax.fori_loop(0, n_blocks, list_block, jnp.int32(0))

    def fetches(number):
        place = lax.rem(number, depth)
        return (
            pltpu.make_async_copy(weights_hbm.at[used[number]], weights.at[place], weight_sems.at[place]),
            pltpu.make_async_copy(values_hbm.at[used[number]], values.at[place], value_sems.at[place]),
        )

    def fetch(number):
        @pl.when(number < n_used)
        def _():
            for copy in fetches(number):
                copy.start()

    for number in range(depth):
        fetch(jnp.int32(number))
    weight_sum[...] = sum_in[...]
    highest[...] = high_in[...]
    last_marks[...] = jnp.zeros_like(last_marks)

    def one_score(block, carry):
        pltpu.make_async_copy(blocks.at[block], blocks.at[block], load_sems.at[block]).wait()

        @pl.when(any_token(limit_ref, n_blocks + block, chunk))
        def _():
            load_block(blocks.at[block], keys, block_limits(limit_ref, n_blocks + block, chunk), key_width)

            def note(part, new):
                last_marks[pl.ds(block, 1), part] = new

            score_block(
                keys, queries_ref, last_weights.at[block], note, highest, weight_sum, tile, scale
            )
            last_values[block] = turn_values(keys, latent_width)

        return carry

    lax.fori_loop(0, n_last, one_score, 0)

    def add_block(weight_block, value_block, mark, begin=False):
        for start in range(0, rows, tile):
            part = slice(start, start + tile)
            factor = jnp.exp2(mark[:, part] - highest[:, part]) / weight_sum[:, part]
            added = jnp.dot(
                value_block[...],
                (weight_block[:, part] * factor).astype(jnp.bfloat16),
                preferred_element_type=jnp.float32,
            )
            total[:, part] = added if begin else total[:, part] + added

    add_block(near_weights, near_values, near_mark, begin=True)

    def one_add(number, carry):
        for copy in fetches(number):
            copy.wait()
        place = lax.rem(number, depth)
        add_block(weights.at[place], values.at[place], marks.at[pl.ds(used[number], 1)])
        fetch(number + depth)
        return carry

    lax.fori_loop(0, n_used, one_add, 0)

    def one_last(block, carry):
        @pl.when(any_token(limit_ref, n_blocks + block, chunk))
        def _():
            add_block(last_weights.at[block], last_values.at[block], last_marks.at[pl.ds(block, 1)])

        return carry

    lax.fori_loop(0, n_last, one_last, 0)
    heads, _, value_width = up_ref.shape
    half_len = out_ref.shape[0]
    steps = lax.broadcasted_iota(jnp.int32, (half_len, value_width), 0)
    steps = steps + lax.axis_index("seq") * half_len
    for head in range(heads):
        latent = total[:, head * half_len : (head + 1) * half_len].astype(jnp.bfloat16)
        raised = lax.dot_general(
            latent, up_ref[head], (((0,), (0,)), ((), ())), preferred_element_type=jnp.float32
        )
        out_ref[:, head * value_width : (head + 1) * value_width] = jnp.where(
            steps < live_ref[0], raised, 0.0
        ).astype(jnp.bfloat16)


def finish(n_blocks, limits, queries, state, near_state, sources, live, up_weight, half_len, shape):
    tile, scale, chunk, key_width = shape
    weights, values, marks, weight_sum, highest = state
    width, rows = queries.shape
    _, latent_width, block_keys = values.shape
    _, pairs, pair_width = sources[0].shape
    heads, _, value_width = up_weight.shape
    depth = 4
    n_last = sum(s.shape[0] for s in sources) // chunk
    row = pltpu.VMEM((1, rows), jnp.float32)
    work = (n_blocks // 2 + n_last) * block_keys * rows
    return pl.pallas_call(
        functools.partial(finish_kernel, shape, depth, n_blocks, len(sources)),
        out_shape=jax.ShapeDtypeStruct((half_len, heads * value_width), jnp.bfloat16),
        in_specs=[smem_spec()]
        + [vmem_spec()] * 7
        + [smem_spec(), vmem_spec()]
        + [hbm_spec()] * (2 + len(sources)),
        out_specs=vmem_spec(),
        scratch_shapes=[
            row,
            row,
            pltpu.VMEM((latent_width, rows), jnp.float32),
            pltpu.VMEM((n_last, chunk, pairs, pair_width), jnp.bfloat16),
            pltpu.VMEM((block_keys, width), jnp.bfloat16),
            pltpu.VMEM((n_last, block_keys, rows), jnp.float32),
            pltpu.VMEM((n_last, latent_width, block_keys), jnp.bfloat16),
            pltpu.VMEM((n_last, rows), jnp.float32),
            pltpu.VMEM((depth, block_keys, rows), jnp.float32),
            pltpu.VMEM((depth, latent_width, block_keys), jnp.bfloat16),
            pltpu.SMEM((n_blocks + depth + 1,), jnp.int32),
            pltpu.SemaphoreType.DMA((n_last,)),
            pltpu.SemaphoreType.DMA((depth,)),
            pltpu.SemaphoreType.DMA((depth,)),
        ],
        compiler_params=pltpu.CompilerParams(vmem_limit_bytes=54 * MIB),
        cost_estimate=pl.CostEstimate(
            flops=2 * work * latent_width, bytes_accessed=3 * 10**7, transcendentals=work // 4
        ),
        name="finish",
    )(
        limits, queries, marks, weight_sum, highest, *near_state, live, up_weight,
        weights, values, *sources,
    )


def local(
    queries,
    hidden,
    w_dkv,
    kv_gain,
    w_uk,
    value_up_weight,
    page_pool,
    page_owner,
    page_slot,
    prefix_len,
    suffix_len,
):
    n_head = lax.axis_size("head")
    n_req = lax.axis_size("req")
    n_seq = lax.axis_size("seq")
    head_idx = lax.axis_index("head")
    req_idx = lax.axis_index("req")
    seq_idx = lax.axis_index("seq")
    _, half_len, d_local = hidden.shape
    heads_dev, nope_width, latent_width = w_uk.shape
    lat_width = w_dkv.shape[1]
    rope_width = lat_width - latent_width
    query_width = queries.shape[2] // heads_dev
    page_width = page_pool.shape[1]
    page_len = page_width // lat_width
    pairs = page_len // 2
    pages_req = page_slot.shape[1]
    cap = max(2, 2 * pages_req // (n_head * n_req))
    chunk = n_req * cap // 4
    score_scale = float(query_width) ** (-0.5)

    owner_rows = page_owner[:, :, 0]
    counts, most, my_prefix, live, first, rest, foreign, partial_value = pick_pages(
        owner_rows, page_slot, prefix_len, suffix_len, page_pool, hidden[0], w_dkv.T,
        cap, chunk, n_head, n_req, n_seq, pairs,
    )
    swap_route = [(i, n_seq - 1 - i) for i in range(n_seq)]
    stream_route = []
    for i in range(n_head - 1):
        stream_route.append((i * n_seq, (i + 1) * n_seq))
        stream_route.append(((i + 1) * n_seq + 1, i * n_seq + 1))

    def swap(block):
        return lax.ppermute(block, "seq", swap_route)

    def stream(block):
        return lax.ppermute(block, ("head", "seq"), stream_route)

    positions = my_prefix + seq_idx * half_len + jnp.arange(half_len, dtype=jnp.int32)
    rows = heads_dev * half_len
    half_rope = rope_width // 2
    frequency = 10000.0 ** (-2.0 * jnp.arange(half_rope, dtype=jnp.float32) / rope_width)
    phases = frequency[:, None] * positions.astype(jnp.float32)[None, :]
    q_turned = turn_queries(queries[0], w_uk, jnp.cos(phases), jnp.sin(phases), lat_width + 64)

    arrived = [
        lax.ppermute(foreign[s - 1], "req", [(i, (i + s) % n_req) for i in range(n_req)])
        for s in range(1, n_req)
    ]
    limits = plan_blocks(owner_rows, prefix_len, n_head, chunk, page_len)
    partial_value, limits = lax.optimization_barrier((partial_value, limits))
    early_steps = [stream(first)]
    for step in range(1, n_head - 1):
        early_steps.append(stream(early_steps[-1]))
    early_steps = [[block, None] for block in early_steps]
    for step in range(n_head - 2):
        early_steps[step][1] = swap(early_steps[step][0])
    mine = arrived[0][None] if n_req == 2 else jnp.stack(arrived)
    mine, q_turned, limits = lax.optimization_barrier((mine, q_turned, limits))
    other = swap(mine)
    middle, late = join_pages(counts, rest, mine, other, chunk, cap, (2 * chunk, chunk))
    share = half_len // n_head
    partials = lax.all_to_all(partial_value, "head", split_axis=0, concat_axis=0, tiled=True)
    partials, middle, most = lax.optimization_barrier((partials, middle, most))
    summed = jnp.sum(partials.reshape(n_head, share, lat_width), axis=0)
    share_t = seq_idx * half_len + head_idx * share + jnp.arange(share, dtype=jnp.int32)
    latent = finish_latent(summed, my_prefix + share_t, share_t < live, kv_gain, latent_width)

    tile = 256 if rows % 256 == 0 and 256 % half_len == 0 else half_len
    shape = (tile, score_scale * math.log2(math.e), chunk, lat_width)
    last = n_head - 2
    near_state = ()
    extra = 4 + 1 + 2 * last
    total = 1 + 2 * (last + 1) + 2 + 4 * last + extra
    n_blocks = 0
    state = None

    def arrays_of(arrived_steps, steps):
        return [arrived_steps[step][side] for step in steps for side in range(2)]

    def score(arrays, near=None):
        nonlocal n_blocks, state, near_state
        result = score_part(
            n_blocks, total, limits, q_turned, arrays, state, shape, latent_width, near
        )
        state = result[:5]
        near_state = result[5:] or near_state
        n_blocks += sum(a.shape[0] for a in arrays) // chunk

    def tie(block):
        nonlocal state
        block, mark = lax.optimization_barrier((block, state[4]))
        state = (*state[:4], mark)
        return block

    middle, early_steps[last - 1][0] = lax.optimization_barrier((middle, early_steps[last - 1][0]))
    middle_steps = []
    block = stream(middle)
    for step in range(last + 1):
        received = block
        if step == 0:
            score([first] + arrays_of(early_steps, range(last)))
        elif step == 1:
            score(arrays_of(early_steps, [last]) + [middle] + arrays_of(middle_steps, [0]))
        else:
            score(
                arrays_of(middle_steps, [step - 1]), (live, suffix_latent) if step == last else None
            )
        received = tie(received)
        if step == 0:
            most = over_groups(most)
            received, latent = lax.optimization_barrier((received, latent))
            copies = jnp.concatenate([latent] * n_head, axis=0)
            fresh = lax.all_to_all(copies, "head", split_axis=0, concat_axis=0, tiled=True)
            received, fresh, most = lax.optimization_barrier((received, fresh, most))
            early_steps[last][0] = tie(early_steps[last][0])
            early_steps[last][1] = swap(early_steps[last][0])
            opposite = swap(fresh)
            suffix_latent = jnp.where(
                seq_idx == 0,
                jnp.concatenate([fresh, opposite], axis=0),
                jnp.concatenate([opposite, fresh], axis=0),
            )
        if step < last:
            block = stream(received)
        middle_steps.append([received, swap(received)])

    last_arrays = arrays_of(middle_steps, [last])

    def end(blocks, final_arrays, current):
        return finish(
            blocks, limits, q_turned, current, near_state, final_arrays, live, value_up_weight, half_len, shape
        )

    def with_late(_):
        block = stream(late)
        arrays = last_arrays + [late]
        current, blocks = state, n_blocks
        for step in range(last + 1):
            received = block
            current = score_part(
                blocks, total, limits, q_turned, arrays, current, shape, latent_width
            )[:5]
            blocks += sum(a.shape[0] for a in arrays) // chunk
            received, mark = lax.optimization_barrier((received, current[4]))
            current = (*current[:4], mark)
            if step < last:
                block = stream(received)
            arrays = [received, swap(received)]
        return end(blocks, arrays, current)

    def without_late(_):
        return end(n_blocks, last_arrays, state)

    attn_out = lax.cond(most > 2 * chunk, with_late, without_late, 0)
    new_pages = fresh.reshape(1, half_len // page_len, page_len * lat_width)
    return (attn_out[None], new_pages)


def solution(mesh):
    placed = (
        P(("groups", "req"), "seq", "head"),
        P(("groups", "req"), "seq", "head"),
        P("head", None),
        P(),
        P("head", None, None),
        P("head", None, None),
        P(("groups", "head", "req"), None),
        P("groups", None, None),
        P("groups", None),
        P("groups"),
        P("groups"),
    )
    return jax.shard_map(
        local,
        mesh=mesh,
        in_specs=placed,
        out_specs=(P(("groups", "req"), "seq", "head"), P(("groups", "req"), "seq", None)),
        check_vma=False,
    )
```

```python
import functools
import math

import jax
import jax.numpy as jnp
from jax import lax
from jax.experimental import pallas as pl
from jax.experimental.pallas import tpu as pltpu
from jax.sharding import PartitionSpec as P

LOWEST = -1e30
MASKED = -1e38
MIB = 1024 * 1024


def rotate(vector, cosine_table, sine_table):
    half_width = vector.shape[-1] // 2
    first_half = vector[..., :half_width]
    second_half = vector[..., half_width:]
    return jnp.concatenate(
        [
            first_half * cosine_table - second_half * sine_table,
            first_half * sine_table + second_half * cosine_table,
        ],
        axis=-1,
    )


def angles(positions, rope_width):
    half_width = rope_width // 2
    frequency = 10000.0 ** (-2.0 * jnp.arange(half_width, dtype=jnp.float32) / rope_width)
    phases = positions.astype(jnp.float32)[:, None] * frequency[None, :]
    return (jnp.cos(phases), jnp.sin(phases))


def finish_latent(summed, positions, live_rows, kv_gain, latent_width):
    latent_part = summed[:, :latent_width]
    mean_square = jnp.mean(latent_part * latent_part, axis=-1, keepdims=True)
    normed = latent_part * lax.rsqrt(mean_square + 1e-06) * kv_gain
    cosine_table, sine_table = angles(positions, summed.shape[1] - latent_width)
    rotated = rotate(summed[:, latent_width:], cosine_table, sine_table)
    joined = jnp.concatenate([normed, rotated], axis=-1).astype(jnp.bfloat16)
    return jnp.where(live_rows[:, None], joined, jnp.zeros_like(joined))


def any_spec():
    return pl.BlockSpec(memory_space=pl.ANY)


def smem_spec():
    return pl.BlockSpec(memory_space=pltpu.SMEM)


def vmem_spec():
    return pl.BlockSpec(memory_space=pltpu.VMEM)


def hbm_spec():
    return pl.BlockSpec(memory_space=pltpu.HBM)


def pick_kernel(
    cap, page_len, owner_hbm, slot_hbm, prefix_hbm, suffix_hbm, pool_hbm, hidden_hbm, down_hbm, count_ref,
    most_ref, length_ref, live_ref, first_ref, rest_ref, foreign_ref, partial_ref, owner_ref, slot_ref,
    prefix_ref, suffix_ref, pool_ref, hidden_ref, down_ref, pages, lists, table, sems,
):
    n_req = lax.axis_size("req")
    head_idx = lax.axis_index("head")
    req_idx = lax.axis_index("req")
    seq_idx = lax.axis_index("seq")
    n_pages = owner_ref.shape[1]
    pool_pages, pairs, pair_width = pages.shape
    chunk = first_ref.shape[0]
    loads = [
        pltpu.make_async_copy(owner_hbm, owner_ref, sems.at[0]),
        pltpu.make_async_copy(slot_hbm, slot_ref, sems.at[1]),
        pltpu.make_async_copy(pool_hbm, pool_ref, sems.at[2]),
        pltpu.make_async_copy(hidden_hbm, hidden_ref, sems.at[6]),
        pltpu.make_async_copy(down_hbm, down_ref, sems.at[7]),
        pltpu.make_async_copy(prefix_hbm, prefix_ref, sems.at[8]),
        pltpu.make_async_copy(suffix_hbm, suffix_ref, sems.at[9]),
    ]
    for load in loads:
        load.start()
    loads[0].wait()
    loads[1].wait()
    loads[5].wait()
    loads[6].wait()
    length_ref[0] = prefix_ref[req_idx]
    live_ref[0] = suffix_ref[req_idx]
    self_owner = head_idx * n_req + req_idx
    n_owners = table.shape[1]
    for shift in range(n_req):
        for owner in range(n_owners):
            table[shift, owner] = 0
    founds = []
    most = jnp.int32(0)
    for shift in range(n_req):
        request = lax.rem(req_idx + shift, n_req)

        def note(page, found, shift=shift, request=request):
            owner = owner_ref[request, page]
            needed = page * page_len < prefix_ref[request]
            table[shift, owner] += needed.astype(jnp.int32)
            lists[shift, found] = slot_ref[request, page]
            return found + (needed & (owner == self_owner)).astype(jnp.int32)

        founds.append(lax.fori_loop(0, n_pages, note, jnp.int32(0), unroll=8))
        for place in range(n_owners // n_req):
            held = functools.reduce(jnp.add, [table[shift, place * n_req + i] for i in range(n_req)])
            early = jnp.minimum(table[shift, place * n_req + request], chunk)
            most = jnp.maximum(most, held - early)
    for shift in range(n_req):
        count_ref[shift] = table[0, head_idx * n_req + lax.rem(req_idx + n_req - shift, n_req)]
    most_ref[0] = most
    loads[2].wait()
    step = 16
    row = lax.broadcasted_iota(jnp.int32, (step * step, step * step), 0)
    column = lax.broadcasted_iota(jnp.int32, (step * step, step * step), 1)
    swap = ((row // step == column % step) & (row % step == column // step)).astype(jnp.bfloat16)
    for page in range(0, pool_pages, step):
        for pair in range(0, pairs, step):
            rows = jnp.concatenate(
                [
                    pool_ref[page : page + step, (pair + i) * pair_width : (pair + i + 1) * pair_width]
                    for i in range(step)
                ],
                axis=0,
            )
            turned = jnp.dot(swap, rows, preferred_element_type=jnp.float32).astype(jnp.bfloat16)
            pages[page : page + step, pair : pair + step, :] = turned.reshape(step, step, pair_width)

    def send(shift, rank, target, sem):
        slot = jnp.where(rank < founds[shift], lists[shift, rank], 0)
        pltpu.make_async_copy(pages.at[slot], target, sem).start()

    for rank in range(cap):
        if rank < chunk:
            send(0, rank, first_ref.at[rank], sems.at[3])
        else:
            send(0, rank, rest_ref.at[rank - chunk], sems.at[4])
    half_cap = foreign_ref.shape[1]
    for shift in range(1, n_req):
        for j in range(half_cap):
            send(shift, seq_idx * half_cap + j, foreign_ref.at[shift - 1, j], sems.at[5])
    loads[3].wait()
    loads[4].wait()
    partial_ref[...] = lax.dot_general(
        hidden_ref[...], down_ref[...], (((1,), (1,)), ((), ())), preferred_element_type=jnp.float32
    )
    pltpu.make_async_copy(first_ref, first_ref, sems.at[3]).wait()
    if cap > chunk:
        pltpu.make_async_copy(rest_ref, rest_ref, sems.at[4]).wait()
    pltpu.make_async_copy(foreign_ref, foreign_ref, sems.at[5]).wait()


def pick_pages(
    page_owner, page_slot, prefix_len, suffix_len, page_pool, hidden, down,
    cap, chunk, n_head, n_req, n_seq, pairs,
):
    pool_pages, page_width = page_pool.shape
    page = (pairs, page_width // pairs)
    return pl.pallas_call(
        functools.partial(pick_kernel, cap, 2 * pairs),
        out_shape=(
            jax.ShapeDtypeStruct((n_req,), jnp.int32),
            jax.ShapeDtypeStruct((1,), jnp.int32),
            jax.ShapeDtypeStruct((1,), jnp.int32),
            jax.ShapeDtypeStruct((1,), jnp.int32),
            jax.ShapeDtypeStruct((chunk, *page), jnp.bfloat16),
            jax.ShapeDtypeStruct((max(1, cap - chunk), *page), jnp.bfloat16),
            jax.ShapeDtypeStruct((n_req - 1, cap // n_seq, *page), jnp.bfloat16),
            jax.ShapeDtypeStruct((hidden.shape[0], down.shape[0]), jnp.float32),
        ),
        in_specs=[any_spec()] * 4 + [hbm_spec()] * 3,
        out_specs=(smem_spec(), smem_spec(), smem_spec(), smem_spec(), hbm_spec(), hbm_spec(), hbm_spec(), vmem_spec()),
        scratch_shapes=[
            pltpu.SMEM(page_owner.shape, jnp.int32),
            pltpu.SMEM(page_slot.shape, jnp.int32),
            pltpu.SMEM(prefix_len.shape, jnp.int32),
            pltpu.SMEM(suffix_len.shape, jnp.int32),
            pltpu.VMEM((pool_pages, page_width), jnp.bfloat16),
            pltpu.VMEM(hidden.shape, jnp.bfloat16),
            pltpu.VMEM(down.shape, jnp.bfloat16),
            pltpu.VMEM((pool_pages, *page), jnp.bfloat16),
            pltpu.SMEM((n_req, cap + 1), jnp.int32),
            pltpu.SMEM((n_req, n_head * n_req), jnp.int32),
            pltpu.SemaphoreType.DMA((10,)),
        ],
        compiler_params=pltpu.CompilerParams(vmem_limit_bytes=60 * MIB),
        cost_estimate=pl.CostEstimate(flops=10**9, bytes_accessed=6 * 10**6, transcendentals=0),
        name="pick_pages",
    )(page_owner, page_slot, prefix_len, suffix_len, page_pool, hidden, down)


def join_kernel(chunk, cap, count_ref, rest_ref, mine_ref, other_ref, *refs):
    n_req = count_ref.shape[0]
    targets, sems = refs[:-1], refs[-1]
    seq_idx = lax.axis_index("seq")
    half_cap = mine_ref.shape[1]
    excess = jnp.maximum(count_ref[0] - chunk, 0)
    j = 0
    for part, target in enumerate(targets):
        for place in range(target.shape[0]):

            def fetch(condition, source, target=target, place=place, part=part):
                @pl.when(condition)
                def _():
                    pltpu.make_async_copy(source, target.at[place], sems.at[part]).start()

            rank = jnp.int32(j)
            taken = rank < excess
            if cap > chunk:
                fetch(taken, rest_ref.at[jnp.minimum(rank, cap - chunk - 1)])
            rank = rank - excess
            for shift in range(1, n_req):
                here = jnp.logical_not(taken) & (rank < count_ref[shift])
                half = rank // half_cap
                slot = jnp.clip(rank - half * half_cap, 0, half_cap - 1)
                fetch(here & (half == seq_idx), mine_ref.at[shift - 1, slot])
                fetch(here & (half != seq_idx), other_ref.at[shift - 1, slot])
                taken = taken | here
                rank = rank - count_ref[shift]
            fetch(jnp.logical_not(taken), mine_ref.at[0, 0])
            j += 1
    for part, target in enumerate(targets):
        pltpu.make_async_copy(target, target, sems.at[part]).wait()


def join_pages(counts, rest, mine, other, chunk, cap, sizes):
    return pl.pallas_call(
        functools.partial(join_kernel, chunk, cap),
        out_shape=tuple(jax.ShapeDtypeStruct((size, *rest.shape[1:]), jnp.bfloat16) for size in sizes),
        in_specs=[smem_spec()] + [hbm_spec()] * 3,
        out_specs=(vmem_spec(),) * len(sizes),
        scratch_shapes=[pltpu.SemaphoreType.DMA((len(sizes),))],
        compiler_params=pltpu.CompilerParams(vmem_limit_bytes=10 * MIB),
        cost_estimate=pl.CostEstimate(flops=0, bytes_accessed=3 * 10**6, transcendentals=0),
        name="join_pages",
    )(counts, rest, mine, other)


def plan_kernel(page_len, chunk, owner_ref, prefix_ref, limit_ref):
    n_head = lax.axis_size("head")
    n_req = lax.axis_size("req")
    head_idx = lax.axis_index("head")
    req_idx = lax.axis_index("req")
    upward = 2 * lax.axis_index("seq") - 1
    n = owner_ref.shape[1]
    prefix = prefix_ref[req_idx]
    diagonal = lax.broadcasted_iota(jnp.int32, (n, n), 0) == lax.broadcasted_iota(jnp.int32, (n, n), 1)

    def column(values):
        return jnp.sum(jnp.where(diagonal, values, 0), axis=1, keepdims=True)

    owner = owner_ref[pl.ds(req_idx, 1), :]
    place = jnp.zeros_like(owner)
    for head in range(1, n_head):
        place = place + (owner >= head * n_req).astype(jnp.int32)
    shift = req_idx - (owner - place * n_req)
    shift = jnp.where(shift < 0, shift + n_req, shift)
    order = lax.broadcasted_iota(jnp.int32, (1, n), 1)
    needed = (order * page_len < prefix).astype(jnp.int32)
    key = shift * n + order
    together = (column(place) == place) & (column(needed) > 0)
    rank = jnp.sum((together & (column(key) < key)).astype(jnp.int32), axis=0, keepdims=True)
    held = jnp.sum((together & (column(shift) == 0)).astype(jnp.int32), axis=0, keepdims=True)
    early = (shift == 0) & (rank < chunk)
    within = jnp.where(early, rank, chunk + rank - jnp.minimum(held, chunk))
    away = place - head_idx
    distance = jnp.abs(away)
    origin = jnp.where(away * upward > 0, 2 * distance - 1, 2 * distance)
    origins = 2 * n_head - 1
    slot = jnp.where(
        within < chunk,
        origin * chunk + within,
        jnp.where(
            within < 3 * chunk,
            (origins + 2 * origin) * chunk + within - chunk,
            (3 * origins + origin) * chunk + within - 3 * chunk,
        ),
    )
    slot = column(jnp.where(needed > 0, slot, -1))
    tokens = column(jnp.clip(prefix - order * page_len, 0, page_len))
    lane = lax.broadcasted_iota(jnp.int32, (n, limit_ref.shape[1]), 1)
    limit_ref[...] = jnp.sum(jnp.where(lane == slot, tokens, 0), axis=0, keepdims=True)


def plan_blocks(page_owner, prefix_len, n_head, chunk, page_len):
    return pl.pallas_call(
        functools.partial(plan_kernel, page_len, chunk),
        out_shape=jax.ShapeDtypeStruct((1, 4 * (2 * n_head - 1) * chunk), jnp.int32),
        in_specs=[vmem_spec(), smem_spec()],
        out_specs=vmem_spec(),
        cost_estimate=pl.CostEstimate(flops=10**4, bytes_accessed=10**4, transcendentals=0),
        name="plan_blocks",
    )(page_owner, prefix_len)


def over_groups(most):
    n_groups = lax.axis_size("groups")
    passed = most
    for _ in range(n_groups - 1):
        passed = lax.ppermute(passed, "groups", [(i, (i + 1) % n_groups) for i in range(n_groups)])
        most = jnp.maximum(most, passed)
    return most[0]


def query_kernel(query_hbm, up_hbm, cosine_ref, sine_ref, out_ref, query_ref, up_ref, sems):
    loads = [
        pltpu.make_async_copy(query_hbm, query_ref, sems.at[0]),
        pltpu.make_async_copy(up_hbm, up_ref, sems.at[1]),
    ]
    for load in loads:
        load.start()
    for load in loads:
        load.wait()
    heads, nope_width, latent_width = up_ref.shape
    half_len, width = query_ref.shape
    query_width = width // heads
    half_rope = cosine_ref.shape[0]
    key_width = latent_width + 2 * half_rope
    for head in range(heads):
        part = slice(head * half_len, (head + 1) * half_len)
        both = query_ref[:, head * query_width : (head + 1) * query_width]
        latent = lax.dot_general(
            up_ref[head], both[:, :nope_width], (((0,), (1,)), ((), ())), preferred_element_type=jnp.float32
        )
        out_ref[:latent_width, part] = latent.astype(jnp.bfloat16)
        turned = both[:, nope_width:].astype(jnp.float32).T
        low, high = turned[:half_rope], turned[half_rope:]
        out_ref[latent_width : latent_width + half_rope, part] = (
            low * cosine_ref[...] - high * sine_ref[...]
        ).astype(jnp.bfloat16)
        out_ref[latent_width + half_rope : key_width, part] = (
            low * sine_ref[...] + high * cosine_ref[...]
        ).astype(jnp.bfloat16)
    rest = out_ref.shape[0] - key_width
    row = lax.broadcasted_iota(jnp.int32, (rest, out_ref.shape[1]), 0)
    out_ref[key_width:, :] = (row == 0).astype(jnp.bfloat16)


def turn_queries(queries, w_uk, cosine_table, sine_table, key_rows):
    heads, nope_width, latent_width = w_uk.shape
    rows = heads * queries.shape[0]
    return pl.pallas_call(
        query_kernel,
        out_shape=jax.ShapeDtypeStruct((key_rows, rows), jnp.bfloat16),
        in_specs=[any_spec()] * 2 + [vmem_spec()] * 2,
        out_specs=vmem_spec(),
        scratch_shapes=[
            pltpu.VMEM(queries.shape, jnp.bfloat16),
            pltpu.VMEM(w_uk.shape, jnp.bfloat16),
            pltpu.SemaphoreType.DMA((2,)),
        ],
        compiler_params=pltpu.CompilerParams(vmem_limit_bytes=60 * MIB),
        cost_estimate=pl.CostEstimate(
            flops=2 * rows * nope_width * latent_width, bytes_accessed=3 * 10**6, transcendentals=0
        ),
        name="turn_queries",
    )(queries, w_uk, cosine_table, sine_table)


def score_block(keys, queries_ref, target, note, highest, weight_sum, tile, scale, bias=None):
    parts = [slice(start, start + tile) for start in range(0, queries_ref.shape[1], tile)]

    def product(part):
        return jnp.dot(keys[...], queries_ref[:, part], preferred_element_type=jnp.float32)

    following = product(parts[0])
    for number, part in enumerate(parts):
        scores = following * scale
        if number + 1 < len(parts):
            following = product(parts[number + 1])
        if bias is not None:
            scores = scores + bias
        old = highest[:, part]
        new = jnp.maximum(old, jnp.max(scores, axis=0, keepdims=True))
        weights = jnp.exp2(scores - new)
        highest[:, part] = new
        weight_sum[:, part] = weight_sum[:, part] * jnp.exp2(old - new) + jnp.sum(
            weights, axis=0, keepdims=True
        )
        target[:, part] = weights
        note(part, new)


def block_limits(limit_ref, block, chunk):
    return [limit_ref[0, block * chunk + j] for j in range(chunk)]


def any_token(limit_ref, block, chunk):
    return functools.reduce(jnp.maximum, block_limits(limit_ref, block, chunk)) > 0


def load_block(block_ref, keys, limits, key_width):
    chunk, pairs, pair_width = block_ref.shape
    pair_rows = chunk * pairs
    page_rows = block_ref[...].reshape(pair_rows, pair_width)
    keys[:pair_rows, :key_width] = page_rows[:, :key_width]
    keys[pair_rows:, :key_width] = page_rows[:, key_width:]
    shape = (2 * pair_rows, keys.shape[1] - key_width)
    row = lax.broadcasted_iota(jnp.int32, shape, 0)
    pair_row = lax.rem(row, pair_rows)
    token = 2 * lax.rem(pair_row, pairs) + row // pair_rows
    limit = jnp.zeros_like(row)
    for j, value in enumerate(limits):
        limit = jnp.where(pair_row // pairs == j, value, limit)
    masked = (lax.broadcasted_iota(jnp.int32, shape, 1) == 0) & (token >= limit)
    keys[:, key_width:] = jnp.where(masked, MASKED, 0.0).astype(jnp.bfloat16)


def turn_values(keys, latent_width):
    return keys[:, :latent_width].T


def near_bias(n_keys, half_len, tile, live):
    seq_idx = lax.axis_index("seq")
    place = lax.broadcasted_iota(jnp.int32, (n_keys, tile), 0)
    query = lax.rem(lax.broadcasted_iota(jnp.int32, (n_keys, tile), 1), half_len) + seq_idx * half_len
    allowed = (place <= query) & (place < live)
    return jnp.where(allowed, 0.0, -jnp.inf)


def score_kernel(shape, base, n_sources, first, near, limit_ref, queries_ref, *refs):
    tile, scale, chunk, key_width = shape
    refs = list(refs)
    if not first:
        marks_in, sum_in, high_in = [refs.pop(0) for _ in range(3)]
        refs.pop(0), refs.pop(0)
    if near:
        live_ref, suffix_ref = refs.pop(0), refs.pop(0)
    sources = [refs.pop(0) for _ in range(n_sources)]
    weights_hbm, values_hbm, marks, weight_sum, highest = [refs.pop(0) for _ in range(5)]
    if near:
        near_weights, near_values, near_mark = [refs.pop(0) for _ in range(3)]
    blocks, keys, weights, values, load_sems, weight_sems, value_sems = [refs.pop(0) for _ in range(7)]
    n_blocks = blocks.shape[0]
    latent_width = values.shape[1]
    index = 0
    for source in sources:
        for i in range(source.shape[0] // chunk):
            pltpu.make_async_copy(
                source.at[i * chunk : (i + 1) * chunk], blocks.at[index], load_sems.at[index]
            ).start()
            index += 1
    if first:
        marks[...] = jnp.zeros_like(marks)
        weight_sum[...] = jnp.zeros_like(weight_sum)
        highest[...] = jnp.full_like(highest, LOWEST)
    else:
        marks[...] = marks_in[...]
        weight_sum[...] = sum_in[...]
        highest[...] = high_in[...]

    def stores(block):
        return (
            pltpu.make_async_copy(weights.at[block], weights_hbm.at[base + block], weight_sems.at[block]),
            pltpu.make_async_copy(values.at[block], values_hbm.at[base + block], value_sems.at[block]),
        )

    def one_block(block, carry):
        pltpu.make_async_copy(blocks.at[block], blocks.at[block], load_sems.at[block]).wait()

        @pl.when(any_token(limit_ref, base + block, chunk))
        def _():
            load_block(blocks.at[block], keys, block_limits(limit_ref, base + block, chunk), key_width)

            def note(part, new):
                marks[pl.ds(base + block, 1), part] = new

            score_block(
                keys, queries_ref, weights.at[block], note, highest, weight_sum, tile, scale
            )
            values[block] = turn_values(keys, latent_width)
            for copy in stores(block):
                copy.start()

        return carry

    lax.fori_loop(0, n_blocks, one_block, 0)
    if near:
        near_keys = refs.pop(0)
        n_near = suffix_ref.shape[0]
        near_keys[:, key_width:] = jnp.zeros_like(near_keys[:, key_width:])
        near_keys[:, :key_width] = suffix_ref[...]

        def note_near(part, new):
            near_mark[:, part] = new

        score_block(
            near_keys, queries_ref, near_weights, note_near, highest, weight_sum, tile, scale,
            near_bias(n_near, n_near // lax.axis_size("seq"), tile, live_ref[0]),
        )
        near_values[...] = turn_values(near_keys, latent_width)

    def one_wait(block, carry):
        @pl.when(any_token(limit_ref, base + block, chunk))
        def _():
            for copy in stores(block):
                copy.wait()

        return carry

    lax.fori_loop(0, n_blocks, one_wait, 0)


def score_part(base, total, limits, queries, sources, state, shape, latent_width, near=None):
    tile, scale, chunk, key_width = shape
    width, rows = queries.shape
    _, pairs, pair_width = sources[0].shape
    block_keys = 2 * chunk * pairs
    n_blocks = sum(s.shape[0] for s in sources) // chunk
    row = jax.ShapeDtypeStruct((1, rows), jnp.float32)
    out_shape = [
        jax.ShapeDtypeStruct((total, block_keys, rows), jnp.float32),
        jax.ShapeDtypeStruct((total, latent_width, block_keys), jnp.bfloat16),
        jax.ShapeDtypeStruct((total, rows), jnp.float32),
        row,
        row,
    ]
    out_specs = [hbm_spec(), hbm_spec(), vmem_spec(), vmem_spec(), vmem_spec()]
    operands = [limits, queries]
    specs = [smem_spec(), vmem_spec()]
    aliases = {}
    if state is not None:
        operands += [state[2], state[3], state[4], state[0], state[1]]
        specs += [vmem_spec()] * 3 + [hbm_spec()] * 2
        aliases = {5: 0, 6: 1}
    scratch = [
        pltpu.VMEM((n_blocks, chunk, pairs, pair_width), jnp.bfloat16),
        pltpu.VMEM((block_keys, width), jnp.bfloat16),
        pltpu.VMEM((n_blocks, block_keys, rows), jnp.float32),
        pltpu.VMEM((n_blocks, latent_width, block_keys), jnp.bfloat16),
        pltpu.SemaphoreType.DMA((n_blocks,)),
        pltpu.SemaphoreType.DMA((n_blocks,)),
        pltpu.SemaphoreType.DMA((n_blocks,)),
    ]
    if near is not None:
        near_keys = near[-1].shape[0]
        operands += list(near)
        specs += [smem_spec(), vmem_spec()]
        out_shape += [
            jax.ShapeDtypeStruct((near_keys, rows), jnp.float32),
            jax.ShapeDtypeStruct((latent_width, near_keys), jnp.bfloat16),
            row,
        ]
        out_specs += [vmem_spec()] * 3
        scratch.append(pltpu.VMEM((near_keys, width), jnp.bfloat16))
    operands += list(sources)
    specs += [hbm_spec()] * len(sources)
    work = n_blocks * block_keys * rows // 2
    return pl.pallas_call(
        functools.partial(score_kernel, shape, base, len(sources), state is None, near is not None),
        out_shape=tuple(out_shape),
        in_specs=specs,
        out_specs=tuple(out_specs),
        scratch_shapes=scratch,
        input_output_aliases=aliases,
        compiler_params=pltpu.CompilerParams(vmem_limit_bytes=54 * MIB),
        cost_estimate=pl.CostEstimate(
            flops=work, bytes_accessed=10**5, transcendentals=0
        ),
        name="score_part",
    )(*operands)


def finish_kernel(
    shape, depth, n_blocks, n_sources, limit_ref, queries_ref, marks, sum_in, high_in,
    near_weights, near_values, near_mark, live_ref, up_ref, weights_hbm, values_hbm, *refs,
):
    tile, scale, chunk, key_width = shape
    sources, refs = refs[:n_sources], refs[n_sources:]
    (
        out_ref, weight_sum, highest, total, blocks, keys, last_weights, last_values, last_marks,
        weights, values, used, load_sems, weight_sems, value_sems,
    ) = refs
    rows = queries_ref.shape[1]
    latent_width = total.shape[0]
    n_last = blocks.shape[0]
    index = 0
    for source in sources:
        for i in range(source.shape[0] // chunk):
            pltpu.make_async_copy(
                source.at[i * chunk : (i + 1) * chunk], blocks.at[index], load_sems.at[index]
            ).start()
            index += 1

    def list_block(block, count):
        used[count] = block
        return count + any_token(limit_ref, block, chunk).astype(jnp.int32)

    n_used = lax.fori_loop(0, n_blocks, list_block, jnp.int32(0))

    def fetches(number):
        place = lax.rem(number, depth)
        return (
            pltpu.make_async_copy(weights_hbm.at[used[number]], weights.at[place], weight_sems.at[place]),
            pltpu.make_async_copy(values_hbm.at[used[number]], values.at[place], value_sems.at[place]),
        )

    def fetch(number):
        @pl.when(number < n_used)
        def _():
            for copy in fetches(number):
                copy.start()

    for number in range(depth):
        fetch(jnp.int32(number))
    weight_sum[...] = sum_in[...]
    highest[...] = high_in[...]
    last_marks[...] = jnp.zeros_like(last_marks)

    def one_score(block, carry):
        pltpu.make_async_copy(blocks.at[block], blocks.at[block], load_sems.at[block]).wait()

        @pl.when(any_token(limit_ref, n_blocks + block, chunk))
        def _():
            load_block(blocks.at[block], keys, block_limits(limit_ref, n_blocks + block, chunk), key_width)

            def note(part, new):
                last_marks[pl.ds(block, 1), part] = new

            score_block(
                keys, queries_ref, last_weights.at[block], note, highest, weight_sum, tile, scale
            )
            last_values[block] = turn_values(keys, latent_width)

        return carry

    lax.fori_loop(0, n_last, one_score, 0)

    def add_block(weight_block, value_block, mark, begin=False):
        parts = [slice(start, start + tile) for start in range(0, rows, tile)]

        def scaled(part):
            factor = jnp.exp2(mark[:, part] - highest[:, part]) / weight_sum[:, part]
            return (weight_block[:, part] * factor).astype(jnp.bfloat16)

        following = scaled(parts[0])
        for number, part in enumerate(parts):
            added = jnp.dot(value_block[...], following, preferred_element_type=jnp.float32)
            if number + 1 < len(parts):
                following = scaled(parts[number + 1])
            total[:, part] = added if begin else total[:, part] + added

    add_block(near_weights, near_values, near_mark, begin=True)

    def one_add(number, carry):
        for copy in fetches(number):
            copy.wait()
        place = lax.rem(number, depth)
        add_block(weights.at[place], values.at[place], marks.at[pl.ds(used[number], 1)])
        fetch(number + depth)
        return carry

    lax.fori_loop(0, n_used, one_add, 0)

    def one_last(block, carry):
        @pl.when(any_token(limit_ref, n_blocks + block, chunk))
        def _():
            add_block(last_weights.at[block], last_values.at[block], last_marks.at[pl.ds(block, 1)])

        return carry

    lax.fori_loop(0, n_last, one_last, 0)
    heads, _, value_width = up_ref.shape
    half_len = out_ref.shape[0]
    steps = lax.broadcasted_iota(jnp.int32, (half_len, value_width), 0)
    steps = steps + lax.axis_index("seq") * half_len
    for head in range(heads):
        latent = total[:, head * half_len : (head + 1) * half_len].astype(jnp.bfloat16)
        raised = lax.dot_general(
            latent, up_ref[head], (((0,), (0,)), ((), ())), preferred_element_type=jnp.float32
        )
        out_ref[:, head * value_width : (head + 1) * value_width] = jnp.where(
            steps < live_ref[0], raised, 0.0
        ).astype(jnp.bfloat16)


def finish(n_blocks, limits, queries, state, near_state, sources, live, up_weight, half_len, shape):
    tile, scale, chunk, key_width = shape
    weights, values, marks, weight_sum, highest = state
    width, rows = queries.shape
    _, latent_width, block_keys = values.shape
    _, pairs, pair_width = sources[0].shape
    heads, _, value_width = up_weight.shape
    depth = 4
    n_last = sum(s.shape[0] for s in sources) // chunk
    row = pltpu.VMEM((1, rows), jnp.float32)
    work = (n_blocks // 2 + n_last) * block_keys * rows
    return pl.pallas_call(
        functools.partial(finish_kernel, shape, depth, n_blocks, len(sources)),
        out_shape=jax.ShapeDtypeStruct((half_len, heads * value_width), jnp.bfloat16),
        in_specs=[smem_spec()]
        + [vmem_spec()] * 7
        + [smem_spec(), vmem_spec()]
        + [hbm_spec()] * (2 + len(sources)),
        out_specs=vmem_spec(),
        scratch_shapes=[
            row,
            row,
            pltpu.VMEM((latent_width, rows), jnp.float32),
            pltpu.VMEM((n_last, chunk, pairs, pair_width), jnp.bfloat16),
            pltpu.VMEM((block_keys, width), jnp.bfloat16),
            pltpu.VMEM((n_last, block_keys, rows), jnp.float32),
            pltpu.VMEM((n_last, latent_width, block_keys), jnp.bfloat16),
            pltpu.VMEM((n_last, rows), jnp.float32),
            pltpu.VMEM((depth, block_keys, rows), jnp.float32),
            pltpu.VMEM((depth, latent_width, block_keys), jnp.bfloat16),
            pltpu.SMEM((n_blocks + depth + 1,), jnp.int32),
            pltpu.SemaphoreType.DMA((n_last,)),
            pltpu.SemaphoreType.DMA((depth,)),
            pltpu.SemaphoreType.DMA((depth,)),
        ],
        compiler_params=pltpu.CompilerParams(vmem_limit_bytes=54 * MIB),
        cost_estimate=pl.CostEstimate(
            flops=2 * work * latent_width, bytes_accessed=3 * 10**7, transcendentals=work // 4
        ),
        name="finish",
    )(
        limits, queries, marks, weight_sum, highest, *near_state, live, up_weight,
        weights, values, *sources,
    )


def local(
    queries,
    hidden,
    w_dkv,
    kv_gain,
    w_uk,
    value_up_weight,
    page_pool,
    page_owner,
    page_slot,
    prefix_len,
    suffix_len,
):
    n_head = lax.axis_size("head")
    n_req = lax.axis_size("req")
    n_seq = lax.axis_size("seq")
    head_idx = lax.axis_index("head")
    req_idx = lax.axis_index("req")
    seq_idx = lax.axis_index("seq")
    _, half_len, d_local = hidden.shape
    heads_dev, nope_width, latent_width = w_uk.shape
    lat_width = w_dkv.shape[1]
    rope_width = lat_width - latent_width
    query_width = queries.shape[2] // heads_dev
    page_width = page_pool.shape[1]
    page_len = page_width // lat_width
    pairs = page_len // 2
    pages_req = page_slot.shape[1]
    cap = max(2, 2 * pages_req // (n_head * n_req))
    chunk = n_req * cap // 4
    score_scale = float(query_width) ** (-0.5)

    owner_rows = page_owner[:, :, 0]
    counts, most, my_prefix, live, first, rest, foreign, partial_value = pick_pages(
        owner_rows, page_slot, prefix_len, suffix_len, page_pool, hidden[0], w_dkv.T,
        cap, chunk, n_head, n_req, n_seq, pairs,
    )
    swap_route = [(i, n_seq - 1 - i) for i in range(n_seq)]
    stream_route = []
    for i in range(n_head - 1):
        stream_route.append((i * n_seq, (i + 1) * n_seq))
        stream_route.append(((i + 1) * n_seq + 1, i * n_seq + 1))

    def swap(block):
        return lax.ppermute(block, "seq", swap_route)

    def stream(block):
        return lax.ppermute(block, ("head", "seq"), stream_route)

    positions = my_prefix + seq_idx * half_len + jnp.arange(half_len, dtype=jnp.int32)
    rows = heads_dev * half_len
    half_rope = rope_width // 2
    frequency = 10000.0 ** (-2.0 * jnp.arange(half_rope, dtype=jnp.float32) / rope_width)
    phases = frequency[:, None] * positions.astype(jnp.float32)[None, :]
    q_turned = turn_queries(queries[0], w_uk, jnp.cos(phases), jnp.sin(phases), lat_width + 64)

    arrived = [
        lax.ppermute(foreign[s - 1], "req", [(i, (i + s) % n_req) for i in range(n_req)])
        for s in range(1, n_req)
    ]
    early_steps = [stream(first)]
    share = half_len // n_head
    partials = lax.all_to_all(partial_value, "head", split_axis=0, concat_axis=0, tiled=True)
    summed = jnp.sum(partials.reshape(n_head, share, lat_width), axis=0)
    share_t = seq_idx * half_len + head_idx * share + jnp.arange(share, dtype=jnp.int32)
    latent = finish_latent(summed, my_prefix + share_t, share_t < live, kv_gain, latent_width)
    copies = jnp.concatenate([latent] * n_head, axis=0)
    fresh = lax.all_to_all(copies, "head", split_axis=0, concat_axis=0, tiled=True)
    early_steps[0], fresh = lax.optimization_barrier((early_steps[0], fresh))
    for step in range(1, n_head - 1):
        early_steps.append(stream(early_steps[-1]))
    early_steps = [[block, None] for block in early_steps]
    for step in range(n_head - 2):
        early_steps[step][1] = swap(early_steps[step][0])
    mine = arrived[0][None] if n_req == 2 else jnp.stack(arrived)
    most = over_groups(most)
    mine, fresh, most = lax.optimization_barrier((mine, fresh, most))
    other = swap(mine)
    middle, late = join_pages(counts, rest, mine, other, chunk, cap, (2 * chunk, chunk))

    tile = 256 if rows % 256 == 0 and 256 % half_len == 0 else half_len
    shape = (tile, score_scale * math.log2(math.e), chunk, lat_width)
    last = n_head - 2
    near_state = ()
    extra = 4 + 1 + 2 * last
    total = 1 + 2 * (last + 1) + 2 + 4 * last + extra
    limits = plan_blocks(owner_rows, prefix_len, n_head, chunk, page_len)
    n_blocks = 0
    state = None

    def arrays_of(arrived_steps, steps):
        return [arrived_steps[step][side] for step in steps for side in range(2)]

    def score(arrays, near=None):
        nonlocal n_blocks, state, near_state
        result = score_part(
            n_blocks, total, limits, q_turned, arrays, state, shape, latent_width, near
        )
        state = result[:5]
        near_state = result[5:] or near_state
        n_blocks += sum(a.shape[0] for a in arrays) // chunk

    def tie(block):
        nonlocal state
        block, mark = lax.optimization_barrier((block, state[4]))
        state = (*state[:4], mark)
        return block

    middle, early_steps[last - 1][0] = lax.optimization_barrier((middle, early_steps[last - 1][0]))
    middle_steps = []
    block = stream(middle)
    for step in range(last + 1):
        received = block
        if step == 0:
            score([first] + arrays_of(early_steps, range(last)))
        elif step == 1:
            score(arrays_of(early_steps, [last]) + [middle] + arrays_of(middle_steps, [0]))
        else:
            score(
                arrays_of(middle_steps, [step - 1]), (live, suffix_latent) if step == last else None
            )
        received = tie(received)
        if step == 0:
            early_steps[last][0] = tie(early_steps[last][0])
            early_steps[last][1] = swap(early_steps[last][0])
            opposite = swap(fresh)
            suffix_latent = jnp.where(
                seq_idx == 0,
                jnp.concatenate([fresh, opposite], axis=0),
                jnp.concatenate([opposite, fresh], axis=0),
            )
        if step < last:
            block = stream(received)
        middle_steps.append([received, swap(received)])

    last_arrays = arrays_of(middle_steps, [last])

    def end(blocks, final_arrays, current):
        return finish(
            blocks, limits, q_turned, current, near_state, final_arrays, live, value_up_weight, half_len, shape
        )

    def with_late(_):
        block = stream(late)
        arrays = last_arrays + [late]
        current, blocks = state, n_blocks
        for step in range(last + 1):
            received = block
            current = score_part(
                blocks, total, limits, q_turned, arrays, current, shape, latent_width
            )[:5]
            blocks += sum(a.shape[0] for a in arrays) // chunk
            received, mark = lax.optimization_barrier((received, current[4]))
            current = (*current[:4], mark)
            if step < last:
                block = stream(received)
            arrays = [received, swap(received)]
        return end(blocks, arrays, current)

    def without_late(_):
        return end(n_blocks, last_arrays, state)

    attn_out = lax.cond(most > 2 * chunk, with_late, without_late, 0)
    new_pages = fresh.reshape(1, half_len // page_len, page_len * lat_width)
    return (attn_out[None], new_pages)


def solution(mesh):
    placed = (
        P(("groups", "req"), "seq", "head"),
        P(("groups", "req"), "seq", "head"),
        P("head", None),
        P(),
        P("head", None, None),
        P("head", None, None),
        P(("groups", "head", "req"), None),
        P("groups", None, None),
        P("groups", None),
        P("groups"),
        P("groups"),
    )
    return jax.shard_map(
        local,
        mesh=mesh,
        in_specs=placed,
        out_specs=(P(("groups", "req"), "seq", "head"), P(("groups", "req"), "seq", None)),
        check_vma=False,
    )
```

```python
import functools
import math

import jax
import jax.numpy as jnp
from jax import lax
from jax.experimental import pallas as pl
from jax.experimental.pallas import tpu as pltpu
from jax.sharding import PartitionSpec as P

LOWEST = -1e30
MASKED = -1e38
MIB = 1024 * 1024


def rotate(vector, cosine_table, sine_table):
    half_width = vector.shape[-1] // 2
    first_half = vector[..., :half_width]
    second_half = vector[..., half_width:]
    return jnp.concatenate(
        [
            first_half * cosine_table - second_half * sine_table,
            first_half * sine_table + second_half * cosine_table,
        ],
        axis=-1,
    )


def angles(positions, rope_width):
    half_width = rope_width // 2
    frequency = 10000.0 ** (-2.0 * jnp.arange(half_width, dtype=jnp.float32) / rope_width)
    phases = positions.astype(jnp.float32)[:, None] * frequency[None, :]
    return (jnp.cos(phases), jnp.sin(phases))


def finish_latent(summed, positions, live_rows, kv_gain, latent_width):
    latent_part = summed[:, :latent_width]
    mean_square = jnp.mean(latent_part * latent_part, axis=-1, keepdims=True)
    normed = latent_part * lax.rsqrt(mean_square + 1e-06) * kv_gain
    cosine_table, sine_table = angles(positions, summed.shape[1] - latent_width)
    rotated = rotate(summed[:, latent_width:], cosine_table, sine_table)
    joined = jnp.concatenate([normed, rotated], axis=-1).astype(jnp.bfloat16)
    return jnp.where(live_rows[:, None], joined, jnp.zeros_like(joined))


def any_spec():
    return pl.BlockSpec(memory_space=pl.ANY)


def smem_spec():
    return pl.BlockSpec(memory_space=pltpu.SMEM)


def vmem_spec():
    return pl.BlockSpec(memory_space=pltpu.VMEM)


def hbm_spec():
    return pl.BlockSpec(memory_space=pltpu.HBM)


def pick_kernel(
    cap, page_len, owner_hbm, slot_hbm, prefix_hbm, suffix_hbm, pool_hbm, hidden_hbm, down_hbm, count_ref,
    most_ref, length_ref, live_ref, first_ref, rest_ref, foreign_ref, partial_ref, owner_ref, slot_ref,
    prefix_ref, suffix_ref, pool_ref, hidden_ref, down_ref, pages, lists, table, sems,
):
    n_req = lax.axis_size("req")
    head_idx = lax.axis_index("head")
    req_idx = lax.axis_index("req")
    seq_idx = lax.axis_index("seq")
    n_pages = owner_ref.shape[1]
    pool_pages, pairs, pair_width = pages.shape
    chunk = first_ref.shape[0]
    loads = [
        pltpu.make_async_copy(owner_hbm, owner_ref, sems.at[0]),
        pltpu.make_async_copy(slot_hbm, slot_ref, sems.at[1]),
        pltpu.make_async_copy(pool_hbm, pool_ref, sems.at[2]),
        pltpu.make_async_copy(hidden_hbm, hidden_ref, sems.at[6]),
        pltpu.make_async_copy(down_hbm, down_ref, sems.at[7]),
        pltpu.make_async_copy(prefix_hbm, prefix_ref, sems.at[8]),
        pltpu.make_async_copy(suffix_hbm, suffix_ref, sems.at[9]),
    ]
    for load in loads:
        load.start()
    loads[0].wait()
    loads[1].wait()
    loads[5].wait()
    loads[6].wait()
    length_ref[0] = prefix_ref[req_idx]
    live_ref[0] = suffix_ref[req_idx]
    self_owner = head_idx * n_req + req_idx
    n_owners = table.shape[1]
    for shift in range(n_req):
        for owner in range(n_owners):
            table[shift, owner] = 0
    founds = []
    most = jnp.int32(0)
    for shift in range(n_req):
        request = lax.rem(req_idx + shift, n_req)

        def note(page, found, shift=shift, request=request):
            owner = owner_ref[request, page]
            needed = page * page_len < prefix_ref[request]
            table[shift, owner] += needed.astype(jnp.int32)
            lists[shift, found] = slot_ref[request, page]
            return found + (needed & (owner == self_owner)).astype(jnp.int32)

        founds.append(lax.fori_loop(0, n_pages, note, jnp.int32(0), unroll=8))
        for place in range(n_owners // n_req):
            held = functools.reduce(jnp.add, [table[shift, place * n_req + i] for i in range(n_req)])
            early = jnp.minimum(table[shift, place * n_req + request], chunk)
            most = jnp.maximum(most, held - early)
    for shift in range(n_req):
        count_ref[shift] = table[0, head_idx * n_req + lax.rem(req_idx + n_req - shift, n_req)]
    most_ref[0] = most
    loads[2].wait()
    step = 16
    row = lax.broadcasted_iota(jnp.int32, (step * step, step * step), 0)
    column = lax.broadcasted_iota(jnp.int32, (step * step, step * step), 1)
    swap = ((row // step == column % step) & (row % step == column // step)).astype(jnp.bfloat16)
    for page in range(0, pool_pages, step):
        for pair in range(0, pairs, step):
            rows = jnp.concatenate(
                [
                    pool_ref[page : page + step, (pair + i) * pair_width : (pair + i + 1) * pair_width]
                    for i in range(step)
                ],
                axis=0,
            )
            turned = jnp.dot(swap, rows, preferred_element_type=jnp.float32).astype(jnp.bfloat16)
            pages[page : page + step, pair : pair + step, :] = turned.reshape(step, step, pair_width)

    def send(shift, rank, target, sem):
        slot = jnp.where(rank < founds[shift], lists[shift, rank], 0)
        pltpu.make_async_copy(pages.at[slot], target, sem).start()

    for rank in range(cap):
        if rank < chunk:
            send(0, rank, first_ref.at[rank], sems.at[3])
        else:
            send(0, rank, rest_ref.at[rank - chunk], sems.at[4])
    half_cap = foreign_ref.shape[1]
    for shift in range(1, n_req):
        for j in range(half_cap):
            send(shift, seq_idx * half_cap + j, foreign_ref.at[shift - 1, j], sems.at[5])
    loads[3].wait()
    loads[4].wait()
    partial_ref[...] = lax.dot_general(
        hidden_ref[...], down_ref[...], (((1,), (1,)), ((), ())), preferred_element_type=jnp.float32
    )
    pltpu.make_async_copy(first_ref, first_ref, sems.at[3]).wait()
    if cap > chunk:
        pltpu.make_async_copy(rest_ref, rest_ref, sems.at[4]).wait()
    pltpu.make_async_copy(foreign_ref, foreign_ref, sems.at[5]).wait()


def pick_pages(
    page_owner, page_slot, prefix_len, suffix_len, page_pool, hidden, down,
    cap, chunk, n_head, n_req, n_seq, pairs,
):
    pool_pages, page_width = page_pool.shape
    page = (pairs, page_width // pairs)
    return pl.pallas_call(
        functools.partial(pick_kernel, cap, 2 * pairs),
        out_shape=(
            jax.ShapeDtypeStruct((n_req,), jnp.int32),
            jax.ShapeDtypeStruct((1,), jnp.int32),
            jax.ShapeDtypeStruct((1,), jnp.int32),
            jax.ShapeDtypeStruct((1,), jnp.int32),
            jax.ShapeDtypeStruct((chunk, *page), jnp.bfloat16),
            jax.ShapeDtypeStruct((max(1, cap - chunk), *page), jnp.bfloat16),
            jax.ShapeDtypeStruct((n_req - 1, cap // n_seq, *page), jnp.bfloat16),
            jax.ShapeDtypeStruct((hidden.shape[0], down.shape[0]), jnp.float32),
        ),
        in_specs=[any_spec()] * 4 + [hbm_spec()] * 3,
        out_specs=(smem_spec(), smem_spec(), smem_spec(), smem_spec(), hbm_spec(), hbm_spec(), hbm_spec(), vmem_spec()),
        scratch_shapes=[
            pltpu.SMEM(page_owner.shape, jnp.int32),
            pltpu.SMEM(page_slot.shape, jnp.int32),
            pltpu.SMEM(prefix_len.shape, jnp.int32),
            pltpu.SMEM(suffix_len.shape, jnp.int32),
            pltpu.VMEM((pool_pages, page_width), jnp.bfloat16),
            pltpu.VMEM(hidden.shape, jnp.bfloat16),
            pltpu.VMEM(down.shape, jnp.bfloat16),
            pltpu.VMEM((pool_pages, *page), jnp.bfloat16),
            pltpu.SMEM((n_req, cap + 1), jnp.int32),
            pltpu.SMEM((n_req, n_head * n_req), jnp.int32),
            pltpu.SemaphoreType.DMA((10,)),
        ],
        compiler_params=pltpu.CompilerParams(vmem_limit_bytes=60 * MIB),
        cost_estimate=pl.CostEstimate(flops=10**9, bytes_accessed=6 * 10**6, transcendentals=0),
        name="pick_pages",
    )(page_owner, page_slot, prefix_len, suffix_len, page_pool, hidden, down)


def join_kernel(chunk, cap, count_ref, rest_ref, mine_ref, other_ref, *refs):
    n_req = count_ref.shape[0]
    targets, sems = refs[:-1], refs[-1]
    seq_idx = lax.axis_index("seq")
    half_cap = mine_ref.shape[1]
    excess = jnp.maximum(count_ref[0] - chunk, 0)
    j = 0
    for part, target in enumerate(targets):
        for place in range(target.shape[0]):

            def fetch(condition, source, target=target, place=place, part=part):
                @pl.when(condition)
                def _():
                    pltpu.make_async_copy(source, target.at[place], sems.at[part]).start()

            rank = jnp.int32(j)
            taken = rank < excess
            if cap > chunk:
                fetch(taken, rest_ref.at[jnp.minimum(rank, cap - chunk - 1)])
            rank = rank - excess
            for shift in range(1, n_req):
                here = jnp.logical_not(taken) & (rank < count_ref[shift])
                half = rank // half_cap
                slot = jnp.clip(rank - half * half_cap, 0, half_cap - 1)
                fetch(here & (half == seq_idx), mine_ref.at[shift - 1, slot])
                fetch(here & (half != seq_idx), other_ref.at[shift - 1, slot])
                taken = taken | here
                rank = rank - count_ref[shift]
            fetch(jnp.logical_not(taken), mine_ref.at[0, 0])
            j += 1
    for part, target in enumerate(targets):
        pltpu.make_async_copy(target, target, sems.at[part]).wait()


def join_pages(counts, rest, mine, other, chunk, cap, sizes):
    return pl.pallas_call(
        functools.partial(join_kernel, chunk, cap),
        out_shape=tuple(jax.ShapeDtypeStruct((size, *rest.shape[1:]), jnp.bfloat16) for size in sizes),
        in_specs=[smem_spec()] + [hbm_spec()] * 3,
        out_specs=(vmem_spec(),) * len(sizes),
        scratch_shapes=[pltpu.SemaphoreType.DMA((len(sizes),))],
        compiler_params=pltpu.CompilerParams(vmem_limit_bytes=10 * MIB),
        cost_estimate=pl.CostEstimate(flops=0, bytes_accessed=3 * 10**6, transcendentals=0),
        name="join_pages",
    )(counts, rest, mine, other)


def plan_kernel(page_len, chunk, owner_ref, prefix_ref, limit_ref):
    n_head = lax.axis_size("head")
    n_req = lax.axis_size("req")
    head_idx = lax.axis_index("head")
    req_idx = lax.axis_index("req")
    upward = 2 * lax.axis_index("seq") - 1
    n = owner_ref.shape[1]
    prefix = prefix_ref[req_idx]
    diagonal = lax.broadcasted_iota(jnp.int32, (n, n), 0) == lax.broadcasted_iota(jnp.int32, (n, n), 1)

    def column(values):
        return jnp.sum(jnp.where(diagonal, values, 0), axis=1, keepdims=True)

    owner = owner_ref[pl.ds(req_idx, 1), :]
    place = jnp.zeros_like(owner)
    for head in range(1, n_head):
        place = place + (owner >= head * n_req).astype(jnp.int32)
    shift = req_idx - (owner - place * n_req)
    shift = jnp.where(shift < 0, shift + n_req, shift)
    order = lax.broadcasted_iota(jnp.int32, (1, n), 1)
    needed = (order * page_len < prefix).astype(jnp.int32)
    key = shift * n + order
    together = (column(place) == place) & (column(needed) > 0)
    rank = jnp.sum((together & (column(key) < key)).astype(jnp.int32), axis=0, keepdims=True)
    held = jnp.sum((together & (column(shift) == 0)).astype(jnp.int32), axis=0, keepdims=True)
    early = (shift == 0) & (rank < chunk)
    within = jnp.where(early, rank, chunk + rank - jnp.minimum(held, chunk))
    away = place - head_idx
    distance = jnp.abs(away)
    origin = jnp.where(away * upward > 0, 2 * distance - 1, 2 * distance)
    origins = 2 * n_head - 1
    slot = jnp.where(
        within < chunk,
        origin * chunk + within,
        jnp.where(
            within < 3 * chunk,
            (origins + 2 * origin) * chunk + within - chunk,
            (3 * origins + origin) * chunk + within - 3 * chunk,
        ),
    )
    slot = column(jnp.where(needed > 0, slot, -1))
    tokens = column(jnp.clip(prefix - order * page_len, 0, page_len))
    lane = lax.broadcasted_iota(jnp.int32, (n, limit_ref.shape[1]), 1)
    limit_ref[...] = jnp.sum(jnp.where(lane == slot, tokens, 0), axis=0, keepdims=True)


def plan_blocks(page_owner, prefix_len, n_head, chunk, page_len):
    return pl.pallas_call(
        functools.partial(plan_kernel, page_len, chunk),
        out_shape=jax.ShapeDtypeStruct((1, 4 * (2 * n_head - 1) * chunk), jnp.int32),
        in_specs=[vmem_spec(), smem_spec()],
        out_specs=vmem_spec(),
        cost_estimate=pl.CostEstimate(flops=10**4, bytes_accessed=10**4, transcendentals=0),
        name="plan_blocks",
    )(page_owner, prefix_len)


def over_groups(most):
    n_groups = lax.axis_size("groups")
    passed = most
    for _ in range(n_groups - 1):
        passed = lax.ppermute(passed, "groups", [(i, (i + 1) % n_groups) for i in range(n_groups)])
        most = jnp.maximum(most, passed)
    return most[0]


def query_kernel(query_hbm, up_hbm, cosine_ref, sine_ref, out_ref, query_ref, up_ref, sems):
    loads = [
        pltpu.make_async_copy(query_hbm, query_ref, sems.at[0]),
        pltpu.make_async_copy(up_hbm, up_ref, sems.at[1]),
    ]
    for load in loads:
        load.start()
    for load in loads:
        load.wait()
    heads, nope_width, latent_width = up_ref.shape
    half_len, width = query_ref.shape
    query_width = width // heads
    half_rope = cosine_ref.shape[0]
    key_width = latent_width + 2 * half_rope
    for head in range(heads):
        part = slice(head * half_len, (head + 1) * half_len)
        both = query_ref[:, head * query_width : (head + 1) * query_width]
        latent = lax.dot_general(
            up_ref[head], both[:, :nope_width], (((0,), (1,)), ((), ())), preferred_element_type=jnp.float32
        )
        out_ref[:latent_width, part] = latent.astype(jnp.bfloat16)
        turned = both[:, nope_width:].astype(jnp.float32).T
        low, high = turned[:half_rope], turned[half_rope:]
        out_ref[latent_width : latent_width + half_rope, part] = (
            low * cosine_ref[...] - high * sine_ref[...]
        ).astype(jnp.bfloat16)
        out_ref[latent_width + half_rope : key_width, part] = (
            low * sine_ref[...] + high * cosine_ref[...]
        ).astype(jnp.bfloat16)
    rest = out_ref.shape[0] - key_width
    row = lax.broadcasted_iota(jnp.int32, (rest, out_ref.shape[1]), 0)
    out_ref[key_width:, :] = (row == 0).astype(jnp.bfloat16)


def turn_queries(queries, w_uk, cosine_table, sine_table, key_rows):
    heads, nope_width, latent_width = w_uk.shape
    rows = heads * queries.shape[0]
    return pl.pallas_call(
        query_kernel,
        out_shape=jax.ShapeDtypeStruct((key_rows, rows), jnp.bfloat16),
        in_specs=[any_spec()] * 2 + [vmem_spec()] * 2,
        out_specs=vmem_spec(),
        scratch_shapes=[
            pltpu.VMEM(queries.shape, jnp.bfloat16),
            pltpu.VMEM(w_uk.shape, jnp.bfloat16),
            pltpu.SemaphoreType.DMA((2,)),
        ],
        compiler_params=pltpu.CompilerParams(vmem_limit_bytes=60 * MIB),
        cost_estimate=pl.CostEstimate(
            flops=2 * rows * nope_width * latent_width, bytes_accessed=3 * 10**6, transcendentals=0
        ),
        name="turn_queries",
    )(queries, w_uk, cosine_table, sine_table)


def score_block(keys, queries_ref, target, note, highest, weight_sum, tile, scale, bias=None):
    parts = [slice(start, start + tile) for start in range(0, queries_ref.shape[1], tile)]

    def product(part):
        return jnp.dot(keys[...], queries_ref[:, part], preferred_element_type=jnp.float32)

    following = product(parts[0])
    for number, part in enumerate(parts):
        scores = following * scale
        if number + 1 < len(parts):
            following = product(parts[number + 1])
        if bias is not None:
            scores = scores + bias
        old = highest[:, part]
        new = jnp.maximum(old, jnp.max(scores, axis=0, keepdims=True))
        weights = jnp.exp2(scores - new)
        highest[:, part] = new
        weight_sum[:, part] = weight_sum[:, part] * jnp.exp2(old - new) + jnp.sum(
            weights, axis=0, keepdims=True
        )
        target[:, part] = weights
        note(part, new)


def block_limits(limit_ref, block, chunk):
    return [limit_ref[0, block * chunk + j] for j in range(chunk)]


def any_token(limit_ref, block, chunk):
    return functools.reduce(jnp.maximum, block_limits(limit_ref, block, chunk)) > 0


def load_block(block_ref, keys, limits, key_width):
    chunk, pairs, pair_width = block_ref.shape
    pair_rows = chunk * pairs
    page_rows = block_ref[...].reshape(pair_rows, pair_width)
    keys[:pair_rows, :key_width] = page_rows[:, :key_width]
    keys[pair_rows:, :key_width] = page_rows[:, key_width:]
    shape = (2 * pair_rows, keys.shape[1] - key_width)
    row = lax.broadcasted_iota(jnp.int32, shape, 0)
    pair_row = lax.rem(row, pair_rows)
    token = 2 * lax.rem(pair_row, pairs) + row // pair_rows
    limit = jnp.zeros_like(row)
    for j, value in enumerate(limits):
        limit = jnp.where(pair_row // pairs == j, value, limit)
    masked = (lax.broadcasted_iota(jnp.int32, shape, 1) == 0) & (token >= limit)
    keys[:, key_width:] = jnp.where(masked, MASKED, 0.0).astype(jnp.bfloat16)


def turn_values(keys, latent_width):
    return keys[:, :latent_width].T


def near_bias(n_keys, half_len, tile, live):
    seq_idx = lax.axis_index("seq")
    place = lax.broadcasted_iota(jnp.int32, (n_keys, tile), 0)
    query = lax.rem(lax.broadcasted_iota(jnp.int32, (n_keys, tile), 1), half_len) + seq_idx * half_len
    allowed = (place <= query) & (place < live)
    return jnp.where(allowed, 0.0, -jnp.inf)


def score_kernel(shape, base, n_sources, first, near, limit_ref, queries_ref, *refs):
    tile, scale, chunk, key_width = shape
    refs = list(refs)
    if not first:
        marks_in, sum_in, high_in = [refs.pop(0) for _ in range(3)]
        refs.pop(0), refs.pop(0)
    if near:
        live_ref, suffix_ref = refs.pop(0), refs.pop(0)
    sources = [refs.pop(0) for _ in range(n_sources)]
    weights_hbm, values_hbm, marks, weight_sum, highest = [refs.pop(0) for _ in range(5)]
    if near:
        near_weights, near_values, near_mark = [refs.pop(0) for _ in range(3)]
    blocks, keys, weights, values, load_sems, weight_sems, value_sems = [refs.pop(0) for _ in range(7)]
    n_blocks = blocks.shape[0]
    latent_width = values.shape[1]
    index = 0
    for source in sources:
        for i in range(source.shape[0] // chunk):
            pltpu.make_async_copy(
                source.at[i * chunk : (i + 1) * chunk], blocks.at[index], load_sems.at[index]
            ).start()
            index += 1
    if first:
        marks[...] = jnp.zeros_like(marks)
        weight_sum[...] = jnp.zeros_like(weight_sum)
        highest[...] = jnp.full_like(highest, LOWEST)
    else:
        marks[...] = marks_in[...]
        weight_sum[...] = sum_in[...]
        highest[...] = high_in[...]

    def stores(block):
        return (
            pltpu.make_async_copy(weights.at[block], weights_hbm.at[base + block], weight_sems.at[block]),
            pltpu.make_async_copy(values.at[block], values_hbm.at[base + block], value_sems.at[block]),
        )

    def one_block(block, carry):
        pltpu.make_async_copy(blocks.at[block], blocks.at[block], load_sems.at[block]).wait()

        @pl.when(any_token(limit_ref, base + block, chunk))
        def _():
            load_block(blocks.at[block], keys, block_limits(limit_ref, base + block, chunk), key_width)

            def note(part, new):
                marks[pl.ds(base + block, 1), part] = new

            score_block(
                keys, queries_ref, weights.at[block], note, highest, weight_sum, tile, scale
            )
            values[block] = turn_values(keys, latent_width)
            for copy in stores(block):
                copy.start()

        return carry

    lax.fori_loop(0, n_blocks, one_block, 0)
    if near:
        near_keys = refs.pop(0)
        n_near = suffix_ref.shape[0]
        near_keys[:, key_width:] = jnp.zeros_like(near_keys[:, key_width:])
        near_keys[:, :key_width] = suffix_ref[...]

        def note_near(part, new):
            near_mark[:, part] = new

        score_block(
            near_keys, queries_ref, near_weights, note_near, highest, weight_sum, tile, scale,
            near_bias(n_near, n_near // lax.axis_size("seq"), tile, live_ref[0]),
        )
        near_values[...] = turn_values(near_keys, latent_width)

    def one_wait(block, carry):
        @pl.when(any_token(limit_ref, base + block, chunk))
        def _():
            for copy in stores(block):
                copy.wait()

        return carry

    lax.fori_loop(0, n_blocks, one_wait, 0)


def score_part(base, total, limits, queries, sources, state, shape, latent_width, near=None):
    tile, scale, chunk, key_width = shape
    width, rows = queries.shape
    _, pairs, pair_width = sources[0].shape
    block_keys = 2 * chunk * pairs
    n_blocks = sum(s.shape[0] for s in sources) // chunk
    row = jax.ShapeDtypeStruct((1, rows), jnp.float32)
    out_shape = [
        jax.ShapeDtypeStruct((total, block_keys, rows), jnp.float32),
        jax.ShapeDtypeStruct((total, latent_width, block_keys), jnp.bfloat16),
        jax.ShapeDtypeStruct((total, rows), jnp.float32),
        row,
        row,
    ]
    out_specs = [hbm_spec(), hbm_spec(), vmem_spec(), vmem_spec(), vmem_spec()]
    operands = [limits, queries]
    specs = [smem_spec(), vmem_spec()]
    aliases = {}
    if state is not None:
        operands += [state[2], state[3], state[4], state[0], state[1]]
        specs += [vmem_spec()] * 3 + [hbm_spec()] * 2
        aliases = {5: 0, 6: 1}
    scratch = [
        pltpu.VMEM((n_blocks, chunk, pairs, pair_width), jnp.bfloat16),
        pltpu.VMEM((block_keys, width), jnp.bfloat16),
        pltpu.VMEM((n_blocks, block_keys, rows), jnp.float32),
        pltpu.VMEM((n_blocks, latent_width, block_keys), jnp.bfloat16),
        pltpu.SemaphoreType.DMA((n_blocks,)),
        pltpu.SemaphoreType.DMA((n_blocks,)),
        pltpu.SemaphoreType.DMA((n_blocks,)),
    ]
    if near is not None:
        near_keys = near[-1].shape[0]
        operands += list(near)
        specs += [smem_spec(), vmem_spec()]
        out_shape += [
            jax.ShapeDtypeStruct((near_keys, rows), jnp.float32),
            jax.ShapeDtypeStruct((latent_width, near_keys), jnp.bfloat16),
            row,
        ]
        out_specs += [vmem_spec()] * 3
        scratch.append(pltpu.VMEM((near_keys, width), jnp.bfloat16))
    operands += list(sources)
    specs += [hbm_spec()] * len(sources)
    work = n_blocks * block_keys * rows // 2
    return pl.pallas_call(
        functools.partial(score_kernel, shape, base, len(sources), state is None, near is not None),
        out_shape=tuple(out_shape),
        in_specs=specs,
        out_specs=tuple(out_specs),
        scratch_shapes=scratch,
        input_output_aliases=aliases,
        compiler_params=pltpu.CompilerParams(vmem_limit_bytes=54 * MIB),
        cost_estimate=pl.CostEstimate(
            flops=work, bytes_accessed=10**5, transcendentals=0
        ),
        name="score_part",
    )(*operands)


def finish_kernel(
    shape, depth, n_blocks, n_sources, limit_ref, queries_ref, marks, sum_in, high_in,
    near_weights, near_values, near_mark, live_ref, up_ref, weights_hbm, values_hbm, *refs,
):
    tile, scale, chunk, key_width = shape
    sources, refs = refs[:n_sources], refs[n_sources:]
    (
        out_ref, weight_sum, highest, total, blocks, keys, last_weights, last_values, last_marks,
        weights, values, used, load_sems, weight_sems, value_sems,
    ) = refs
    rows = queries_ref.shape[1]
    latent_width = total.shape[0]
    n_last = blocks.shape[0]
    index = 0
    for source in sources:
        for i in range(source.shape[0] // chunk):
            pltpu.make_async_copy(
                source.at[i * chunk : (i + 1) * chunk], blocks.at[index], load_sems.at[index]
            ).start()
            index += 1

    def list_block(block, count):
        used[count] = block
        return count + any_token(limit_ref, block, chunk).astype(jnp.int32)

    n_used = lax.fori_loop(0, n_blocks, list_block, jnp.int32(0))

    def fetches(number):
        place = lax.rem(number, depth)
        return (
            pltpu.make_async_copy(weights_hbm.at[used[number]], weights.at[place], weight_sems.at[place]),
            pltpu.make_async_copy(values_hbm.at[used[number]], values.at[place], value_sems.at[place]),
        )

    def fetch(number):
        @pl.when(number < n_used)
        def _():
            for copy in fetches(number):
                copy.start()

    for number in range(depth):
        fetch(jnp.int32(number))
    weight_sum[...] = sum_in[...]
    highest[...] = high_in[...]
    last_marks[...] = jnp.zeros_like(last_marks)

    def one_score(block, carry):
        pltpu.make_async_copy(blocks.at[block], blocks.at[block], load_sems.at[block]).wait()

        @pl.when(any_token(limit_ref, n_blocks + block, chunk))
        def _():
            load_block(blocks.at[block], keys, block_limits(limit_ref, n_blocks + block, chunk), key_width)

            def note(part, new):
                last_marks[pl.ds(block, 1), part] = new

            score_block(
                keys, queries_ref, last_weights.at[block], note, highest, weight_sum, tile, scale
            )
            last_values[block] = turn_values(keys, latent_width)

        return carry

    lax.fori_loop(0, n_last, one_score, 0)

    def add_block(weight_block, value_block, mark, begin=False):
        parts = [slice(start, start + tile) for start in range(0, rows, tile)]

        def scaled(part):
            factor = jnp.exp2(mark[:, part] - highest[:, part]) / weight_sum[:, part]
            return (weight_block[:, part] * factor).astype(jnp.bfloat16)

        following = scaled(parts[0])
        for number, part in enumerate(parts):
            added = jnp.dot(value_block[...], following, preferred_element_type=jnp.float32)
            if number + 1 < len(parts):
                following = scaled(parts[number + 1])
            total[:, part] = added if begin else total[:, part] + added

    add_block(near_weights, near_values, near_mark, begin=True)

    def one_add(number, carry):
        for copy in fetches(number):
            copy.wait()
        place = lax.rem(number, depth)
        add_block(weights.at[place], values.at[place], marks.at[pl.ds(used[number], 1)])
        fetch(number + depth)
        return carry

    lax.fori_loop(0, n_used, one_add, 0)

    def one_last(block, carry):
        @pl.when(any_token(limit_ref, n_blocks + block, chunk))
        def _():
            add_block(last_weights.at[block], last_values.at[block], last_marks.at[pl.ds(block, 1)])

        return carry

    lax.fori_loop(0, n_last, one_last, 0)
    heads, _, value_width = up_ref.shape
    half_len = out_ref.shape[0]
    steps = lax.broadcasted_iota(jnp.int32, (half_len, value_width), 0)
    steps = steps + lax.axis_index("seq") * half_len
    for head in range(heads):
        latent = total[:, head * half_len : (head + 1) * half_len].astype(jnp.bfloat16)
        raised = lax.dot_general(
            latent, up_ref[head], (((0,), (0,)), ((), ())), preferred_element_type=jnp.float32
        )
        out_ref[:, head * value_width : (head + 1) * value_width] = jnp.where(
            steps < live_ref[0], raised, 0.0
        ).astype(jnp.bfloat16)


def finish(n_blocks, limits, queries, state, near_state, sources, live, up_weight, half_len, shape):
    tile, scale, chunk, key_width = shape
    weights, values, marks, weight_sum, highest = state
    width, rows = queries.shape
    _, latent_width, block_keys = values.shape
    _, pairs, pair_width = sources[0].shape
    heads, _, value_width = up_weight.shape
    depth = 4
    n_last = sum(s.shape[0] for s in sources) // chunk
    row = pltpu.VMEM((1, rows), jnp.float32)
    work = (n_blocks // 2 + n_last) * block_keys * rows
    return pl.pallas_call(
        functools.partial(finish_kernel, shape, depth, n_blocks, len(sources)),
        out_shape=jax.ShapeDtypeStruct((half_len, heads * value_width), jnp.bfloat16),
        in_specs=[smem_spec()]
        + [vmem_spec()] * 7
        + [smem_spec(), vmem_spec()]
        + [hbm_spec()] * (2 + len(sources)),
        out_specs=vmem_spec(),
        scratch_shapes=[
            row,
            row,
            pltpu.VMEM((latent_width, rows), jnp.float32),
            pltpu.VMEM((n_last, chunk, pairs, pair_width), jnp.bfloat16),
            pltpu.VMEM((block_keys, width), jnp.bfloat16),
            pltpu.VMEM((n_last, block_keys, rows), jnp.float32),
            pltpu.VMEM((n_last, latent_width, block_keys), jnp.bfloat16),
            pltpu.VMEM((n_last, rows), jnp.float32),
            pltpu.VMEM((depth, block_keys, rows), jnp.float32),
            pltpu.VMEM((depth, latent_width, block_keys), jnp.bfloat16),
            pltpu.SMEM((n_blocks + depth + 1,), jnp.int32),
            pltpu.SemaphoreType.DMA((n_last,)),
            pltpu.SemaphoreType.DMA((depth,)),
            pltpu.SemaphoreType.DMA((depth,)),
        ],
        compiler_params=pltpu.CompilerParams(vmem_limit_bytes=54 * MIB),
        cost_estimate=pl.CostEstimate(
            flops=2 * work * latent_width, bytes_accessed=3 * 10**7, transcendentals=work // 4
        ),
        name="finish",
    )(
        limits, queries, marks, weight_sum, highest, *near_state, live, up_weight,
        weights, values, *sources,
    )


def local(
    queries,
    hidden,
    w_dkv,
    kv_gain,
    w_uk,
    value_up_weight,
    page_pool,
    page_owner,
    page_slot,
    prefix_len,
    suffix_len,
):
    n_head = lax.axis_size("head")
    n_req = lax.axis_size("req")
    n_seq = lax.axis_size("seq")
    head_idx = lax.axis_index("head")
    req_idx = lax.axis_index("req")
    seq_idx = lax.axis_index("seq")
    _, half_len, d_local = hidden.shape
    heads_dev, nope_width, latent_width = w_uk.shape
    lat_width = w_dkv.shape[1]
    rope_width = lat_width - latent_width
    query_width = queries.shape[2] // heads_dev
    page_width = page_pool.shape[1]
    page_len = page_width // lat_width
    pairs = page_len // 2
    pages_req = page_slot.shape[1]
    cap = max(2, 2 * pages_req // (n_head * n_req))
    chunk = n_req * cap // 4
    score_scale = float(query_width) ** (-0.5)

    owner_rows = page_owner[:, :, 0]
    counts, most, my_prefix, live, first, rest, foreign, partial_value = pick_pages(
        owner_rows, page_slot, prefix_len, suffix_len, page_pool, hidden[0], w_dkv.T,
        cap, chunk, n_head, n_req, n_seq, pairs,
    )
    swap_route = [(i, n_seq - 1 - i) for i in range(n_seq)]
    stream_route = []
    for i in range(n_head - 1):
        stream_route.append((i * n_seq, (i + 1) * n_seq))
        stream_route.append(((i + 1) * n_seq + 1, i * n_seq + 1))

    def swap(block):
        return lax.ppermute(block, "seq", swap_route)

    def stream(block):
        return lax.ppermute(block, ("head", "seq"), stream_route)

    positions = my_prefix + seq_idx * half_len + jnp.arange(half_len, dtype=jnp.int32)
    rows = heads_dev * half_len
    half_rope = rope_width // 2
    frequency = 10000.0 ** (-2.0 * jnp.arange(half_rope, dtype=jnp.float32) / rope_width)
    phases = frequency[:, None] * positions.astype(jnp.float32)[None, :]
    q_turned = turn_queries(queries[0], w_uk, jnp.cos(phases), jnp.sin(phases), lat_width + 64)

    arrived = [
        lax.ppermute(foreign[s - 1], "req", [(i, (i + s) % n_req) for i in range(n_req)])
        for s in range(1, n_req)
    ]
    early_steps = [stream(first)]
    share = half_len // n_head
    partials = lax.all_to_all(partial_value, "head", split_axis=0, concat_axis=0, tiled=True)
    limits = plan_blocks(owner_rows, prefix_len, n_head, chunk, page_len)
    partials, q_turned, limits, early_steps[0] = lax.optimization_barrier(
        (partials, q_turned, limits, early_steps[0])
    )
    summed = jnp.sum(partials.reshape(n_head, share, lat_width), axis=0)
    share_t = seq_idx * half_len + head_idx * share + jnp.arange(share, dtype=jnp.int32)
    latent = finish_latent(summed, my_prefix + share_t, share_t < live, kv_gain, latent_width)
    copies = jnp.concatenate([latent] * n_head, axis=0)
    fresh = lax.all_to_all(copies, "head", split_axis=0, concat_axis=0, tiled=True)
    for step in range(1, n_head - 1):
        early_steps.append(stream(early_steps[-1]))
    early_steps = [[block, None] for block in early_steps]
    for step in range(n_head - 2):
        early_steps[step][1] = swap(early_steps[step][0])
    mine = arrived[0][None] if n_req == 2 else jnp.stack(arrived)
    mine, partials = lax.optimization_barrier((mine, partials))
    other = swap(mine)
    middle, late = join_pages(counts, rest, mine, other, chunk, cap, (2 * chunk, chunk))
    middle, fresh = lax.optimization_barrier((middle, fresh))

    tile = 256 if rows % 256 == 0 and 256 % half_len == 0 else half_len
    shape = (tile, score_scale * math.log2(math.e), chunk, lat_width)
    last = n_head - 2
    near_state = ()
    extra = 4 + 1 + 2 * last
    total = 1 + 2 * (last + 1) + 2 + 4 * last + extra
    n_blocks = 0
    state = None

    def arrays_of(arrived_steps, steps):
        return [arrived_steps[step][side] for step in steps for side in range(2)]

    def score(arrays, near=None):
        nonlocal n_blocks, state, near_state
        result = score_part(
            n_blocks, total, limits, q_turned, arrays, state, shape, latent_width, near
        )
        state = result[:5]
        near_state = result[5:] or near_state
        n_blocks += sum(a.shape[0] for a in arrays) // chunk

    def tie(block):
        nonlocal state
        block, mark = lax.optimization_barrier((block, state[4]))
        state = (*state[:4], mark)
        return block

    middle, early_steps[last - 1][0] = lax.optimization_barrier((middle, early_steps[last - 1][0]))
    middle_steps = []
    block = stream(middle)
    for step in range(last + 1):
        received = block
        if step == 0:
            score([first] + arrays_of(early_steps, range(last)))
        elif step == 1:
            score(arrays_of(early_steps, [last]) + [middle] + arrays_of(middle_steps, [0]))
        else:
            score(
                arrays_of(middle_steps, [step - 1]), (live, suffix_latent) if step == last else None
            )
        received = tie(received)
        if step == 0:
            early_steps[last][0] = tie(early_steps[last][0])
            received, most = lax.optimization_barrier((received, most))
            most = over_groups(most)
            early_steps[last][1] = swap(early_steps[last][0])
            opposite = swap(fresh)
            suffix_latent = jnp.where(
                seq_idx == 0,
                jnp.concatenate([fresh, opposite], axis=0),
                jnp.concatenate([opposite, fresh], axis=0),
            )
        if step == last - 1:
            received, most = lax.optimization_barrier((received, most))
        if step < last:
            block = stream(received)
        middle_steps.append([received, swap(received)])

    last_arrays = arrays_of(middle_steps, [last])

    def end(blocks, final_arrays, current):
        return finish(
            blocks, limits, q_turned, current, near_state, final_arrays, live, value_up_weight, half_len, shape
        )

    def with_late(_):
        block = stream(late)
        arrays = last_arrays + [late]
        current, blocks = state, n_blocks
        for step in range(last + 1):
            received = block
            current = score_part(
                blocks, total, limits, q_turned, arrays, current, shape, latent_width
            )[:5]
            blocks += sum(a.shape[0] for a in arrays) // chunk
            received, mark = lax.optimization_barrier((received, current[4]))
            current = (*current[:4], mark)
            if step < last:
                block = stream(received)
            arrays = [received, swap(received)]
        return end(blocks, arrays, current)

    def without_late(_):
        return end(n_blocks, last_arrays, state)

    attn_out = lax.cond(most > 2 * chunk, with_late, without_late, 0)
    new_pages = fresh.reshape(1, half_len // page_len, page_len * lat_width)
    return (attn_out[None], new_pages)


def solution(mesh):
    placed = (
        P(("groups", "req"), "seq", "head"),
        P(("groups", "req"), "seq", "head"),
        P("head", None),
        P(),
        P("head", None, None),
        P("head", None, None),
        P(("groups", "head", "req"), None),
        P("groups", None, None),
        P("groups", None),
        P("groups"),
        P("groups"),
    )
    return jax.shard_map(
        local,
        mesh=mesh,
        in_specs=placed,
        out_specs=(P(("groups", "req"), "seq", "head"), P(("groups", "req"), "seq", None)),
        check_vma=False,
    )
```

```python
import functools
import math

import jax
import jax.numpy as jnp
from jax import lax
from jax.experimental import pallas as pl
from jax.experimental.pallas import tpu as pltpu
from jax.sharding import PartitionSpec as P

LOWEST = -1e30
MASKED = -1e38
MIB = 1024 * 1024


def rotate(vector, cosine_table, sine_table):
    half_width = vector.shape[-1] // 2
    first_half = vector[..., :half_width]
    second_half = vector[..., half_width:]
    return jnp.concatenate(
        [
            first_half * cosine_table - second_half * sine_table,
            first_half * sine_table + second_half * cosine_table,
        ],
        axis=-1,
    )


def angles(positions, rope_width):
    half_width = rope_width // 2
    frequency = 10000.0 ** (-2.0 * jnp.arange(half_width, dtype=jnp.float32) / rope_width)
    phases = positions.astype(jnp.float32)[:, None] * frequency[None, :]
    return (jnp.cos(phases), jnp.sin(phases))


def finish_latent(summed, positions, live_rows, kv_gain, latent_width):
    latent_part = summed[:, :latent_width]
    mean_square = jnp.mean(latent_part * latent_part, axis=-1, keepdims=True)
    normed = latent_part * lax.rsqrt(mean_square + 1e-06) * kv_gain
    cosine_table, sine_table = angles(positions, summed.shape[1] - latent_width)
    rotated = rotate(summed[:, latent_width:], cosine_table, sine_table)
    joined = jnp.concatenate([normed, rotated], axis=-1).astype(jnp.bfloat16)
    return jnp.where(live_rows[:, None], joined, jnp.zeros_like(joined))


def any_spec():
    return pl.BlockSpec(memory_space=pl.ANY)


def smem_spec():
    return pl.BlockSpec(memory_space=pltpu.SMEM)


def vmem_spec():
    return pl.BlockSpec(memory_space=pltpu.VMEM)


def hbm_spec():
    return pl.BlockSpec(memory_space=pltpu.HBM)


def pick_kernel(
    cap, page_len, owner_hbm, slot_hbm, prefix_hbm, suffix_hbm, pool_hbm, hidden_hbm, down_hbm, count_ref,
    most_ref, length_ref, live_ref, first_ref, rest_ref, foreign_ref, partial_ref, owner_ref, slot_ref,
    prefix_ref, suffix_ref, pool_ref, hidden_ref, down_ref, pages, lists, table, sems,
):
    n_req = lax.axis_size("req")
    head_idx = lax.axis_index("head")
    req_idx = lax.axis_index("req")
    seq_idx = lax.axis_index("seq")
    n_pages = owner_ref.shape[1]
    pool_pages, pairs, pair_width = pages.shape
    chunk = first_ref.shape[0]
    loads = [
        pltpu.make_async_copy(owner_hbm, owner_ref, sems.at[0]),
        pltpu.make_async_copy(slot_hbm, slot_ref, sems.at[1]),
        pltpu.make_async_copy(pool_hbm, pool_ref, sems.at[2]),
        pltpu.make_async_copy(hidden_hbm, hidden_ref, sems.at[6]),
        pltpu.make_async_copy(down_hbm, down_ref, sems.at[7]),
        pltpu.make_async_copy(prefix_hbm, prefix_ref, sems.at[8]),
        pltpu.make_async_copy(suffix_hbm, suffix_ref, sems.at[9]),
    ]
    for load in loads:
        load.start()
    loads[0].wait()
    loads[1].wait()
    loads[5].wait()
    loads[6].wait()
    length_ref[0] = prefix_ref[req_idx]
    live_ref[0] = suffix_ref[req_idx]
    self_owner = head_idx * n_req + req_idx
    n_owners = table.shape[1]
    for shift in range(n_req):
        for owner in range(n_owners):
            table[shift, owner] = 0
    founds = []
    most = jnp.int32(0)
    for shift in range(n_req):
        request = lax.rem(req_idx + shift, n_req)

        def note(page, found, shift=shift, request=request):
            owner = owner_ref[request, page]
            needed = page * page_len < prefix_ref[request]
            table[shift, owner] += needed.astype(jnp.int32)
            lists[shift, found] = slot_ref[request, page]
            return found + (needed & (owner == self_owner)).astype(jnp.int32)

        founds.append(lax.fori_loop(0, n_pages, note, jnp.int32(0), unroll=8))
        for place in range(n_owners // n_req):
            held = functools.reduce(jnp.add, [table[shift, place * n_req + i] for i in range(n_req)])
            early = jnp.minimum(table[shift, place * n_req + request], chunk)
            most = jnp.maximum(most, held - early)
    for shift in range(n_req):
        count_ref[shift] = table[0, head_idx * n_req + lax.rem(req_idx + n_req - shift, n_req)]
    most_ref[0] = most
    loads[2].wait()
    step = 16
    row = lax.broadcasted_iota(jnp.int32, (step * step, step * step), 0)
    column = lax.broadcasted_iota(jnp.int32, (step * step, step * step), 1)
    swap = ((row // step == column % step) & (row % step == column // step)).astype(jnp.bfloat16)
    for page in range(0, pool_pages, step):
        for pair in range(0, pairs, step):
            rows = jnp.concatenate(
                [
                    pool_ref[page : page + step, (pair + i) * pair_width : (pair + i + 1) * pair_width]
                    for i in range(step)
                ],
                axis=0,
            )
            turned = jnp.dot(swap, rows, preferred_element_type=jnp.float32).astype(jnp.bfloat16)
            pages[page : page + step, pair : pair + step, :] = turned.reshape(step, step, pair_width)

    def send(shift, rank, target, sem):
        slot = jnp.where(rank < founds[shift], lists[shift, rank], 0)
        pltpu.make_async_copy(pages.at[slot], target, sem).start()

    for rank in range(cap):
        if rank < chunk:
            send(0, rank, first_ref.at[rank], sems.at[3])
        else:
            send(0, rank, rest_ref.at[rank - chunk], sems.at[4])
    half_cap = foreign_ref.shape[1]
    for shift in range(1, n_req):
        for j in range(half_cap):
            send(shift, seq_idx * half_cap + j, foreign_ref.at[shift - 1, j], sems.at[5])
    loads[3].wait()
    loads[4].wait()
    partial_ref[...] = lax.dot_general(
        hidden_ref[...], down_ref[...], (((1,), (1,)), ((), ())), preferred_element_type=jnp.float32
    )
    pltpu.make_async_copy(first_ref, first_ref, sems.at[3]).wait()
    if cap > chunk:
        pltpu.make_async_copy(rest_ref, rest_ref, sems.at[4]).wait()
    pltpu.make_async_copy(foreign_ref, foreign_ref, sems.at[5]).wait()


def pick_pages(
    page_owner, page_slot, prefix_len, suffix_len, page_pool, hidden, down,
    cap, chunk, n_head, n_req, n_seq, pairs,
):
    pool_pages, page_width = page_pool.shape
    page = (pairs, page_width // pairs)
    return pl.pallas_call(
        functools.partial(pick_kernel, cap, 2 * pairs),
        out_shape=(
            jax.ShapeDtypeStruct((n_req,), jnp.int32),
            jax.ShapeDtypeStruct((1,), jnp.int32),
            jax.ShapeDtypeStruct((1,), jnp.int32),
            jax.ShapeDtypeStruct((1,), jnp.int32),
            jax.ShapeDtypeStruct((chunk, *page), jnp.bfloat16),
            jax.ShapeDtypeStruct((max(1, cap - chunk), *page), jnp.bfloat16),
            jax.ShapeDtypeStruct((n_req - 1, cap // n_seq, *page), jnp.bfloat16),
            jax.ShapeDtypeStruct((hidden.shape[0], down.shape[0]), jnp.float32),
        ),
        in_specs=[any_spec()] * 4 + [hbm_spec()] * 3,
        out_specs=(smem_spec(), smem_spec(), smem_spec(), smem_spec(), hbm_spec(), hbm_spec(), hbm_spec(), vmem_spec()),
        scratch_shapes=[
            pltpu.SMEM(page_owner.shape, jnp.int32),
            pltpu.SMEM(page_slot.shape, jnp.int32),
            pltpu.SMEM(prefix_len.shape, jnp.int32),
            pltpu.SMEM(suffix_len.shape, jnp.int32),
            pltpu.VMEM((pool_pages, page_width), jnp.bfloat16),
            pltpu.VMEM(hidden.shape, jnp.bfloat16),
            pltpu.VMEM(down.shape, jnp.bfloat16),
            pltpu.VMEM((pool_pages, *page), jnp.bfloat16),
            pltpu.SMEM((n_req, cap + 1), jnp.int32),
            pltpu.SMEM((n_req, n_head * n_req), jnp.int32),
            pltpu.SemaphoreType.DMA((10,)),
        ],
        compiler_params=pltpu.CompilerParams(vmem_limit_bytes=60 * MIB),
        cost_estimate=pl.CostEstimate(flops=10**9, bytes_accessed=6 * 10**6, transcendentals=0),
        name="pick_pages",
    )(page_owner, page_slot, prefix_len, suffix_len, page_pool, hidden, down)


def join_kernel(chunk, cap, count_ref, rest_ref, mine_ref, other_ref, *refs):
    n_req = count_ref.shape[0]
    targets, sems = refs[:-1], refs[-1]
    seq_idx = lax.axis_index("seq")
    half_cap = mine_ref.shape[1]
    excess = jnp.maximum(count_ref[0] - chunk, 0)
    j = 0
    for part, target in enumerate(targets):
        for place in range(target.shape[0]):

            def fetch(condition, source, target=target, place=place, part=part):
                @pl.when(condition)
                def _():
                    pltpu.make_async_copy(source, target.at[place], sems.at[part]).start()

            rank = jnp.int32(j)
            taken = rank < excess
            if cap > chunk:
                fetch(taken, rest_ref.at[jnp.minimum(rank, cap - chunk - 1)])
            rank = rank - excess
            for shift in range(1, n_req):
                here = jnp.logical_not(taken) & (rank < count_ref[shift])
                half = rank // half_cap
                slot = jnp.clip(rank - half * half_cap, 0, half_cap - 1)
                fetch(here & (half == seq_idx), mine_ref.at[shift - 1, slot])
                fetch(here & (half != seq_idx), other_ref.at[shift - 1, slot])
                taken = taken | here
                rank = rank - count_ref[shift]
            fetch(jnp.logical_not(taken), mine_ref.at[0, 0])
            j += 1
    for part, target in enumerate(targets):
        pltpu.make_async_copy(target, target, sems.at[part]).wait()


def join_pages(counts, rest, mine, other, chunk, cap, sizes):
    return pl.pallas_call(
        functools.partial(join_kernel, chunk, cap),
        out_shape=tuple(jax.ShapeDtypeStruct((size, *rest.shape[1:]), jnp.bfloat16) for size in sizes),
        in_specs=[smem_spec()] + [hbm_spec()] * 3,
        out_specs=(vmem_spec(),) * len(sizes),
        scratch_shapes=[pltpu.SemaphoreType.DMA((len(sizes),))],
        compiler_params=pltpu.CompilerParams(vmem_limit_bytes=10 * MIB),
        cost_estimate=pl.CostEstimate(flops=0, bytes_accessed=3 * 10**6, transcendentals=0),
        name="join_pages",
    )(counts, rest, mine, other)


def plan_kernel(page_len, chunk, owner_ref, prefix_ref, limit_ref):
    n_head = lax.axis_size("head")
    n_req = lax.axis_size("req")
    head_idx = lax.axis_index("head")
    req_idx = lax.axis_index("req")
    upward = 2 * lax.axis_index("seq") - 1
    n = owner_ref.shape[1]
    prefix = prefix_ref[req_idx]
    diagonal = lax.broadcasted_iota(jnp.int32, (n, n), 0) == lax.broadcasted_iota(jnp.int32, (n, n), 1)

    def column(values):
        return jnp.sum(jnp.where(diagonal, values, 0), axis=1, keepdims=True)

    owner = owner_ref[pl.ds(req_idx, 1), :]
    place = jnp.zeros_like(owner)
    for head in range(1, n_head):
        place = place + (owner >= head * n_req).astype(jnp.int32)
    shift = req_idx - (owner - place * n_req)
    shift = jnp.where(shift < 0, shift + n_req, shift)
    order = lax.broadcasted_iota(jnp.int32, (1, n), 1)
    needed = (order * page_len < prefix).astype(jnp.int32)
    key = shift * n + order
    together = (column(place) == place) & (column(needed) > 0)
    rank = jnp.sum((together & (column(key) < key)).astype(jnp.int32), axis=0, keepdims=True)
    held = jnp.sum((together & (column(shift) == 0)).astype(jnp.int32), axis=0, keepdims=True)
    early = (shift == 0) & (rank < chunk)
    within = jnp.where(early, rank, chunk + rank - jnp.minimum(held, chunk))
    away = place - head_idx
    distance = jnp.abs(away)
    origin = jnp.where(away * upward > 0, 2 * distance - 1, 2 * distance)
    origins = 2 * n_head - 1
    slot = jnp.where(
        within < chunk,
        origin * chunk + within,
        jnp.where(
            within < 3 * chunk,
            (origins + 2 * origin) * chunk + within - chunk,
            (3 * origins + origin) * chunk + within - 3 * chunk,
        ),
    )
    slot = column(jnp.where(needed > 0, slot, -1))
    tokens = column(jnp.clip(prefix - order * page_len, 0, page_len))
    lane = lax.broadcasted_iota(jnp.int32, (n, limit_ref.shape[1]), 1)
    limit_ref[...] = jnp.sum(jnp.where(lane == slot, tokens, 0), axis=0, keepdims=True)


def plan_blocks(page_owner, prefix_len, n_head, chunk, page_len):
    return pl.pallas_call(
        functools.partial(plan_kernel, page_len, chunk),
        out_shape=jax.ShapeDtypeStruct((1, 4 * (2 * n_head - 1) * chunk), jnp.int32),
        in_specs=[vmem_spec(), smem_spec()],
        out_specs=vmem_spec(),
        cost_estimate=pl.CostEstimate(flops=10**4, bytes_accessed=10**4, transcendentals=0),
        name="plan_blocks",
    )(page_owner, prefix_len)


def over_groups(most):
    n_groups = lax.axis_size("groups")
    passed = most
    for _ in range(n_groups - 1):
        passed = lax.ppermute(passed, "groups", [(i, (i + 1) % n_groups) for i in range(n_groups)])
        most = jnp.maximum(most, passed)
    return most[0]


def query_kernel(query_hbm, up_hbm, cosine_ref, sine_ref, out_ref, query_ref, up_ref, sems):
    loads = [
        pltpu.make_async_copy(query_hbm, query_ref, sems.at[0]),
        pltpu.make_async_copy(up_hbm, up_ref, sems.at[1]),
    ]
    for load in loads:
        load.start()
    for load in loads:
        load.wait()
    heads, nope_width, latent_width = up_ref.shape
    half_len, width = query_ref.shape
    query_width = width // heads
    half_rope = cosine_ref.shape[0]
    key_width = latent_width + 2 * half_rope
    for head in range(heads):
        part = slice(head * half_len, (head + 1) * half_len)
        both = query_ref[:, head * query_width : (head + 1) * query_width]
        latent = lax.dot_general(
            up_ref[head], both[:, :nope_width], (((0,), (1,)), ((), ())), preferred_element_type=jnp.float32
        )
        out_ref[:latent_width, part] = latent.astype(jnp.bfloat16)
        turned = both[:, nope_width:].astype(jnp.float32).T
        low, high = turned[:half_rope], turned[half_rope:]
        out_ref[latent_width : latent_width + half_rope, part] = (
            low * cosine_ref[...] - high * sine_ref[...]
        ).astype(jnp.bfloat16)
        out_ref[latent_width + half_rope : key_width, part] = (
            low * sine_ref[...] + high * cosine_ref[...]
        ).astype(jnp.bfloat16)
    rest = out_ref.shape[0] - key_width
    row = lax.broadcasted_iota(jnp.int32, (rest, out_ref.shape[1]), 0)
    out_ref[key_width:, :] = (row == 0).astype(jnp.bfloat16)


def turn_queries(queries, w_uk, cosine_table, sine_table, key_rows):
    heads, nope_width, latent_width = w_uk.shape
    rows = heads * queries.shape[0]
    return pl.pallas_call(
        query_kernel,
        out_shape=jax.ShapeDtypeStruct((key_rows, rows), jnp.bfloat16),
        in_specs=[any_spec()] * 2 + [vmem_spec()] * 2,
        out_specs=vmem_spec(),
        scratch_shapes=[
            pltpu.VMEM(queries.shape, jnp.bfloat16),
            pltpu.VMEM(w_uk.shape, jnp.bfloat16),
            pltpu.SemaphoreType.DMA((2,)),
        ],
        compiler_params=pltpu.CompilerParams(vmem_limit_bytes=60 * MIB),
        cost_estimate=pl.CostEstimate(
            flops=2 * rows * nope_width * latent_width, bytes_accessed=3 * 10**6, transcendentals=0
        ),
        name="turn_queries",
    )(queries, w_uk, cosine_table, sine_table)


def score_block(keys, queries_ref, target, note, highest, weight_sum, tile, scale, bias=None):
    parts = [slice(start, start + tile) for start in range(0, queries_ref.shape[1], tile)]

    def product(part):
        return jnp.dot(keys[...], queries_ref[:, part], preferred_element_type=jnp.float32)

    following = product(parts[0])
    for number, part in enumerate(parts):
        scores = following * scale
        if number + 1 < len(parts):
            following = product(parts[number + 1])
        if bias is not None:
            scores = scores + bias
        old = highest[:, part]
        new = jnp.maximum(old, jnp.max(scores, axis=0, keepdims=True))
        weights = jnp.exp2(scores - new)
        highest[:, part] = new
        weight_sum[:, part] = weight_sum[:, part] * jnp.exp2(old - new) + jnp.sum(
            weights, axis=0, keepdims=True
        )
        target[:, part] = weights
        note(part, new)


def block_limits(limit_ref, block, chunk):
    return [limit_ref[0, block * chunk + j] for j in range(chunk)]


def any_token(limit_ref, block, chunk):
    return functools.reduce(jnp.maximum, block_limits(limit_ref, block, chunk)) > 0


def load_block(block_ref, keys, limits, key_width):
    chunk, pairs, pair_width = block_ref.shape
    pair_rows = chunk * pairs
    page_rows = block_ref[...].reshape(pair_rows, pair_width)
    keys[:pair_rows, :key_width] = page_rows[:, :key_width]
    keys[pair_rows:, :key_width] = page_rows[:, key_width:]
    shape = (2 * pair_rows, keys.shape[1] - key_width)
    row = lax.broadcasted_iota(jnp.int32, shape, 0)
    pair_row = lax.rem(row, pair_rows)
    token = 2 * lax.rem(pair_row, pairs) + row // pair_rows
    limit = jnp.zeros_like(row)
    for j, value in enumerate(limits):
        limit = jnp.where(pair_row // pairs == j, value, limit)
    masked = (lax.broadcasted_iota(jnp.int32, shape, 1) == 0) & (token >= limit)
    keys[:, key_width:] = jnp.where(masked, MASKED, 0.0).astype(jnp.bfloat16)


def turn_values(keys, latent_width):
    return keys[:, :latent_width].T


def near_bias(n_keys, half_len, tile, live):
    seq_idx = lax.axis_index("seq")
    place = lax.broadcasted_iota(jnp.int32, (n_keys, tile), 0)
    query = lax.rem(lax.broadcasted_iota(jnp.int32, (n_keys, tile), 1), half_len) + seq_idx * half_len
    allowed = (place <= query) & (place < live)
    return jnp.where(allowed, 0.0, -jnp.inf)


def score_kernel(shape, base, n_sources, first, near, limit_ref, queries_ref, *refs):
    tile, scale, chunk, key_width = shape
    refs = list(refs)
    if not first:
        marks_in, sum_in, high_in = [refs.pop(0) for _ in range(3)]
        refs.pop(0), refs.pop(0)
    if near:
        live_ref, suffix_ref = refs.pop(0), refs.pop(0)
    sources = [refs.pop(0) for _ in range(n_sources)]
    weights_hbm, values_hbm, marks, weight_sum, highest = [refs.pop(0) for _ in range(5)]
    if near:
        near_weights, near_values, near_mark = [refs.pop(0) for _ in range(3)]
    blocks, keys, weights, values, load_sems, weight_sems, value_sems = [refs.pop(0) for _ in range(7)]
    n_blocks = blocks.shape[0]
    latent_width = values.shape[1]
    index = 0
    for source in sources:
        for i in range(source.shape[0] // chunk):
            pltpu.make_async_copy(
                source.at[i * chunk : (i + 1) * chunk], blocks.at[index], load_sems.at[index]
            ).start()
            index += 1
    if first:
        marks[...] = jnp.zeros_like(marks)
        weight_sum[...] = jnp.zeros_like(weight_sum)
        highest[...] = jnp.full_like(highest, LOWEST)
    else:
        marks[...] = marks_in[...]
        weight_sum[...] = sum_in[...]
        highest[...] = high_in[...]

    def stores(block):
        return (
            pltpu.make_async_copy(weights.at[block], weights_hbm.at[base + block], weight_sems.at[block]),
            pltpu.make_async_copy(values.at[block], values_hbm.at[base + block], value_sems.at[block]),
        )

    def one_block(block, carry):
        pltpu.make_async_copy(blocks.at[block], blocks.at[block], load_sems.at[block]).wait()

        @pl.when(any_token(limit_ref, base + block, chunk))
        def _():
            load_block(blocks.at[block], keys, block_limits(limit_ref, base + block, chunk), key_width)

            def note(part, new):
                marks[pl.ds(base + block, 1), part] = new

            score_block(
                keys, queries_ref, weights.at[block], note, highest, weight_sum, tile, scale
            )
            values[block] = turn_values(keys, latent_width)
            for copy in stores(block):
                copy.start()

        return carry

    lax.fori_loop(0, n_blocks, one_block, 0)
    if near:
        near_keys = refs.pop(0)
        n_near = suffix_ref.shape[0]
        near_keys[:, key_width:] = jnp.zeros_like(near_keys[:, key_width:])
        near_keys[:, :key_width] = suffix_ref[...]

        def note_near(part, new):
            near_mark[:, part] = new

        score_block(
            near_keys, queries_ref, near_weights, note_near, highest, weight_sum, tile, scale,
            near_bias(n_near, n_near // lax.axis_size("seq"), tile, live_ref[0]),
        )
        near_values[...] = turn_values(near_keys, latent_width)

    def one_wait(block, carry):
        @pl.when(any_token(limit_ref, base + block, chunk))
        def _():
            for copy in stores(block):
                copy.wait()

        return carry

    lax.fori_loop(0, n_blocks, one_wait, 0)


def score_part(base, total, limits, queries, sources, state, shape, latent_width, near=None):
    tile, scale, chunk, key_width = shape
    width, rows = queries.shape
    _, pairs, pair_width = sources[0].shape
    block_keys = 2 * chunk * pairs
    n_blocks = sum(s.shape[0] for s in sources) // chunk
    row = jax.ShapeDtypeStruct((1, rows), jnp.float32)
    out_shape = [
        jax.ShapeDtypeStruct((total, block_keys, rows), jnp.float32),
        jax.ShapeDtypeStruct((total, latent_width, block_keys), jnp.bfloat16),
        jax.ShapeDtypeStruct((total, rows), jnp.float32),
        row,
        row,
    ]
    out_specs = [hbm_spec(), hbm_spec(), vmem_spec(), vmem_spec(), vmem_spec()]
    operands = [limits, queries]
    specs = [smem_spec(), vmem_spec()]
    aliases = {}
    if state is not None:
        operands += [state[2], state[3], state[4], state[0], state[1]]
        specs += [vmem_spec()] * 3 + [hbm_spec()] * 2
        aliases = {5: 0, 6: 1}
    scratch = [
        pltpu.VMEM((n_blocks, chunk, pairs, pair_width), jnp.bfloat16),
        pltpu.VMEM((block_keys, width), jnp.bfloat16),
        pltpu.VMEM((n_blocks, block_keys, rows), jnp.float32),
        pltpu.VMEM((n_blocks, latent_width, block_keys), jnp.bfloat16),
        pltpu.SemaphoreType.DMA((n_blocks,)),
        pltpu.SemaphoreType.DMA((n_blocks,)),
        pltpu.SemaphoreType.DMA((n_blocks,)),
    ]
    if near is not None:
        near_keys = near[-1].shape[0]
        operands += list(near)
        specs += [smem_spec(), vmem_spec()]
        out_shape += [
            jax.ShapeDtypeStruct((near_keys, rows), jnp.float32),
            jax.ShapeDtypeStruct((latent_width, near_keys), jnp.bfloat16),
            row,
        ]
        out_specs += [vmem_spec()] * 3
        scratch.append(pltpu.VMEM((near_keys, width), jnp.bfloat16))
    operands += list(sources)
    specs += [hbm_spec()] * len(sources)
    work = n_blocks * block_keys * rows // 2
    return pl.pallas_call(
        functools.partial(score_kernel, shape, base, len(sources), state is None, near is not None),
        out_shape=tuple(out_shape),
        in_specs=specs,
        out_specs=tuple(out_specs),
        scratch_shapes=scratch,
        input_output_aliases=aliases,
        compiler_params=pltpu.CompilerParams(vmem_limit_bytes=54 * MIB),
        cost_estimate=pl.CostEstimate(
            flops=work, bytes_accessed=10**5, transcendentals=0
        ),
        name="score_part",
    )(*operands)


def finish_kernel(
    shape, depth, n_blocks, n_sources, limit_ref, queries_ref, marks, sum_in, high_in,
    near_weights, near_values, near_mark, live_ref, up_ref, weights_hbm, values_hbm, *refs,
):
    tile, scale, chunk, key_width = shape
    sources, refs = refs[:n_sources], refs[n_sources:]
    (
        out_ref, weight_sum, highest, total, blocks, keys, last_weights, last_values, last_marks,
        weights, values, used, load_sems, weight_sems, value_sems,
    ) = refs
    rows = queries_ref.shape[1]
    latent_width = total.shape[0]
    n_last = blocks.shape[0]
    index = 0
    for source in sources:
        for i in range(source.shape[0] // chunk):
            pltpu.make_async_copy(
                source.at[i * chunk : (i + 1) * chunk], blocks.at[index], load_sems.at[index]
            ).start()
            index += 1

    def list_block(block, count):
        used[count] = block
        return count + any_token(limit_ref, block, chunk).astype(jnp.int32)

    n_used = lax.fori_loop(0, n_blocks, list_block, jnp.int32(0))

    def fetches(number):
        place = lax.rem(number, depth)
        return (
            pltpu.make_async_copy(weights_hbm.at[used[number]], weights.at[place], weight_sems.at[place]),
            pltpu.make_async_copy(values_hbm.at[used[number]], values.at[place], value_sems.at[place]),
        )

    def fetch(number):
        @pl.when(number < n_used)
        def _():
            for copy in fetches(number):
                copy.start()

    for number in range(depth):
        fetch(jnp.int32(number))
    weight_sum[...] = sum_in[...]
    highest[...] = high_in[...]
    last_marks[...] = jnp.zeros_like(last_marks)

    def one_score(block, carry):
        pltpu.make_async_copy(blocks.at[block], blocks.at[block], load_sems.at[block]).wait()

        @pl.when(any_token(limit_ref, n_blocks + block, chunk))
        def _():
            load_block(blocks.at[block], keys, block_limits(limit_ref, n_blocks + block, chunk), key_width)

            def note(part, new):
                last_marks[pl.ds(block, 1), part] = new

            score_block(
                keys, queries_ref, last_weights.at[block], note, highest, weight_sum, tile, scale
            )
            last_values[block] = turn_values(keys, latent_width)

        return carry

    lax.fori_loop(0, n_last, one_score, 0)

    def add_block(weight_block, value_block, mark, begin=False):
        parts = [slice(start, start + tile) for start in range(0, rows, tile)]

        def scaled(part):
            factor = jnp.exp2(mark[:, part] - highest[:, part]) / weight_sum[:, part]
            return (weight_block[:, part] * factor).astype(jnp.bfloat16)

        following = scaled(parts[0])
        for number, part in enumerate(parts):
            added = jnp.dot(value_block[...], following, preferred_element_type=jnp.float32)
            if number + 1 < len(parts):
                following = scaled(parts[number + 1])
            total[:, part] = added if begin else total[:, part] + added

    add_block(near_weights, near_values, near_mark, begin=True)

    def one_add(number, carry):
        for copy in fetches(number):
            copy.wait()
        place = lax.rem(number, depth)
        add_block(weights.at[place], values.at[place], marks.at[pl.ds(used[number], 1)])
        fetch(number + depth)
        return carry

    lax.fori_loop(0, n_used, one_add, 0)

    def one_last(block, carry):
        @pl.when(any_token(limit_ref, n_blocks + block, chunk))
        def _():
            add_block(last_weights.at[block], last_values.at[block], last_marks.at[pl.ds(block, 1)])

        return carry

    lax.fori_loop(0, n_last, one_last, 0)
    heads, _, value_width = up_ref.shape
    half_len = out_ref.shape[0]
    steps = lax.broadcasted_iota(jnp.int32, (half_len, value_width), 0)
    steps = steps + lax.axis_index("seq") * half_len
    for head in range(heads):
        latent = total[:, head * half_len : (head + 1) * half_len].astype(jnp.bfloat16)
        raised = lax.dot_general(
            latent, up_ref[head], (((0,), (0,)), ((), ())), preferred_element_type=jnp.float32
        )
        out_ref[:, head * value_width : (head + 1) * value_width] = jnp.where(
            steps < live_ref[0], raised, 0.0
        ).astype(jnp.bfloat16)


def finish(n_blocks, limits, queries, state, near_state, sources, live, up_weight, half_len, shape):
    tile, scale, chunk, key_width = shape
    weights, values, marks, weight_sum, highest = state
    width, rows = queries.shape
    _, latent_width, block_keys = values.shape
    _, pairs, pair_width = sources[0].shape
    heads, _, value_width = up_weight.shape
    depth = 8
    n_last = sum(s.shape[0] for s in sources) // chunk
    row = pltpu.VMEM((1, rows), jnp.float32)
    work = (n_blocks // 2 + n_last) * block_keys * rows
    return pl.pallas_call(
        functools.partial(finish_kernel, shape, depth, n_blocks, len(sources)),
        out_shape=jax.ShapeDtypeStruct((half_len, heads * value_width), jnp.bfloat16),
        in_specs=[smem_spec()]
        + [vmem_spec()] * 7
        + [smem_spec(), vmem_spec()]
        + [hbm_spec()] * (2 + len(sources)),
        out_specs=vmem_spec(),
        scratch_shapes=[
            row,
            row,
            pltpu.VMEM((latent_width, rows), jnp.float32),
            pltpu.VMEM((n_last, chunk, pairs, pair_width), jnp.bfloat16),
            pltpu.VMEM((block_keys, width), jnp.bfloat16),
            pltpu.VMEM((n_last, block_keys, rows), jnp.float32),
            pltpu.VMEM((n_last, latent_width, block_keys), jnp.bfloat16),
            pltpu.VMEM((n_last, rows), jnp.float32),
            pltpu.VMEM((depth, block_keys, rows), jnp.float32),
            pltpu.VMEM((depth, latent_width, block_keys), jnp.bfloat16),
            pltpu.SMEM((n_blocks + depth + 1,), jnp.int32),
            pltpu.SemaphoreType.DMA((n_last,)),
            pltpu.SemaphoreType.DMA((depth,)),
            pltpu.SemaphoreType.DMA((depth,)),
        ],
        compiler_params=pltpu.CompilerParams(vmem_limit_bytes=54 * MIB),
        cost_estimate=pl.CostEstimate(
            flops=2 * work * latent_width, bytes_accessed=3 * 10**7, transcendentals=work // 4
        ),
        name="finish",
    )(
        limits, queries, marks, weight_sum, highest, *near_state, live, up_weight,
        weights, values, *sources,
    )


def local(
    queries,
    hidden,
    w_dkv,
    kv_gain,
    w_uk,
    value_up_weight,
    page_pool,
    page_owner,
    page_slot,
    prefix_len,
    suffix_len,
):
    n_head = lax.axis_size("head")
    n_req = lax.axis_size("req")
    n_seq = lax.axis_size("seq")
    head_idx = lax.axis_index("head")
    req_idx = lax.axis_index("req")
    seq_idx = lax.axis_index("seq")
    _, half_len, d_local = hidden.shape
    heads_dev, nope_width, latent_width = w_uk.shape
    lat_width = w_dkv.shape[1]
    rope_width = lat_width - latent_width
    query_width = queries.shape[2] // heads_dev
    page_width = page_pool.shape[1]
    page_len = page_width // lat_width
    pairs = page_len // 2
    pages_req = page_slot.shape[1]
    cap = max(2, 2 * pages_req // (n_head * n_req))
    chunk = n_req * cap // 4
    score_scale = float(query_width) ** (-0.5)

    owner_rows = page_owner[:, :, 0]
    counts, most, my_prefix, live, first, rest, foreign, partial_value = pick_pages(
        owner_rows, page_slot, prefix_len, suffix_len, page_pool, hidden[0], w_dkv.T,
        cap, chunk, n_head, n_req, n_seq, pairs,
    )
    swap_route = [(i, n_seq - 1 - i) for i in range(n_seq)]
    stream_route = []
    for i in range(n_head - 1):
        stream_route.append((i * n_seq, (i + 1) * n_seq))
        stream_route.append(((i + 1) * n_seq + 1, i * n_seq + 1))

    def swap(block):
        return lax.ppermute(block, "seq", swap_route)

    def stream(block):
        return lax.ppermute(block, ("head", "seq"), stream_route)

    positions = my_prefix + seq_idx * half_len + jnp.arange(half_len, dtype=jnp.int32)
    rows = heads_dev * half_len
    half_rope = rope_width // 2
    frequency = 10000.0 ** (-2.0 * jnp.arange(half_rope, dtype=jnp.float32) / rope_width)
    phases = frequency[:, None] * positions.astype(jnp.float32)[None, :]
    q_turned = turn_queries(queries[0], w_uk, jnp.cos(phases), jnp.sin(phases), lat_width + 64)

    arrived = [
        lax.ppermute(foreign[s - 1], "req", [(i, (i + s) % n_req) for i in range(n_req)])
        for s in range(1, n_req)
    ]
    early_steps = [stream(first)]
    share = half_len // n_head
    limits = plan_blocks(owner_rows, prefix_len, n_head, chunk, page_len)
    partial_value, limits = lax.optimization_barrier((partial_value, limits))
    partials = lax.all_to_all(partial_value, "head", split_axis=0, concat_axis=0, tiled=True)
    partials, q_turned, limits, early_steps[0] = lax.optimization_barrier(
        (partials, q_turned, limits, early_steps[0])
    )
    summed = jnp.sum(partials.reshape(n_head, share, lat_width), axis=0)
    share_t = seq_idx * half_len + head_idx * share + jnp.arange(share, dtype=jnp.int32)
    latent = finish_latent(summed, my_prefix + share_t, share_t < live, kv_gain, latent_width)
    copies = jnp.concatenate([latent] * n_head, axis=0)
    fresh = lax.all_to_all(copies, "head", split_axis=0, concat_axis=0, tiled=True)
    for step in range(1, n_head - 1):
        early_steps.append(stream(early_steps[-1]))
    early_steps = [[block, None] for block in early_steps]
    for step in range(n_head - 2):
        early_steps[step][1] = swap(early_steps[step][0])
    mine = arrived[0][None] if n_req == 2 else jnp.stack(arrived)
    mine, partials = lax.optimization_barrier((mine, partials))
    other = swap(mine)
    middle, late = join_pages(counts, rest, mine, other, chunk, cap, (2 * chunk, chunk))
    middle, fresh = lax.optimization_barrier((middle, fresh))

    tile = 256 if rows % 256 == 0 and 256 % half_len == 0 else half_len
    shape = (tile, score_scale * math.log2(math.e), chunk, lat_width)
    last = n_head - 2
    near_state = ()
    extra = 4 + 1 + 2 * last
    total = 1 + 2 * (last + 1) + 2 + 4 * last + extra
    n_blocks = 0
    state = None

    def arrays_of(arrived_steps, steps):
        return [arrived_steps[step][side] for step in steps for side in range(2)]

    def score(arrays, near=None):
        nonlocal n_blocks, state, near_state
        result = score_part(
            n_blocks, total, limits, q_turned, arrays, state, shape, latent_width, near
        )
        state = result[:5]
        near_state = result[5:] or near_state
        n_blocks += sum(a.shape[0] for a in arrays) // chunk

    def tie(block):
        nonlocal state
        block, mark = lax.optimization_barrier((block, state[4]))
        state = (*state[:4], mark)
        return block

    middle, early_steps[last - 1][0] = lax.optimization_barrier((middle, early_steps[last - 1][0]))
    middle_steps = []
    block = stream(middle)
    for step in range(last + 1):
        received = block
        if step == 0:
            score([first] + arrays_of(early_steps, range(last)))
        elif step == 1:
            score(arrays_of(early_steps, [last]) + [middle] + arrays_of(middle_steps, [0]))
        else:
            score(
                arrays_of(middle_steps, [step - 1]), (live, suffix_latent) if step == last else None
            )
        received = tie(received)
        if step == 0:
            early_steps[last][0] = tie(early_steps[last][0])
            received, most = lax.optimization_barrier((received, most))
            most = over_groups(most)
            early_steps[last][1] = swap(early_steps[last][0])
            opposite = swap(fresh)
            suffix_latent = jnp.where(
                seq_idx == 0,
                jnp.concatenate([fresh, opposite], axis=0),
                jnp.concatenate([opposite, fresh], axis=0),
            )
        if step == last - 1:
            received, most = lax.optimization_barrier((received, most))
        if step < last:
            block = stream(received)
        middle_steps.append([received, swap(received)])

    last_arrays = arrays_of(middle_steps, [last])

    def end(blocks, final_arrays, current):
        return finish(
            blocks, limits, q_turned, current, near_state, final_arrays, live, value_up_weight, half_len, shape
        )

    def with_late(_):
        block = stream(late)
        arrays = last_arrays + [late]
        current, blocks = state, n_blocks
        for step in range(last + 1):
            received = block
            current = score_part(
                blocks, total, limits, q_turned, arrays, current, shape, latent_width
            )[:5]
            blocks += sum(a.shape[0] for a in arrays) // chunk
            received, mark = lax.optimization_barrier((received, current[4]))
            current = (*current[:4], mark)
            if step < last:
                block = stream(received)
            arrays = [received, swap(received)]
        return end(blocks, arrays, current)

    def without_late(_):
        return end(n_blocks, last_arrays, state)

    attn_out = lax.cond(most > 2 * chunk, with_late, without_late, 0)
    new_pages = fresh.reshape(1, half_len // page_len, page_len * lat_width)
    return (attn_out[None], new_pages)


def solution(mesh):
    placed = (
        P(("groups", "req"), "seq", "head"),
        P(("groups", "req"), "seq", "head"),
        P("head", None),
        P(),
        P("head", None, None),
        P("head", None, None),
        P(("groups", "head", "req"), None),
        P("groups", None, None),
        P("groups", None),
        P("groups"),
        P("groups"),
    )
    return jax.shard_map(
        local,
        mesh=mesh,
        in_specs=placed,
        out_specs=(P(("groups", "req"), "seq", "head"), P(("groups", "req"), "seq", None)),
        check_vma=False,
    )
```

```python
import functools
import math

import jax
import jax.numpy as jnp
from jax import lax
from jax.experimental import pallas as pl
from jax.experimental.pallas import tpu as pltpu
from jax.sharding import PartitionSpec as P

LOWEST = -1e30
MASKED = -1e38
MIB = 1024 * 1024


def rotate(vector, cosine_table, sine_table):
    half_width = vector.shape[-1] // 2
    first_half = vector[..., :half_width]
    second_half = vector[..., half_width:]
    return jnp.concatenate(
        [
            first_half * cosine_table - second_half * sine_table,
            first_half * sine_table + second_half * cosine_table,
        ],
        axis=-1,
    )


def angles(positions, rope_width):
    half_width = rope_width // 2
    frequency = 10000.0 ** (-2.0 * jnp.arange(half_width, dtype=jnp.float32) / rope_width)
    phases = positions.astype(jnp.float32)[:, None] * frequency[None, :]
    return (jnp.cos(phases), jnp.sin(phases))


def finish_latent(summed, positions, live_rows, kv_gain, latent_width):
    latent_part = summed[:, :latent_width]
    mean_square = jnp.mean(latent_part * latent_part, axis=-1, keepdims=True)
    normed = latent_part * lax.rsqrt(mean_square + 1e-06) * kv_gain
    cosine_table, sine_table = angles(positions, summed.shape[1] - latent_width)
    rotated = rotate(summed[:, latent_width:], cosine_table, sine_table)
    joined = jnp.concatenate([normed, rotated], axis=-1).astype(jnp.bfloat16)
    return jnp.where(live_rows[:, None], joined, jnp.zeros_like(joined))


def any_spec():
    return pl.BlockSpec(memory_space=pl.ANY)


def smem_spec():
    return pl.BlockSpec(memory_space=pltpu.SMEM)


def vmem_spec():
    return pl.BlockSpec(memory_space=pltpu.VMEM)


def hbm_spec():
    return pl.BlockSpec(memory_space=pltpu.HBM)


def pick_kernel(
    cap, page_len, owner_hbm, slot_hbm, prefix_hbm, suffix_hbm, pool_hbm, hidden_hbm, down_hbm, count_ref,
    most_ref, length_ref, live_ref, first_ref, rest_ref, foreign_ref, partial_ref, owner_ref, slot_ref,
    prefix_ref, suffix_ref, pool_ref, hidden_ref, down_ref, pages, lists, table, sems,
):
    n_req = lax.axis_size("req")
    head_idx = lax.axis_index("head")
    req_idx = lax.axis_index("req")
    seq_idx = lax.axis_index("seq")
    n_pages = owner_ref.shape[1]
    pool_pages, pairs, pair_width = pages.shape
    chunk = first_ref.shape[0]
    loads = [
        pltpu.make_async_copy(owner_hbm, owner_ref, sems.at[0]),
        pltpu.make_async_copy(slot_hbm, slot_ref, sems.at[1]),
        pltpu.make_async_copy(pool_hbm, pool_ref, sems.at[2]),
        pltpu.make_async_copy(hidden_hbm, hidden_ref, sems.at[6]),
        pltpu.make_async_copy(down_hbm, down_ref, sems.at[7]),
        pltpu.make_async_copy(prefix_hbm, prefix_ref, sems.at[8]),
        pltpu.make_async_copy(suffix_hbm, suffix_ref, sems.at[9]),
    ]
    for load in loads:
        load.start()
    loads[0].wait()
    loads[1].wait()
    loads[5].wait()
    loads[6].wait()
    length_ref[0] = prefix_ref[req_idx]
    live_ref[0] = suffix_ref[req_idx]
    self_owner = head_idx * n_req + req_idx
    n_owners = table.shape[1]
    for shift in range(n_req):
        for owner in range(n_owners):
            table[shift, owner] = 0
    founds = []
    most = jnp.int32(0)
    for shift in range(n_req):
        request = lax.rem(req_idx + shift, n_req)

        def note(page, found, shift=shift, request=request):
            owner = owner_ref[request, page]
            needed = page * page_len < prefix_ref[request]
            table[shift, owner] += needed.astype(jnp.int32)
            lists[shift, found] = slot_ref[request, page]
            return found + (needed & (owner == self_owner)).astype(jnp.int32)

        founds.append(lax.fori_loop(0, n_pages, note, jnp.int32(0), unroll=8))
        for place in range(n_owners // n_req):
            held = functools.reduce(jnp.add, [table[shift, place * n_req + i] for i in range(n_req)])
            early = jnp.minimum(table[shift, place * n_req + request], chunk)
            most = jnp.maximum(most, held - early)
    for shift in range(n_req):
        count_ref[shift] = table[0, head_idx * n_req + lax.rem(req_idx + n_req - shift, n_req)]
    most_ref[0] = most
    loads[2].wait()
    step = 16
    row = lax.broadcasted_iota(jnp.int32, (step * step, step * step), 0)
    column = lax.broadcasted_iota(jnp.int32, (step * step, step * step), 1)
    swap = ((row // step == column % step) & (row % step == column // step)).astype(jnp.bfloat16)
    for page in range(0, pool_pages, step):
        for pair in range(0, pairs, step):
            rows = jnp.concatenate(
                [
                    pool_ref[page : page + step, (pair + i) * pair_width : (pair + i + 1) * pair_width]
                    for i in range(step)
                ],
                axis=0,
            )
            turned = jnp.dot(swap, rows, preferred_element_type=jnp.float32).astype(jnp.bfloat16)
            pages[page : page + step, pair : pair + step, :] = turned.reshape(step, step, pair_width)

    def send(shift, rank, target, sem):
        slot = jnp.where(rank < founds[shift], lists[shift, rank], 0)
        pltpu.make_async_copy(pages.at[slot], target, sem).start()

    for rank in range(cap):
        if rank < chunk:
            send(0, rank, first_ref.at[rank], sems.at[3])
        else:
            send(0, rank, rest_ref.at[rank - chunk], sems.at[4])
    half_cap = foreign_ref.shape[1]
    for shift in range(1, n_req):
        for j in range(half_cap):
            send(shift, seq_idx * half_cap + j, foreign_ref.at[shift - 1, j], sems.at[5])
    loads[3].wait()
    loads[4].wait()
    partial_ref[...] = lax.dot_general(
        hidden_ref[...], down_ref[...], (((1,), (1,)), ((), ())), preferred_element_type=jnp.float32
    )
    pltpu.make_async_copy(first_ref, first_ref, sems.at[3]).wait()
    if cap > chunk:
        pltpu.make_async_copy(rest_ref, rest_ref, sems.at[4]).wait()
    pltpu.make_async_copy(foreign_ref, foreign_ref, sems.at[5]).wait()


def pick_pages(
    page_owner, page_slot, prefix_len, suffix_len, page_pool, hidden, down,
    cap, chunk, n_head, n_req, n_seq, pairs,
):
    pool_pages, page_width = page_pool.shape
    page = (pairs, page_width // pairs)
    return pl.pallas_call(
        functools.partial(pick_kernel, cap, 2 * pairs),
        out_shape=(
            jax.ShapeDtypeStruct((n_req,), jnp.int32),
            jax.ShapeDtypeStruct((1,), jnp.int32),
            jax.ShapeDtypeStruct((1,), jnp.int32),
            jax.ShapeDtypeStruct((1,), jnp.int32),
            jax.ShapeDtypeStruct((chunk, *page), jnp.bfloat16),
            jax.ShapeDtypeStruct((max(1, cap - chunk), *page), jnp.bfloat16),
            jax.ShapeDtypeStruct((n_req - 1, cap // n_seq, *page), jnp.bfloat16),
            jax.ShapeDtypeStruct((hidden.shape[0], down.shape[0]), jnp.float32),
        ),
        in_specs=[any_spec()] * 4 + [hbm_spec()] * 3,
        out_specs=(smem_spec(), smem_spec(), smem_spec(), smem_spec(), hbm_spec(), hbm_spec(), hbm_spec(), vmem_spec()),
        scratch_shapes=[
            pltpu.SMEM(page_owner.shape, jnp.int32),
            pltpu.SMEM(page_slot.shape, jnp.int32),
            pltpu.SMEM(prefix_len.shape, jnp.int32),
            pltpu.SMEM(suffix_len.shape, jnp.int32),
            pltpu.VMEM((pool_pages, page_width), jnp.bfloat16),
            pltpu.VMEM(hidden.shape, jnp.bfloat16),
            pltpu.VMEM(down.shape, jnp.bfloat16),
            pltpu.VMEM((pool_pages, *page), jnp.bfloat16),
            pltpu.SMEM((n_req, cap + 1), jnp.int32),
            pltpu.SMEM((n_req, n_head * n_req), jnp.int32),
            pltpu.SemaphoreType.DMA((10,)),
        ],
        compiler_params=pltpu.CompilerParams(vmem_limit_bytes=60 * MIB),
        cost_estimate=pl.CostEstimate(flops=10**9, bytes_accessed=6 * 10**6, transcendentals=0),
        name="pick_pages",
    )(page_owner, page_slot, prefix_len, suffix_len, page_pool, hidden, down)


def join_kernel(chunk, cap, count_ref, rest_ref, mine_ref, other_ref, *refs):
    n_req = count_ref.shape[0]
    targets, sems = refs[:-1], refs[-1]
    seq_idx = lax.axis_index("seq")
    half_cap = mine_ref.shape[1]
    excess = jnp.maximum(count_ref[0] - chunk, 0)
    j = 0
    for part, target in enumerate(targets):
        for place in range(target.shape[0]):

            def fetch(condition, source, target=target, place=place, part=part):
                @pl.when(condition)
                def _():
                    pltpu.make_async_copy(source, target.at[place], sems.at[part]).start()

            rank = jnp.int32(j)
            taken = rank < excess
            if cap > chunk:
                fetch(taken, rest_ref.at[jnp.minimum(rank, cap - chunk - 1)])
            rank = rank - excess
            for shift in range(1, n_req):
                here = jnp.logical_not(taken) & (rank < count_ref[shift])
                half = rank // half_cap
                slot = jnp.clip(rank - half * half_cap, 0, half_cap - 1)
                fetch(here & (half == seq_idx), mine_ref.at[shift - 1, slot])
                fetch(here & (half != seq_idx), other_ref.at[shift - 1, slot])
                taken = taken | here
                rank = rank - count_ref[shift]
            fetch(jnp.logical_not(taken), mine_ref.at[0, 0])
            j += 1
    for part, target in enumerate(targets):
        pltpu.make_async_copy(target, target, sems.at[part]).wait()


def join_pages(counts, rest, mine, other, chunk, cap, sizes):
    return pl.pallas_call(
        functools.partial(join_kernel, chunk, cap),
        out_shape=tuple(jax.ShapeDtypeStruct((size, *rest.shape[1:]), jnp.bfloat16) for size in sizes),
        in_specs=[smem_spec()] + [hbm_spec()] * 3,
        out_specs=(vmem_spec(),) * len(sizes),
        scratch_shapes=[pltpu.SemaphoreType.DMA((len(sizes),))],
        compiler_params=pltpu.CompilerParams(vmem_limit_bytes=10 * MIB),
        cost_estimate=pl.CostEstimate(flops=0, bytes_accessed=3 * 10**6, transcendentals=0),
        name="join_pages",
    )(counts, rest, mine, other)


def plan_kernel(page_len, chunk, owner_ref, prefix_ref, limit_ref):
    n_head = lax.axis_size("head")
    n_req = lax.axis_size("req")
    head_idx = lax.axis_index("head")
    req_idx = lax.axis_index("req")
    upward = 2 * lax.axis_index("seq") - 1
    n = owner_ref.shape[1]
    prefix = prefix_ref[req_idx]
    diagonal = lax.broadcasted_iota(jnp.int32, (n, n), 0) == lax.broadcasted_iota(jnp.int32, (n, n), 1)

    def column(values):
        return jnp.sum(jnp.where(diagonal, values, 0), axis=1, keepdims=True)

    owner = owner_ref[pl.ds(req_idx, 1), :]
    place = jnp.zeros_like(owner)
    for head in range(1, n_head):
        place = place + (owner >= head * n_req).astype(jnp.int32)
    shift = req_idx - (owner - place * n_req)
    shift = jnp.where(shift < 0, shift + n_req, shift)
    order = lax.broadcasted_iota(jnp.int32, (1, n), 1)
    needed = (order * page_len < prefix).astype(jnp.int32)
    key = shift * n + order
    together = (column(place) == place) & (column(needed) > 0)
    rank = jnp.sum((together & (column(key) < key)).astype(jnp.int32), axis=0, keepdims=True)
    held = jnp.sum((together & (column(shift) == 0)).astype(jnp.int32), axis=0, keepdims=True)
    early = (shift == 0) & (rank < chunk)
    within = jnp.where(early, rank, chunk + rank - jnp.minimum(held, chunk))
    away = place - head_idx
    distance = jnp.abs(away)
    origin = jnp.where(away * upward > 0, 2 * distance - 1, 2 * distance)
    origins = 2 * n_head - 1
    slot = jnp.where(
        within < chunk,
        origin * chunk + within,
        jnp.where(
            within < 3 * chunk,
            (origins + 2 * origin) * chunk + within - chunk,
            (3 * origins + origin) * chunk + within - 3 * chunk,
        ),
    )
    slot = column(jnp.where(needed > 0, slot, -1))
    tokens = column(jnp.clip(prefix - order * page_len, 0, page_len))
    lane = lax.broadcasted_iota(jnp.int32, (n, limit_ref.shape[1]), 1)
    limit_ref[...] = jnp.sum(jnp.where(lane == slot, tokens, 0), axis=0, keepdims=True)


def plan_blocks(page_owner, prefix_len, n_head, chunk, page_len):
    return pl.pallas_call(
        functools.partial(plan_kernel, page_len, chunk),
        out_shape=jax.ShapeDtypeStruct((1, 4 * (2 * n_head - 1) * chunk), jnp.int32),
        in_specs=[vmem_spec(), smem_spec()],
        out_specs=vmem_spec(),
        cost_estimate=pl.CostEstimate(flops=10**4, bytes_accessed=10**4, transcendentals=0),
        name="plan_blocks",
    )(page_owner, prefix_len)


def over_groups(most):
    n_groups = lax.axis_size("groups")
    passed = most
    for _ in range(n_groups - 1):
        passed = lax.ppermute(passed, "groups", [(i, (i + 1) % n_groups) for i in range(n_groups)])
        most = jnp.maximum(most, passed)
    return most[0]


def query_kernel(query_hbm, up_hbm, cosine_ref, sine_ref, out_ref, query_ref, up_ref, sems):
    loads = [
        pltpu.make_async_copy(query_hbm, query_ref, sems.at[0]),
        pltpu.make_async_copy(up_hbm, up_ref, sems.at[1]),
    ]
    for load in loads:
        load.start()
    for load in loads:
        load.wait()
    heads, nope_width, latent_width = up_ref.shape
    half_len, width = query_ref.shape
    query_width = width // heads
    half_rope = cosine_ref.shape[0]
    key_width = latent_width + 2 * half_rope
    for head in range(heads):
        part = slice(head * half_len, (head + 1) * half_len)
        both = query_ref[:, head * query_width : (head + 1) * query_width]
        latent = lax.dot_general(
            up_ref[head], both[:, :nope_width], (((0,), (1,)), ((), ())), preferred_element_type=jnp.float32
        )
        out_ref[:latent_width, part] = latent.astype(jnp.bfloat16)
        turned = both[:, nope_width:].astype(jnp.float32).T
        low, high = turned[:half_rope], turned[half_rope:]
        out_ref[latent_width : latent_width + half_rope, part] = (
            low * cosine_ref[...] - high * sine_ref[...]
        ).astype(jnp.bfloat16)
        out_ref[latent_width + half_rope : key_width, part] = (
            low * sine_ref[...] + high * cosine_ref[...]
        ).astype(jnp.bfloat16)
    rest = out_ref.shape[0] - key_width
    row = lax.broadcasted_iota(jnp.int32, (rest, out_ref.shape[1]), 0)
    out_ref[key_width:, :] = (row == 0).astype(jnp.bfloat16)


def turn_queries(queries, w_uk, cosine_table, sine_table, key_rows):
    heads, nope_width, latent_width = w_uk.shape
    rows = heads * queries.shape[0]
    return pl.pallas_call(
        query_kernel,
        out_shape=jax.ShapeDtypeStruct((key_rows, rows), jnp.bfloat16),
        in_specs=[any_spec()] * 2 + [vmem_spec()] * 2,
        out_specs=vmem_spec(),
        scratch_shapes=[
            pltpu.VMEM(queries.shape, jnp.bfloat16),
            pltpu.VMEM(w_uk.shape, jnp.bfloat16),
            pltpu.SemaphoreType.DMA((2,)),
        ],
        compiler_params=pltpu.CompilerParams(vmem_limit_bytes=60 * MIB),
        cost_estimate=pl.CostEstimate(
            flops=2 * rows * nope_width * latent_width, bytes_accessed=3 * 10**6, transcendentals=0
        ),
        name="turn_queries",
    )(queries, w_uk, cosine_table, sine_table)


def score_block(keys, queries_ref, target, note, highest, weight_sum, tile, scale, bias=None):
    parts = [slice(start, start + tile) for start in range(0, queries_ref.shape[1], tile)]

    def product(part):
        return jnp.dot(keys[...], queries_ref[:, part], preferred_element_type=jnp.float32)

    following = product(parts[0])
    for number, part in enumerate(parts):
        scores = following * scale
        if number + 1 < len(parts):
            following = product(parts[number + 1])
        if bias is not None:
            scores = scores + bias
        old = highest[:, part]
        new = jnp.maximum(old, jnp.max(scores, axis=0, keepdims=True))
        weights = jnp.exp2(scores - new)
        highest[:, part] = new
        weight_sum[:, part] = weight_sum[:, part] * jnp.exp2(old - new) + jnp.sum(
            weights, axis=0, keepdims=True
        )
        target[:, part] = weights
        note(part, new)


def block_limits(limit_ref, block, chunk):
    return [limit_ref[0, block * chunk + j] for j in range(chunk)]


def any_token(limit_ref, block, chunk):
    return functools.reduce(jnp.maximum, block_limits(limit_ref, block, chunk)) > 0


def load_block(block_ref, keys, limits, key_width):
    chunk, pairs, pair_width = block_ref.shape
    pair_rows = chunk * pairs
    page_rows = block_ref[...].reshape(pair_rows, pair_width)
    keys[:pair_rows, :key_width] = page_rows[:, :key_width]
    keys[pair_rows:, :key_width] = page_rows[:, key_width:]
    shape = (2 * pair_rows, keys.shape[1] - key_width)
    row = lax.broadcasted_iota(jnp.int32, shape, 0)
    pair_row = lax.rem(row, pair_rows)
    token = 2 * lax.rem(pair_row, pairs) + row // pair_rows
    limit = jnp.zeros_like(row)
    for j, value in enumerate(limits):
        limit = jnp.where(pair_row // pairs == j, value, limit)
    masked = (lax.broadcasted_iota(jnp.int32, shape, 1) == 0) & (token >= limit)
    keys[:, key_width:] = jnp.where(masked, MASKED, 0.0).astype(jnp.bfloat16)


def turn_values(keys, latent_width):
    return keys[:, :latent_width].T


def near_bias(n_keys, half_len, tile, live):
    seq_idx = lax.axis_index("seq")
    place = lax.broadcasted_iota(jnp.int32, (n_keys, tile), 0)
    query = lax.rem(lax.broadcasted_iota(jnp.int32, (n_keys, tile), 1), half_len) + seq_idx * half_len
    allowed = (place <= query) & (place < live)
    return jnp.where(allowed, 0.0, -jnp.inf)


def score_kernel(shape, base, n_sources, first, near, limit_ref, queries_ref, *refs):
    tile, scale, chunk, key_width = shape
    refs = list(refs)
    if not first:
        marks_in, sum_in, high_in = [refs.pop(0) for _ in range(3)]
        refs.pop(0), refs.pop(0)
    if near:
        live_ref, suffix_ref = refs.pop(0), refs.pop(0)
    sources = [refs.pop(0) for _ in range(n_sources)]
    weights_hbm, values_hbm, marks, weight_sum, highest = [refs.pop(0) for _ in range(5)]
    if near:
        near_weights, near_values, near_mark = [refs.pop(0) for _ in range(3)]
    blocks, keys, weights, values, load_sems, weight_sems, value_sems = [refs.pop(0) for _ in range(7)]
    n_blocks = blocks.shape[0]
    latent_width = values.shape[1]
    index = 0
    for source in sources:
        for i in range(source.shape[0] // chunk):
            pltpu.make_async_copy(
                source.at[i * chunk : (i + 1) * chunk], blocks.at[index], load_sems.at[index]
            ).start()
            index += 1
    if first:
        marks[...] = jnp.zeros_like(marks)
        weight_sum[...] = jnp.zeros_like(weight_sum)
        highest[...] = jnp.full_like(highest, LOWEST)
    else:
        marks[...] = marks_in[...]
        weight_sum[...] = sum_in[...]
        highest[...] = high_in[...]

    def stores(block):
        return (
            pltpu.make_async_copy(weights.at[block], weights_hbm.at[base + block], weight_sems.at[block]),
            pltpu.make_async_copy(values.at[block], values_hbm.at[base + block], value_sems.at[block]),
        )

    def one_block(block, carry):
        pltpu.make_async_copy(blocks.at[block], blocks.at[block], load_sems.at[block]).wait()

        @pl.when(any_token(limit_ref, base + block, chunk))
        def _():
            load_block(blocks.at[block], keys, block_limits(limit_ref, base + block, chunk), key_width)

            def note(part, new):
                marks[pl.ds(base + block, 1), part] = new

            score_block(
                keys, queries_ref, weights.at[block], note, highest, weight_sum, tile, scale
            )
            values[block] = turn_values(keys, latent_width)
            for copy in stores(block):
                copy.start()

        return carry

    lax.fori_loop(0, n_blocks, one_block, 0)
    if near:
        near_keys = refs.pop(0)
        n_near = suffix_ref.shape[0]
        near_keys[:, key_width:] = jnp.zeros_like(near_keys[:, key_width:])
        near_keys[:, :key_width] = suffix_ref[...]

        def note_near(part, new):
            near_mark[:, part] = new

        score_block(
            near_keys, queries_ref, near_weights, note_near, highest, weight_sum, tile, scale,
            near_bias(n_near, n_near // lax.axis_size("seq"), tile, live_ref[0]),
        )
        near_values[...] = turn_values(near_keys, latent_width)

    def one_wait(block, carry):
        @pl.when(any_token(limit_ref, base + block, chunk))
        def _():
            for copy in stores(block):
                copy.wait()

        return carry

    lax.fori_loop(0, n_blocks, one_wait, 0)


def score_part(base, total, limits, queries, sources, state, shape, latent_width, near=None):
    tile, scale, chunk, key_width = shape
    width, rows = queries.shape
    _, pairs, pair_width = sources[0].shape
    block_keys = 2 * chunk * pairs
    n_blocks = sum(s.shape[0] for s in sources) // chunk
    row = jax.ShapeDtypeStruct((1, rows), jnp.float32)
    out_shape = [
        jax.ShapeDtypeStruct((total, block_keys, rows), jnp.float32),
        jax.ShapeDtypeStruct((total, latent_width, block_keys), jnp.bfloat16),
        jax.ShapeDtypeStruct((total, rows), jnp.float32),
        row,
        row,
    ]
    out_specs = [hbm_spec(), hbm_spec(), vmem_spec(), vmem_spec(), vmem_spec()]
    operands = [limits, queries]
    specs = [smem_spec(), vmem_spec()]
    aliases = {}
    if state is not None:
        operands += [state[2], state[3], state[4], state[0], state[1]]
        specs += [vmem_spec()] * 3 + [hbm_spec()] * 2
        aliases = {5: 0, 6: 1}
    scratch = [
        pltpu.VMEM((n_blocks, chunk, pairs, pair_width), jnp.bfloat16),
        pltpu.VMEM((block_keys, width), jnp.bfloat16),
        pltpu.VMEM((n_blocks, block_keys, rows), jnp.float32),
        pltpu.VMEM((n_blocks, latent_width, block_keys), jnp.bfloat16),
        pltpu.SemaphoreType.DMA((n_blocks,)),
        pltpu.SemaphoreType.DMA((n_blocks,)),
        pltpu.SemaphoreType.DMA((n_blocks,)),
    ]
    if near is not None:
        near_keys = near[-1].shape[0]
        operands += list(near)
        specs += [smem_spec(), vmem_spec()]
        out_shape += [
            jax.ShapeDtypeStruct((near_keys, rows), jnp.float32),
            jax.ShapeDtypeStruct((latent_width, near_keys), jnp.bfloat16),
            row,
        ]
        out_specs += [vmem_spec()] * 3
        scratch.append(pltpu.VMEM((near_keys, width), jnp.bfloat16))
    operands += list(sources)
    specs += [hbm_spec()] * len(sources)
    work = n_blocks * block_keys * rows // 2
    return pl.pallas_call(
        functools.partial(score_kernel, shape, base, len(sources), state is None, near is not None),
        out_shape=tuple(out_shape),
        in_specs=specs,
        out_specs=tuple(out_specs),
        scratch_shapes=scratch,
        input_output_aliases=aliases,
        compiler_params=pltpu.CompilerParams(vmem_limit_bytes=54 * MIB),
        cost_estimate=pl.CostEstimate(
            flops=work, bytes_accessed=10**5, transcendentals=0
        ),
        name="score_part",
    )(*operands)


def finish_kernel(
    shape, depth, n_blocks, n_sources, limit_ref, queries_ref, marks, sum_in, high_in,
    near_weights, near_values, near_mark, live_ref, up_ref, weights_hbm, values_hbm, *refs,
):
    tile, scale, chunk, key_width = shape
    sources, refs = refs[:n_sources], refs[n_sources:]
    (
        out_ref, weight_sum, highest, total, blocks, keys, last_weights, last_values, last_marks,
        weights, values, used, load_sems, weight_sems, value_sems,
    ) = refs
    rows = queries_ref.shape[1]
    latent_width = total.shape[0]
    n_last = blocks.shape[0]
    index = 0
    for source in sources:
        for i in range(source.shape[0] // chunk):
            pltpu.make_async_copy(
                source.at[i * chunk : (i + 1) * chunk], blocks.at[index], load_sems.at[index]
            ).start()
            index += 1

    def list_block(block, count):
        used[count] = block
        return count + any_token(limit_ref, block, chunk).astype(jnp.int32)

    n_used = lax.fori_loop(0, n_blocks, list_block, jnp.int32(0))

    def fetches(number):
        place = lax.rem(number, depth)
        return (
            pltpu.make_async_copy(weights_hbm.at[used[number]], weights.at[place], weight_sems.at[place]),
            pltpu.make_async_copy(values_hbm.at[used[number]], values.at[place], value_sems.at[place]),
        )

    def fetch(number):
        @pl.when(number < n_used)
        def _():
            for copy in fetches(number):
                copy.start()

    for number in range(depth):
        fetch(jnp.int32(number))
    weight_sum[...] = sum_in[...]
    highest[...] = high_in[...]
    last_marks[...] = jnp.zeros_like(last_marks)

    def one_score(block, carry):
        pltpu.make_async_copy(blocks.at[block], blocks.at[block], load_sems.at[block]).wait()

        @pl.when(any_token(limit_ref, n_blocks + block, chunk))
        def _():
            load_block(blocks.at[block], keys, block_limits(limit_ref, n_blocks + block, chunk), key_width)

            def note(part, new):
                last_marks[pl.ds(block, 1), part] = new

            score_block(
                keys, queries_ref, last_weights.at[block], note, highest, weight_sum, tile, scale
            )
            last_values[block] = turn_values(keys, latent_width)

        return carry

    lax.fori_loop(0, n_last, one_score, 0)

    def add_block(weight_block, value_block, mark, begin=False):
        parts = [slice(start, start + tile) for start in range(0, rows, tile)]

        def scaled(part):
            factor = jnp.exp2(mark[:, part] - highest[:, part]) / weight_sum[:, part]
            return (weight_block[:, part] * factor).astype(jnp.bfloat16)

        following = scaled(parts[0])
        for number, part in enumerate(parts):
            added = jnp.dot(value_block[...], following, preferred_element_type=jnp.float32)
            if number + 1 < len(parts):
                following = scaled(parts[number + 1])
            total[:, part] = added if begin else total[:, part] + added

    add_block(near_weights, near_values, near_mark, begin=True)

    def one_add(number, carry):
        for copy in fetches(number):
            copy.wait()
        place = lax.rem(number, depth)
        add_block(weights.at[place], values.at[place], marks.at[pl.ds(used[number], 1)])
        fetch(number + depth)
        return carry

    lax.fori_loop(0, n_used, one_add, 0)

    def one_last(block, carry):
        @pl.when(any_token(limit_ref, n_blocks + block, chunk))
        def _():
            add_block(last_weights.at[block], last_values.at[block], last_marks.at[pl.ds(block, 1)])

        return carry

    lax.fori_loop(0, n_last, one_last, 0)
    heads, _, value_width = up_ref.shape
    half_len = out_ref.shape[0]
    steps = lax.broadcasted_iota(jnp.int32, (half_len, value_width), 0)
    steps = steps + lax.axis_index("seq") * half_len
    for head in range(heads):
        latent = total[:, head * half_len : (head + 1) * half_len].astype(jnp.bfloat16)
        raised = lax.dot_general(
            latent, up_ref[head], (((0,), (0,)), ((), ())), preferred_element_type=jnp.float32
        )
        out_ref[:, head * value_width : (head + 1) * value_width] = jnp.where(
            steps < live_ref[0], raised, 0.0
        ).astype(jnp.bfloat16)


def finish(n_blocks, limits, queries, state, near_state, sources, live, up_weight, half_len, shape):
    tile, scale, chunk, key_width = shape
    weights, values, marks, weight_sum, highest = state
    width, rows = queries.shape
    _, latent_width, block_keys = values.shape
    _, pairs, pair_width = sources[0].shape
    heads, _, value_width = up_weight.shape
    depth = 8
    n_last = sum(s.shape[0] for s in sources) // chunk
    row = pltpu.VMEM((1, rows), jnp.float32)
    work = (n_blocks // 2 + n_last) * block_keys * rows
    return pl.pallas_call(
        functools.partial(finish_kernel, shape, depth, n_blocks, len(sources)),
        out_shape=jax.ShapeDtypeStruct((half_len, heads * value_width), jnp.bfloat16),
        in_specs=[smem_spec()]
        + [vmem_spec()] * 7
        + [smem_spec(), vmem_spec()]
        + [hbm_spec()] * (2 + len(sources)),
        out_specs=vmem_spec(),
        scratch_shapes=[
            row,
            row,
            pltpu.VMEM((latent_width, rows), jnp.float32),
            pltpu.VMEM((n_last, chunk, pairs, pair_width), jnp.bfloat16),
            pltpu.VMEM((block_keys, width), jnp.bfloat16),
            pltpu.VMEM((n_last, block_keys, rows), jnp.float32),
            pltpu.VMEM((n_last, latent_width, block_keys), jnp.bfloat16),
            pltpu.VMEM((n_last, rows), jnp.float32),
            pltpu.VMEM((depth, block_keys, rows), jnp.float32),
            pltpu.VMEM((depth, latent_width, block_keys), jnp.bfloat16),
            pltpu.SMEM((n_blocks + depth + 1,), jnp.int32),
            pltpu.SemaphoreType.DMA((n_last,)),
            pltpu.SemaphoreType.DMA((depth,)),
            pltpu.SemaphoreType.DMA((depth,)),
        ],
        compiler_params=pltpu.CompilerParams(vmem_limit_bytes=54 * MIB),
        cost_estimate=pl.CostEstimate(
            flops=2 * work * latent_width, bytes_accessed=3 * 10**7, transcendentals=work // 4
        ),
        name="finish",
    )(
        limits, queries, marks, weight_sum, highest, *near_state, live, up_weight,
        weights, values, *sources,
    )


def local(
    queries,
    hidden,
    w_dkv,
    kv_gain,
    w_uk,
    value_up_weight,
    page_pool,
    page_owner,
    page_slot,
    prefix_len,
    suffix_len,
):
    n_head = lax.axis_size("head")
    n_req = lax.axis_size("req")
    n_seq = lax.axis_size("seq")
    head_idx = lax.axis_index("head")
    req_idx = lax.axis_index("req")
    seq_idx = lax.axis_index("seq")
    _, half_len, d_local = hidden.shape
    heads_dev, nope_width, latent_width = w_uk.shape
    lat_width = w_dkv.shape[1]
    rope_width = lat_width - latent_width
    query_width = queries.shape[2] // heads_dev
    page_width = page_pool.shape[1]
    page_len = page_width // lat_width
    pairs = page_len // 2
    pages_req = page_slot.shape[1]
    cap = max(2, 2 * pages_req // (n_head * n_req))
    chunk = n_req * cap // 4
    score_scale = float(query_width) ** (-0.5)

    owner_rows = page_owner[:, :, 0]
    counts, most, my_prefix, live, first, rest, foreign, partial_value = pick_pages(
        owner_rows, page_slot, prefix_len, suffix_len, page_pool, hidden[0], w_dkv.T,
        cap, chunk, n_head, n_req, n_seq, pairs,
    )
    swap_route = [(i, n_seq - 1 - i) for i in range(n_seq)]
    stream_route = []
    for i in range(n_head - 1):
        stream_route.append((i * n_seq, (i + 1) * n_seq))
        stream_route.append(((i + 1) * n_seq + 1, i * n_seq + 1))

    def swap(block):
        return lax.ppermute(block, "seq", swap_route)

    def stream(block):
        return lax.ppermute(block, ("head", "seq"), stream_route)

    positions = my_prefix + seq_idx * half_len + jnp.arange(half_len, dtype=jnp.int32)
    rows = heads_dev * half_len
    half_rope = rope_width // 2
    frequency = 10000.0 ** (-2.0 * jnp.arange(half_rope, dtype=jnp.float32) / rope_width)
    phases = frequency[:, None] * positions.astype(jnp.float32)[None, :]
    q_turned = turn_queries(queries[0], w_uk, jnp.cos(phases), jnp.sin(phases), lat_width + 64)

    arrived = [
        lax.ppermute(foreign[s - 1], "req", [(i, (i + s) % n_req) for i in range(n_req)])
        for s in range(1, n_req)
    ]
    early_steps = [stream(first)]
    share = half_len // n_head
    partials = lax.all_to_all(partial_value, "head", split_axis=0, concat_axis=0, tiled=True)
    limits = plan_blocks(owner_rows, prefix_len, n_head, chunk, page_len)
    partials, q_turned, limits, early_steps[0] = lax.optimization_barrier(
        (partials, q_turned, limits, early_steps[0])
    )
    summed = jnp.sum(partials.reshape(n_head, share, lat_width), axis=0)
    share_t = seq_idx * half_len + head_idx * share + jnp.arange(share, dtype=jnp.int32)
    latent = finish_latent(summed, my_prefix + share_t, share_t < live, kv_gain, latent_width)
    copies = jnp.concatenate([latent] * n_head, axis=0)
    fresh = lax.all_to_all(copies, "head", split_axis=0, concat_axis=0, tiled=True)
    for step in range(1, n_head - 1):
        early_steps.append(stream(early_steps[-1]))
    early_steps = [[block, None] for block in early_steps]
    for step in range(n_head - 2):
        early_steps[step][1] = swap(early_steps[step][0])
    mine = arrived[0][None] if n_req == 2 else jnp.stack(arrived)
    mine, partials = lax.optimization_barrier((mine, partials))
    other = swap(mine)
    middle, late = join_pages(counts, rest, mine, other, chunk, cap, (2 * chunk, chunk))
    middle, fresh = lax.optimization_barrier((middle, fresh))

    tile = 256 if rows % 256 == 0 and 256 % half_len == 0 else half_len
    shape = (tile, score_scale * math.log2(math.e), chunk, lat_width)
    last = n_head - 2
    near_state = ()
    extra = 4 + 1 + 2 * last
    total = 1 + 2 * (last + 1) + 2 + 4 * last + extra
    n_blocks = 0
    state = None

    def arrays_of(arrived_steps, steps):
        return [arrived_steps[step][side] for step in steps for side in range(2)]

    def score(arrays, near=None):
        nonlocal n_blocks, state, near_state
        result = score_part(
            n_blocks, total, limits, q_turned, arrays, state, shape, latent_width, near
        )
        state = result[:5]
        near_state = result[5:] or near_state
        n_blocks += sum(a.shape[0] for a in arrays) // chunk

    def tie(block):
        nonlocal state
        block, mark = lax.optimization_barrier((block, state[4]))
        state = (*state[:4], mark)
        return block

    middle, early_steps[last - 1][0] = lax.optimization_barrier((middle, early_steps[last - 1][0]))
    middle_steps = []
    block = stream(middle)
    for step in range(last + 1):
        received = block
        if step == 0:
            score([first] + arrays_of(early_steps, range(last)))
        elif step == 1:
            score(arrays_of(early_steps, [last]) + [middle] + arrays_of(middle_steps, [0]))
        else:
            score(
                arrays_of(middle_steps, [step - 1]), (live, suffix_latent) if step == last else None
            )
        received = tie(received)
        if step == 0:
            early_steps[last][0] = tie(early_steps[last][0])
            received, most = lax.optimization_barrier((received, most))
            most = over_groups(most)
            early_steps[last][1] = swap(early_steps[last][0])
            opposite = swap(fresh)
            suffix_latent = jnp.where(
                seq_idx == 0,
                jnp.concatenate([fresh, opposite], axis=0),
                jnp.concatenate([opposite, fresh], axis=0),
            )
        if step == last - 1:
            received, most = lax.optimization_barrier((received, most))
        if step < last:
            block = stream(received)
        middle_steps.append([received, swap(received)])

    last_arrays = arrays_of(middle_steps, [last])

    def end(blocks, final_arrays, current):
        return finish(
            blocks, limits, q_turned, current, near_state, final_arrays, live, value_up_weight, half_len, shape
        )

    def with_late(_):
        block = stream(late)
        arrays = last_arrays + [late]
        current, blocks = state, n_blocks
        for step in range(last + 1):
            received = block
            current = score_part(
                blocks, total, limits, q_turned, arrays, current, shape, latent_width
            )[:5]
            blocks += sum(a.shape[0] for a in arrays) // chunk
            received, mark = lax.optimization_barrier((received, current[4]))
            current = (*current[:4], mark)
            if step < last:
                block = stream(received)
            arrays = [received, swap(received)]
        return end(blocks, arrays, current)

    def without_late(_):
        return end(n_blocks, last_arrays, state)

    attn_out = lax.cond(most > 2 * chunk, with_late, without_late, 0)
    new_pages = fresh.reshape(1, half_len // page_len, page_len * lat_width)
    return (attn_out[None], new_pages)


def solution(mesh):
    placed = (
        P(("groups", "req"), "seq", "head"),
        P(("groups", "req"), "seq", "head"),
        P("head", None),
        P(),
        P("head", None, None),
        P("head", None, None),
        P(("groups", "head", "req"), None),
        P("groups", None, None),
        P("groups", None),
        P("groups"),
        P("groups"),
    )
    return jax.shard_map(
        local,
        mesh=mesh,
        in_specs=placed,
        out_specs=(P(("groups", "req"), "seq", "head"), P(("groups", "req"), "seq", None)),
        check_vma=False,
    )
```
